32 devices in a mesh: dp: 4 (over x, core), fsdp: 8 (over z, y).
Axes of the slice: x: 2, y: 2, z: 4, core: 2. Of those that a mesh axis runs over, the one named last changes fastest.
Arguments:
- tokens: bfloat16 [32, 512, 768], P(('dp', 'fsdp')), may hold values from -6 to 6
- lengths: int32 [32], P(('dp', 'fsdp')), may hold values from 8 to 512, as said below
- weight_shards: bfloat16 [7088640], P(('dp', 'fsdp')), may hold values from -1.6 to 1.6, as said below
- hidden_cotangent: bfloat16 [32, 512, 768], P(('dp', 'fsdp')), may hold values from -6 to 6
- nested_cotangent: float32 [32, 1728], P(('dp', 'fsdp')), may hold values from -6 to 6
Outputs:
- hidden_states: bfloat16 [32, 512, 768], P(('dp', 'fsdp'))
- nested_embedding: float32 [32, 1728], P(('dp', 'fsdp'))
- input_grad: float32 [32, 512, 768], P(('dp', 'fsdp'))
- weight_grad: float32 [7088640], P(('dp', 'fsdp'))
The draws below stay inside these ranges and needn't reach their ends.
Inputs may be any that keep to these rules, and one draw needn't show every extreme that they name: lengths[n] counts the real tokens of sentence n; slots from lengths[n] on are padding. `weight_shards`: the layer's parameters, laid out as in the reference program.
All inputs are finite; a program needn't handle non-finite values.
Results may differ from the reference program's by a relative error of at most 0.01.
Values may be sent and summed in bfloat16 or wider, within the bound.
A program may use at most 192 MiB of HBM per device.

```python
import math
import jax
import jax.numpy as jnp
from jax import lax

D = 768
H = 12
HD = 64
FF = 3072
LEN = 512
E2 = 512
E3 = 256
E4 = 128
E5 = 64
NEST = 1728
PARAMS = 7088640
SENT = 32


def draw_lengths(key, part):
    key = jax.random.fold_in(key, 5)
    first_key, second_key = jax.random.split(key)
    uniform_ints = jax.random.randint(first_key, (SENT,), 0, 256)
    distance = 256 - uniform_ints
    spans = 8 + (LEN - 8) * (65536 - distance * distance) // 65536
    chosen = jax.random.randint(second_key, (), 0, SENT)
    places = jnp.arange(SENT)
    spans = jnp.where(places == chosen, LEN, spans)
    spans = jnp.where(places == (chosen + 1) % SENT, 8, spans)
    return spans.astype(jnp.int32)


def draw_weight_shards(key, part):
    key = jax.random.fold_in(key, 7)
    plan = [(3 * D * D, D ** (-0.5), 0.0), (D, 0.3, 0.0), (D, 0.3, 0.0), (D * D, 4.0 * D ** (-0.5), 0.0), (D, 0.3, 0.0), (D, 0.15, 1.0), (D, 0.3, 0.0), (D * FF, D ** (-0.5), 0.0), (FF, 0.5, 0.0), (FF * D, FF ** (-0.5), 0.0), (D, 0.3, 0.0), (D, 0.15, 1.0), (D, 0.1, 0.0), (D, 0.15, 1.0), (D, 0.3, 0.0)]
    scales = jnp.concatenate([jnp.full((amount,), factor, jnp.float32) for amount, factor, middle in plan])
    centres = jnp.concatenate([jnp.full((amount,), middle, jnp.float32) for amount, factor, middle in plan])
    noise = jax.random.truncated_normal(key, -3.0, 3.0, (PARAMS,), jnp.float32)
    return (noise * scales + centres).astype(jnp.bfloat16)


def shard_levels(own_key, extent, shards, smallest, high):
    gain, own = 1.0, jax.random.fold_in(own_key, 6)
    for axis_at, parts in shards:
        draws = jnp.exp(jax.random.uniform(jax.random.fold_in(own, axis_at), (parts,), jnp.float32, smallest / len(shards), high / len(shards)))
        gain = gain * jnp.repeat(draws, extent[axis_at] // parts).reshape([-1 if axis == axis_at else 1 for axis in range(len(extent))])
    return gain


def scatter_about(stream_key, extent, scale, most, cuts=(), kind=jnp.bfloat16):
    values = scale * jax.random.normal(stream_key, extent, jnp.float32)
    if cuts:
        values = values * shard_levels(stream_key, extent, cuts, -0.22, 0.18)
    return jnp.clip(values, -most, most).astype(kind)


def setup_inputs(seed: int = 0) -> dict:
    streams_of = jax.random.split(jax.random.key(seed), 6)
    tokens = scatter_about(streams_of[0], (SENT, LEN, D), 1.0, 6.0, ((0, 32),))
    lengths = draw_lengths(jax.random.fold_in(streams_of[5], 71), 0)
    weight_shards = draw_weight_shards(jax.random.fold_in(streams_of[5], 71), 0)
    hidden_cotangent = scatter_about(streams_of[3], (SENT, LEN, D), 1.0, 6.0, ((0, 32),))
    nested_cotangent = scatter_about(streams_of[4], (SENT, NEST), 1.0, 6.0, ((0, 32),), jnp.float32)
    return dict(tokens=tokens, lengths=lengths, weight_shards=weight_shards, hidden_cotangent=hidden_cotangent, nested_cotangent=nested_cotangent)


@jax.custom_vjp
def low(v):
    return lax.optimization_barrier(v.astype(jnp.bfloat16)).astype(jnp.float32)

@jax.custom_vjp
def low_back(v):
    return v

def low_keep(v):
    return (low(v), None)

def low_pass(kept, grad):
    return (grad,)

def back_keep(v):
    return (v, None)

def back_low(kept, grad):
    return (low(grad),)
low.defvjp(low_keep, low_pass)
low_back.defvjp(back_keep, back_low)
epsilon = 1e-05

def layout(model_width, hidden_width):
    return [('w_qkv', (model_width, 3 * model_width)), ('q_bias', (model_width,)), ('v_bias', (model_width,)), ('w_out', (model_width, model_width)), ('out_bias', (model_width,)), ('first_gain', (model_width,)), ('first_shift', (model_width,)), ('w_up', (model_width, hidden_width)), ('up_bias', (hidden_width,)), ('w_down', (hidden_width, model_width)), ('down_bias', (model_width,)), ('second_gain', (model_width,)), ('second_shift', (model_width,)), ('exit_gain', (model_width,)), ('exit_shift', (model_width,))]

def unpack(flat_buffer, model_width, hidden_width):
    pieces = {}
    offset = 0
    for entry_name, extents in layout(model_width, hidden_width):
        amount = math.prod(extents)
        pieces[entry_name] = flat_buffer[offset:offset + amount].reshape(extents)
        offset = offset + amount
    return pieces

def product(left, right):
    return jnp.dot(left, right, precision=lax.Precision.HIGHEST, preferred_element_type=left.dtype)

def layer_norm(values, norm_gain, norm_shift):
    centred = values - lax.optimization_barrier(jnp.mean(values, axis=-1, keepdims=True))
    spread = lax.optimization_barrier(jnp.mean(centred * centred, axis=-1, keepdims=True))
    return centred * lax.rsqrt(spread + epsilon) * norm_gain + norm_shift

def nest(embedded):
    pieces = []
    for prefix in (D, E2, E3, E4, E5):
        window = embedded[..., :prefix]
        pieces.append(window * lax.rsqrt(lax.optimization_barrier(jnp.mean(window * window, axis=-1, keepdims=True)) + epsilon))
    return jnp.concatenate(pieces, axis=-1)

def forward(params, tokens_row, length):
    score_scale = 1.0 / math.sqrt(HD)
    token_valid = (jnp.arange(LEN) < length).astype(tokens_row.dtype)
    zeros_bias = jnp.zeros_like(params['q_bias'])
    projected = product(low(tokens_row), params['w_qkv']) + jnp.concatenate([params['q_bias'], zeros_bias, params['v_bias']])
    rounded = low_back(low(projected)).reshape(LEN, 3, H, HD)
    queries = rounded[:, 0]
    key_rows = rounded[:, 1]
    value_rows = rounded[:, 2]
    scores = jnp.einsum('qhd,khd->hqk', queries, key_rows, precision=lax.Precision.HIGHEST) * score_scale
    scores = low_back(jnp.where(token_valid[None, None, :] > 0, scores, -1000000000.0))
    attention = jax.nn.softmax(scores, axis=-1)
    mixed_rows = jnp.einsum('hqk,khd->qhd', low(attention), value_rows, precision=lax.Precision.HIGHEST).reshape(LEN, D)
    mixed_rows = low_back(low(mixed_rows))
    branch = low_back(product(mixed_rows, params['w_out']) + params['out_bias'])
    first_norm = layer_norm(tokens_row + branch, params['first_gain'], params['first_shift'])
    inner_sum = low_back(product(low(first_norm), params['w_up']) + params['up_bias'])
    activated = low(jax.nn.gelu(inner_sum, approximate=False))
    outer_sum = low_back(product(activated, params['w_down']) + params['down_bias'])
    second = layer_norm(first_norm + outer_sum, params['second_gain'], params['second_shift'])
    hidden = second * token_valid[:, None]
    pooled = lax.optimization_barrier(jnp.sum(hidden, axis=0)) / length.astype(hidden.dtype)
    embedded = layer_norm(pooled, params['exit_gain'], params['exit_shift'])
    return (hidden, nest(embedded))

def reference(tokens, lengths, weight_shards, hidden_cotangent, nested_cotangent):
    weights = unpack(weight_shards.astype(jnp.float32), D, FF)

    def one_sentence(totals, operands):
        tokens_row, length, hidden_cot, nested_cot = operands

        def local_forward(params, inputs_row):
            return forward(params, inputs_row, length)
        outputs, pullback = jax.vjp(local_forward, weights, tokens_row.astype(jnp.float32))
        weight_part, token_part = pullback((hidden_cot.astype(jnp.float32), nested_cot.astype(jnp.float32)))
        totals = jax.tree.map(jnp.add, totals, weight_part)
        return (totals, (outputs[0].astype(jnp.bfloat16), outputs[1], token_part))
    zeros_tree = jax.tree.map(jnp.zeros_like, weights)
    totals, results = lax.scan(one_sentence, zeros_tree, (tokens, lengths, hidden_cotangent, nested_cotangent))
    hidden_states, nested_embedding, input_grad = results
    weight_grad = jnp.concatenate([totals[entry_name].reshape(-1) for entry_name, extents in layout(D, FF)])
    return (hidden_states, nested_embedding, input_grad, weight_grad)
```

```python
import functools
import math

import jax
import jax.numpy as jnp
from jax import lax
from jax.experimental import pallas as pl
from jax.experimental.pallas import tpu as pltpu
from jax.sharding import PartitionSpec as P

AX = ("dp", "fsdp")
MESH = pl.DeviceIdType.MESH
D = 768
H = 12
HD = 64
FF = 3072
LEN = 512
E2 = 512
E3 = 256
E4 = 128
E5 = 64


epsilon = 1e-05


PAR=7088640; LN=128
class Plan: pass
def plan(n):
    p=Plan(); p.n=n; p.sh=PAR//n
    st=[i*p.sh for i in range(n)]
    p.g0=[s//LN//16 for s in st]
    p.g1=[(s+p.sh-1)//LN//16 for s in st]
    p.slot=16*max(b-a+1 for a,b in zip(p.g0,p.g1))
    p.rows_in=-(-p.sh//LN)
    return p
MATS=[("wqkv",0,D,18),("wo",13836,D,6),("w1",18462,D,24),("w2",36918,FF,6)]
VECS=[(13824,12),(18444,18),(36894,24),(55350,30)]

def build_slot_kernel(p,me_of,x_ref,o_ref,q_ref):
    i=me_of(); start=i*p.sh; r_first=start//LN; s=start-r_first*LN; r0=r_first%16
    lead=32
    q_ref[...]=jnp.zeros_like(q_ref)
    q=pltpu.roll(x_ref[...].astype(jnp.float32),s,1)
    q_ref[lead:lead+p.rows_in]=q
    lane=lax.broadcasted_iota(jnp.int32,(p.slot,LN),1)
    a=q_ref[pl.ds(lead-r0,p.slot),:]
    b=q_ref[pl.ds(lead-1-r0,p.slot),:]
    o_ref[...]=jnp.where(lane>=s,a,b).astype(jnp.bfloat16)

def build_slot(p,shard,me_of):
    x=jnp.pad(shard,(0,p.rows_in*LN-p.sh)).reshape(p.rows_in,LN)
    return pl.pallas_call(functools.partial(build_slot_kernel,p,me_of),out_shape=jax.ShapeDtypeStruct((p.slot,LN),jnp.bfloat16),
        scratch_shapes=[pltpu.VMEM((32+p.slot+32,LN),jnp.float32)])(x)

def load_flat(p,slots,F,g_lo,g_hi):
    for i in range(p.n):
        a=max(g_lo,p.g0[i]); b=min(g_hi,p.g1[i]+1)
        if a>=b: continue
        shared_first = i>0 and p.g0[i]==p.g1[i-1] and a==p.g0[i]
        a2=a+1 if shared_first else a
        b2=b
        if i+1<p.n and p.g1[i]==p.g0[i+1] and b==p.g1[i]+1: b2=b-1
        if i+1<p.n and b2<b and b-1>=g_lo:
            g=b-1
            F[16*(g-g_lo):16*(g-g_lo)+16]=slots[i,16*(g-p.g0[i]):16*(g-p.g0[i])+16].astype(jnp.float32)+slots[i+1,0:16].astype(jnp.float32)
        cnt=b2-a2
        if cnt<=0: continue
        U=16
        nb,rem=cnt//U,cnt%U
        def body(t,_,i=i,a2=a2):
            src=pl.multiple_of(16*(a2-p.g0[i])+t*16*U,16); dst=pl.multiple_of(16*(a2-g_lo)+t*16*U,16)
            F[pl.ds(dst,16*U)]=slots[i,pl.ds(src,16*U)].astype(jnp.float32)
            return 0
        lax.fori_loop(0,nb,body,0)
        if rem:
            src=16*(a2-p.g0[i])+nb*16*U; dst=16*(a2-g_lo)+nb*16*U
            F[dst:dst+16*rem]=slots[i,src:src+16*rem].astype(jnp.float32)
def tile_matrix(F,W,off,rows,w,RB=64):
    def body(t,_):
        r=pl.multiple_of(t*RB,RB)
        for j in range(w):
            W[pl.ds(r,RB),j*LN:(j+1)*LN]=F[pl.ds(off+r*w+j,RB,stride=w),:].astype(jnp.bfloat16)
        return 0
    lax.fori_loop(0,rows//RB,body,0)
def relayout_kernel(p,slots,wqkv,wo,w1,w2,vec,F):
    outs=dict(wqkv=wqkv,wo=wo,w1=w1,w2=w2)
    for name,base,rows,w in MATS:
        g_lo=base//16; g_hi=-(-(base+rows*w)//16)
        load_flat(p,slots,F,g_lo,g_hi)
        tile_matrix(F,outs[name],base-16*g_lo,rows,w)
    at=0
    for base,cnt in VECS:
        g_lo=base//16; g_hi=-(-(base+cnt)//16)
        load_flat(p,slots,F,g_lo,g_hi)
        vec[at:at+cnt]=F[base-16*g_lo:base-16*g_lo+cnt]
        at+=cnt
def relayout(p,slots):
    shp=[jax.ShapeDtypeStruct((r,w*LN),jnp.bfloat16) for _,_,r,w in MATS]+[jax.ShapeDtypeStruct((84,LN),jnp.float32)]
    return pl.pallas_call(functools.partial(relayout_kernel,p),out_shape=shp,
        scratch_shapes=[pltpu.VMEM((18432+32,LN),jnp.float32)],
        compiler_params=pltpu.CompilerParams(vmem_limit_bytes=58<<20))(slots)

def coords():
    dp=lax.axis_index("dp"); fs=lax.axis_index("fsdp")
    return dp//2,fs%2,fs//2,dp%2
def dev(x,y,z,c): return (x*2+c, z*2+y)
def lin(x,y,z,c): return (x*2+c)*8+z*2+y
def barrier(partners):
    bar=pltpu.get_barrier_semaphore()
    for q in partners: pl.semaphore_signal(bar,inc=1,device_id=q,device_id_type=MESH)
    pl.semaphore_wait(bar,len(partners))
def gather_kernel(p,slot_ref,G,ssem,rsem,lsem):
    x,y,z,c=coords(); me=lin(x,y,z,c)
    half=p.slot//32*16
    H=((0,half),(half,p.slot-half))
    px,py,pc=dev(1-x,y,z,c),dev(x,1-y,z,c),dev(x,y,z,1-c)
    def zz(d):
        if d==1: return z+1-2*(z%2)
        if d==2: return lax.rem(z+2,4)
        return 3-z
    barrier([px,py,pc]+[dev(x,y,zz(d),c) for d in (1,2,3)])
    n_send=[0]; pend=[]
    def send(src,dst,to,sl,h,who):
        r0,rn=(H[h] if h<2 else (0,p.slot))
        k=n_send[0]; n_send[0]+=1
        cp=pltpu.make_async_remote_copy(src_ref=src(r0,rn),dst_ref=G.at[sl,pl.ds(r0,rn)],send_sem=ssem.at[k],recv_sem=rsem.at[sl,h],device_id=to,device_id_type=MESH)
        cp.start(); pend.append(cp)
    def wait(sl,h):
        r0,rn=(H[h] if h<2 else (0,p.slot))
        pltpu.make_async_copy(G.at[sl,pl.ds(r0,rn)],G.at[sl,pl.ds(r0,rn)],rsem.at[sl,h]).wait()
    def from_own(r0,rn): return slot_ref.at[pl.ds(r0,rn)]
    def from_g(sl): return lambda r0,rn: G.at[sl,pl.ds(r0,rn)]
    for to in (px,py,dev(x,y,zz(1),c),dev(x,y,zz(2),c),dev(x,y,zz(3),c),pc):
        send(from_own,None,to,me,2,None)
    loc=pltpu.make_async_copy(slot_ref,G.at[me],lsem); loc.start()
    def fwd_x(zq):
        sl=lin(1-x,y,zq,c); wait(sl,2); send(from_g(sl),None,py,sl,0,None); send(from_g(sl),None,pc,sl,2,None)
    def fwd_y(zq):
        sl=lin(x,1-y,zq,c); wait(sl,2); send(from_g(sl),None,px,sl,1,None); send(from_g(sl),None,pc,sl,2,None)
    def fwd_z(zq):
        sl=lin(x,y,zq,c); wait(sl,2)
        for to in (px,py,pc): send(from_g(sl),None,to,sl,2,None)
    def fwd_d(zq):
        sl=lin(1-x,1-y,zq,c)
        for h in (0,1):
            wait(sl,h); send(from_g(sl),None,pc,sl,h,None)
    fwd_x(z); fwd_y(z)
    for d in (1,3,2): fwd_z(zz(d))
    fwd_d(z)
    for d in (1,3,2): fwd_x(zz(d)); fwd_y(zz(d))
    for d in (1,3,2): fwd_d(zz(d))
    for zq in [z]+[zz(d) for d in (1,3,2)]:
        for (a,b) in ((x,y),(1-x,y),(x,1-y)): wait(lin(a,b,zq,1-c),2)
    for zq in [z]+[zz(d) for d in (1,3,2)]:
        for h in (0,1): wait(lin(1-x,1-y,zq,1-c),h)
    loc.wait()
    for cp in pend: cp.wait_send()
def gather(p,slot):
    return pl.pallas_call(functools.partial(gather_kernel,p),out_shape=jax.ShapeDtypeStruct((p.n,p.slot,LN),jnp.bfloat16),
        in_specs=[pl.BlockSpec(memory_space=pl.ANY)],out_specs=pl.BlockSpec(memory_space=pl.ANY),
        scratch_shapes=[pltpu.SemaphoreType.DMA((40,)),pltpu.SemaphoreType.DMA((p.n,3)),pltpu.SemaphoreType.DMA],
        compiler_params=pltpu.CompilerParams(collective_id=0,has_side_effects=True))(slot)

TOT=PAR//LN
def flat_rows(p): return max(16*p.g0[-1]+p.slot, -(-TOT//16)*16)
def owner_row(rho):
    for k,(name,base,rows,w) in enumerate(MATS):
        if base<=rho<base+rows*w: return ("m",k,(rho-base)//w,(rho-base)%w)
    at=0
    for base,cnt in VECS:
        if base<=rho<base+cnt: return ("v",at+rho-base)
        at+=cnt
    return None
def untile_matrix(F,W,off,rows,w,RB=64):
    def body(t,_):
        r=pl.multiple_of(t*RB,RB)
        for j in range(w):
            F[pl.ds(off+r*w+j,RB,stride=w),:]=W[pl.ds(r,RB),j*LN:(j+1)*LN].astype(jnp.float32)
        return 0
    lax.fori_loop(0,rows//RB,body,0)
def store_flat(F,FG,f_row,g_row,rows,U=256):
    nb,rem=rows//U,rows%U
    def body(t,_):
        FG[pl.ds(pl.multiple_of(g_row+t*U,16),U)]=F[pl.ds(pl.multiple_of(f_row+t*U,16),U)].astype(jnp.bfloat16)
        return 0
    lax.fori_loop(0,nb,body,0)
    if rem: FG[g_row+nb*U:g_row+nb*U+rem]=F[f_row+nb*U:f_row+nb*U+rem].astype(jnp.bfloat16)
def flatten_kernel(p,wqkv,wo,w1,w2,vec,FG,F):
    ms=[wqkv,wo,w1,w2]
    end=flat_rows(p)
    def put(rho,lo):
        o=owner_row(rho)
        if o is None: F[rho-lo:rho-lo+1]=jnp.zeros((1,LN),jnp.float32)
        elif o[0]=="v": F[rho-lo:rho-lo+1]=vec[o[1]:o[1]+1]
        else: F[rho-lo:rho-lo+1]=ms[o[1]][o[2]:o[2]+1,o[3]*LN:(o[3]+1)*LN].astype(jnp.float32)
    cuts=[0,13824,18464,36928,end]
    for k,(name,base,rows,w) in enumerate(MATS):
        lo=cuts[k]//16*16; hi=cuts[k+1]
        f0=min(lo,base//16*16)
        untile_matrix(F,ms[k],base-f0,rows,w)
        for rho in list(range(lo,max(lo,base)))+list(range(base+rows*w,hi)): put(rho,f0)
        store_flat(F,FG,lo-f0,lo,hi-lo)
def flatten(p,dws,vec):
    return pl.pallas_call(functools.partial(flatten_kernel,p),out_shape=jax.ShapeDtypeStruct((flat_rows(p),LN),jnp.bfloat16),
        scratch_shapes=[pltpu.VMEM((18432+80,LN),jnp.float32)],
        compiler_params=pltpu.CompilerParams(vmem_limit_bytes=58<<20))(*dws,vec)

def scatter_kernel(p,FG,out,S,R,D0,D1,X,Y,Z,A,lsem,ssem,sib,dsem,xsem,ysem,zsem):
    x,y,z,c=coords(); me=lin(x,y,z,c)
    SL=p.slot
    half=SL//32*16
    px,py,pc=dev(1-x,y,z,c),dev(x,1-y,z,c),dev(x,y,z,1-c)
    def zz(d):
        if d==1: return z+1-2*(z%2)
        if d==2: return lax.rem(z+2,4)
        return 3-z
    pz={d:dev(x,y,zz(d),c) for d in (1,2,3)}
    pend=[]; ns=[0]
    def row0(i): return pl.multiple_of((i*p.sh)//LN//16*16,16)
    def send(src,dst,rsem,to):
        k=ns[0]; ns[0]+=1
        cp=pltpu.make_async_remote_copy(src_ref=src,dst_ref=dst,send_sem=ssem.at[k],recv_sem=rsem,device_id=to,device_id_type=MESH)
        cp.start(); pend.append(cp)
    def wait(ref,sem): pltpu.make_async_copy(ref,ref,sem).wait()
    zs=[zz(1),zz(2),zz(3),z]
    lines=[(1-x,1-y),(1-x,y),(x,1-y),(x,y)]
    for a,(xq,yq) in enumerate(lines):
        for b,zq in enumerate(zs):
            pltpu.make_async_copy(FG.at[pl.ds(row0(lin(xq,yq,zq,c)),SL)],S.at[4*a+b],lsem.at[4*a+b]).start()
    barrier([px,py,pc]+[pz[d] for d in (1,2,3)])
    for a,(xq,yq) in enumerate(lines):
        for b,zq in enumerate(zs):
            send(FG.at[pl.ds(row0(lin(xq,yq,zq,1-c)),SL)],R.at[4*a+b],sib.at[4*a+b],pc)
    U=176
    def add(dst,d0,rows,srcs):
        def body(t,_):
            r=pl.multiple_of(t*U,16)
            v=None
            for s,s0 in srcs:
                e=s[pl.ds(s0+r,U)].astype(jnp.float32); v=e if v is None else v+e
            dst[pl.ds(d0+r,U)]=v.astype(dst.dtype)
            return 0
        lax.fori_loop(0,rows//U,body,0)
    def have(k): wait(S.at[k],lsem.at[k]); wait(R.at[k],sib.at[k])
    for b in range(4):
        have(b)
        add(S.at[b],0,SL,[(S.at[b],0),(R.at[b],0)])
        send(S.at[b,pl.ds(0,half)],D0.at[b],dsem.at[0,b],py)
        send(S.at[b,pl.ds(half,SL-half)],D1.at[b],dsem.at[1,b],px)
    for b in range(4):
        k=4+b; have(k); wait(D0.at[b],dsem.at[0,b])
        add(S.at[k],0,half,[(S.at[k],0),(R.at[k],0),(D0.at[b],0)])
        add(S.at[k],half,SL-half,[(S.at[k],half),(R.at[k],half)])
        send(S.at[k],X.at[b],xsem.at[b],px)
        k=8+b; have(k); wait(D1.at[b],dsem.at[1,b])
        add(S.at[k],0,half,[(S.at[k],0),(R.at[k],0)])
        add(S.at[k],half,SL-half,[(S.at[k],half),(R.at[k],half),(D1.at[b],0)])
        send(S.at[k],Y.at[b],ysem.at[b],py)
    for b in range(4):
        k=12+b; have(k); wait(X.at[b],xsem.at[b]); wait(Y.at[b],ysem.at[b])
        if b<3:
            add(S.at[k],0,SL,[(S.at[k],0),(R.at[k],0),(X.at[b],0),(Y.at[b],0)])
            send(S.at[k],Z.at[b],zsem.at[b],pz[b+1])
    for b in range(3): wait(Z.at[b],zsem.at[b])
    add(A,0,SL,[(S.at[15],0),(R.at[15],0),(X.at[3],0),(Y.at[3],0),(Z.at[0],0),(Z.at[1],0),(Z.at[2],0)])
    start=me*p.sh; r_first=start//LN; s=start-r_first*LN; r0=r_first%16
    A[0:SL]=pltpu.roll(A[0:SL],lax.rem(LN-s,LN),1)
    lane=lax.broadcasted_iota(jnp.int32,(p.rows_in,LN),1)
    out[...]=jnp.where(lane<LN-s,A[pl.ds(r0,p.rows_in),:],A[pl.ds(r0+1,p.rows_in),:])
    for cp in pend: cp.wait_send()
def scatter(p,FG):
    SL=p.slot; half=SL//32*16; bf=jnp.bfloat16
    DM=pltpu.SemaphoreType.DMA
    o=pl.pallas_call(functools.partial(scatter_kernel,p),out_shape=jax.ShapeDtypeStruct((p.rows_in,LN),jnp.float32),
        in_specs=[pl.BlockSpec(memory_space=pl.ANY)],
        scratch_shapes=[pltpu.VMEM((16,SL,LN),bf),pltpu.VMEM((16,SL,LN),bf),pltpu.VMEM((4,half,LN),bf),pltpu.VMEM((4,SL-half,LN),bf),
            pltpu.VMEM((4,SL,LN),bf),pltpu.VMEM((4,SL,LN),bf),pltpu.VMEM((3,SL,LN),bf),pltpu.VMEM((SL+32,LN),jnp.float32),
            DM((16,)),DM((40,)),DM((16,)),DM((2,4)),DM((4,)),DM((4,)),DM((3,))],
        compiler_params=pltpu.CompilerParams(collective_id=1,has_side_effects=True,vmem_limit_bytes=58<<20))(FG)
    return o.reshape(-1)[:p.sh]

def unpack(arrays):
    w_qkv, w_out, w_up, w_down, vec = arrays
    pieces = dict(w_qkv=w_qkv, w_out=w_out, w_up=w_up, w_down=w_down)
    row = 0
    for name in VEC_NAMES:
        rows = (FF if name == "up_bias" else D) // LN
        pieces[name] = vec[row : row + rows].reshape(rows * LN)
        row = row + rows
    return pieces


VEC_NAMES = (
    "q_bias",
    "v_bias",
    "out_bias",
    "first_gain",
    "first_shift",
    "up_bias",
    "down_bias",
    "second_gain",
    "second_shift",
    "exit_gain",
    "exit_shift",
)


def me_of():
    return lax.axis_index(AX)


def finish_kernel(p, a_ref, out, A):
    SL = p.slot
    start = me_of() * p.sh
    r_first = start // LN
    s = start - r_first * LN
    r0 = r_first % 16
    A[0:SL] = pltpu.roll(a_ref[...], lax.rem(LN - s, LN), 1)
    lane = lax.broadcasted_iota(jnp.int32, (p.rows_in, LN), 1)
    out[...] = jnp.where(lane < LN - s, A[pl.ds(r0, p.rows_in), :], A[pl.ds(r0 + 1, p.rows_in), :])


def scatter_plain(p, flat):
    parts = jnp.concatenate([flat[16 * g : 16 * g + p.slot] for g in p.g0]).astype(jnp.float32)
    mine = lax.psum_scatter(parts, AX, scatter_dimension=0, tiled=True)
    o = pl.pallas_call(
        functools.partial(finish_kernel, p),
        out_shape=jax.ShapeDtypeStruct((p.rows_in, LN), jnp.float32),
        scratch_shapes=[pltpu.VMEM((p.slot + 32, LN), jnp.float32)],
    )(mine)
    return o.reshape(-1)[: p.sh]

def layer_norm(values, norm_gain, norm_shift):
    centred = values - jnp.mean(values, axis=-1, keepdims=True)
    spread = jnp.mean(centred * centred, axis=-1, keepdims=True)
    return centred * lax.rsqrt(spread + epsilon) * norm_gain + norm_shift


def gelu_exact(values):
    return jax.nn.gelu(values, approximate=False)


def pool_head(hidden, norm_gain, norm_shift, lengths):
    pooled = jnp.sum(hidden, axis=1) / lengths.astype(jnp.float32)[:, None]
    embedded = layer_norm(pooled, norm_gain, norm_shift)
    pieces = []
    for prefix in (D, E2, E3, E4, E5):
        window = embedded[:, :prefix]
        pieces.append(
            window * lax.rsqrt(jnp.mean(window * window, axis=-1, keepdims=True) + epsilon)
        )
    return jnp.concatenate(pieces, axis=-1)


def contract_rows(left, right):
    return lax.dot_general(
        left, right, (((0,), (0,)), ((), ())), preferred_element_type=jnp.float32
    )


def contract_cols(left, right):
    return lax.dot_general(
        left, right, (((1,), (1,)), ((), ())), preferred_element_type=jnp.float32
    )


def score_block(queries, key_rows, key_valid):
    score_scale = 1.0 / math.sqrt(HD)
    scores = (
        jnp.einsum("qhd,khd->hqk", queries, key_rows, preferred_element_type=jnp.float32)
        * score_scale
    )
    return jnp.where(key_valid[None, None, :], scores, -1000000000.0)


def attend(operands):
    queries, key_rows, value_rows, key_valid = operands
    scores = score_block(queries, key_rows, key_valid)
    log_total = jax.nn.logsumexp(scores, axis=-1, keepdims=True)
    attention = jnp.exp(scores - log_total).astype(jnp.bfloat16)
    mixed_rows = jnp.einsum(
        "hqk,khd->qhd", attention, value_rows, preferred_element_type=jnp.float32
    )
    return (mixed_rows.reshape(LEN, D).astype(jnp.bfloat16), log_total)


def attend_back(operands):
    queries, key_rows, value_rows, key_valid, log_total, mixed_grad = operands
    score_scale = 1.0 / math.sqrt(HD)
    attention = jnp.exp(score_block(queries, key_rows, key_valid) - log_total)
    attention_low = attention.astype(jnp.bfloat16)
    value_grad = jnp.einsum(
        "hqk,qhd->khd", attention_low, mixed_grad, preferred_element_type=jnp.float32
    ).astype(jnp.bfloat16)
    prob_grad = jnp.einsum(
        "qhd,khd->hqk", mixed_grad, value_rows, preferred_element_type=jnp.float32
    )
    score_grad = attention * (prob_grad - jnp.sum(prob_grad * attention, axis=-1, keepdims=True))
    score_low = score_grad.astype(jnp.bfloat16)
    query_grad = (
        jnp.einsum("hqk,khd->qhd", score_low, key_rows, preferred_element_type=jnp.float32)
        * score_scale
    ).astype(jnp.bfloat16)
    key_grad = (
        jnp.einsum("hqk,qhd->khd", score_low, queries, preferred_element_type=jnp.float32)
        * score_scale
    ).astype(jnp.bfloat16)
    return (query_grad, key_grad, value_grad)


def on_device(p, fast, tokens, lengths, weight_shards, hidden_cotangent, nested_cotangent):
    slot = build_slot(p, weight_shards, me_of)
    if fast:
        slots = gather(p, slot)
    else:
        slots = lax.all_gather(slot, AX, axis=0)
    weights = unpack(relayout(p, slots))
    back_weights = weights
    sentences = tokens.shape[0]
    row_count = sentences * LEN
    positions = lax.broadcasted_iota(jnp.int32, (sentences, LEN), 1)
    key_valid = positions < lengths[:, None]
    token_valid = key_valid.astype(jnp.float32)
    flat_tokens = tokens.reshape(row_count, D)
    qkv_bias = jnp.concatenate(
        [weights["q_bias"], jnp.zeros((D,), jnp.bfloat16), weights["v_bias"]]
    ).astype(jnp.float32)
    projected = (
        jnp.dot(flat_tokens, weights["w_qkv"], preferred_element_type=jnp.float32) + qkv_bias
    )
    head_rows = projected.astype(jnp.bfloat16).reshape(sentences, LEN, 3, H, HD)
    queries = head_rows[:, :, 0]
    key_rows = head_rows[:, :, 1]
    value_rows = head_rows[:, :, 2]
    mixed_rows, log_total = lax.map(attend, (queries, key_rows, value_rows, key_valid))
    mixed_flat = mixed_rows.reshape(row_count, D)
    branch = jnp.dot(mixed_flat, weights["w_out"], preferred_element_type=jnp.float32) + weights[
        "out_bias"
    ].astype(jnp.float32)
    first_norm, first_back = jax.vjp(
        layer_norm,
        flat_tokens.astype(jnp.float32) + branch,
        weights["first_gain"].astype(jnp.float32),
        weights["first_shift"].astype(jnp.float32),
    )
    first_low = first_norm.astype(jnp.bfloat16)
    inner_sum = jnp.dot(first_low, weights["w_up"], preferred_element_type=jnp.float32) + weights[
        "up_bias"
    ].astype(jnp.float32)
    activated, gelu_back = jax.vjp(gelu_exact, inner_sum)
    active_low = activated.astype(jnp.bfloat16)
    outer_sum = jnp.dot(
        active_low, weights["w_down"], preferred_element_type=jnp.float32
    ) + weights["down_bias"].astype(jnp.float32)
    second, second_back = jax.vjp(
        layer_norm,
        first_norm + outer_sum,
        weights["second_gain"].astype(jnp.float32),
        weights["second_shift"].astype(jnp.float32),
    )
    hidden = second.reshape(sentences, LEN, D) * token_valid[:, :, None]
    nested, head_back = jax.vjp(
        lambda states, norm_gain, norm_shift: pool_head(states, norm_gain, norm_shift, lengths),
        hidden,
        weights["exit_gain"].astype(jnp.float32),
        weights["exit_shift"].astype(jnp.float32),
    )
    hidden_grad, exit_gain_grad, exit_shift_grad = head_back(nested_cotangent)
    second_grad = (
        (hidden_cotangent.astype(jnp.float32) + hidden_grad) * token_valid[:, :, None]
    ).reshape(row_count, D)
    sum_grad, second_gain_grad, second_shift_grad = second_back(second_grad)
    outer_low = sum_grad.astype(jnp.bfloat16)
    down_bias_grad = jnp.sum(outer_low, axis=0, dtype=jnp.float32)
    w_down_grad = contract_rows(active_low, outer_low)
    active_grad = contract_cols(outer_low, back_weights["w_down"])
    (inner_grad,) = gelu_back(active_grad)
    inner_low = inner_grad.astype(jnp.bfloat16)
    up_bias_grad = jnp.sum(inner_low, axis=0, dtype=jnp.float32)
    w_up_grad = contract_rows(first_low, inner_low)
    first_grad = contract_cols(inner_low, back_weights["w_up"]) + sum_grad
    residual_grad, first_gain_grad, first_shift_grad = first_back(first_grad)
    branch_low = residual_grad.astype(jnp.bfloat16)
    out_bias_grad = jnp.sum(branch_low, axis=0, dtype=jnp.float32)
    w_out_grad = contract_rows(mixed_flat, branch_low)
    mixed_grad = (
        contract_cols(branch_low, back_weights["w_out"])
        .astype(jnp.bfloat16)
        .reshape(sentences, LEN, H, HD)
    )
    query_grad, key_grad, value_grad = lax.map(
        attend_back, (queries, key_rows, value_rows, key_valid, log_total, mixed_grad)
    )
    qkv_grad = jnp.stack([query_grad, key_grad, value_grad], axis=2).reshape(row_count, 3 * D)
    q_bias_grad = jnp.sum(query_grad.reshape(row_count, D), axis=0, dtype=jnp.float32)
    v_bias_grad = jnp.sum(value_grad.reshape(row_count, D), axis=0, dtype=jnp.float32)
    w_qkv_grad = contract_rows(flat_tokens, qkv_grad)
    token_grad = contract_cols(qkv_grad, back_weights["w_qkv"]) + residual_grad
    low = jnp.bfloat16
    mats = (w_qkv_grad.astype(low), w_out_grad.astype(low), w_up_grad.astype(low), w_down_grad.astype(low))
    vec = jnp.concatenate(
        [
            q_bias_grad,
            v_bias_grad,
            out_bias_grad,
            first_gain_grad,
            first_shift_grad,
            up_bias_grad,
            down_bias_grad,
            second_gain_grad,
            second_shift_grad,
            exit_gain_grad,
            exit_shift_grad,
        ]
    ).reshape(84, LN)
    flat = flatten(p, mats, vec)
    if fast:
        shards = scatter(p, flat)
    else:
        shards = scatter_plain(p, flat)
    return (hidden.astype(jnp.bfloat16), nested, token_grad.reshape(sentences, LEN, D), shards)


def solution(mesh):
    in_specs = (
        P(("dp", "fsdp"), None, None),
        P(("dp", "fsdp")),
        P(("dp", "fsdp")),
        P(("dp", "fsdp"), None, None),
        P(("dp", "fsdp"), None),
    )
    out_specs = (
        P(("dp", "fsdp"), None, None),
        P(("dp", "fsdp"), None),
        P(("dp", "fsdp"), None, None),
        P(("dp", "fsdp")),
    )
    p = plan(mesh.shape["dp"] * mesh.shape["fsdp"])
    fast = (mesh.shape["dp"], mesh.shape["fsdp"]) == (4, 8)
    return jax.shard_map(
        functools.partial(on_device, p, fast), mesh=mesh, in_specs=in_specs, out_specs=out_specs, check_vma=False
    )
```

```python
import functools
import math

import jax
import jax.numpy as jnp
from jax import lax
from jax.experimental import pallas as pl
from jax.experimental.pallas import tpu as pltpu
from jax.sharding import PartitionSpec as P

AX = ("dp", "fsdp")
MESH = pl.DeviceIdType.MESH
D = 768
H = 12
HD = 64
FF = 3072
LEN = 512
E2 = 512
E3 = 256
E4 = 128
E5 = 64


epsilon = 1e-05


PAR=7088640; LN=128
class Plan: pass
def plan(n):
    p=Plan(); p.n=n; p.sh=PAR//n
    st=[i*p.sh for i in range(n)]
    p.g0=[s//LN//16 for s in st]
    p.g1=[(s+p.sh-1)//LN//16 for s in st]
    p.slot=16*max(b-a+1 for a,b in zip(p.g0,p.g1))
    p.rows_in=-(-p.sh//LN)
    return p
MATS=[("wqkv",0,D,18),("wo",13836,D,6),("w1",18462,D,24),("w2",36918,FF,6)]
VECS=[(13824,12),(18444,18),(36894,24),(55350,30)]

def build_slot_kernel(p,me_of,x_ref,o_ref,q_ref):
    i=me_of(); start=i*p.sh; r_first=start//LN; s=start-r_first*LN; r0=r_first%16
    lead=32
    q_ref[...]=jnp.zeros_like(q_ref)
    q=pltpu.roll(x_ref[...].astype(jnp.float32),s,1)
    q_ref[lead:lead+p.rows_in]=q
    lane=lax.broadcasted_iota(jnp.int32,(p.slot,LN),1)
    a=q_ref[pl.ds(lead-r0,p.slot),:]
    b=q_ref[pl.ds(lead-1-r0,p.slot),:]
    o_ref[...]=jnp.where(lane>=s,a,b).astype(jnp.bfloat16)

def build_slot(p,shard,me_of):
    x=jnp.pad(shard,(0,p.rows_in*LN-p.sh)).reshape(p.rows_in,LN)
    return pl.pallas_call(functools.partial(build_slot_kernel,p,me_of),out_shape=jax.ShapeDtypeStruct((p.slot,LN),jnp.bfloat16),
        scratch_shapes=[pltpu.VMEM((32+p.slot+32,LN),jnp.float32)])(x)

def load_flat(p,slots,F,g_lo,g_hi):
    for i in range(p.n):
        a=max(g_lo,p.g0[i]); b=min(g_hi,p.g1[i]+1)
        if a>=b: continue
        shared_first = i>0 and p.g0[i]==p.g1[i-1] and a==p.g0[i]
        a2=a+1 if shared_first else a
        b2=b
        if i+1<p.n and p.g1[i]==p.g0[i+1] and b==p.g1[i]+1: b2=b-1
        if i+1<p.n and b2<b and b-1>=g_lo:
            g=b-1
            F[16*(g-g_lo):16*(g-g_lo)+16]=slots[i,16*(g-p.g0[i]):16*(g-p.g0[i])+16].astype(jnp.float32)+slots[i+1,0:16].astype(jnp.float32)
        cnt=b2-a2
        if cnt<=0: continue
        U=16
        nb,rem=cnt//U,cnt%U
        def body(t,_,i=i,a2=a2):
            src=pl.multiple_of(16*(a2-p.g0[i])+t*16*U,16); dst=pl.multiple_of(16*(a2-g_lo)+t*16*U,16)
            F[pl.ds(dst,16*U)]=slots[i,pl.ds(src,16*U)].astype(jnp.float32)
            return 0
        lax.fori_loop(0,nb,body,0)
        if rem:
            src=16*(a2-p.g0[i])+nb*16*U; dst=16*(a2-g_lo)+nb*16*U
            F[dst:dst+16*rem]=slots[i,src:src+16*rem].astype(jnp.float32)
def tile_matrix(F,W,off,rows,w,RB=64):
    def body(t,_):
        r=pl.multiple_of(t*RB,RB)
        for j in range(w):
            W[pl.ds(r,RB),j*LN:(j+1)*LN]=F[pl.ds(off+r*w+j,RB,stride=w),:].astype(jnp.bfloat16)
        return 0
    lax.fori_loop(0,rows//RB,body,0)
def relayout_kernel(p,slots,wqkv,wo,w1,w2,vec,F):
    outs=dict(wqkv=wqkv,wo=wo,w1=w1,w2=w2)
    for name,base,rows,w in MATS:
        g_lo=base//16; g_hi=-(-(base+rows*w)//16)
        load_flat(p,slots,F,g_lo,g_hi)
        tile_matrix(F,outs[name],base-16*g_lo,rows,w)
    at=0
    for base,cnt in VECS:
        g_lo=base//16; g_hi=-(-(base+cnt)//16)
        load_flat(p,slots,F,g_lo,g_hi)
        vec[at:at+cnt]=F[base-16*g_lo:base-16*g_lo+cnt]
        at+=cnt
def relayout(p,slots):
    shp=[jax.ShapeDtypeStruct((r,w*LN),jnp.bfloat16) for _,_,r,w in MATS]+[jax.ShapeDtypeStruct((84,LN),jnp.float32)]
    return pl.pallas_call(functools.partial(relayout_kernel,p),out_shape=shp,
        scratch_shapes=[pltpu.VMEM((18432+32,LN),jnp.float32)],
        compiler_params=pltpu.CompilerParams(vmem_limit_bytes=58<<20))(slots)

def coords():
    dp=lax.axis_index("dp"); fs=lax.axis_index("fsdp")
    return dp//2,fs%2,fs//2,dp%2
def dev(x,y,z,c): return (x*2+c, z*2+y)
def lin(x,y,z,c): return (x*2+c)*8+z*2+y
def barrier(partners):
    bar=pltpu.get_barrier_semaphore()
    for q in partners: pl.semaphore_signal(bar,inc=1,device_id=q,device_id_type=MESH)
    pl.semaphore_wait(bar,len(partners))
def gather_kernel(p,slot_ref,G,ssem,rsem,lsem):
    x,y,z,c=coords(); me=lin(x,y,z,c)
    half=p.slot//32*16
    H=((0,half),(half,p.slot-half))
    px,py,pc=dev(1-x,y,z,c),dev(x,1-y,z,c),dev(x,y,z,1-c)
    def zz(d):
        if d==1: return z+1-2*(z%2)
        if d==2: return lax.rem(z+2,4)
        return 3-z
    barrier([px,py,pc]+[dev(x,y,zz(d),c) for d in (1,2,3)])
    n_send=[0]; pend=[]
    def send(src,dst,to,sl,h,who):
        r0,rn=(H[h] if h<2 else (0,p.slot))
        k=n_send[0]; n_send[0]+=1
        cp=pltpu.make_async_remote_copy(src_ref=src(r0,rn),dst_ref=G.at[sl,pl.ds(r0,rn)],send_sem=ssem.at[k],recv_sem=rsem.at[sl,h],device_id=to,device_id_type=MESH)
        cp.start(); pend.append(cp)
    def wait(sl,h):
        r0,rn=(H[h] if h<2 else (0,p.slot))
        pltpu.make_async_copy(G.at[sl,pl.ds(r0,rn)],G.at[sl,pl.ds(r0,rn)],rsem.at[sl,h]).wait()
    def from_own(r0,rn): return slot_ref.at[pl.ds(r0,rn)]
    def from_g(sl): return lambda r0,rn: G.at[sl,pl.ds(r0,rn)]
    for to in (px,py,dev(x,y,zz(1),c),dev(x,y,zz(2),c),dev(x,y,zz(3),c),pc):
        send(from_own,None,to,me,2,None)
    loc=pltpu.make_async_copy(slot_ref,G.at[me],lsem); loc.start()
    def fwd_x(zq):
        sl=lin(1-x,y,zq,c); wait(sl,2); send(from_g(sl),None,py,sl,0,None); send(from_g(sl),None,pc,sl,2,None)
    def fwd_y(zq):
        sl=lin(x,1-y,zq,c); wait(sl,2); send(from_g(sl),None,px,sl,1,None); send(from_g(sl),None,pc,sl,2,None)
    def fwd_z(zq):
        sl=lin(x,y,zq,c); wait(sl,2)
        for to in (px,py,pc): send(from_g(sl),None,to,sl,2,None)
    def fwd_d(zq):
        sl=lin(1-x,1-y,zq,c)
        for h in (0,1):
            wait(sl,h); send(from_g(sl),None,pc,sl,h,None)
    fwd_x(z); fwd_y(z)
    for d in (1,3,2): fwd_z(zz(d))
    fwd_d(z)
    for d in (1,3,2): fwd_x(zz(d)); fwd_y(zz(d))
    for d in (1,3,2): fwd_d(zz(d))
    for zq in [z]+[zz(d) for d in (1,3,2)]:
        for (a,b) in ((x,y),(1-x,y),(x,1-y)): wait(lin(a,b,zq,1-c),2)
    for zq in [z]+[zz(d) for d in (1,3,2)]:
        for h in (0,1): wait(lin(1-x,1-y,zq,1-c),h)
    loc.wait()
    for cp in pend: cp.wait_send()
def gather(p,slot):
    return pl.pallas_call(functools.partial(gather_kernel,p),out_shape=jax.ShapeDtypeStruct((p.n,p.slot,LN),jnp.bfloat16),
        in_specs=[pl.BlockSpec(memory_space=pl.ANY)],out_specs=pl.BlockSpec(memory_space=pl.ANY),
        scratch_shapes=[pltpu.SemaphoreType.DMA((40,)),pltpu.SemaphoreType.DMA((p.n,3)),pltpu.SemaphoreType.DMA],
        compiler_params=pltpu.CompilerParams(collective_id=0,has_side_effects=True))(slot)

TOT=PAR//LN
def flat_rows(p): return max(16*p.g0[-1]+p.slot, EDGES[-1][0]+EDGES[-1][1])
def owner_row(rho):
    for k,(name,base,rows,w) in enumerate(MATS):
        if base<=rho<base+rows*w: return ("m",k,(rho-base)//w,(rho-base)%w)
    at=0
    for base,cnt in VECS:
        if base<=rho<base+cnt: return ("v",at+rho-base)
        at+=cnt
    return None
def untile_matrix(F,W,off,rows,w,RB=64):
    def body(t,_):
        r=pl.multiple_of(t*RB,RB)
        for j in range(w):
            F[pl.ds(off+r*w+j,RB,stride=w),:]=W[pl.ds(r,RB),j*LN:(j+1)*LN].astype(jnp.float32)
        return 0
    lax.fori_loop(0,rows//RB,body,0)
def store_flat(F,FG,f_row,g_row,rows,U=256):
    nb,rem=rows//U,rows%U
    def body(t,_):
        FG[pl.ds(pl.multiple_of(g_row+t*U,16),U)]=F[pl.ds(pl.multiple_of(f_row+t*U,16),U)].astype(jnp.bfloat16)
        return 0
    lax.fori_loop(0,nb,body,0)
    if rem: FG[g_row+nb*U:g_row+nb*U+rem]=F[f_row+nb*U:f_row+nb*U+rem].astype(jnp.bfloat16)
def flatten_kernel(p,wqkv,wo,w1,w2,vec,FG,F):
    ms=[wqkv,wo,w1,w2]
    end=flat_rows(p)
    def put(rho,lo):
        o=owner_row(rho)
        if o is None: F[rho-lo:rho-lo+1]=jnp.zeros((1,LN),jnp.float32)
        elif o[0]=="v": F[rho-lo:rho-lo+1]=vec[o[1]:o[1]+1]
        else: F[rho-lo:rho-lo+1]=ms[o[1]][o[2]:o[2]+1,o[3]*LN:(o[3]+1)*LN].astype(jnp.float32)
    cuts=[0,13824,18464,36928,end]
    for k,(name,base,rows,w) in enumerate(MATS):
        lo=cuts[k]//16*16; hi=cuts[k+1]
        f0=min(lo,base//16*16)
        untile_matrix(F,ms[k],base-f0,rows,w)
        for rho in list(range(lo,max(lo,base)))+list(range(base+rows*w,hi)): put(rho,f0)
        store_flat(F,FG,lo-f0,lo,hi-lo)
def flatten(p,dws,vec):
    return pl.pallas_call(functools.partial(flatten_kernel,p),out_shape=jax.ShapeDtypeStruct((flat_rows(p),LN),jnp.bfloat16),
        scratch_shapes=[pltpu.VMEM((18432+80,LN),jnp.float32)],
        compiler_params=pltpu.CompilerParams(vmem_limit_bytes=58<<20))(*dws,vec)

def scatter_kernel(p,FG,out,S,R,D0,D1,X,Y,Z,A,lsem,ssem,sib,dsem,xsem,ysem,zsem):
    x,y,z,c=coords(); me=lin(x,y,z,c)
    SL=p.slot
    half=SL//32*16
    px,py,pc=dev(1-x,y,z,c),dev(x,1-y,z,c),dev(x,y,z,1-c)
    def zz(d):
        if d==1: return z+1-2*(z%2)
        if d==2: return lax.rem(z+2,4)
        return 3-z
    pz={d:dev(x,y,zz(d),c) for d in (1,2,3)}
    pend=[]; ns=[0]
    def row0(i): return pl.multiple_of((i*p.sh)//LN//16*16,16)
    def send(src,dst,rsem,to):
        k=ns[0]; ns[0]+=1
        cp=pltpu.make_async_remote_copy(src_ref=src,dst_ref=dst,send_sem=ssem.at[k],recv_sem=rsem,device_id=to,device_id_type=MESH)
        cp.start(); pend.append(cp)
    def wait(ref,sem): pltpu.make_async_copy(ref,ref,sem).wait()
    zs=[zz(1),zz(2),zz(3),z]
    lines=[(1-x,1-y),(1-x,y),(x,1-y),(x,y)]
    for a,(xq,yq) in enumerate(lines):
        for b,zq in enumerate(zs):
            pltpu.make_async_copy(FG.at[pl.ds(row0(lin(xq,yq,zq,c)),SL)],S.at[4*a+b],lsem.at[4*a+b]).start()
    barrier([px,py,pc]+[pz[d] for d in (1,2,3)])
    for a,(xq,yq) in enumerate(lines):
        for b,zq in enumerate(zs):
            send(FG.at[pl.ds(row0(lin(xq,yq,zq,1-c)),SL)],R.at[4*a+b],sib.at[4*a+b],pc)
    U=176
    def add(dst,d0,rows,srcs):
        def body(t,_):
            r=pl.multiple_of(t*U,16)
            v=None
            for s,s0 in srcs:
                e=s[pl.ds(s0+r,U)].astype(jnp.float32); v=e if v is None else v+e
            dst[pl.ds(d0+r,U)]=v.astype(dst.dtype)
            return 0
        lax.fori_loop(0,rows//U,body,0)
    def have(k): wait(S.at[k],lsem.at[k]); wait(R.at[k],sib.at[k])
    for b in range(4):
        have(b)
        add(S.at[b],0,SL,[(S.at[b],0),(R.at[b],0)])
        send(S.at[b,pl.ds(0,half)],D0.at[b],dsem.at[0,b],py)
        send(S.at[b,pl.ds(half,SL-half)],D1.at[b],dsem.at[1,b],px)
    for b in range(4):
        k=4+b; have(k); wait(D0.at[b],dsem.at[0,b])
        add(S.at[k],0,half,[(S.at[k],0),(R.at[k],0),(D0.at[b],0)])
        add(S.at[k],half,SL-half,[(S.at[k],half),(R.at[k],half)])
        send(S.at[k],X.at[b],xsem.at[b],px)
        k=8+b; have(k); wait(D1.at[b],dsem.at[1,b])
        add(S.at[k],0,half,[(S.at[k],0),(R.at[k],0)])
        add(S.at[k],half,SL-half,[(S.at[k],half),(R.at[k],half),(D1.at[b],0)])
        send(S.at[k],Y.at[b],ysem.at[b],py)
    for b in range(4):
        k=12+b; have(k); wait(X.at[b],xsem.at[b]); wait(Y.at[b],ysem.at[b])
        if b<3:
            add(S.at[k],0,SL,[(S.at[k],0),(R.at[k],0),(X.at[b],0),(Y.at[b],0)])
            send(S.at[k],Z.at[b],zsem.at[b],pz[b+1])
    for b in range(3): wait(Z.at[b],zsem.at[b])
    add(A,0,SL,[(S.at[15],0),(R.at[15],0),(X.at[3],0),(Y.at[3],0),(Z.at[0],0),(Z.at[1],0),(Z.at[2],0)])
    start=me*p.sh; r_first=start//LN; s=start-r_first*LN; r0=r_first%16
    A[0:SL]=pltpu.roll(A[0:SL],lax.rem(LN-s,LN),1)
    lane=lax.broadcasted_iota(jnp.int32,(p.rows_in,LN),1)
    out[...]=jnp.where(lane<LN-s,A[pl.ds(r0,p.rows_in),:],A[pl.ds(r0+1,p.rows_in),:])
    for cp in pend: cp.wait_send()
def scatter(p,FG):
    SL=p.slot; half=SL//32*16; bf=jnp.bfloat16
    DM=pltpu.SemaphoreType.DMA
    o=pl.pallas_call(functools.partial(scatter_kernel,p),out_shape=jax.ShapeDtypeStruct((p.rows_in,LN),jnp.float32),
        in_specs=[pl.BlockSpec(memory_space=pl.ANY)],
        scratch_shapes=[pltpu.VMEM((16,SL,LN),bf),pltpu.VMEM((16,SL,LN),bf),pltpu.VMEM((4,half,LN),bf),pltpu.VMEM((4,SL-half,LN),bf),
            pltpu.VMEM((4,SL,LN),bf),pltpu.VMEM((4,SL,LN),bf),pltpu.VMEM((3,SL,LN),bf),pltpu.VMEM((SL+32,LN),jnp.float32),
            DM((16,)),DM((40,)),DM((16,)),DM((2,4)),DM((4,)),DM((4,)),DM((3,))],
        compiler_params=pltpu.CompilerParams(collective_id=1,has_side_effects=True,vmem_limit_bytes=58<<20))(FG)
    return o.reshape(-1)[:p.sh]

def me_of():
    return lax.axis_index(AX)


def finish_kernel(p, a_ref, out, A):
    SL = p.slot
    start = me_of() * p.sh
    r_first = start // LN
    s = start - r_first * LN
    r0 = r_first % 16
    A[0:SL] = pltpu.roll(a_ref[...], lax.rem(LN - s, LN), 1)
    lane = lax.broadcasted_iota(jnp.int32, (p.rows_in, LN), 1)
    out[...] = jnp.where(lane < LN - s, A[pl.ds(r0, p.rows_in), :], A[pl.ds(r0 + 1, p.rows_in), :])


def scatter_plain(p, flat):
    parts = jnp.concatenate([flat[16 * g : 16 * g + p.slot] for g in p.g0]).astype(jnp.float32)
    mine = lax.psum_scatter(parts, AX, scatter_dimension=0, tiled=True)
    o = pl.pallas_call(
        functools.partial(finish_kernel, p),
        out_shape=jax.ShapeDtypeStruct((p.rows_in, LN), jnp.float32),
        scratch_shapes=[pltpu.VMEM((p.slot + 32, LN), jnp.float32)],
    )(mine)
    return o.reshape(-1)[: p.sh]

EPS = 1e-05
F32 = jnp.float32
BF = jnp.bfloat16
SQ = math.sqrt(0.5)
PHI = 1.0 / math.sqrt(2.0 * math.pi)
VNAMES = (
    ("q_bias", D),
    ("v_bias", D),
    ("out_bias", D),
    ("first_gain", D),
    ("first_shift", D),
    ("up_bias", FF),
    ("down_bias", D),
    ("second_gain", D),
    ("second_shift", D),
    ("exit_gain", D),
    ("exit_shift", D),
)
VI = {name: k for k, (name, _) in enumerate(VNAMES)}
PREFIXES = (D, E2, E3, E4, E5)


def mm(a, b):
    return jnp.dot(a, b, preferred_element_type=F32)


def mm_nt(a, b):
    return lax.dot_general(a, b, (((1,), (1,)), ((), ())), preferred_element_type=F32)


def mm_tn(a, b):
    return lax.dot_general(a, b, (((0,), (0,)), ((), ())), preferred_element_type=F32)


def vrow(V, name):
    k = VI[name]
    return V[k : k + 1, : VNAMES[k][1]]


def mean_last(a):
    return jnp.mean(a, axis=-1, keepdims=True)


def sum_rows(a):
    return jnp.sum(a, axis=0, keepdims=True)


def forward_qkv(r):
    bias = jnp.concatenate([vrow(r.V, "q_bias"), jnp.zeros((1, D), F32), vrow(r.V, "v_bias")], axis=1)
    r.qb[...] = bias

    def body(j, _):
        o = pl.ds(pl.multiple_of(j * 256, 256), 256)
        r.qkv[:, o] = (mm(r.tok[...], r.wqkv[:, o]) + r.qb[:, o]).astype(BF)
        return 0

    lax.fori_loop(0, 3 * D // 256, body, 0)


def half_lanes(h):
    lane = lax.broadcasted_iota(jnp.int32, (LEN, LN), 1)
    return lane < HD if h == 0 else lane >= HD


def pair(r, part, hp):
    return r.qkv[:, pl.ds(pl.multiple_of(part * D + hp * LN, LN), LN)]


def forward_heads(r, hp):
    q, k, v = pair(r, 0, hp), pair(r, 1, hp), pair(r, 2, hp)
    valid = lax.broadcasted_iota(jnp.int32, (1, LEN), 1) < r.length
    out = None
    lse_all = r.lse[...]
    lane = lax.broadcasted_iota(jnp.int32, (LEN, LN), 1)
    for h in range(2):
        qh = jnp.where(half_lanes(h), q, jnp.zeros_like(q))
        s = jnp.where(valid, mm_nt(qh, k) * 0.125, -1e9)
        m = jnp.max(s, axis=1, keepdims=True)
        e = jnp.exp(s - m)
        l = jnp.sum(e, axis=1, keepdims=True)
        low = (e * (1.0 / l)).astype(BF)
        o = mm(low, v)
        out = o if out is None else jnp.where(half_lanes(0), out, o)
        lse_all = jnp.where(lane == 2 * hp + h, m + jnp.log(l), lse_all)
    r.lse[...] = lse_all
    r.mixed[:, pl.ds(pl.multiple_of(hp * LN, LN), LN)] = out.astype(BF)


def rows_of(b, n):
    return pl.ds(pl.multiple_of(b * n, n), n)


def forward_first(r):
    def body(b, _):
        o = rows_of(b, 256)
        v = r.tok[o, :].astype(F32) + mm(r.mixed[o, :], r.wo[...]) + vrow(r.V, "out_bias")
        cen = v - mean_last(v)
        rstd = lax.rsqrt(mean_last(cen * cen) + EPS)
        xh = cen * rstd
        r.xh1[o, :] = xh
        r.rstd1[o, :] = rstd
        r.first_low[o, :] = (xh * vrow(r.V, "first_gain") + vrow(r.V, "first_shift")).astype(BF)
        return 0

    lax.fori_loop(0, LEN // 256, body, 0)


def forward_up(r, j):
    o = pl.ds(pl.multiple_of(j * 256, 256), 256)
    v = mm(r.first_low[...], r.w1[:, o]) + r.V[VI["up_bias"] : VI["up_bias"] + 1, o]
    cdf = 0.5 * (1.0 + lax.erf(v * SQ))
    r.act[:, o] = (v * cdf).astype(BF)
    r.gd[:, o] = (cdf + v * (PHI * jnp.exp(-0.5 * v * v))).astype(BF)


def forward_second(r):
    def body(b, tot):
        o = rows_of(b, 256)
        first = r.xh1[o, :] * vrow(r.V, "first_gain") + vrow(r.V, "first_shift")
        v = first + mm(r.act[o, :], r.w2[...]) + vrow(r.V, "down_bias")
        cen = v - mean_last(v)
        rstd = lax.rsqrt(mean_last(cen * cen) + EPS)
        xh = cen * rstd
        r.xh2[o, :] = xh
        r.rstd2[o, :] = rstd
        t = lax.broadcasted_iota(jnp.int32, (256, 1), 0) + b * 256
        hid = (xh * vrow(r.V, "second_gain") + vrow(r.V, "second_shift")) * (t < r.length).astype(F32)
        r.hidden[o, :] = hid.astype(BF)
        return tot + sum_rows(hid)

    return lax.fori_loop(0, LEN // 256, body, jnp.zeros((1, D), F32))


def head(r, tot):
    inv_len = 1.0 / jnp.full((1, 1), r.length, jnp.int32).astype(F32)
    pooled = tot * inv_len
    cen = pooled - mean_last(pooled)
    rstd = lax.rsqrt(mean_last(cen * cen) + EPS)
    xh = cen * rstd
    gain = vrow(r.V, "exit_gain")
    emb = xh * gain + vrow(r.V, "exit_shift")
    d_emb = jnp.zeros((1, D), F32)
    at = 0
    for m in PREFIXES:
        e = emb[:, :m]
        inv = lax.rsqrt(jnp.sum(e * e, axis=1, keepdims=True) * (1.0 / m) + EPS)
        out = e * inv
        r.nested[:, at : at + m] = out
        c = r.ncot[:, at : at + m]
        g = inv * (c - out * (jnp.sum(c * out, axis=1, keepdims=True) * (1.0 / m)))
        d_emb = d_emb + (g if m == D else jnp.concatenate([g, jnp.zeros((1, D - m), F32)], axis=1))
        at += m
    put_grad(r, "exit_gain", d_emb * xh)
    put_grad(r, "exit_shift", d_emb)
    dx = d_emb * gain
    return rstd * (dx - mean_last(dx) - xh * mean_last(dx * xh)) * inv_len


def put_grad(r, name, value):
    k = VI[name]
    r.VG[k : k + 1, : VNAMES[k][1]] = value


def norm_back(dy, gain, xh, rstd):
    dx = dy * gain
    return rstd * (dx - mean_last(dx) - xh * mean_last(dx * xh))


def backward_second(r, d_pool):
    def body(b, c):
        o = rows_of(b, 128)
        t = lax.broadcasted_iota(jnp.int32, (128, 1), 0) + b * 128
        dy = (r.hcot[o, :].astype(F32) + d_pool) * (t < r.length).astype(F32)
        xh = r.xh2[o, :]
        res = norm_back(dy, vrow(r.V, "second_gain"), xh, r.rstd2[o, :])
        r.res[o, :] = res
        low = res.astype(BF)
        r.d_outer[o, :] = low
        return (c[0] + sum_rows(dy * xh), c[1] + sum_rows(dy), c[2] + sum_rows(low.astype(F32)))

    z = jnp.zeros((1, D), F32)
    a, b, c = lax.fori_loop(0, LEN // 128, body, (z, z, z))
    put_grad(r, "second_gain", a)
    put_grad(r, "second_shift", b)
    put_grad(r, "down_bias", c)


def backward_act(r, j):
    o = pl.ds(pl.multiple_of(j * 256, 256), 256)
    d = (mm_nt(r.d_outer[...], r.w2[o, :]) * r.gd[:, o].astype(F32)).astype(BF)
    r.gd[:, o] = d
    r.VG[VI["up_bias"] : VI["up_bias"] + 1, o] = sum_rows(d.astype(F32))


def backward_first(r):
    def body(b, c):
        o = rows_of(b, 256)
        dy = mm_nt(r.gd[o, :], r.w1[...]) + r.res[o, :]
        xh = r.xh1[o, :]
        res = norm_back(dy, vrow(r.V, "first_gain"), xh, r.rstd1[o, :])
        r.res[o, :] = res
        low = res.astype(BF)
        r.d_branch[o, :] = low
        return (c[0] + sum_rows(dy * xh), c[1] + sum_rows(dy), c[2] + sum_rows(low.astype(F32)))

    z = jnp.zeros((1, D), F32)
    a, b, c = lax.fori_loop(0, LEN // 256, body, (z, z, z))
    put_grad(r, "first_gain", a)
    put_grad(r, "first_shift", b)
    put_grad(r, "out_bias", c)


def backward_mixed(r):
    r.d_mixed[...] = mm_nt(r.d_branch[...], r.wo[...]).astype(BF)


def backward_heads(r, hp):
    q, k, v = pair(r, 0, hp), pair(r, 1, hp), pair(r, 2, hp)
    cols = pl.ds(pl.multiple_of(hp * LN, LN), LN)
    dm = r.d_mixed[:, cols]
    valid = lax.broadcasted_iota(jnp.int32, (1, LEN), 1) < r.length
    lane = lax.broadcasted_iota(jnp.int32, (LEN, LN), 1)
    zero = jnp.zeros_like(q)
    dq = dk = dv = None
    for h in range(2):
        here = half_lanes(h)
        qh, kh, dmh = jnp.where(here, q, zero), jnp.where(here, k, zero), jnp.where(here, dm, zero)
        lse = jnp.sum(jnp.where(lane == 2 * hp + h, r.lse[...], 0.0), axis=1, keepdims=True)
        s = jnp.where(valid, mm_nt(qh, k) * 0.125, -1e9)
        p = jnp.exp(s - lse)
        dp = mm_nt(dmh, v)
        ds = (p * (dp - jnp.sum(dp * p, axis=1, keepdims=True))).astype(BF)
        a, b, c = mm(ds, kh), mm_tn(ds, qh), mm_tn(p.astype(BF), dmh)
        dq, dk, dv = (a, b, c) if dq is None else (dq + a, dk + b, dv + c)
    dq, dk, dv = (dq * 0.125).astype(BF), (dk * 0.125).astype(BF), dv.astype(BF)
    for part, g in ((0, dq), (1, dk), (2, dv)):
        r.dqkv[:, pl.ds(pl.multiple_of(part * D + hp * LN, LN), LN)] = g
    k = VI["q_bias"]
    r.VG[k : k + 1, cols] = sum_rows(dq.astype(F32))
    k = VI["v_bias"]
    r.VG[k : k + 1, cols] = sum_rows(dv.astype(F32))


def backward_tokens(r, b):
    o = rows_of(b, 128)
    v = r.res[o, :]
    for part in range(3):
        v = v + mm_nt(r.dqkv[o, part * D : (part + 1) * D], r.wqkv[:, part * D : (part + 1) * D])
    r.res[o, :] = v


EDGES = ((13824, 16), (18432, 32), (36880, 48), (55344, 64))


def edge_at(row):
    at = 0
    for base, rows in EDGES:
        if base <= row < base + rows:
            return at + row - base
        at += rows
    return None


def weight_grad(r, lhs, rhs, base, rows, w, RB=256, CB=6):
    lead = base % 16
    step_rows = RB * w
    F = r.F
    if lead:
        F[0:16] = jnp.zeros((16, LN), F32)

    def body(s, _):
        o = pl.ds(pl.multiple_of(s * RB, RB), RB)
        for ch in range(w // CB):
            g = mm_tn(lhs[:, o], rhs[:, ch * CB * LN : (ch + 1) * CB * LN])
            for j in range(CB):
                F[pl.ds(lead + ch * CB + j, RB, stride=w), :] = g[:, j * LN : (j + 1) * LN]
        if lead:
            @pl.when(s == 0)
            def _():
                e = edge_at(base)
                r.E[e : e + 16 - lead] = F[lead:16]

        U = 256
        to = base - lead + s * step_rows

        def emit(t, _):
            r.FG[pl.ds(pl.multiple_of(to + t * U, 16), U)] = F[pl.ds(pl.multiple_of(t * U, 16), U)].astype(BF)
            return 0

        lax.fori_loop(0, step_rows // U, emit, 0)
        if lead:
            F[0:16] = F[step_rows : step_rows + 16]
        return 0

    lax.fori_loop(0, rows // RB, body, 0)
    if lead:
        e = edge_at(base + rows * w - lead)
        r.E[e : e + lead] = F[0:lead]


def edge_grads(r, which):
    base, rows = EDGES[which]
    at = 0
    for vbase, cnt in VECS:
        for k in range(cnt):
            row = vbase + k
            if base <= row < base + rows:
                name, j = vec_at(at + k)
                e = edge_at(row)
                r.E[e : e + 1] = r.VG[name : name + 1, j * LN : (j + 1) * LN]
        at += cnt
    if which == len(EDGES) - 1:
        e = edge_at(TOT)
        r.E[e : e + base + rows - TOT] = jnp.zeros((base + rows - TOT, LN), F32)
    e = edge_at(base)
    r.FG[base : base + rows] = r.E[e : e + rows].astype(BF)


def vec_at(row):
    for k, (_, n) in enumerate(VNAMES):
        if row < n // LN:
            return k, row
        row -= n // LN


class Refs:
    def __init__(self, **refs):
        self.__dict__.update(refs)


def relayout_vectors(p, r):
    at = 0
    for base, cnt in VECS:
        g_lo = base // 16
        g_hi = -(-(base + cnt) // 16)
        load_flat(p, r.slots, r.F, g_lo, g_hi)
        for k in range(cnt):
            name, j = vec_at(at + k)
            f = base - 16 * g_lo + k
            r.V[name : name + 1, j * LN : (j + 1) * LN] = r.F[f : f + 1]
        at += cnt


def relayout_matrix(p, r, name, W, RB):
    base, rows, w = {n: (b, k, c) for n, b, k, c in MATS}[name]
    for s in range(rows // RB):
        lo = base + s * RB * w
        g_lo = lo // 16
        load_flat(p, r.slots, r.F, g_lo, -(-(lo + RB * w) // 16))
        tile_rows(r.F, W, lo - 16 * g_lo, s * RB, RB, w)


def tile_rows(F, W, off, row, rows, w, RB=64):
    def body(t, _):
        q = pl.multiple_of(t * RB, RB)
        for j in range(w):
            W[pl.ds(row + q, RB), j * LN : (j + 1) * LN] = F[pl.ds(off + q * w + j, RB, stride=w), :].astype(BF)
        return 0

    lax.fori_loop(0, rows // RB, body, 0)


def forward_kernel(p, slots, length, tok, hcot, ncot, hidden, nested, wqkv, wo, w1, w2, V, VG, qkv, lse, mixed, xh1, rstd1, first_low, act, gd, res, d_outer, F, qb, xh2, rstd2):
    r = Refs(slots=slots, length=length[0], tok=tok, hcot=hcot, ncot=ncot, hidden=hidden, nested=nested, wqkv=wqkv, wo=wo, w1=w1, w2=w2, V=V, VG=VG, qkv=qkv, lse=lse, mixed=mixed, xh1=xh1, rstd1=rstd1, first_low=first_low, act=act, gd=gd, res=res, d_outer=d_outer, F=F, qb=qb, xh2=xh2, rstd2=rstd2)
    relayout_vectors(p, r)
    relayout_matrix(p, r, "wqkv", wqkv, 256)
    forward_qkv(r)
    lse[...] = jnp.zeros_like(lse)
    lax.fori_loop(0, H // 2, lambda hp, c: (forward_heads(r, hp), c)[1], 0)
    relayout_matrix(p, r, "wo", wo, 768)
    forward_first(r)
    relayout_matrix(p, r, "w1", w1, 256)
    lax.fori_loop(0, FF // 256, lambda j, c: (forward_up(r, j), c)[1], 0)
    relayout_matrix(p, r, "w2", w2, 768)
    tot = forward_second(r)
    d_pool = head(r, tot)
    backward_second(r, d_pool)


def forward_local(p, slots, length, tok, hcot, ncot):
    S = jax.ShapeDtypeStruct
    outs = [S((LEN, D), BF), S((1, 1728), F32), S((D, 3 * D), BF), S((D, D), BF), S((D, FF), BF), S((FF, D), BF), S((16, FF), F32), S((16, FF), F32), S((LEN, 3 * D), BF), S((LEN, LN), F32), S((LEN, D), BF), S((LEN, D), F32), S((LEN, 1), F32), S((LEN, D), BF), S((LEN, FF), BF), S((LEN, FF), BF), S((LEN, D), F32), S((LEN, D), BF)]
    vm = pl.BlockSpec(memory_space=pltpu.VMEM)
    sm = pl.BlockSpec(memory_space=pltpu.SMEM)
    return pl.pallas_call(
        functools.partial(forward_kernel, p),
        out_shape=outs,
        in_specs=[vm, sm, vm, vm, vm],
        scratch_shapes=[pltpu.VMEM((6144 + 32, LN), F32), pltpu.VMEM((1, 3 * D), F32), pltpu.VMEM((LEN, D), F32), pltpu.VMEM((LEN, 1), F32)],
        compiler_params=pltpu.CompilerParams(vmem_limit_bytes=60 << 20),
    )(slots, length, tok, hcot, ncot)


def backward_kernel(p, length, tok, V, VG0, qkv, lse, mixed, xh1, rstd1, first_low, act, gd, res, d_outer, wqkv, wo, w1, w2, igrad, FG, VG, d_branch, d_mixed, dqkv, F, E):
    r = Refs(length=length[0], tok=tok, V=V, VG=VG, qkv=qkv, lse=lse, mixed=mixed, xh1=xh1, rstd1=rstd1, first_low=first_low, act=act, gd=gd, res=igrad, d_outer=d_outer, wqkv=wqkv, wo=wo, w1=w1, w2=w2, FG=FG, d_branch=d_branch, d_mixed=d_mixed, dqkv=dqkv, F=F, E=E)
    VG[...] = VG0[...]
    igrad[...] = res[...]
    mats = {n: (b, k, c) for n, b, k, c in MATS}
    weight_grad(r, act, d_outer, *mats["w2"])
    edge_grads(r, 3)
    lax.fori_loop(0, FF // 256, lambda j, c: (backward_act(r, j), c)[1], 0)
    weight_grad(r, first_low, gd, *mats["w1"])
    edge_grads(r, 2)
    backward_first(r)
    weight_grad(r, mixed, d_branch, *mats["wo"])
    edge_grads(r, 1)
    backward_mixed(r)
    lax.fori_loop(0, H // 2, lambda hp, c: (backward_heads(r, hp), c)[1], 0)
    weight_grad(r, tok, dqkv, *mats["wqkv"])
    edge_grads(r, 0)
    lax.fori_loop(0, LEN // 128, lambda b, c: (backward_tokens(r, b), c)[1], 0)


def backward_local(p, length, tok, V, VG, qkv, lse, mixed, xh1, rstd1, first_low, act, gd, res, d_outer, wqkv, wo, w1, w2):
    S = jax.ShapeDtypeStruct
    vm = pl.BlockSpec(memory_space=pltpu.VMEM)
    sm = pl.BlockSpec(memory_space=pltpu.SMEM)
    return pl.pallas_call(
        functools.partial(backward_kernel, p),
        out_shape=[S((LEN, D), F32), S((flat_rows(p), LN), BF)],
        in_specs=[sm] + [vm] * 17,
        scratch_shapes=[pltpu.VMEM((16, FF), F32), pltpu.VMEM((LEN, D), BF), pltpu.VMEM((LEN, D), BF), pltpu.VMEM((LEN, 3 * D), BF), pltpu.VMEM((6144 + 32, LN), F32), pltpu.VMEM((160, LN), F32)],
        compiler_params=pltpu.CompilerParams(vmem_limit_bytes=60 << 20),
    )(length, tok, V, VG, qkv, lse, mixed, xh1, rstd1, first_low, act, gd, res, d_outer, wqkv, wo, w1, w2)


def on_device(p, fast, tokens, lengths, weight_shards, hidden_cotangent, nested_cotangent):
    slot = build_slot(p, weight_shards, me_of)
    slots = gather(p, slot) if fast else lax.all_gather(slot, AX, axis=0)
    tok = tokens.reshape(LEN, D)
    (hidden, nested, wqkv, wo, w1, w2, V, VG, qkv, lse, mixed, xh1, rstd1, first_low, act, gd, res, d_outer) = forward_local(p, slots, lengths, tok, hidden_cotangent.reshape(LEN, D), nested_cotangent)
    igrad, flat = backward_local(p, lengths, tok, V, VG, qkv, lse, mixed, xh1, rstd1, first_low, act, gd, res, d_outer, wqkv, wo, w1, w2)
    shards = scatter(p, flat) if fast else scatter_plain(p, flat)
    return (hidden.reshape(1, LEN, D), nested, igrad.reshape(1, LEN, D), shards)


def solution(mesh):
    in_specs = (
        P(("dp", "fsdp"), None, None),
        P(("dp", "fsdp")),
        P(("dp", "fsdp")),
        P(("dp", "fsdp"), None, None),
        P(("dp", "fsdp"), None),
    )
    out_specs = (
        P(("dp", "fsdp"), None, None),
        P(("dp", "fsdp"), None),
        P(("dp", "fsdp"), None, None),
        P(("dp", "fsdp")),
    )
    p = plan(mesh.shape["dp"] * mesh.shape["fsdp"])
    fast = (mesh.shape["dp"], mesh.shape["fsdp"]) == (4, 8)
    return jax.shard_map(
        functools.partial(on_device, p, fast), mesh=mesh, in_specs=in_specs, out_specs=out_specs, check_vma=False
    )
```

```python
import functools
import math

import jax
import jax.numpy as jnp
from jax import lax
from jax.experimental import pallas as pl
from jax.experimental.pallas import tpu as pltpu
from jax.sharding import PartitionSpec as P

AX = ("dp", "fsdp")
MESH = pl.DeviceIdType.MESH
D = 768
H = 12
HD = 64
FF = 3072
LEN = 512
E2 = 512
E3 = 256
E4 = 128
E5 = 64


epsilon = 1e-05


PAR=7088640; LN=128
class Plan: pass
def plan(n):
    p=Plan(); p.n=n; p.sh=PAR//n
    st=[i*p.sh for i in range(n)]
    p.g0=[s//LN//16 for s in st]
    p.g1=[(s+p.sh-1)//LN//16 for s in st]
    p.slot=16*max(b-a+1 for a,b in zip(p.g0,p.g1))
    p.rows_in=-(-p.sh//LN)
    return p
MATS=[("wqkv",0,D,18),("wo",13836,D,6),("w1",18462,D,24),("w2",36918,FF,6)]
VECS=[(13824,12),(18444,18),(36894,24),(55350,30)]

def build_slot_kernel(p,me_of,x_ref,o_ref,q_ref):
    i=me_of(); start=i*p.sh; r_first=start//LN; s=start-r_first*LN; r0=r_first%16
    lead=32
    q_ref[...]=jnp.zeros_like(q_ref)
    q=pltpu.roll(x_ref[...].astype(jnp.float32),s,1)
    q_ref[lead:lead+p.rows_in]=q
    lane=lax.broadcasted_iota(jnp.int32,(p.slot,LN),1)
    a=q_ref[pl.ds(lead-r0,p.slot),:]
    b=q_ref[pl.ds(lead-1-r0,p.slot),:]
    o_ref[...]=jnp.where(lane>=s,a,b).astype(jnp.bfloat16)

def build_slot(p,shard,me_of):
    x=jnp.pad(shard,(0,p.rows_in*LN-p.sh)).reshape(p.rows_in,LN)
    return pl.pallas_call(functools.partial(build_slot_kernel,p,me_of),out_shape=jax.ShapeDtypeStruct((p.slot,LN),jnp.bfloat16),
        scratch_shapes=[pltpu.VMEM((32+p.slot+32,LN),jnp.float32)])(x)

def load_flat(p,slots,F,g_lo,g_hi,need=None):
    for i in range(p.n):
        a=max(g_lo,p.g0[i]); b=min(g_hi,p.g1[i]+1)
        if a>=b: continue
        shared_first = i>0 and p.g0[i]==p.g1[i-1] and a==p.g0[i]
        a2=a+1 if shared_first else a
        b2=b
        apart=need is not None and need<=(i+1)*p.sh//LN
        if i+1<p.n and p.g1[i]==p.g0[i+1] and b==p.g1[i]+1 and not apart: b2=b-1
        if i+1<p.n and b2<b and b-1>=g_lo:
            g=b-1
            F[16*(g-g_lo):16*(g-g_lo)+16]=slots[i,16*(g-p.g0[i]):16*(g-p.g0[i])+16].astype(jnp.float32)+slots[i+1,0:16].astype(jnp.float32)
        cnt=b2-a2
        if cnt<=0: continue
        U=16
        nb,rem=cnt//U,cnt%U
        def body(t,_,i=i,a2=a2):
            src=pl.multiple_of(16*(a2-p.g0[i])+t*16*U,16); dst=pl.multiple_of(16*(a2-g_lo)+t*16*U,16)
            F[pl.ds(dst,16*U)]=slots[i,pl.ds(src,16*U)].astype(jnp.float32)
            return 0
        lax.fori_loop(0,nb,body,0)
        if rem:
            src=16*(a2-p.g0[i])+nb*16*U; dst=16*(a2-g_lo)+nb*16*U
            F[dst:dst+16*rem]=slots[i,src:src+16*rem].astype(jnp.float32)

def coords():
    dp=lax.axis_index("dp"); fs=lax.axis_index("fsdp")
    return dp//2,fs%2,fs//2,dp%2
def dev(x,y,z,c): return (x*2+c, z*2+y)
def lin(x,y,z,c): return (x*2+c)*8+z*2+y
def barrier(partners):
    bar=pltpu.get_barrier_semaphore()
    for q in partners: pl.semaphore_signal(bar,inc=1,device_id=q,device_id_type=MESH)
    pl.semaphore_wait(bar,len(partners))

TOT=PAR//LN
def flat_rows(p): return max(16*p.g0[-1]+p.slot, EDGES[-1][0]+EDGES[-1][1])
def owner_row(rho):
    for k,(name,base,rows,w) in enumerate(MATS):
        if base<=rho<base+rows*w: return ("m",k,(rho-base)//w,(rho-base)%w)
    at=0
    for base,cnt in VECS:
        if base<=rho<base+cnt: return ("v",at+rho-base)
        at+=cnt
    return None

def me_of():
    return lax.axis_index(AX)


def finish_kernel(p, a_ref, out, A):
    SL = p.slot
    start = me_of() * p.sh
    r_first = start // LN
    s = start - r_first * LN
    r0 = r_first % 16
    A[0:SL] = pltpu.roll(a_ref[...], lax.rem(LN - s, LN), 1)
    lane = lax.broadcasted_iota(jnp.int32, (p.rows_in, LN), 1)
    out[...] = jnp.where(lane < LN - s, A[pl.ds(r0, p.rows_in), :], A[pl.ds(r0 + 1, p.rows_in), :])


def scatter_plain(p, flat):
    parts = jnp.concatenate([flat[16 * g : 16 * g + p.slot] for g in p.g0]).astype(jnp.float32)
    mine = lax.psum_scatter(parts, AX, scatter_dimension=0, tiled=True)
    o = pl.pallas_call(
        functools.partial(finish_kernel, p),
        out_shape=jax.ShapeDtypeStruct((p.rows_in, LN), jnp.float32),
        scratch_shapes=[pltpu.VMEM((p.slot + 32, LN), jnp.float32)],
    )(mine)
    return o.reshape(-1)[: p.sh]

EPS = 1e-05
F32 = jnp.float32
BF = jnp.bfloat16
SQ = math.sqrt(0.5)
PHI = 1.0 / math.sqrt(2.0 * math.pi)
VNAMES = (
    ("q_bias", D),
    ("v_bias", D),
    ("out_bias", D),
    ("first_gain", D),
    ("first_shift", D),
    ("up_bias", FF),
    ("down_bias", D),
    ("second_gain", D),
    ("second_shift", D),
    ("exit_gain", D),
    ("exit_shift", D),
)
VI = {name: k for k, (name, _) in enumerate(VNAMES)}
PREFIXES = (D, E2, E3, E4, E5)


def mm(a, b):
    return jnp.dot(a, b, preferred_element_type=F32)


def mm_nt(a, b):
    return lax.dot_general(a, b, (((1,), (1,)), ((), ())), preferred_element_type=F32)


def mm_tn(a, b):
    return lax.dot_general(a, b, (((0,), (0,)), ((), ())), preferred_element_type=F32)


def vrow(V, name):
    k = VI[name]
    return V[k : k + 1, : VNAMES[k][1]]


def mean_last(a):
    return jnp.mean(a, axis=-1, keepdims=True)


def sum_rows(a):
    return jnp.sum(a, axis=0, keepdims=True)


def forward_qkv(r):
    bias = jnp.concatenate([vrow(r.V, "q_bias"), jnp.zeros((1, D), F32), vrow(r.V, "v_bias")], axis=1)
    r.qb[...] = bias

    def body(j, _):
        o = pl.ds(pl.multiple_of(j * 256, 256), 256)
        r.qkv[:, o] = (mm(r.tok[...], r.wqkv[:, o]) + r.qb[:, o]).astype(BF)
        return 0

    lax.fori_loop(0, 3 * D // 256, body, 0)


def half_lanes(h):
    lane = lax.broadcasted_iota(jnp.int32, (LEN, LN), 1)
    return lane < HD if h == 0 else lane >= HD


def pair(r, part, hp):
    return r.qkv[:, pl.ds(pl.multiple_of(part * D + hp * LN, LN), LN)]


def forward_heads(r, hp):
    q, k, v = pair(r, 0, hp), pair(r, 1, hp), pair(r, 2, hp)
    valid = lax.broadcasted_iota(jnp.int32, (1, LEN), 1) < r.length
    out = None
    lse_all = r.lse[...]
    lane = lax.broadcasted_iota(jnp.int32, (LEN, LN), 1)
    for h in range(2):
        qh = jnp.where(half_lanes(h), q, jnp.zeros_like(q))
        s = jnp.where(valid, mm_nt(qh, k) * 0.125, -1e9)
        m = jnp.max(s, axis=1, keepdims=True)
        e = jnp.exp(s - m)
        l = jnp.sum(e, axis=1, keepdims=True)
        low = (e * (1.0 / l)).astype(BF)
        o = mm(low, v)
        out = o if out is None else jnp.where(half_lanes(0), out, o)
        lse_all = jnp.where(lane == 2 * hp + h, m + jnp.log(l), lse_all)
    r.lse[...] = lse_all
    r.mixed[:, pl.ds(pl.multiple_of(hp * LN, LN), LN)] = out.astype(BF)


def rows_of(b, n):
    return pl.ds(pl.multiple_of(b * n, n), n)


def forward_first(r):
    def body(b, _):
        o = rows_of(b, 256)
        v = r.tok[o, :].astype(F32) + mm(r.mixed[o, :], r.wo[...]) + vrow(r.V, "out_bias")
        cen = v - mean_last(v)
        rstd = lax.rsqrt(mean_last(cen * cen) + EPS)
        xh = cen * rstd
        r.xh1[o, :] = xh
        r.rstd1[o, :] = rstd
        r.first_low[o, :] = (xh * vrow(r.V, "first_gain") + vrow(r.V, "first_shift")).astype(BF)
        return 0

    lax.fori_loop(0, LEN // 256, body, 0)


def forward_up(r, j):
    o = pl.ds(pl.multiple_of(j * 256, 256), 256)
    v = mm(r.first_low[...], r.w1[:, o]) + r.V[VI["up_bias"] : VI["up_bias"] + 1, o]
    cdf = 0.5 * (1.0 + lax.erf(v * SQ))
    r.act[:, o] = (v * cdf).astype(BF)
    r.gd[:, o] = (cdf + v * (PHI * jnp.exp(-0.5 * v * v))).astype(BF)


def forward_second(r):
    def body(b, tot):
        o = rows_of(b, 256)
        first = r.xh1[o, :] * vrow(r.V, "first_gain") + vrow(r.V, "first_shift")
        v = first + mm(r.act[o, :], r.w2[...]) + vrow(r.V, "down_bias")
        cen = v - mean_last(v)
        rstd = lax.rsqrt(mean_last(cen * cen) + EPS)
        xh = cen * rstd
        r.xh2[o, :] = xh
        r.rstd2[o, :] = rstd
        t = lax.broadcasted_iota(jnp.int32, (256, 1), 0) + b * 256
        hid = (xh * vrow(r.V, "second_gain") + vrow(r.V, "second_shift")) * (t < r.length).astype(F32)
        r.hidden[o, :] = hid.astype(BF)
        return tot + sum_rows(hid)

    return lax.fori_loop(0, LEN // 256, body, jnp.zeros((1, D), F32))


def head(r, tot):
    inv_len = 1.0 / jnp.full((1, 1), r.length, jnp.int32).astype(F32)
    pooled = tot * inv_len
    cen = pooled - mean_last(pooled)
    rstd = lax.rsqrt(mean_last(cen * cen) + EPS)
    xh = cen * rstd
    gain = vrow(r.V, "exit_gain")
    emb = xh * gain + vrow(r.V, "exit_shift")
    d_emb = jnp.zeros((1, D), F32)
    at = 0
    for m in PREFIXES:
        e = emb[:, :m]
        inv = lax.rsqrt(jnp.sum(e * e, axis=1, keepdims=True) * (1.0 / m) + EPS)
        out = e * inv
        r.nested[:, at : at + m] = out
        c = r.ncot[:, at : at + m]
        g = inv * (c - out * (jnp.sum(c * out, axis=1, keepdims=True) * (1.0 / m)))
        d_emb = d_emb + (g if m == D else jnp.concatenate([g, jnp.zeros((1, D - m), F32)], axis=1))
        at += m
    put_grad(r, "exit_gain", d_emb * xh)
    put_grad(r, "exit_shift", d_emb)
    dx = d_emb * gain
    return rstd * (dx - mean_last(dx) - xh * mean_last(dx * xh)) * inv_len


def put_grad(r, name, value):
    k = VI[name]
    r.VG[k : k + 1, : VNAMES[k][1]] = value


def norm_back(dy, gain, xh, rstd):
    dx = dy * gain
    return rstd * (dx - mean_last(dx) - xh * mean_last(dx * xh))


def backward_second(r, d_pool):
    def body(b, c):
        o = rows_of(b, 128)
        t = lax.broadcasted_iota(jnp.int32, (128, 1), 0) + b * 128
        dy = (r.hcot[o, :].astype(F32) + d_pool) * (t < r.length).astype(F32)
        xh = r.xh2[o, :]
        res = norm_back(dy, vrow(r.V, "second_gain"), xh, r.rstd2[o, :])
        r.res[o, :] = res
        low = res.astype(BF)
        r.d_outer[o, :] = low
        return (c[0] + sum_rows(dy * xh), c[1] + sum_rows(dy), c[2] + sum_rows(low.astype(F32)))

    z = jnp.zeros((1, D), F32)
    a, b, c = lax.fori_loop(0, LEN // 128, body, (z, z, z))
    put_grad(r, "second_gain", a)
    put_grad(r, "second_shift", b)
    put_grad(r, "down_bias", c)


def backward_act(r, j):
    o = pl.ds(pl.multiple_of(j * 256, 256), 256)
    d = (mm_nt(r.d_outer[...], r.w2[o, :]) * r.gd[:, o].astype(F32)).astype(BF)
    r.gd[:, o] = d
    r.VG[VI["up_bias"] : VI["up_bias"] + 1, o] = sum_rows(d.astype(F32))


def backward_first(r):
    def body(b, c):
        o = rows_of(b, 256)
        dy = mm_nt(r.gd[o, :], r.w1[...]) + r.res[o, :]
        xh = r.xh1[o, :]
        res = norm_back(dy, vrow(r.V, "first_gain"), xh, r.rstd1[o, :])
        r.res[o, :] = res
        low = res.astype(BF)
        r.d_branch[o, :] = low
        return (c[0] + sum_rows(dy * xh), c[1] + sum_rows(dy), c[2] + sum_rows(low.astype(F32)))

    z = jnp.zeros((1, D), F32)
    a, b, c = lax.fori_loop(0, LEN // 256, body, (z, z, z))
    put_grad(r, "first_gain", a)
    put_grad(r, "first_shift", b)
    put_grad(r, "out_bias", c)


def backward_mixed(r):
    r.d_mixed[...] = mm_nt(r.d_branch[...], r.wo[...]).astype(BF)


def backward_heads(r, hp):
    q, k, v = pair(r, 0, hp), pair(r, 1, hp), pair(r, 2, hp)
    cols = pl.ds(pl.multiple_of(hp * LN, LN), LN)
    dm = r.d_mixed[:, cols]
    valid = lax.broadcasted_iota(jnp.int32, (1, LEN), 1) < r.length
    lane = lax.broadcasted_iota(jnp.int32, (LEN, LN), 1)
    zero = jnp.zeros_like(q)
    dq = dk = dv = None
    for h in range(2):
        here = half_lanes(h)
        qh, kh, dmh = jnp.where(here, q, zero), jnp.where(here, k, zero), jnp.where(here, dm, zero)
        lse = jnp.sum(jnp.where(lane == 2 * hp + h, r.lse[...], 0.0), axis=1, keepdims=True)
        s = jnp.where(valid, mm_nt(qh, k) * 0.125, -1e9)
        p = jnp.exp(s - lse)
        dp = mm_nt(dmh, v)
        ds = (p * (dp - jnp.sum(dp * p, axis=1, keepdims=True))).astype(BF)
        a, b, c = mm(ds, kh), mm_tn(ds, qh), mm_tn(p.astype(BF), dmh)
        dq, dk, dv = (a, b, c) if dq is None else (dq + a, dk + b, dv + c)
    dq, dk, dv = (dq * 0.125).astype(BF), (dk * 0.125).astype(BF), dv.astype(BF)
    for part, g in ((0, dq), (1, dk), (2, dv)):
        r.dqkv[:, pl.ds(pl.multiple_of(part * D + hp * LN, LN), LN)] = g
    k = VI["q_bias"]
    r.VG[k : k + 1, cols] = sum_rows(dq.astype(F32))
    k = VI["v_bias"]
    r.VG[k : k + 1, cols] = sum_rows(dv.astype(F32))


def backward_tokens(r, b):
    o = rows_of(b, 128)
    v = r.res[o, :]
    for part in range(3):
        v = v + mm_nt(r.dqkv[o, part * D : (part + 1) * D], r.wqkv[:, part * D : (part + 1) * D])
    r.res[o, :] = v


EDGES = ((13824, 16), (18432, 32), (36880, 48), (55344, 64))


def edge_at(row):
    at = 0
    for base, rows in EDGES:
        if base <= row < base + rows:
            return at + row - base
        at += rows
    return None


def weight_grad(r, lhs, rhs, base, rows, w, RB=256, CB=6, hook=None):
    lead = base % 16
    step_rows = RB * w
    F = r.F
    if lead:
        F[0:16] = jnp.zeros((16, LN), F32)

    def body(s, _):
        o = pl.ds(pl.multiple_of(s * RB, RB), RB)
        for ch in range(w // CB):
            g = mm_tn(lhs[:, o], rhs[:, ch * CB * LN : (ch + 1) * CB * LN])
            for j in range(CB):
                F[pl.ds(lead + ch * CB + j, RB, stride=w), :] = g[:, j * LN : (j + 1) * LN]
        if lead:
            @pl.when(s == 0)
            def _():
                e = edge_at(base)
                r.E[e : e + 16 - lead] = F[lead:16]

        U = 256
        to = base - lead + s * step_rows

        def emit(t, _):
            r.FG[pl.ds(pl.multiple_of(to + t * U, 16), U)] = F[pl.ds(pl.multiple_of(t * U, 16), U)].astype(BF)
            return 0

        lax.fori_loop(0, step_rows // U, emit, 0)
        if lead:
            F[0:16] = F[step_rows : step_rows + 16]
        if hook is not None:
            hook(s)
        return 0

    lax.fori_loop(0, rows // RB, body, 0)
    if lead:
        e = edge_at(base + rows * w - lead)
        r.E[e : e + lead] = F[0:lead]


def edge_grads(r, which):
    base, rows = EDGES[which]
    at = 0
    for vbase, cnt in VECS:
        for k in range(cnt):
            row = vbase + k
            if base <= row < base + rows:
                name, j = vec_at(at + k)
                e = edge_at(row)
                r.E[e : e + 1] = r.VG[name : name + 1, j * LN : (j + 1) * LN]
        at += cnt
    if which == len(EDGES) - 1:
        e = edge_at(TOT)
        r.E[e : e + base + rows - TOT] = jnp.zeros((base + rows - TOT, LN), F32)
    e = edge_at(base)
    r.FG[base : base + rows] = r.E[e : e + rows].astype(BF)


def vec_at(row):
    for k, (_, n) in enumerate(VNAMES):
        if row < n // LN:
            return k, row
        row -= n // LN


class Refs:
    def __init__(self, **refs):
        self.__dict__.update(refs)


def relayout_vectors(p, r):
    at = 0
    for base, cnt in VECS:
        g_lo = base // 16
        g_hi = -(-(base + cnt) // 16)
        load_flat(p, r.slots, r.F, g_lo, g_hi)
        for k in range(cnt):
            name, j = vec_at(at + k)
            f = base - 16 * g_lo + k
            r.V[name : name + 1, j * LN : (j + 1) * LN] = r.F[f : f + 1]
        at += cnt


def relayout_matrix(p, r, name, W, RB):
    base, rows, w = {n: (b, k, c) for n, b, k, c in MATS}[name]
    for s in range(rows // RB):
        lo = base + s * RB * w
        g_lo = lo // 16
        load_flat(p, r.slots, r.F, g_lo, -(-(lo + RB * w) // 16))
        tile_rows(r.F, W, lo - 16 * g_lo, s * RB, RB, w)


def tile_rows(F, W, off, row, rows, w, RB=64):
    def body(t, _):
        q = pl.multiple_of(t * RB, RB)
        for j in range(w):
            W[pl.ds(row + q, RB), j * LN : (j + 1) * LN] = F[pl.ds(off + q * w + j, RB, stride=w), :].astype(BF)
        return 0

    lax.fori_loop(0, rows // RB, body, 0)


def forward_kernel(p, slots, length, tok, hcot, ncot, hidden, nested, wqkv, wo, w1, w2, V, VG, qkv, lse, mixed, xh1, rstd1, first_low, act, gd, res, d_outer, F, qb, xh2, rstd2):
    r = Refs(slots=slots, length=length[0], tok=tok, hcot=hcot, ncot=ncot, hidden=hidden, nested=nested, wqkv=wqkv, wo=wo, w1=w1, w2=w2, V=V, VG=VG, qkv=qkv, lse=lse, mixed=mixed, xh1=xh1, rstd1=rstd1, first_low=first_low, act=act, gd=gd, res=res, d_outer=d_outer, F=F, qb=qb, xh2=xh2, rstd2=rstd2)
    relayout_vectors(p, r)
    relayout_matrix(p, r, "wqkv", wqkv, 256)
    forward_qkv(r)
    lse[...] = jnp.zeros_like(lse)
    lax.fori_loop(0, H // 2, lambda hp, c: (forward_heads(r, hp), c)[1], 0)
    relayout_matrix(p, r, "wo", wo, 768)
    forward_first(r)
    relayout_matrix(p, r, "w1", w1, 256)
    lax.fori_loop(0, FF // 256, lambda j, c: (forward_up(r, j), c)[1], 0)
    relayout_matrix(p, r, "w2", w2, 768)
    tot = forward_second(r)
    d_pool = head(r, tot)
    backward_second(r, d_pool)


def forward_local(p, slots, length, tok, hcot, ncot):
    S = jax.ShapeDtypeStruct
    outs = [S((LEN, D), BF), S((1, 1728), F32), S((D, 3 * D), BF), S((D, D), BF), S((D, FF), BF), S((FF, D), BF), S((16, FF), F32), S((16, FF), F32), S((LEN, 3 * D), BF), S((LEN, LN), F32), S((LEN, D), BF), S((LEN, D), F32), S((LEN, 1), F32), S((LEN, D), BF), S((LEN, FF), BF), S((LEN, FF), BF), S((LEN, D), F32), S((LEN, D), BF)]
    vm = pl.BlockSpec(memory_space=pltpu.VMEM)
    sm = pl.BlockSpec(memory_space=pltpu.SMEM)
    return pl.pallas_call(
        functools.partial(forward_kernel, p),
        out_shape=outs,
        in_specs=[vm, sm, vm, vm, vm],
        scratch_shapes=[pltpu.VMEM((6144 + 32, LN), F32), pltpu.VMEM((1, 3 * D), F32), pltpu.VMEM((LEN, D), F32), pltpu.VMEM((LEN, 1), F32)],
        compiler_params=pltpu.CompilerParams(vmem_limit_bytes=60 << 20),
    )(slots, length, tok, hcot, ncot)


def backward_kernel(p, length, tok, V, VG0, qkv, lse, mixed, xh1, rstd1, first_low, act, gd, res, d_outer, wqkv, wo, w1, w2, igrad, FG, VG, d_branch, d_mixed, dqkv, F, E):
    r = Refs(length=length[0], tok=tok, V=V, VG=VG, qkv=qkv, lse=lse, mixed=mixed, xh1=xh1, rstd1=rstd1, first_low=first_low, act=act, gd=gd, res=igrad, d_outer=d_outer, wqkv=wqkv, wo=wo, w1=w1, w2=w2, FG=FG, d_branch=d_branch, d_mixed=d_mixed, dqkv=dqkv, F=F, E=E)
    VG[...] = VG0[...]
    igrad[...] = res[...]
    mats = {n: (b, k, c) for n, b, k, c in MATS}
    weight_grad(r, act, d_outer, *mats["w2"])
    edge_grads(r, 3)
    lax.fori_loop(0, FF // 256, lambda j, c: (backward_act(r, j), c)[1], 0)
    weight_grad(r, first_low, gd, *mats["w1"])
    edge_grads(r, 2)
    backward_first(r)
    weight_grad(r, mixed, d_branch, *mats["wo"])
    edge_grads(r, 1)
    backward_mixed(r)
    lax.fori_loop(0, H // 2, lambda hp, c: (backward_heads(r, hp), c)[1], 0)
    weight_grad(r, tok, dqkv, *mats["wqkv"])
    edge_grads(r, 0)
    lax.fori_loop(0, LEN // 128, lambda b, c: (backward_tokens(r, b), c)[1], 0)


def backward_local(p, length, tok, V, VG, qkv, lse, mixed, xh1, rstd1, first_low, act, gd, res, d_outer, wqkv, wo, w1, w2):
    S = jax.ShapeDtypeStruct
    vm = pl.BlockSpec(memory_space=pltpu.VMEM)
    sm = pl.BlockSpec(memory_space=pltpu.SMEM)
    return pl.pallas_call(
        functools.partial(backward_kernel, p),
        out_shape=[S((LEN, D), F32), S((flat_rows(p), LN), BF)],
        in_specs=[sm] + [vm] * 17,
        scratch_shapes=[pltpu.VMEM((16, FF), F32), pltpu.VMEM((LEN, D), BF), pltpu.VMEM((LEN, D), BF), pltpu.VMEM((LEN, 3 * D), BF), pltpu.VMEM((6144 + 32, LN), F32), pltpu.VMEM((160, LN), F32)],
        compiler_params=pltpu.CompilerParams(vmem_limit_bytes=60 << 20),
    )(length, tok, V, VG, qkv, lse, mixed, xh1, rstd1, first_low, act, gd, res, d_outer, wqkv, wo, w1, w2)


class Gather:
    def __init__(self, p, G, ssem, rsem, gosem):
        self.p, self.G, self.ssem, self.rsem, self.gosem = p, G, ssem, rsem, gosem
        self.x, self.y, self.z, self.c = coords()
        x, y, z, c = self.x, self.y, self.z, self.c
        self.me = lin(x, y, z, c)
        half = p.slot // 32 * 16
        self.H = ((0, half), (half, p.slot - half), (0, p.slot))
        self.px, self.py, self.pc = dev(1 - x, y, z, c), dev(x, 1 - y, z, c), dev(x, y, z, 1 - c)

    def enter(self):
        x, y, z, c = self.x, self.y, self.z, self.c
        bar = pltpu.get_barrier_semaphore()

        def greet(to):
            pl.semaphore_signal(bar, inc=1, device_id=to, device_id_type=MESH)

        for to in (self.px, self.py, self.pc):
            greet(to)
        pl.when(z > 0)(lambda: greet(dev(x, y, z - 1, c)))
        pl.when(z < 3)(lambda: greet(dev(x, y, z + 1, c)))
        middle = (z > 0) & (z < 3)
        pl.when(middle)(lambda: pl.semaphore_wait(bar, 5))
        pl.when(jnp.logical_not(middle))(lambda: pl.semaphore_wait(bar, 4))

    def send(self, sl, h, to, t):
        r0, rn = self.H[h]
        ref = self.G.at[sl, pl.ds(r0, rn)]
        pltpu.make_async_remote_copy(src_ref=ref, dst_ref=ref, send_sem=self.ssem.at[sl, t], recv_sem=self.rsem.at[sl, h], device_id=to, device_id_type=MESH).start()

    def wait(self, sl, h, sem=None):
        r0, rn = self.H[h]
        ref = self.G.at[sl, pl.ds(r0, rn)]
        pltpu.make_async_copy(ref, ref, self.rsem.at[sl, h] if sem is None else sem).wait()

    def up(self, sl):
        pl.when(self.z < 3)(lambda: self.send(sl, 2, dev(self.x, self.y, self.z + 1, self.c), 3))

    def down(self, sl):
        pl.when(self.z > 0)(lambda: self.send(sl, 2, dev(self.x, self.y, self.z - 1, self.c), 4))

    def core(self, sl, h=2):
        self.send(sl, h, self.pc, 2)

    def xy(self, sl):
        self.send(sl, 2, self.px, 0)
        self.send(sl, 2, self.py, 1)

    def go(self, k):
        pl.semaphore_signal(self.gosem.at[k], inc=1, device_id=self.pc, device_id_type=MESH)

    def wait_go(self, k):
        pl.semaphore_wait(self.gosem.at[k], 1)

    def at(self, k, fn):
        if k == 0:
            fn(self.z)
            return
        pl.when(self.z - k >= 0)(lambda: fn(self.z - k))
        pl.when(self.z + k <= 3)(lambda: fn(self.z + k))

    def along_z(self, k, xy):
        x, y, z, c = self.x, self.y, self.z, self.c

        def below():
            sl = lin(x, y, z - k, c)
            self.wait(sl, 2)
            self.up(sl)
            if xy:
                self.xy(sl)
            self.core(sl)

        def above():
            sl = lin(x, y, z + k, c)
            self.wait(sl, 2)
            self.down(sl)
            if xy:
                self.xy(sl)
            self.core(sl)

        pl.when(z - k >= 0)(below)
        pl.when(z + k <= 3)(above)

    def sides(self, k):
        x, y, c = self.x, self.y, self.c

        def fn(zq):
            sl = lin(1 - x, y, zq, c)
            self.wait(sl, 2)
            self.send(sl, 0, self.py, 1)
            self.core(sl)
            sl = lin(x, 1 - y, zq, c)
            self.wait(sl, 2)
            self.send(sl, 1, self.px, 0)
            self.core(sl)

        self.at(k, fn)

    def diagonal(self, k):
        def fn(zq):
            sl = lin(1 - self.x, 1 - self.y, zq, self.c)
            for h in (0, 1):
                self.wait(sl, h)
                self.core(sl, h)

        self.at(k, fn)

    def from_sibling(self, xp):
        x, y, c = self.x, self.y, self.c

        def body(zq, carry):
            self.wait(lin(xp, y, zq, 1 - c), 2)
            other = lin(xp, 1 - y, zq, 1 - c)
            pl.when(x == xp)(lambda: self.wait(other, 2))

            def halves():
                self.wait(other, 0)
                self.wait(other, 1)

            pl.when(x != xp)(halves)
            return carry

        lax.fori_loop(0, 4, body, 0)

    def leave(self):
        x, y, z, c = self.x, self.y, self.z, self.c
        W = self.wait

        def body(zq, carry):
            sl = lin(x, y, zq, c)
            for t in (0, 1, 2):
                W(sl, 2, self.ssem.at[sl, t])
            pl.when((zq <= z) & (z < 3))(lambda: W(sl, 2, self.ssem.at[sl, 3]))
            pl.when((zq >= z) & (z > 0))(lambda: W(sl, 2, self.ssem.at[sl, 4]))
            sx = lin(1 - x, y, zq, c)
            W(sx, 0, self.ssem.at[sx, 1])
            W(sx, 2, self.ssem.at[sx, 2])
            sy = lin(x, 1 - y, zq, c)
            W(sy, 1, self.ssem.at[sy, 0])
            W(sy, 2, self.ssem.at[sy, 2])
            sd = lin(1 - x, 1 - y, zq, c)
            W(sd, 2, self.ssem.at[sd, 2])
            return carry

        lax.fori_loop(0, 4, body, 0)


FORWARD_OUT = ("hidden", "nested", "wqkv", "wo", "w1", "w2", "V", "VG", "qkv", "lse", "mixed", "xh1", "rstd1", "first_low", "act", "gd", "res", "d_outer")
FORWARD_SHAPES = dict(
    hidden=((LEN, D), jnp.bfloat16),
    nested=((1, 1728), jnp.float32),
    wqkv=((D, 3 * D), jnp.bfloat16),
    wo=((D, D), jnp.bfloat16),
    w1=((D, FF), jnp.bfloat16),
    w2=((FF, D), jnp.bfloat16),
    V=((16, FF), jnp.float32),
    VG=((16, FF), jnp.float32),
    qkv=((LEN, 3 * D), jnp.bfloat16),
    lse=((LEN, LN), jnp.float32),
    mixed=((LEN, D), jnp.bfloat16),
    xh1=((LEN, D), jnp.float32),
    rstd1=((LEN, 1), jnp.float32),
    first_low=((LEN, D), jnp.bfloat16),
    act=((LEN, FF), jnp.bfloat16),
    gd=((LEN, FF), jnp.bfloat16),
    res=((LEN, D), jnp.float32),
    d_outer=((LEN, D), jnp.bfloat16),
)


def own_slot(p, me, x_ref, F, G):
    start = me * p.sh
    r_first = start // LN
    s = start - r_first * LN
    r0 = r_first % 16
    lead = 32
    F[0 : lead + p.slot + 32] = jnp.zeros((lead + p.slot + 32, LN), F32)
    F[lead : lead + p.rows_in] = pltpu.roll(x_ref[...].astype(F32), s, 1)
    lane = lax.broadcasted_iota(jnp.int32, (p.slot, LN), 1)
    G[me] = jnp.where(lane >= s, F[pl.ds(lead - r0, p.slot), :], F[pl.ds(lead - 1 - r0, p.slot), :]).astype(BF)


def relayout_vector(p, r, which):
    at = sum(cnt for _, cnt in VECS[:which])
    base, cnt = VECS[which]
    g_lo = base // 16
    load_flat(p, r.slots, r.F, g_lo, -(-(base + cnt) // 16), base + cnt)
    for k in range(cnt):
        name, j = vec_at(at + k)
        f = base - 16 * g_lo + k
        r.V[name : name + 1, j * LN : (j + 1) * LN] = r.F[f : f + 1]


def relayout_rows(p, r, name, W, row, rows):
    base, _, w = {n: (b, k, c) for n, b, k, c in MATS}[name]
    lo = base + row * w
    g_lo = lo // 16
    load_flat(p, r.slots, r.F, g_lo, -(-(lo + rows * w) // 16), lo + rows * w)
    tile_rows(r.F, W, lo - 16 * g_lo, row, rows, w)


def gather_forward_kernel(p, x_ref, length, tok, hcot, ncot, *refs):
    n = len(FORWARD_OUT)
    outs = dict(zip(FORWARD_OUT, refs[:n]))
    loc = dict(zip(FORWARD_OUT, refs[n : 2 * n]))
    G, F, qb, xh2, rstd2, ssem, rsem, gosem, osem = refs[2 * n :]
    r = Refs(slots=G, length=length[0], tok=tok, hcot=hcot, ncot=ncot, F=F, qb=qb, xh2=xh2, rstd2=rstd2, **loc)
    g = Gather(p, G, ssem, rsem, gosem)
    own_slot(p, g.me, x_ref, F, G)
    g.enter()
    c0, c1 = g.c == 0, g.c == 1

    def first_planes():
        g.up(g.me)
        g.down(g.me)
        g.xy(g.me)
        g.core(g.me)
        g.along_z(1, True)
        g.sides(0)
        g.along_z(2, True)
        g.sides(1)
        g.along_z(3, True)
        g.go(0)
        g.diagonal(0)
        g.sides(2)
        g.diagonal(1)
        g.go(1)
        g.sides(3)
        g.diagonal(2)
        g.diagonal(3)

    def second_planes():
        g.wait_go(0)
        g.up(g.me)
        g.down(g.me)
        g.core(g.me)
        for k in (1, 2, 3):
            g.along_z(k, False)
        g.wait_go(1)
        for k in range(4):
            g.at(k, lambda zq: g.xy(lin(g.x, g.y, zq, g.c)))
        g.from_sibling(0)

    pl.when(c0)(first_planes)
    pl.when(c1)(second_planes)
    started = []

    def out(*names):
        for m in names:
            k = FORWARD_OUT.index(m)
            cp = pltpu.make_async_copy(loc[m], outs[m], osem.at[k])
            cp.start()
            started.append(cp)

    relayout_vector(p, r, 0)
    for k in range(3):
        relayout_rows(p, r, "wqkv", r.wqkv, 256 * k, 256)
    out("wqkv")
    forward_qkv(r)
    out("qkv")
    pl.when(c1)(lambda: g.sides(0))
    r.lse[...] = jnp.zeros_like(r.lse)

    def heads(hp, carry):
        forward_heads(r, hp)
        pl.when((hp == 1) & c1)(lambda: g.sides(1))
        pl.when((hp == 3) & c1)(lambda: g.sides(2))
        pl.when((hp == 4) & c1)(lambda: g.diagonal(0))
        pl.when((hp == 5) & c1)(lambda: g.sides(3))
        return carry

    lax.fori_loop(0, H // 2, heads, 0)
    out("lse", "mixed")
    pl.when(c1)(lambda: g.from_sibling(1))
    relayout_rows(p, r, "w1", r.w1, 448, 128)
    relayout_rows(p, r, "w1", r.w1, 576, 192)
    pl.when(c1)(lambda: g.diagonal(1))
    relayout_rows(p, r, "w2", r.w2, 0, 768)
    relayout_vector(p, r, 2)

    def rest():
        g.diagonal(2)
        g.diagonal(3)

    pl.when(c1)(rest)
    pl.when(c0)(lambda: g.from_sibling(0))
    relayout_rows(p, r, "wo", r.wo, 0, 768)
    relayout_vector(p, r, 1)
    out("wo")
    forward_first(r)
    out("xh1", "rstd1", "first_low")
    relayout_rows(p, r, "w1", r.w1, 0, 256)
    relayout_rows(p, r, "w1", r.w1, 256, 192)
    out("w1")
    lax.fori_loop(0, FF // 256, lambda j, c: (forward_up(r, j), c)[1], 0)
    out("act", "gd")
    pl.when(c0)(lambda: g.from_sibling(1))
    for k in range(1, 4):
        relayout_rows(p, r, "w2", r.w2, 768 * k, 768)
    relayout_vector(p, r, 3)
    out("w2", "V")
    tot = forward_second(r)
    out("hidden")
    d_pool = head(r, tot)
    out("nested")
    backward_second(r, d_pool)
    out("VG", "res", "d_outer")
    g.leave()
    for cp in started:
        cp.wait()


def gather_forward(p, shard, length, tok, hcot, ncot):
    x = jnp.pad(shard, (0, p.rows_in * LN - p.sh)).reshape(p.rows_in, LN)
    S = jax.ShapeDtypeStruct
    vm = pl.BlockSpec(memory_space=pltpu.VMEM)
    sm = pl.BlockSpec(memory_space=pltpu.SMEM)
    hbm = pl.BlockSpec(memory_space=pl.ANY)
    VM = pltpu.VMEM
    DM = pltpu.SemaphoreType.DMA
    shapes = [FORWARD_SHAPES[m] for m in FORWARD_OUT]
    res = pl.pallas_call(
        functools.partial(gather_forward_kernel, p),
        out_shape=[S(*s) for s in shapes],
        in_specs=[vm, sm, vm, vm, vm],
        out_specs=[hbm] * len(shapes),
        scratch_shapes=[VM(*s) for s in shapes]
        + [VM((p.n, p.slot, LN), BF), VM((6144 + 32, LN), F32), VM((1, 3 * D), F32), VM((LEN, D), F32), VM((LEN, 1), F32)]
        + [DM((p.n, 5)), DM((p.n, 3)), pltpu.SemaphoreType.REGULAR((2,)), DM((len(shapes),))],
        compiler_params=pltpu.CompilerParams(collective_id=0, has_side_effects=True, vmem_limit_bytes=64 << 20),
    )(x, length, tok, hcot, ncot)
    return dict(zip(FORWARD_OUT, res))


SCHEDULE = (
    (2, 1, 0, "diag", 1, 2, 2),
    (4, 1, 0, "diag", 1, 0, 2),
    (7, 1, 1, "yline", 1, 2, 2),
    (7, 1, 0, "xline", 1, 2, 2),
    (9, 0, 0, "diag", 1, 2, 2),
    (10, 1, 1, "diag", 0, 2, 2),
    (11, 1, 0, "xline", 1, 0, 2),
    (11, 1, 1, "diag", 0, 0, 2),
    (11, 1, 1, "yline", 1, 0, 2),
    (12, 0, 0, "diag", 1, 0, 2),
    (12, 0, 0, "xline", 1, 2, 2),
    (13, 1, 1, "xline", 0, 2, 2),
    (14, 1, 1, "xline", 0, 0, 2),
    (14, 1, 1, "own", 1, 2, 1),
    (17, 1, 0, "yline", 0, 2, 2),
    (18, 0, 1, "yline", 1, 2, 2),
    (20, 0, 0, "yline", 0, 0, 2),
    (20, 0, 1, "diag", 0, 0, 2),
    (20, 0, 1, "xline", 0, 0, 2),
    (20, 0, 1, "diag", 0, 2, 2),
    (20, 0, 0, "xline", 1, 0, 2),
    (20, 0, 0, "own", 0, 0, 2),
    (20, 1, 0, "own", 0, 2, 1),
    (21, 0, 1, "xline", 0, 2, 2),
    (21, 0, 0, "yline", 0, 2, 2),
    (21, 1, 0, "yline", 0, 0, 2),
    (21, 0, 1, "yline", 1, 0, 2),
    (21, 1, 0, "own", 0, 0, 2),
    (21, 0, 0, "own", 0, 2, 1),
    (21, 0, 1, "own", 1, 2, 1),
    (22, 0, 1, "own", 1, 0, 2),
    (22, 1, 1, "own", 1, 0, 2),
)


class Scatter:
    def __init__(self, p, FG, R, D0, D1, X, Y, Z, A, sems):
        self.p, self.FG, self.R, self.D0, self.D1, self.X, self.Y, self.Z, self.A = p, FG, R, D0, D1, X, Y, Z, A
        self.sib_s, self.sib_r, self.d_s, self.d_r, self.x_s, self.x_r, self.y_s, self.y_r, self.z_s, self.z_r = sems
        self.x, self.y, self.z, self.c = coords()
        x, y, z, c = self.x, self.y, self.z, self.c
        self.SL = p.slot
        self.half = p.slot // 32 * 16
        self.px, self.py, self.pc = dev(1 - x, y, z, c), dev(x, 1 - y, z, c), dev(x, y, z, 1 - c)

    def zq(self, b):
        d = lax.rem(b + 1, 4)
        z = self.z
        return lax.rem(z % 2 + d % 2, 2) + 2 * lax.rem(z // 2 + d // 2, 2)

    def enter(self):
        x, y, c = self.x, self.y, self.c
        barrier([self.px, self.py, self.pc] + [dev(x, y, self.zq(b), c) for b in range(3)])

    def row0(self, slot):
        return pl.multiple_of((slot * self.p.sh) // LN // 16 * 16, 16)

    def fg(self, slot):
        return self.row0(slot)

    def copy(self, src, dst, ssem, rsem, to):
        return pltpu.make_async_remote_copy(src_ref=src, dst_ref=dst, send_sem=ssem, recv_sem=rsem, device_id=to, device_id_type=MESH)

    def wait(self, ref, sem):
        pltpu.make_async_copy(ref, ref, sem).wait()

    def to_sibling(self, xp):
        def body(k, _):
            dp = 2 * xp + 1 - self.c
            i = 8 * xp + k
            self.copy(self.FG.at[pl.ds(self.row0(dp * 8 + k), self.SL)], self.R.at[i], self.sib_s.at[i], self.sib_r.at[i], self.pc).start()
            return 0

        lax.fori_loop(0, 8, body, 0)

    def add(self, dst, d0, rows, srcs, U=176):
        def body(t, _):
            r = pl.multiple_of(t * U, 16)
            v = None
            for s, s0 in srcs:
                e = s[pl.ds(s0 + r, U)].astype(F32)
                v = e if v is None else v + e
            dst[pl.ds(d0 + r, U)] = v.astype(dst.dtype)
            return 0

        lax.fori_loop(0, rows // U, body, 0)

    def have(self, xp, yq, zq):
        fs = zq * 2 + yq
        i = 8 * xp + fs
        self.wait(self.R.at[i], self.sib_r.at[i])
        return i, self.row0((2 * xp + self.c) * 8 + fs)

    def diag(self, xp, b):
        i, g = self.have(xp, 1 - self.y, self.zq(b))
        half, rest = self.half, self.SL - self.half
        R = self.R.at[i]
        self.add(R, 0, self.SL, [(self.FG, g), (R, 0)])
        self.copy(R.at[pl.ds(0, half)], self.D0.at[b], self.d_s.at[0, b], self.d_r.at[0, b], self.py).start()
        self.copy(R.at[pl.ds(half, rest)], self.D1.at[b], self.d_s.at[1, b], self.d_r.at[1, b], self.px).start()

    def xline(self, xp, b):
        i, g = self.have(xp, self.y, self.zq(b))
        half, rest = self.half, self.SL - self.half
        R = self.R.at[i]
        self.wait(self.D0.at[b], self.d_r.at[0, b])
        self.add(R, half, rest, [(self.FG, g + half), (R, half)])
        self.add(R, 0, half, [(self.FG, g), (R, 0), (self.D0.at[b], 0)])
        self.copy(R, self.X.at[b], self.x_s.at[b], self.x_r.at[b], self.px).start()

    def yline(self, xp, b):
        i, g = self.have(xp, 1 - self.y, self.zq(b))
        half, rest = self.half, self.SL - self.half
        R = self.R.at[i]
        self.wait(self.D1.at[b], self.d_r.at[1, b])
        self.add(R, 0, half, [(self.FG, g), (R, 0)])
        self.add(R, half, rest, [(self.FG, g + half), (R, half), (self.D1.at[b], 0)])
        self.copy(R, self.Y.at[b], self.y_s.at[b], self.y_r.at[b], self.py).start()

    def own(self, xp, b):
        i, g = self.have(xp, self.y, self.zq(b))
        R = self.R.at[i]
        self.wait(self.X.at[b], self.x_r.at[b])
        self.wait(self.Y.at[b], self.y_r.at[b])
        self.add(R, 0, self.SL, [(self.FG, g), (R, 0), (self.X.at[b], 0), (self.Y.at[b], 0)])
        self.copy(R, self.Z.at[b], self.z_s.at[b], self.z_r.at[b], dev(self.x, self.y, self.zq(b), self.c)).start()

    def last(self, xp, out):
        p, SL, A = self.p, self.SL, self.A
        i, g = self.have(xp, self.y, self.z)
        self.wait(self.X.at[3], self.x_r.at[3])
        self.wait(self.Y.at[3], self.y_r.at[3])
        for b in range(3):
            self.wait(self.Z.at[b], self.z_r.at[b])
        self.add(A, 0, SL, [(self.FG, g), (self.R.at[i], 0), (self.X.at[3], 0), (self.Y.at[3], 0)] + [(self.Z.at[b], 0) for b in range(3)])
        start = lin(self.x, self.y, self.z, self.c) * p.sh
        r_first = start // LN
        s = start - r_first * LN
        r0 = r_first % 16
        A[0:SL] = pltpu.roll(A[0:SL], lax.rem(LN - s, LN), 1)
        lane = lax.broadcasted_iota(jnp.int32, (p.rows_in, LN), 1)
        out[...] = jnp.where(lane < LN - s, A[pl.ds(r0, p.rows_in), :], A[pl.ds(r0 + 1, p.rows_in), :])

    def after(self, part, index=None):
        for c in (0, 1):
            for x in (0, 1):
                todo = [e for e in SCHEDULE if e[:3] == (part, c, x)]
                if todo:
                    here = (self.c == c) & (self.x == x)
                    if index is not None:
                        here = here & (index[0] == index[1])

                    def run(todo=todo):
                        for _, _, _, step, xp, b0, n in todo:
                            lax.fori_loop(b0, b0 + n, lambda b, k: (getattr(self, step)(xp, b), k)[1], 0)

                    pl.when(here)(run)

    def leave(self):
        for k in range(16):
            self.wait(self.R.at[k], self.sib_s.at[k])
        for b in range(4):
            self.wait(self.D0.at[b], self.d_s.at[0, b])
            self.wait(self.D1.at[b], self.d_s.at[1, b])
            self.wait(self.X.at[b], self.x_s.at[b])
            self.wait(self.Y.at[b], self.y_s.at[b])
        for b in range(3):
            self.wait(self.Z.at[b], self.z_s.at[b])


BACK_IN = ("act", "d_outer", "w2", "gd", "first_low", "w1", "res", "xh1", "rstd1", "V", "VG", "mixed", "wo", "qkv", "lse", "tok")


def backward_scatter_kernel(p, length, *refs):
    n = len(BACK_IN)
    src = dict(zip(BACK_IN, refs[:n]))
    wqkv_in = refs[n]
    igrad, out = refs[n + 1 : n + 3]
    loc = dict(zip(BACK_IN, refs[n + 3 : 2 * n + 3]))
    FG, F, E, R, D0, D1, X, Y, Z, A, lsem, osem, *sems = refs[2 * n + 3 :]
    r = Refs(length=length[0], FG=FG, F=F, E=E, **loc)
    r.dqkv, r.d_branch, r.d_mixed = r.act, r.first_low, r.d_outer
    sc = Scatter(p, FG, R, D0, D1, X, Y, Z, A, sems)
    mats = {m: (b, k, c) for m, b, k, c in MATS}
    loads = {m: pltpu.make_async_copy(src[m], loc[m], lsem.at[k]) for k, m in enumerate(BACK_IN)}
    for m in BACK_IN:
        loads[m].start()

    def need(*names):
        for m in names:
            loads[m].wait()

    sc.enter()
    c0, c1 = sc.c == 0, sc.c == 1
    x0, x1 = sc.x == 0, sc.x == 1

    def both(cond, fn):
        pl.when(cond)(fn)

    need("act", "d_outer", "VG")
    weight_grad(r, r.act, r.d_outer, *mats["w2"])
    edge_grads(r, 3)
    both(c0, lambda: sc.to_sibling(1))
    sc.after(1)
    need("w2", "gd")

    def act_part(j, carry):
        backward_act(r, j)
        for k in range(4):
            sc.after(2 + k, (j, 3 * k + 2))
        return carry

    lax.fori_loop(0, FF // 256, act_part, 0)
    q_loads = [pltpu.make_async_copy(wqkv_in.at[:, pl.ds(k * D, D)], r.w2.at[pl.ds(k * D, D)], lsem.at[n + k]) for k in range(3)]
    for q in q_loads:
        q.start()
    need("first_low")
    weight_grad(r, r.first_low, r.gd, *mats["w1"], hook=lambda i: [sc.after(6 + k, (i, k)) for k in range(2)])
    edge_grads(r, 2)
    both(c1, lambda: sc.to_sibling(1))
    sc.after(8)
    need("w1", "res", "xh1", "rstd1", "V")
    backward_first(r)
    sc.after(9)
    need("mixed")
    weight_grad(r, r.mixed, r.d_branch, *mats["wo"])
    edge_grads(r, 1)
    both(c0, lambda: sc.to_sibling(0))
    sc.after(10)
    need("wo")
    backward_mixed(r)
    sc.after(11)
    need("qkv", "lse")

    def heads(hp, carry):
        backward_heads(r, hp)
        for k in range(6):
            sc.after(12 + k, (hp, k))
        return carry

    lax.fori_loop(0, H // 2, heads, 0)
    need("tok")
    weight_grad(r, r.tok, r.dqkv, *mats["wqkv"], hook=lambda i: [sc.after(18 + k, (i, k)) for k in range(2)])
    edge_grads(r, 0)
    both(c1, lambda: sc.to_sibling(0))
    sc.after(20)
    for q in q_loads:
        q.wait()

    def tokens(b, carry):
        o = rows_of(b, 256)
        v = r.res[o, :]
        for part in range(3):
            v = v + mm_nt(r.dqkv[o, part * D : (part + 1) * D], r.w2[part * D : (part + 1) * D, :])
        r.res[o, :] = v
        sc.after(21, (b, 0))
        return carry

    lax.fori_loop(0, LEN // 256, tokens, 0)
    grad_out = pltpu.make_async_copy(r.res, igrad, osem)
    grad_out.start()
    sc.after(22)
    both(x0, lambda: sc.last(0, out))
    both(x1, lambda: sc.last(1, out))
    sc.leave()
    grad_out.wait()


def backward_scatter(p, length, wqkv, **arrays):
    S = jax.ShapeDtypeStruct
    sm = pl.BlockSpec(memory_space=pltpu.SMEM)
    hbm = pl.BlockSpec(memory_space=pl.ANY)
    ins = [arrays[m] for m in BACK_IN]
    SL = p.slot
    half = SL // 32 * 16
    VM = pltpu.VMEM
    DM = pltpu.SemaphoreType.DMA
    igrad, o = pl.pallas_call(
        functools.partial(backward_scatter_kernel, p),
        out_shape=[S((LEN, D), F32), S((p.rows_in, LN), F32)],
        in_specs=[sm] + [hbm] * (len(ins) + 1),
        out_specs=[hbm, pl.BlockSpec(memory_space=pltpu.VMEM)],
        scratch_shapes=[VM(a.shape, a.dtype) for a in ins]
        + [VM((flat_rows(p), LN), BF), VM((6144 + 32, LN), F32), VM((160, LN), F32), VM((16, SL, LN), BF), VM((4, half, LN), BF), VM((4, SL - half, LN), BF), VM((4, SL, LN), BF), VM((4, SL, LN), BF), VM((3, SL, LN), BF), VM((SL + 32, LN), F32)]
        + [DM((len(ins) + 3,)), DM, DM((16,)), DM((16,)), DM((2, 4)), DM((2, 4)), DM((4,)), DM((4,)), DM((4,)), DM((4,)), DM((3,)), DM((3,))],
        compiler_params=pltpu.CompilerParams(collective_id=1, has_side_effects=True, vmem_limit_bytes=64 << 20),
    )(length, *ins, wqkv)
    return igrad, o.reshape(-1)[: p.sh]


def on_device(p, fast, tokens, lengths, weight_shards, hidden_cotangent, nested_cotangent):
    tok = tokens.reshape(LEN, D)
    hcot = hidden_cotangent.reshape(LEN, D)
    if fast:
        f = gather_forward(p, weight_shards, lengths, tok, hcot, nested_cotangent)
        igrad, shards = backward_scatter(p, lengths, tok=tok, **{m: f[m] for m in BACK_IN + ("wqkv",) if m != "tok"})
    else:
        slots = lax.all_gather(build_slot(p, weight_shards, me_of), AX, axis=0)
        f = dict(zip(FORWARD_OUT, forward_local(p, slots, lengths, tok, hcot, nested_cotangent)))
        igrad, flat = backward_local(p, lengths, tok, *[f[m] for m in FORWARD_OUT[6:] + FORWARD_OUT[2:6]])
        shards = scatter_plain(p, flat)
    return (f["hidden"].reshape(1, LEN, D), f["nested"], igrad.reshape(1, LEN, D), shards)


def solution(mesh):
    in_specs = (
        P(("dp", "fsdp"), None, None),
        P(("dp", "fsdp")),
        P(("dp", "fsdp")),
        P(("dp", "fsdp"), None, None),
        P(("dp", "fsdp"), None),
    )
    out_specs = (
        P(("dp", "fsdp"), None, None),
        P(("dp", "fsdp"), None),
        P(("dp", "fsdp"), None, None),
        P(("dp", "fsdp")),
    )
    p = plan(mesh.shape["dp"] * mesh.shape["fsdp"])
    fast = (mesh.shape["dp"], mesh.shape["fsdp"]) == (4, 8)
    return jax.shard_map(
        functools.partial(on_device, p, fast), mesh=mesh, in_specs=in_specs, out_specs=out_specs, check_vma=False
    )
```

```python
import functools
import math

import jax
import jax.numpy as jnp
from jax import lax
from jax.experimental import pallas as pl
from jax.experimental.pallas import tpu as pltpu
from jax.sharding import PartitionSpec as P

AX = ("dp", "fsdp")
MESH = pl.DeviceIdType.MESH
D = 768
H = 12
HD = 64
FF = 3072
LEN = 512
E2 = 512
E3 = 256
E4 = 128
E5 = 64


epsilon = 1e-05


PAR=7088640; LN=128
class Plan: pass
def plan(n):
    p=Plan(); p.n=n; p.sh=PAR//n
    st=[i*p.sh for i in range(n)]
    p.g0=[s//LN//16 for s in st]
    p.g1=[(s+p.sh-1)//LN//16 for s in st]
    p.slot=16*max(b-a+1 for a,b in zip(p.g0,p.g1))
    p.rows_in=-(-p.sh//LN)
    return p
MATS=[("wqkv",0,D,18),("wo",13836,D,6),("w1",18462,D,24),("w2",36918,FF,6)]
VECS=[(13824,12),(18444,18),(36894,24),(55350,30)]

def build_slot_kernel(p,me_of,x_ref,o_ref,q_ref):
    i=me_of(); start=i*p.sh; r_first=start//LN; s=start-r_first*LN; r0=r_first%16
    lead=32
    q_ref[...]=jnp.zeros_like(q_ref)
    q=pltpu.roll(x_ref[...].astype(jnp.float32),s,1)
    q_ref[lead:lead+p.rows_in]=q
    lane=lax.broadcasted_iota(jnp.int32,(p.slot,LN),1)
    a=q_ref[pl.ds(lead-r0,p.slot),:]
    b=q_ref[pl.ds(lead-1-r0,p.slot),:]
    o_ref[...]=jnp.where(lane>=s,a,b).astype(jnp.bfloat16)

def build_slot(p,shard,me_of):
    x=jnp.pad(shard,(0,p.rows_in*LN-p.sh)).reshape(p.rows_in,LN)
    return pl.pallas_call(functools.partial(build_slot_kernel,p,me_of),out_shape=jax.ShapeDtypeStruct((p.slot,LN),jnp.bfloat16),
        scratch_shapes=[pltpu.VMEM((32+p.slot+32,LN),jnp.float32)])(x)

def load_flat(p,slots,F,g_lo,g_hi,need=None):
    for i in range(p.n):
        a=max(g_lo,p.g0[i]); b=min(g_hi,p.g1[i]+1)
        if a>=b: continue
        shared_first = i>0 and p.g0[i]==p.g1[i-1] and a==p.g0[i]
        a2=a+1 if shared_first else a
        b2=b
        apart=need is not None and need<=(i+1)*p.sh//LN
        if i+1<p.n and p.g1[i]==p.g0[i+1] and b==p.g1[i]+1 and not apart: b2=b-1
        if i+1<p.n and b2<b and b-1>=g_lo:
            g=b-1
            F[16*(g-g_lo):16*(g-g_lo)+16]=slots[i,16*(g-p.g0[i]):16*(g-p.g0[i])+16].astype(jnp.float32)+slots[i+1,0:16].astype(jnp.float32)
        cnt=b2-a2
        if cnt<=0: continue
        U=16
        nb,rem=cnt//U,cnt%U
        def body(t,_,i=i,a2=a2):
            src=pl.multiple_of(16*(a2-p.g0[i])+t*16*U,16); dst=pl.multiple_of(16*(a2-g_lo)+t*16*U,16)
            F[pl.ds(dst,16*U)]=slots[i,pl.ds(src,16*U)].astype(jnp.float32)
            return 0
        lax.fori_loop(0,nb,body,0)
        if rem:
            src=16*(a2-p.g0[i])+nb*16*U; dst=16*(a2-g_lo)+nb*16*U
            F[dst:dst+16*rem]=slots[i,src:src+16*rem].astype(jnp.float32)

def coords():
    dp=lax.axis_index("dp"); fs=lax.axis_index("fsdp")
    return dp//2,fs%2,fs//2,dp%2
def dev(x,y,z,c): return (x*2+c, z*2+y)
def lin(x,y,z,c): return (x*2+c)*8+z*2+y
def barrier(partners):
    bar=pltpu.get_barrier_semaphore()
    for q in partners: pl.semaphore_signal(bar,inc=1,device_id=q,device_id_type=MESH)
    pl.semaphore_wait(bar,len(partners))

TOT=PAR//LN
def flat_rows(p): return max(16*p.g0[-1]+p.slot, EDGES[-1][0]+EDGES[-1][1])
def owner_row(rho):
    for k,(name,base,rows,w) in enumerate(MATS):
        if base<=rho<base+rows*w: return ("m",k,(rho-base)//w,(rho-base)%w)
    at=0
    for base,cnt in VECS:
        if base<=rho<base+cnt: return ("v",at+rho-base)
        at+=cnt
    return None

def me_of():
    return lax.axis_index(AX)


def finish_kernel(p, a_ref, out, A):
    SL = p.slot
    start = me_of() * p.sh
    r_first = start // LN
    s = start - r_first * LN
    r0 = r_first % 16
    A[0:SL] = pltpu.roll(a_ref[...], lax.rem(LN - s, LN), 1)
    lane = lax.broadcasted_iota(jnp.int32, (p.rows_in, LN), 1)
    out[...] = jnp.where(lane < LN - s, A[pl.ds(r0, p.rows_in), :], A[pl.ds(r0 + 1, p.rows_in), :])


def scatter_plain(p, flat):
    parts = jnp.concatenate([flat[16 * g : 16 * g + p.slot] for g in p.g0]).astype(jnp.float32)
    mine = lax.psum_scatter(parts, AX, scatter_dimension=0, tiled=True)
    o = pl.pallas_call(
        functools.partial(finish_kernel, p),
        out_shape=jax.ShapeDtypeStruct((p.rows_in, LN), jnp.float32),
        scratch_shapes=[pltpu.VMEM((p.slot + 32, LN), jnp.float32)],
    )(mine)
    return o.reshape(-1)[: p.sh]

EPS = 1e-05
F32 = jnp.float32
BF = jnp.bfloat16
SQ = math.sqrt(0.5)
PHI = 1.0 / math.sqrt(2.0 * math.pi)
VNAMES = (
    ("q_bias", D),
    ("v_bias", D),
    ("out_bias", D),
    ("first_gain", D),
    ("first_shift", D),
    ("up_bias", FF),
    ("down_bias", D),
    ("second_gain", D),
    ("second_shift", D),
    ("exit_gain", D),
    ("exit_shift", D),
)
VI = {name: k for k, (name, _) in enumerate(VNAMES)}
PREFIXES = (D, E2, E3, E4, E5)
UP = 768


def mm(a, b):
    return jnp.dot(a, b, preferred_element_type=F32)


def mm_nt(a, b):
    return lax.dot_general(a, b, (((1,), (1,)), ((), ())), preferred_element_type=F32)


def mm_tn(a, b):
    return lax.dot_general(a, b, (((0,), (0,)), ((), ())), preferred_element_type=F32)


def vrow(V, name):
    k = VI[name]
    return V[k : k + 1, : VNAMES[k][1]]


def mean_last(a):
    return jnp.mean(a, axis=-1, keepdims=True)


def sum_rows(a):
    return jnp.sum(a, axis=0, keepdims=True)


def forward_qkv(r):
    bias = jnp.concatenate([vrow(r.V, "q_bias"), jnp.zeros((1, D), F32), vrow(r.V, "v_bias")], axis=1)
    r.qb[...] = bias

    def body(j, _):
        o = pl.ds(pl.multiple_of(j * D, D), D)
        r.qkv[:, o] = (mm(r.tok[...], r.wqkv[:, o]) + r.qb[:, o]).astype(BF)
        return 0

    lax.fori_loop(0, 3, body, 0)


def half_lanes(h):
    lane = lax.broadcasted_iota(jnp.int32, (LEN, LN), 1)
    return lane < HD if h == 0 else lane >= HD


def pair(r, part, hp):
    return r.qkv[:, pl.ds(pl.multiple_of(part * D + hp * LN, LN), LN)]


def forward_heads(r, hp):
    q, k, v = pair(r, 0, hp), pair(r, 1, hp), pair(r, 2, hp)
    valid = lax.broadcasted_iota(jnp.int32, (1, LEN), 1) < r.length
    out = None
    lse_all = r.lse[...]
    lane = lax.broadcasted_iota(jnp.int32, (LEN, LN), 1)
    for h in range(2):
        qh = jnp.where(half_lanes(h), q, jnp.zeros_like(q))
        s = jnp.where(valid, mm_nt(qh, k) * 0.125, -1e9)
        m = jnp.max(s, axis=1, keepdims=True)
        e = jnp.exp(s - m)
        l = jnp.sum(e, axis=1, keepdims=True)
        low = (e * (1.0 / l)).astype(BF)
        o = mm(low, v)
        out = o if out is None else jnp.where(half_lanes(0), out, o)
        lse_all = jnp.where(lane == 2 * hp + h, m + jnp.log(l), lse_all)
    r.lse[...] = lse_all
    r.mixed[:, pl.ds(pl.multiple_of(hp * LN, LN), LN)] = out.astype(BF)


def rows_of(b, n):
    return pl.ds(pl.multiple_of(b * n, n), n)


def forward_first(r):
    def body(b, _):
        o = rows_of(b, 256)
        v = r.tok[o, :].astype(F32) + mm(r.mixed[o, :], r.wo[...]) + vrow(r.V, "out_bias")
        cen = v - mean_last(v)
        rstd = lax.rsqrt(mean_last(cen * cen) + EPS)
        xh = cen * rstd
        r.xh1[o, :] = xh
        r.rstd1[o, :] = rstd
        r.first_low[o, :] = (xh * vrow(r.V, "first_gain") + vrow(r.V, "first_shift")).astype(BF)
        return 0

    lax.fori_loop(0, LEN // 256, body, 0)


def forward_up(r, j):
    o = pl.ds(pl.multiple_of(j * UP, UP), UP)
    v = mm(r.first_low[...], r.w1[:, o]) + r.V[VI["up_bias"] : VI["up_bias"] + 1, o]
    cdf = 0.5 * (1.0 + lax.erf(v * SQ))
    r.act[:, o] = (v * cdf).astype(BF)
    r.gd[:, o] = (cdf + v * (PHI * jnp.exp(-0.5 * v * v))).astype(BF)


def forward_second(r):
    def body(b, tot):
        o = rows_of(b, 256)
        first = r.xh1[o, :] * vrow(r.V, "first_gain") + vrow(r.V, "first_shift")
        v = first + mm(r.act[o, :], r.w2[...]) + vrow(r.V, "down_bias")
        cen = v - mean_last(v)
        rstd = lax.rsqrt(mean_last(cen * cen) + EPS)
        xh = cen * rstd
        r.xh2[o, :] = xh
        r.rstd2[o, :] = rstd
        t = lax.broadcasted_iota(jnp.int32, (256, 1), 0) + b * 256
        hid = (xh * vrow(r.V, "second_gain") + vrow(r.V, "second_shift")) * (t < r.length).astype(F32)
        r.hidden[o, :] = hid.astype(BF)
        return tot + sum_rows(hid)

    return lax.fori_loop(0, LEN // 256, body, jnp.zeros((1, D), F32))


def head(r, tot):
    inv_len = 1.0 / jnp.full((1, 1), r.length, jnp.int32).astype(F32)
    pooled = tot * inv_len
    cen = pooled - mean_last(pooled)
    rstd = lax.rsqrt(mean_last(cen * cen) + EPS)
    xh = cen * rstd
    gain = vrow(r.V, "exit_gain")
    emb = xh * gain + vrow(r.V, "exit_shift")
    d_emb = jnp.zeros((1, D), F32)
    at = 0
    for m in PREFIXES:
        e = emb[:, :m]
        inv = lax.rsqrt(jnp.sum(e * e, axis=1, keepdims=True) * (1.0 / m) + EPS)
        out = e * inv
        r.nested[:, at : at + m] = out
        c = r.ncot[:, at : at + m]
        g = inv * (c - out * (jnp.sum(c * out, axis=1, keepdims=True) * (1.0 / m)))
        d_emb = d_emb + (g if m == D else jnp.concatenate([g, jnp.zeros((1, D - m), F32)], axis=1))
        at += m
    put_grad(r, "exit_gain", d_emb * xh)
    put_grad(r, "exit_shift", d_emb)
    dx = d_emb * gain
    return rstd * (dx - mean_last(dx) - xh * mean_last(dx * xh)) * inv_len


def put_grad(r, name, value):
    k = VI[name]
    r.VG[k : k + 1, : VNAMES[k][1]] = value


def norm_back(dy, gain, xh, rstd):
    dx = dy * gain
    return rstd * (dx - mean_last(dx) - xh * mean_last(dx * xh))


def backward_second(r, d_pool):
    def body(b, c):
        o = rows_of(b, 256)
        t = lax.broadcasted_iota(jnp.int32, (256, 1), 0) + b * 256
        dy = (r.hcot[o, :].astype(F32) + d_pool) * (t < r.length).astype(F32)
        xh = r.xh2[o, :]
        res = norm_back(dy, vrow(r.V, "second_gain"), xh, r.rstd2[o, :])
        r.res[o, :] = res
        low = res.astype(BF)
        r.d_outer[o, :] = low
        return (c[0] + sum_rows(dy * xh), c[1] + sum_rows(dy), c[2] + sum_rows(low.astype(F32)))

    z = jnp.zeros((1, D), F32)
    a, b, c = lax.fori_loop(0, LEN // 256, body, (z, z, z))
    put_grad(r, "second_gain", a)
    put_grad(r, "second_shift", b)
    put_grad(r, "down_bias", c)


def backward_act(r, j):
    o = pl.ds(pl.multiple_of(j * UP, UP), UP)
    d = (mm_nt(r.d_outer[...], r.w2[o, :]) * r.gd[:, o].astype(F32)).astype(BF)
    r.gd[:, o] = d
    r.VG[VI["up_bias"] : VI["up_bias"] + 1, o] = sum_rows(d.astype(F32))


def backward_first(r):
    def body(b, c):
        o = rows_of(b, 256)
        dy = mm_nt(r.gd[o, :], r.w1[...]) + r.res[o, :]
        xh = r.xh1[o, :]
        res = norm_back(dy, vrow(r.V, "first_gain"), xh, r.rstd1[o, :])
        r.res[o, :] = res
        low = res.astype(BF)
        r.d_branch[o, :] = low
        return (c[0] + sum_rows(dy * xh), c[1] + sum_rows(dy), c[2] + sum_rows(low.astype(F32)))

    z = jnp.zeros((1, D), F32)
    a, b, c = lax.fori_loop(0, LEN // 256, body, (z, z, z))
    put_grad(r, "first_gain", a)
    put_grad(r, "first_shift", b)
    put_grad(r, "out_bias", c)


def backward_mixed(r):
    r.d_mixed[...] = mm_nt(r.d_branch[...], r.wo[...]).astype(BF)


def backward_heads(r, hp):
    q, k, v = pair(r, 0, hp), pair(r, 1, hp), pair(r, 2, hp)
    cols = pl.ds(pl.multiple_of(hp * LN, LN), LN)
    dm = r.d_mixed[:, cols]
    valid = lax.broadcasted_iota(jnp.int32, (1, LEN), 1) < r.length
    lane = lax.broadcasted_iota(jnp.int32, (LEN, LN), 1)
    zero = jnp.zeros_like(q)
    dq = dk = dv = None
    for h in range(2):
        here = half_lanes(h)
        qh, kh, dmh = jnp.where(here, q, zero), jnp.where(here, k, zero), jnp.where(here, dm, zero)
        lse = jnp.sum(jnp.where(lane == 2 * hp + h, r.lse[...], 0.0), axis=1, keepdims=True)
        s = jnp.where(valid, mm_nt(qh, k) * 0.125, -1e9)
        p = jnp.exp(s - lse)
        dp = mm_nt(dmh, v)
        ds = (p * (dp - jnp.sum(dp * p, axis=1, keepdims=True))).astype(BF)
        a, b, c = mm(ds, kh), mm_tn(ds, qh), mm_tn(p.astype(BF), dmh)
        dq, dk, dv = (a, b, c) if dq is None else (dq + a, dk + b, dv + c)
    dq, dk, dv = (dq * 0.125).astype(BF), (dk * 0.125).astype(BF), dv.astype(BF)
    for part, g in ((0, dq), (1, dk), (2, dv)):
        r.dqkv[:, pl.ds(pl.multiple_of(part * D + hp * LN, LN), LN)] = g
    k = VI["q_bias"]
    r.VG[k : k + 1, cols] = sum_rows(dq.astype(F32))
    k = VI["v_bias"]
    r.VG[k : k + 1, cols] = sum_rows(dv.astype(F32))


def backward_tokens(r, b):
    o = rows_of(b, 128)
    v = r.res[o, :]
    for part in range(3):
        v = v + mm_nt(r.dqkv[o, part * D : (part + 1) * D], r.wqkv[:, part * D : (part + 1) * D])
    r.res[o, :] = v


EDGES = ((13824, 16), (18432, 32), (36880, 48), (55344, 64))


def edge_at(row):
    at = 0
    for base, rows in EDGES:
        if base <= row < base + rows:
            return at + row - base
        at += rows
    return None


def weight_grad(r, lhs, rhs, base, rows, w, RB=256, CB=6, hook=None):
    lead = base % 16
    step_rows = RB * w
    F = r.F
    if lead:
        F[0:16] = jnp.zeros((16, LN), F32)

    def body(s, _):
        o = pl.ds(pl.multiple_of(s * RB, RB), RB)
        for ch in range(w // CB):
            g = mm_tn(lhs[:, o], rhs[:, ch * CB * LN : (ch + 1) * CB * LN])
            for j in range(CB):
                F[pl.ds(lead + ch * CB + j, RB, stride=w), :] = g[:, j * LN : (j + 1) * LN]
        if lead:
            @pl.when(s == 0)
            def _():
                e = edge_at(base)
                r.E[e : e + 16 - lead] = F[lead:16]

        U = 256
        to = base - lead + s * step_rows

        def emit(t, _):
            r.FG[pl.ds(pl.multiple_of(to + t * U, 16), U)] = F[pl.ds(pl.multiple_of(t * U, 16), U)].astype(BF)
            return 0

        lax.fori_loop(0, step_rows // U, emit, 0)
        if lead:
            F[0:16] = F[step_rows : step_rows + 16]
        if hook is not None:
            hook(s)
        return 0

    lax.fori_loop(0, rows // RB, body, 0)
    if lead:
        e = edge_at(base + rows * w - lead)
        r.E[e : e + lead] = F[0:lead]


def edge_grads(r, which):
    base, rows = EDGES[which]
    at = 0
    for vbase, cnt in VECS:
        for k in range(cnt):
            row = vbase + k
            if base <= row < base + rows:
                name, j = vec_at(at + k)
                e = edge_at(row)
                r.E[e : e + 1] = r.VG[name : name + 1, j * LN : (j + 1) * LN]
        at += cnt
    if which == len(EDGES) - 1:
        e = edge_at(TOT)
        r.E[e : e + base + rows - TOT] = jnp.zeros((base + rows - TOT, LN), F32)
    e = edge_at(base)
    r.FG[base : base + rows] = r.E[e : e + rows].astype(BF)


def vec_at(row):
    for k, (_, n) in enumerate(VNAMES):
        if row < n // LN:
            return k, row
        row -= n // LN


class Refs:
    def __init__(self, **refs):
        self.__dict__.update(refs)


def relayout_vectors(p, r):
    at = 0
    for base, cnt in VECS:
        g_lo = base // 16
        g_hi = -(-(base + cnt) // 16)
        load_flat(p, r.slots, r.F, g_lo, g_hi)
        for k in range(cnt):
            name, j = vec_at(at + k)
            f = base - 16 * g_lo + k
            r.V[name : name + 1, j * LN : (j + 1) * LN] = r.F[f : f + 1]
        at += cnt


def relayout_matrix(p, r, name, W, RB):
    base, rows, w = {n: (b, k, c) for n, b, k, c in MATS}[name]
    for s in range(rows // RB):
        lo = base + s * RB * w
        g_lo = lo // 16
        load_flat(p, r.slots, r.F, g_lo, -(-(lo + RB * w) // 16))
        tile_rows(r.F, W, lo - 16 * g_lo, s * RB, RB, w)


def tile_rows(F, W, off, row, rows, w, RB=64):
    def body(t, _):
        q = pl.multiple_of(t * RB, RB)
        for j in range(w):
            W[pl.ds(row + q, RB), j * LN : (j + 1) * LN] = F[pl.ds(off + q * w + j, RB, stride=w), :].astype(BF)
        return 0

    lax.fori_loop(0, rows // RB, body, 0)


def forward_kernel(p, slots, length, tok, hcot, ncot, hidden, nested, wqkv, wo, w1, w2, V, VG, qkv, lse, mixed, xh1, rstd1, first_low, act, gd, res, d_outer, F, qb, xh2, rstd2):
    r = Refs(slots=slots, length=length[0], tok=tok, hcot=hcot, ncot=ncot, hidden=hidden, nested=nested, wqkv=wqkv, wo=wo, w1=w1, w2=w2, V=V, VG=VG, qkv=qkv, lse=lse, mixed=mixed, xh1=xh1, rstd1=rstd1, first_low=first_low, act=act, gd=gd, res=res, d_outer=d_outer, F=F, qb=qb, xh2=xh2, rstd2=rstd2)
    relayout_vectors(p, r)
    relayout_matrix(p, r, "wqkv", wqkv, 256)
    forward_qkv(r)
    lse[...] = jnp.zeros_like(lse)
    lax.fori_loop(0, H // 2, lambda hp, c: (forward_heads(r, hp), c)[1], 0)
    relayout_matrix(p, r, "wo", wo, 768)
    forward_first(r)
    relayout_matrix(p, r, "w1", w1, 256)
    lax.fori_loop(0, FF // UP, lambda j, c: (forward_up(r, j), c)[1], 0)
    relayout_matrix(p, r, "w2", w2, 768)
    tot = forward_second(r)
    d_pool = head(r, tot)
    backward_second(r, d_pool)


def forward_local(p, slots, length, tok, hcot, ncot):
    S = jax.ShapeDtypeStruct
    outs = [S((LEN, D), BF), S((1, 1728), F32), S((D, 3 * D), BF), S((D, D), BF), S((D, FF), BF), S((FF, D), BF), S((16, FF), F32), S((16, FF), F32), S((LEN, 3 * D), BF), S((LEN, LN), F32), S((LEN, D), BF), S((LEN, D), F32), S((LEN, 1), F32), S((LEN, D), BF), S((LEN, FF), BF), S((LEN, FF), BF), S((LEN, D), F32), S((LEN, D), BF)]
    vm = pl.BlockSpec(memory_space=pltpu.VMEM)
    sm = pl.BlockSpec(memory_space=pltpu.SMEM)
    return pl.pallas_call(
        functools.partial(forward_kernel, p),
        out_shape=outs,
        in_specs=[vm, sm, vm, vm, vm],
        scratch_shapes=[pltpu.VMEM((6144 + 32, LN), F32), pltpu.VMEM((1, 3 * D), F32), pltpu.VMEM((LEN, D), F32), pltpu.VMEM((LEN, 1), F32)],
        compiler_params=pltpu.CompilerParams(vmem_limit_bytes=60 << 20),
    )(slots, length, tok, hcot, ncot)


def backward_kernel(p, length, tok, V, VG0, qkv, lse, mixed, xh1, rstd1, first_low, act, gd, res, d_outer, wqkv, wo, w1, w2, igrad, FG, VG, d_branch, d_mixed, dqkv, F, E):
    r = Refs(length=length[0], tok=tok, V=V, VG=VG, qkv=qkv, lse=lse, mixed=mixed, xh1=xh1, rstd1=rstd1, first_low=first_low, act=act, gd=gd, res=igrad, d_outer=d_outer, wqkv=wqkv, wo=wo, w1=w1, w2=w2, FG=FG, d_branch=d_branch, d_mixed=d_mixed, dqkv=dqkv, F=F, E=E)
    VG[...] = VG0[...]
    igrad[...] = res[...]
    mats = {n: (b, k, c) for n, b, k, c in MATS}
    weight_grad(r, act, d_outer, *mats["w2"], RB=1024, CB=2)
    edge_grads(r, 3)
    lax.fori_loop(0, FF // UP, lambda j, c: (backward_act(r, j), c)[1], 0)
    weight_grad(r, first_low, gd, *mats["w1"])
    edge_grads(r, 2)
    backward_first(r)
    weight_grad(r, mixed, d_branch, *mats["wo"])
    edge_grads(r, 1)
    backward_mixed(r)
    lax.fori_loop(0, H // 2, lambda hp, c: (backward_heads(r, hp), c)[1], 0)
    weight_grad(r, tok, dqkv, *mats["wqkv"])
    edge_grads(r, 0)
    lax.fori_loop(0, LEN // 128, lambda b, c: (backward_tokens(r, b), c)[1], 0)


def backward_local(p, length, tok, V, VG, qkv, lse, mixed, xh1, rstd1, first_low, act, gd, res, d_outer, wqkv, wo, w1, w2):
    S = jax.ShapeDtypeStruct
    vm = pl.BlockSpec(memory_space=pltpu.VMEM)
    sm = pl.BlockSpec(memory_space=pltpu.SMEM)
    return pl.pallas_call(
        functools.partial(backward_kernel, p),
        out_shape=[S((LEN, D), F32), S((flat_rows(p), LN), BF)],
        in_specs=[sm] + [vm] * 17,
        scratch_shapes=[pltpu.VMEM((16, FF), F32), pltpu.VMEM((LEN, D), BF), pltpu.VMEM((LEN, D), BF), pltpu.VMEM((LEN, 3 * D), BF), pltpu.VMEM((6144 + 32, LN), F32), pltpu.VMEM((160, LN), F32)],
        compiler_params=pltpu.CompilerParams(vmem_limit_bytes=60 << 20),
    )(length, tok, V, VG, qkv, lse, mixed, xh1, rstd1, first_low, act, gd, res, d_outer, wqkv, wo, w1, w2)


class Gather:
    def __init__(self, p, G, ssem, rsem, gosem):
        self.p, self.G, self.ssem, self.rsem, self.gosem = p, G, ssem, rsem, gosem
        self.x, self.y, self.z, self.c = coords()
        x, y, z, c = self.x, self.y, self.z, self.c
        self.me = lin(x, y, z, c)
        half = p.slot // 32 * 16
        self.H = ((0, half), (half, p.slot - half), (0, p.slot))
        self.px, self.py, self.pc = dev(1 - x, y, z, c), dev(x, 1 - y, z, c), dev(x, y, z, 1 - c)

    def enter(self):
        x, y, z, c = self.x, self.y, self.z, self.c
        bar = pltpu.get_barrier_semaphore()

        def greet(to):
            pl.semaphore_signal(bar, inc=1, device_id=to, device_id_type=MESH)

        for to in (self.px, self.py, self.pc):
            greet(to)
        pl.when(z > 0)(lambda: greet(dev(x, y, z - 1, c)))
        pl.when(z < 3)(lambda: greet(dev(x, y, z + 1, c)))
        middle = (z > 0) & (z < 3)
        pl.when(middle)(lambda: pl.semaphore_wait(bar, 5))
        pl.when(jnp.logical_not(middle))(lambda: pl.semaphore_wait(bar, 4))

    def send(self, sl, h, to, t):
        r0, rn = self.H[h]
        ref = self.G.at[sl, pl.ds(r0, rn)]
        pltpu.make_async_remote_copy(src_ref=ref, dst_ref=ref, send_sem=self.ssem.at[sl, t], recv_sem=self.rsem.at[sl, h], device_id=to, device_id_type=MESH).start()

    def wait(self, sl, h, sem=None):
        r0, rn = self.H[h]
        ref = self.G.at[sl, pl.ds(r0, rn)]
        pltpu.make_async_copy(ref, ref, self.rsem.at[sl, h] if sem is None else sem).wait()

    def up(self, sl):
        pl.when(self.z < 3)(lambda: self.send(sl, 2, dev(self.x, self.y, self.z + 1, self.c), 3))

    def down(self, sl):
        pl.when(self.z > 0)(lambda: self.send(sl, 2, dev(self.x, self.y, self.z - 1, self.c), 4))

    def core(self, sl, h=2):
        self.send(sl, h, self.pc, 2)

    def xy(self, sl):
        self.send(sl, 2, self.px, 0)
        self.send(sl, 2, self.py, 1)

    def own_line(self, k):
        self.at(k, lambda zq: self.xy(lin(self.x, self.y, zq, self.c)))

    def go(self, k):
        pl.semaphore_signal(self.gosem.at[k], inc=1, device_id=self.pc, device_id_type=MESH)

    def wait_go(self, k):
        pl.semaphore_wait(self.gosem.at[k], 1)

    def at(self, k, fn):
        if k == 0:
            fn(self.z)
            return
        pl.when(self.z - k >= 0)(lambda: fn(self.z - k))
        pl.when(self.z + k <= 3)(lambda: fn(self.z + k))

    def along_z(self, k, xy):
        x, y, z, c = self.x, self.y, self.z, self.c

        def below():
            sl = lin(x, y, z - k, c)
            self.wait(sl, 2)
            self.up(sl)
            if xy:
                self.xy(sl)
            self.core(sl)

        def above():
            sl = lin(x, y, z + k, c)
            self.wait(sl, 2)
            self.down(sl)
            if xy:
                self.xy(sl)
            self.core(sl)

        pl.when(z - k >= 0)(below)
        pl.when(z + k <= 3)(above)

    def sides(self, k):
        x, y, c = self.x, self.y, self.c

        def fn(zq):
            sl = lin(1 - x, y, zq, c)
            self.wait(sl, 2)
            self.send(sl, 0, self.py, 1)
            self.core(sl)
            sl = lin(x, 1 - y, zq, c)
            self.wait(sl, 2)
            self.send(sl, 1, self.px, 0)
            self.core(sl)

        self.at(k, fn)

    def diagonal(self, k):
        def fn(zq):
            sl = lin(1 - self.x, 1 - self.y, zq, self.c)
            for h in (0, 1):
                self.wait(sl, h)
                self.core(sl, h)

        self.at(k, fn)

    def from_sibling(self, xp):
        x, y, c = self.x, self.y, self.c

        def body(zq, carry):
            self.wait(lin(xp, y, zq, 1 - c), 2)
            other = lin(xp, 1 - y, zq, 1 - c)
            pl.when(x == xp)(lambda: self.wait(other, 2))

            def halves():
                self.wait(other, 0)
                self.wait(other, 1)

            pl.when(x != xp)(halves)
            return carry

        lax.fori_loop(0, 4, body, 0)

    def leave(self):
        x, y, z, c = self.x, self.y, self.z, self.c
        W = self.wait

        def body(zq, carry):
            sl = lin(x, y, zq, c)
            for t in (0, 1, 2):
                W(sl, 2, self.ssem.at[sl, t])
            pl.when((zq <= z) & (z < 3))(lambda: W(sl, 2, self.ssem.at[sl, 3]))
            pl.when((zq >= z) & (z > 0))(lambda: W(sl, 2, self.ssem.at[sl, 4]))
            sx = lin(1 - x, y, zq, c)
            W(sx, 0, self.ssem.at[sx, 1])
            W(sx, 2, self.ssem.at[sx, 2])
            sy = lin(x, 1 - y, zq, c)
            W(sy, 1, self.ssem.at[sy, 0])
            W(sy, 2, self.ssem.at[sy, 2])
            sd = lin(1 - x, 1 - y, zq, c)
            W(sd, 2, self.ssem.at[sd, 2])
            return carry

        lax.fori_loop(0, 4, body, 0)


FORWARD_OUT = ("hidden", "nested", "wqkv", "wo", "w1", "w2", "V", "VG", "qkv", "lse", "mixed", "xh1", "rstd1", "first_low", "act", "gd", "res", "d_outer")
FORWARD_SHAPES = dict(
    hidden=((LEN, D), jnp.bfloat16),
    nested=((1, 1728), jnp.float32),
    wqkv=((D, 3 * D), jnp.bfloat16),
    wo=((D, D), jnp.bfloat16),
    w1=((D, FF), jnp.bfloat16),
    w2=((FF, D), jnp.bfloat16),
    V=((16, FF), jnp.float32),
    VG=((16, FF), jnp.float32),
    qkv=((LEN, 3 * D), jnp.bfloat16),
    lse=((LEN, LN), jnp.float32),
    mixed=((LEN, D), jnp.bfloat16),
    xh1=((LEN, D), jnp.float32),
    rstd1=((LEN, 1), jnp.float32),
    first_low=((LEN, D), jnp.bfloat16),
    act=((LEN, FF), jnp.bfloat16),
    gd=((LEN, FF), jnp.bfloat16),
    res=((LEN, D), jnp.float32),
    d_outer=((LEN, D), jnp.bfloat16),
)


def own_slot(p, me, x_ref, F, G):
    start = me * p.sh
    r_first = start // LN
    s = start - r_first * LN
    r0 = r_first % 16
    lead = 32
    F[0 : lead + p.slot + 32] = jnp.zeros((lead + p.slot + 32, LN), F32)
    F[lead : lead + p.rows_in] = pltpu.roll(x_ref[...].astype(F32), s, 1)
    lane = lax.broadcasted_iota(jnp.int32, (p.slot, LN), 1)
    G[me] = jnp.where(lane >= s, F[pl.ds(lead - r0, p.slot), :], F[pl.ds(lead - 1 - r0, p.slot), :]).astype(BF)


def relayout_vector(p, r, which):
    at = sum(cnt for _, cnt in VECS[:which])
    base, cnt = VECS[which]
    g_lo = base // 16
    load_flat(p, r.slots, r.F, g_lo, -(-(base + cnt) // 16), base + cnt)
    for k in range(cnt):
        name, j = vec_at(at + k)
        f = base - 16 * g_lo + k
        r.V[name : name + 1, j * LN : (j + 1) * LN] = r.F[f : f + 1]


def relayout_rows(p, r, name, W, row, rows):
    base, _, w = {n: (b, k, c) for n, b, k, c in MATS}[name]
    lo = base + row * w
    g_lo = lo // 16
    load_flat(p, r.slots, r.F, g_lo, -(-(lo + rows * w) // 16), lo + rows * w)
    tile_rows(r.F, W, lo - 16 * g_lo, row, rows, w)


def gather_forward_kernel(p, x_ref, length, tok, hcot, ncot, *refs):
    n = len(FORWARD_OUT)
    outs = dict(zip(FORWARD_OUT, refs[:n]))
    loc = dict(zip(FORWARD_OUT, refs[n : 2 * n]))
    G, F, qb, xh2, rstd2, ssem, rsem, gosem, osem = refs[2 * n :]
    r = Refs(slots=G, length=length[0], tok=tok, hcot=hcot, ncot=ncot, F=F, qb=qb, xh2=xh2, rstd2=rstd2, **loc)
    g = Gather(p, G, ssem, rsem, gosem)
    own_slot(p, g.me, x_ref, F, G)
    g.enter()
    c0, c1 = g.c == 0, g.c == 1

    started = []

    def out(*names):
        for m in names:
            k = FORWARD_OUT.index(m)
            cp = pltpu.make_async_copy(loc[m], outs[m], osem.at[k])
            cp.start()
            started.append(cp)

    def part_rq_0():
        g.up(g.me)
        g.down(g.me)
        g.xy(g.me)
        g.core(g.me)
        g.along_z(1, True)
        g.sides(0)
        g.along_z(2, True)
        g.go(0)
        g.sides(1)
        g.go(1)
        g.along_z(3, True)
        g.sides(2)
        g.sides(3)
        g.diagonal(0)
        g.diagonal(1)
        g.diagonal(2)
        g.diagonal(3)

    pl.when(c0)(part_rq_0)
    def part_rq_1():
        g.wait_go(0)
        g.up(g.me)
        g.down(g.me)
        g.core(g.me)
        g.along_z(1, False)
        g.along_z(2, False)
        g.along_z(3, False)
        g.wait_go(1)
        g.own_line(0)
        g.own_line(1)
        g.own_line(2)
        g.own_line(3)
        g.from_sibling(0)

    pl.when(c1)(part_rq_1)
    relayout_vector(p, r, 0)
    for k in range(3):
        relayout_rows(p, r, "wqkv", r.wqkv, 256 * k, 256)
    out("wqkv")
    def part_qkv_1():
        g.sides(0)

    pl.when(c1)(part_qkv_1)
    forward_qkv(r)
    out("qkv")
    r.lse[...] = jnp.zeros_like(r.lse)

    def heads(hp, carry):
        def part_hd1_1():
            g.sides(1)

        pl.when((hp == 1) & c1)(part_hd1_1)
        def part_hd3_1():
            g.sides(2)

        pl.when((hp == 3) & c1)(part_hd3_1)
        def part_hd5_1():
            g.diagonal(0)
            g.sides(3)

        pl.when((hp == 5) & c1)(part_hd5_1)
        forward_heads(r, hp)
        return carry

    lax.fori_loop(0, H // 2, heads, 0)
    out("lse", "mixed")
    def part_rwo_0():
        g.from_sibling(0)

    pl.when(c0)(part_rwo_0)
    def part_rwo_1():
        g.diagonal(1)
        g.diagonal(2)
        g.diagonal(3)
        g.from_sibling(1)

    pl.when(c1)(part_rwo_1)
    relayout_rows(p, r, "w1", r.w1, 448, 128)
    relayout_rows(p, r, "w1", r.w1, 576, 192)
    relayout_rows(p, r, "w2", r.w2, 0, 768)
    relayout_vector(p, r, 2)
    relayout_rows(p, r, "wo", r.wo, 0, 768)
    relayout_vector(p, r, 1)
    out("wo")
    forward_first(r)
    out("xh1", "rstd1", "first_low")
    relayout_rows(p, r, "w1", r.w1, 0, 256)
    relayout_rows(p, r, "w1", r.w1, 256, 192)
    out("w1")
    lax.fori_loop(0, FF // UP, lambda j, c: (forward_up(r, j), c)[1], 0)
    out("act", "gd")
    def part_rw2b_0():
        g.from_sibling(1)

    pl.when(c0)(part_rw2b_0)
    for k in range(1, 4):
        relayout_rows(p, r, "w2", r.w2, 768 * k, 768)
    relayout_vector(p, r, 3)
    out("w2", "V")
    tot = forward_second(r)
    out("hidden")
    d_pool = head(r, tot)
    out("nested")
    backward_second(r, d_pool)
    out("VG", "res", "d_outer")
    g.leave()
    for cp in started:
        cp.wait()


def gather_forward(p, shard, length, tok, hcot, ncot):
    x = jnp.pad(shard, (0, p.rows_in * LN - p.sh)).reshape(p.rows_in, LN)
    S = jax.ShapeDtypeStruct
    vm = pl.BlockSpec(memory_space=pltpu.VMEM)
    sm = pl.BlockSpec(memory_space=pltpu.SMEM)
    hbm = pl.BlockSpec(memory_space=pl.ANY)
    VM = pltpu.VMEM
    DM = pltpu.SemaphoreType.DMA
    shapes = [FORWARD_SHAPES[m] for m in FORWARD_OUT]
    res = pl.pallas_call(
        functools.partial(gather_forward_kernel, p),
        out_shape=[S(*s) for s in shapes],
        in_specs=[vm, sm, vm, vm, vm],
        out_specs=[hbm] * len(shapes),
        scratch_shapes=[VM(*s) for s in shapes]
        + [VM((p.n, p.slot, LN), BF), VM((6144 + 32, LN), F32), VM((1, 3 * D), F32), VM((LEN, D), F32), VM((LEN, 1), F32)]
        + [DM((p.n, 5)), DM((p.n, 3)), pltpu.SemaphoreType.REGULAR((2,)), DM((len(shapes),))],
        compiler_params=pltpu.CompilerParams(collective_id=0, has_side_effects=True, vmem_limit_bytes=64 << 20),
    )(x, length, tok, hcot, ncot)
    return dict(zip(FORWARD_OUT, res))


SCHEDULE = (
    (2, 1, 0, "diag", 1, 2, 2),
    (4, 1, 0, "diag", 1, 0, 2),
    (7, 1, 1, "yline", 1, 2, 2),
    (7, 1, 0, "xline", 1, 2, 2),
    (9, 0, 0, "diag", 1, 2, 2),
    (10, 1, 1, "diag", 0, 2, 2),
    (11, 1, 0, "xline", 1, 0, 2),
    (11, 1, 1, "diag", 0, 0, 2),
    (11, 1, 1, "yline", 1, 0, 2),
    (12, 0, 0, "diag", 1, 0, 2),
    (12, 0, 0, "xline", 1, 2, 2),
    (13, 1, 1, "xline", 0, 2, 2),
    (14, 1, 1, "xline", 0, 0, 2),
    (14, 1, 1, "own", 1, 2, 1),
    (17, 1, 0, "yline", 0, 2, 2),
    (18, 0, 1, "yline", 1, 2, 2),
    (20, 0, 0, "yline", 0, 0, 2),
    (20, 0, 1, "diag", 0, 0, 2),
    (20, 0, 1, "xline", 0, 0, 2),
    (20, 0, 1, "diag", 0, 2, 2),
    (20, 0, 0, "xline", 1, 0, 2),
    (20, 0, 0, "own", 0, 0, 2),
    (20, 1, 0, "own", 0, 2, 1),
    (21, 0, 1, "xline", 0, 2, 2),
    (21, 0, 0, "yline", 0, 2, 2),
    (21, 1, 0, "yline", 0, 0, 2),
    (21, 0, 1, "yline", 1, 0, 2),
    (21, 1, 0, "own", 0, 0, 2),
    (21, 0, 0, "own", 0, 2, 1),
    (21, 0, 1, "own", 1, 2, 1),
    (22, 0, 1, "own", 1, 0, 2),
    (22, 1, 1, "own", 1, 0, 2),
)


class Scatter:
    def __init__(self, p, FG, R, D0, D1, X, Y, Z, A, sems):
        self.p, self.FG, self.R, self.D0, self.D1, self.X, self.Y, self.Z, self.A = p, FG, R, D0, D1, X, Y, Z, A
        self.sib_s, self.sib_r, self.d_s, self.d_r, self.x_s, self.x_r, self.y_s, self.y_r, self.z_s, self.z_r = sems
        self.x, self.y, self.z, self.c = coords()
        x, y, z, c = self.x, self.y, self.z, self.c
        self.SL = p.slot
        self.half = p.slot // 32 * 16
        self.px, self.py, self.pc = dev(1 - x, y, z, c), dev(x, 1 - y, z, c), dev(x, y, z, 1 - c)

    def zq(self, b):
        d = lax.rem(b + 1, 4)
        z = self.z
        return lax.rem(z % 2 + d % 2, 2) + 2 * lax.rem(z // 2 + d // 2, 2)

    def enter(self):
        x, y, c = self.x, self.y, self.c
        barrier([self.px, self.py, self.pc] + [dev(x, y, self.zq(b), c) for b in range(3)])

    def row0(self, slot):
        return pl.multiple_of((slot * self.p.sh) // LN // 16 * 16, 16)

    def fg(self, slot):
        return self.row0(slot)

    def copy(self, src, dst, ssem, rsem, to):
        return pltpu.make_async_remote_copy(src_ref=src, dst_ref=dst, send_sem=ssem, recv_sem=rsem, device_id=to, device_id_type=MESH)

    def wait(self, ref, sem):
        pltpu.make_async_copy(ref, ref, sem).wait()

    def to_sibling(self, xp):
        def body(k, _):
            dp = 2 * xp + 1 - self.c
            i = 8 * xp + k
            self.copy(self.FG.at[pl.ds(self.row0(dp * 8 + k), self.SL)], self.R.at[i], self.sib_s.at[i], self.sib_r.at[i], self.pc).start()
            return 0

        lax.fori_loop(0, 8, body, 0)

    def add(self, dst, d0, rows, srcs, U=176):
        def body(t, _):
            r = pl.multiple_of(t * U, 16)
            v = None
            for s, s0 in srcs:
                e = s[pl.ds(s0 + r, U)].astype(F32)
                v = e if v is None else v + e
            dst[pl.ds(d0 + r, U)] = v.astype(dst.dtype)
            return 0

        lax.fori_loop(0, rows // U, body, 0)

    def have(self, xp, yq, zq):
        fs = zq * 2 + yq
        i = 8 * xp + fs
        self.wait(self.R.at[i], self.sib_r.at[i])
        return i, self.row0((2 * xp + self.c) * 8 + fs)

    def diag(self, xp, b):
        i, g = self.have(xp, 1 - self.y, self.zq(b))
        half, rest = self.half, self.SL - self.half
        R = self.R.at[i]
        self.add(R, 0, self.SL, [(self.FG, g), (R, 0)])
        self.copy(R.at[pl.ds(0, half)], self.D0.at[b], self.d_s.at[0, b], self.d_r.at[0, b], self.py).start()
        self.copy(R.at[pl.ds(half, rest)], self.D1.at[b], self.d_s.at[1, b], self.d_r.at[1, b], self.px).start()

    def xline(self, xp, b):
        i, g = self.have(xp, self.y, self.zq(b))
        half, rest = self.half, self.SL - self.half
        R = self.R.at[i]
        self.wait(self.D0.at[b], self.d_r.at[0, b])
        self.add(R, half, rest, [(self.FG, g + half), (R, half)])
        self.add(R, 0, half, [(self.FG, g), (R, 0), (self.D0.at[b], 0)])
        self.copy(R, self.X.at[b], self.x_s.at[b], self.x_r.at[b], self.px).start()

    def yline(self, xp, b):
        i, g = self.have(xp, 1 - self.y, self.zq(b))
        half, rest = self.half, self.SL - self.half
        R = self.R.at[i]
        self.wait(self.D1.at[b], self.d_r.at[1, b])
        self.add(R, 0, half, [(self.FG, g), (R, 0)])
        self.add(R, half, rest, [(self.FG, g + half), (R, half), (self.D1.at[b], 0)])
        self.copy(R, self.Y.at[b], self.y_s.at[b], self.y_r.at[b], self.py).start()

    def own(self, xp, b):
        i, g = self.have(xp, self.y, self.zq(b))
        R = self.R.at[i]
        self.wait(self.X.at[b], self.x_r.at[b])
        self.wait(self.Y.at[b], self.y_r.at[b])
        self.add(R, 0, self.SL, [(self.FG, g), (R, 0), (self.X.at[b], 0), (self.Y.at[b], 0)])
        self.copy(R, self.Z.at[b], self.z_s.at[b], self.z_r.at[b], dev(self.x, self.y, self.zq(b), self.c)).start()

    def last(self, xp, out):
        p, SL, A = self.p, self.SL, self.A
        i, g = self.have(xp, self.y, self.z)
        self.wait(self.X.at[3], self.x_r.at[3])
        self.wait(self.Y.at[3], self.y_r.at[3])
        for b in range(3):
            self.wait(self.Z.at[b], self.z_r.at[b])
        self.add(A, 0, SL, [(self.FG, g), (self.R.at[i], 0), (self.X.at[3], 0), (self.Y.at[3], 0)] + [(self.Z.at[b], 0) for b in range(3)])
        start = lin(self.x, self.y, self.z, self.c) * p.sh
        r_first = start // LN
        s = start - r_first * LN
        r0 = r_first % 16
        A[0:SL] = pltpu.roll(A[0:SL], lax.rem(LN - s, LN), 1)
        lane = lax.broadcasted_iota(jnp.int32, (p.rows_in, LN), 1)
        out[...] = jnp.where(lane < LN - s, A[pl.ds(r0, p.rows_in), :], A[pl.ds(r0 + 1, p.rows_in), :])

    def after(self, part, index=None):
        for c in (0, 1):
            for x in (0, 1):
                todo = [e for e in SCHEDULE if e[:3] == (part, c, x)]
                if todo:
                    here = (self.c == c) & (self.x == x)
                    if index is not None:
                        here = here & (index[0] == index[1])

                    def run(todo=todo):
                        for _, _, _, step, xp, b0, n in todo:
                            lax.fori_loop(b0, b0 + n, lambda b, k: (getattr(self, step)(xp, b), k)[1], 0)

                    pl.when(here)(run)

    def leave(self):
        for k in range(16):
            self.wait(self.R.at[k], self.sib_s.at[k])
        for b in range(4):
            self.wait(self.D0.at[b], self.d_s.at[0, b])
            self.wait(self.D1.at[b], self.d_s.at[1, b])
            self.wait(self.X.at[b], self.x_s.at[b])
            self.wait(self.Y.at[b], self.y_s.at[b])
        for b in range(3):
            self.wait(self.Z.at[b], self.z_s.at[b])


BACK_IN = ("act", "d_outer", "w2", "gd", "first_low", "w1", "res", "xh1", "rstd1", "V", "VG", "mixed", "wo", "qkv", "lse", "tok")


def backward_scatter_kernel(p, length, *refs):
    n = len(BACK_IN)
    src = dict(zip(BACK_IN, refs[:n]))
    wqkv_in = refs[n]
    igrad, out = refs[n + 1 : n + 3]
    loc = dict(zip(BACK_IN, refs[n + 3 : 2 * n + 3]))
    FG, F, E, R, D0, D1, X, Y, Z, A, lsem, osem, *sems = refs[2 * n + 3 :]
    r = Refs(length=length[0], FG=FG, F=F, E=E, **loc)
    r.dqkv, r.d_branch, r.d_mixed = r.act, r.first_low, r.d_outer
    sc = Scatter(p, FG, R, D0, D1, X, Y, Z, A, sems)
    mats = {m: (b, k, c) for m, b, k, c in MATS}
    loads = {m: pltpu.make_async_copy(src[m], loc[m], lsem.at[k]) for k, m in enumerate(BACK_IN)}
    for m in BACK_IN:
        loads[m].start()

    def need(*names):
        for m in names:
            loads[m].wait()

    sc.enter()
    c0, c1 = sc.c == 0, sc.c == 1
    x0, x1 = sc.x == 0, sc.x == 1

    def both(cond, fn):
        pl.when(cond)(fn)

    need("act", "d_outer", "VG")
    weight_grad(r, r.act, r.d_outer, *mats["w2"], RB=1024, CB=2)
    edge_grads(r, 3)
    both(c0, lambda: sc.to_sibling(1))
    sc.after(1)
    need("w2", "gd")

    def act_part(j, carry):
        backward_act(r, j)
        for k in range(4):
            sc.after(2 + k, (j, k))
        return carry

    lax.fori_loop(0, FF // UP, act_part, 0)
    q_loads = [pltpu.make_async_copy(wqkv_in.at[:, pl.ds(k * D, D)], r.w2.at[pl.ds(k * D, D)], lsem.at[n + k]) for k in range(3)]
    for q in q_loads:
        q.start()
    need("first_low")
    weight_grad(r, r.first_low, r.gd, *mats["w1"], hook=lambda i: [sc.after(6 + k, (i, k)) for k in range(2)])
    edge_grads(r, 2)
    both(c1, lambda: sc.to_sibling(1))
    sc.after(8)
    need("w1", "res", "xh1", "rstd1", "V")
    backward_first(r)
    sc.after(9)
    need("mixed")
    weight_grad(r, r.mixed, r.d_branch, *mats["wo"])
    edge_grads(r, 1)
    both(c0, lambda: sc.to_sibling(0))
    sc.after(10)
    need("wo")
    backward_mixed(r)
    sc.after(11)
    need("qkv", "lse")

    def heads(hp, carry):
        backward_heads(r, hp)
        for k in range(6):
            sc.after(12 + k, (hp, k))
        return carry

    lax.fori_loop(0, H // 2, heads, 0)
    need("tok")
    weight_grad(r, r.tok, r.dqkv, *mats["wqkv"], hook=lambda i: [sc.after(18 + k, (i, k)) for k in range(2)])
    edge_grads(r, 0)
    both(c1, lambda: sc.to_sibling(0))
    sc.after(20)
    for q in q_loads:
        q.wait()

    def tokens(b, carry):
        o = rows_of(b, 256)
        v = r.res[o, :]
        for part in range(3):
            v = v + mm_nt(r.dqkv[o, part * D : (part + 1) * D], r.w2[part * D : (part + 1) * D, :])
        r.res[o, :] = v
        sc.after(21, (b, 0))
        return carry

    lax.fori_loop(0, LEN // 256, tokens, 0)
    grad_out = pltpu.make_async_copy(r.res, igrad, osem)
    grad_out.start()
    sc.after(22)
    both(x0, lambda: sc.last(0, out))
    both(x1, lambda: sc.last(1, out))
    sc.leave()
    grad_out.wait()


def backward_scatter(p, length, wqkv, **arrays):
    S = jax.ShapeDtypeStruct
    sm = pl.BlockSpec(memory_space=pltpu.SMEM)
    hbm = pl.BlockSpec(memory_space=pl.ANY)
    ins = [arrays[m] for m in BACK_IN]
    SL = p.slot
    half = SL // 32 * 16
    VM = pltpu.VMEM
    DM = pltpu.SemaphoreType.DMA
    igrad, o = pl.pallas_call(
        functools.partial(backward_scatter_kernel, p),
        out_shape=[S((LEN, D), F32), S((p.rows_in, LN), F32)],
        in_specs=[sm] + [hbm] * (len(ins) + 1),
        out_specs=[hbm, pl.BlockSpec(memory_space=pltpu.VMEM)],
        scratch_shapes=[VM(a.shape, a.dtype) for a in ins]
        + [VM((flat_rows(p), LN), BF), VM((6144 + 32, LN), F32), VM((160, LN), F32), VM((16, SL, LN), BF), VM((4, half, LN), BF), VM((4, SL - half, LN), BF), VM((4, SL, LN), BF), VM((4, SL, LN), BF), VM((3, SL, LN), BF), VM((SL + 32, LN), F32)]
        + [DM((len(ins) + 3,)), DM, DM((16,)), DM((16,)), DM((2, 4)), DM((2, 4)), DM((4,)), DM((4,)), DM((4,)), DM((4,)), DM((3,)), DM((3,))],
        compiler_params=pltpu.CompilerParams(collective_id=1, has_side_effects=True, vmem_limit_bytes=64 << 20),
    )(length, *ins, wqkv)
    return igrad, o.reshape(-1)[: p.sh]


def on_device(p, fast, tokens, lengths, weight_shards, hidden_cotangent, nested_cotangent):
    tok = tokens.reshape(LEN, D)
    hcot = hidden_cotangent.reshape(LEN, D)
    if fast:
        f = gather_forward(p, weight_shards, lengths, tok, hcot, nested_cotangent)
        igrad, shards = backward_scatter(p, lengths, tok=tok, **{m: f[m] for m in BACK_IN + ("wqkv",) if m != "tok"})
    else:
        slots = lax.all_gather(build_slot(p, weight_shards, me_of), AX, axis=0)
        f = dict(zip(FORWARD_OUT, forward_local(p, slots, lengths, tok, hcot, nested_cotangent)))
        igrad, flat = backward_local(p, lengths, tok, *[f[m] for m in FORWARD_OUT[6:] + FORWARD_OUT[2:6]])
        shards = scatter_plain(p, flat)
    return (f["hidden"].reshape(1, LEN, D), f["nested"], igrad.reshape(1, LEN, D), shards)


def solution(mesh):
    in_specs = (
        P(("dp", "fsdp"), None, None),
        P(("dp", "fsdp")),
        P(("dp", "fsdp")),
        P(("dp", "fsdp"), None, None),
        P(("dp", "fsdp"), None),
    )
    out_specs = (
        P(("dp", "fsdp"), None, None),
        P(("dp", "fsdp"), None),
        P(("dp", "fsdp"), None, None),
        P(("dp", "fsdp")),
    )
    p = plan(mesh.shape["dp"] * mesh.shape["fsdp"])
    fast = (mesh.shape["dp"], mesh.shape["fsdp"]) == (4, 8)
    return jax.shard_map(
        functools.partial(on_device, p, fast), mesh=mesh, in_specs=in_specs, out_specs=out_specs, check_vma=False
    )
```

```python
import functools
import math

import jax
import jax.numpy as jnp
from jax import lax
from jax.experimental import pallas as pl
from jax.experimental.pallas import tpu as pltpu
from jax.sharding import PartitionSpec as P

AX = ("dp", "fsdp")
MESH = pl.DeviceIdType.MESH
D = 768
H = 12
HD = 64
FF = 3072
LEN = 512
E2 = 512
E3 = 256
E4 = 128
E5 = 64


epsilon = 1e-05


PAR=7088640; LN=128
class Plan: pass
def plan(n):
    p=Plan(); p.n=n; p.sh=PAR//n
    st=[i*p.sh for i in range(n)]
    p.g0=[s//LN//16 for s in st]
    p.g1=[(s+p.sh-1)//LN//16 for s in st]
    p.slot=16*max(b-a+1 for a,b in zip(p.g0,p.g1))
    p.rows_in=-(-p.sh//LN)
    return p
MATS=[("wqkv",0,D,18),("wo",13836,D,6),("w1",18462,D,24),("w2",36918,FF,6)]
VECS=[(13824,12),(18444,18),(36894,24),(55350,30)]

def build_slot_kernel(p,me_of,x_ref,o_ref,q_ref):
    i=me_of(); start=i*p.sh; r_first=start//LN; s=start-r_first*LN; r0=r_first%16
    lead=32
    q_ref[...]=jnp.zeros_like(q_ref)
    q=pltpu.roll(x_ref[...].astype(jnp.float32),s,1)
    q_ref[lead:lead+p.rows_in]=q
    lane=lax.broadcasted_iota(jnp.int32,(p.slot,LN),1)
    a=q_ref[pl.ds(lead-r0,p.slot),:]
    b=q_ref[pl.ds(lead-1-r0,p.slot),:]
    o_ref[...]=jnp.where(lane>=s,a,b).astype(jnp.bfloat16)

def build_slot(p,shard,me_of):
    x=jnp.pad(shard,(0,p.rows_in*LN-p.sh)).reshape(p.rows_in,LN)
    return pl.pallas_call(functools.partial(build_slot_kernel,p,me_of),out_shape=jax.ShapeDtypeStruct((p.slot,LN),jnp.bfloat16),
        scratch_shapes=[pltpu.VMEM((32+p.slot+32,LN),jnp.float32)])(x)

def load_flat(p,slots,F,g_lo,g_hi,need=None):
    for i in range(p.n):
        a=max(g_lo,p.g0[i]); b=min(g_hi,p.g1[i]+1)
        if a>=b: continue
        shared_first = i>0 and p.g0[i]==p.g1[i-1] and a==p.g0[i]
        a2=a+1 if shared_first else a
        b2=b
        apart=need is not None and need<=(i+1)*p.sh//LN
        if i+1<p.n and p.g1[i]==p.g0[i+1] and b==p.g1[i]+1 and not apart: b2=b-1
        if i+1<p.n and b2<b and b-1>=g_lo:
            g=b-1
            F[16*(g-g_lo):16*(g-g_lo)+16]=slots[i,16*(g-p.g0[i]):16*(g-p.g0[i])+16].astype(jnp.float32)+slots[i+1,0:16].astype(jnp.float32)
        cnt=b2-a2
        if cnt<=0: continue
        U=16
        nb,rem=cnt//U,cnt%U
        def body(t,_,i=i,a2=a2):
            src=pl.multiple_of(16*(a2-p.g0[i])+t*16*U,16); dst=pl.multiple_of(16*(a2-g_lo)+t*16*U,16)
            F[pl.ds(dst,16*U)]=slots[i,pl.ds(src,16*U)].astype(jnp.float32)
            return 0
        lax.fori_loop(0,nb,body,0)
        if rem:
            src=16*(a2-p.g0[i])+nb*16*U; dst=16*(a2-g_lo)+nb*16*U
            F[dst:dst+16*rem]=slots[i,src:src+16*rem].astype(jnp.float32)

def coords():
    dp=lax.axis_index("dp"); fs=lax.axis_index("fsdp")
    return dp//2,fs%2,fs//2,dp%2
def dev(x,y,z,c): return (x*2+c, z*2+y)
def lin(x,y,z,c): return (x*2+c)*8+z*2+y
def barrier(partners):
    bar=pltpu.get_barrier_semaphore()
    for q in partners: pl.semaphore_signal(bar,inc=1,device_id=q,device_id_type=MESH)
    pl.semaphore_wait(bar,len(partners))

TOT=PAR//LN
def flat_rows(p): return max(16*p.g0[-1]+p.slot, EDGES[-1][0]+EDGES[-1][1])
def owner_row(rho):
    for k,(name,base,rows,w) in enumerate(MATS):
        if base<=rho<base+rows*w: return ("m",k,(rho-base)//w,(rho-base)%w)
    at=0
    for base,cnt in VECS:
        if base<=rho<base+cnt: return ("v",at+rho-base)
        at+=cnt
    return None

def me_of():
    return lax.axis_index(AX)


def finish_kernel(p, a_ref, out, A):
    SL = p.slot
    start = me_of() * p.sh
    r_first = start // LN
    s = start - r_first * LN
    r0 = r_first % 16
    A[0:SL] = pltpu.roll(a_ref[...], lax.rem(LN - s, LN), 1)
    lane = lax.broadcasted_iota(jnp.int32, (p.rows_in, LN), 1)
    out[...] = jnp.where(lane < LN - s, A[pl.ds(r0, p.rows_in), :], A[pl.ds(r0 + 1, p.rows_in), :])


def scatter_plain(p, flat):
    parts = jnp.concatenate([flat[16 * g : 16 * g + p.slot] for g in p.g0]).astype(jnp.float32)
    mine = lax.psum_scatter(parts, AX, scatter_dimension=0, tiled=True)
    o = pl.pallas_call(
        functools.partial(finish_kernel, p),
        out_shape=jax.ShapeDtypeStruct((p.rows_in, LN), jnp.float32),
        scratch_shapes=[pltpu.VMEM((p.slot + 32, LN), jnp.float32)],
    )(mine)
    return o.reshape(-1)[: p.sh]

EPS = 1e-05
F32 = jnp.float32
BF = jnp.bfloat16
SQ = math.sqrt(0.5)
PHI = 1.0 / math.sqrt(2.0 * math.pi)
VNAMES = (
    ("q_bias", D),
    ("v_bias", D),
    ("out_bias", D),
    ("first_gain", D),
    ("first_shift", D),
    ("up_bias", FF),
    ("down_bias", D),
    ("second_gain", D),
    ("second_shift", D),
    ("exit_gain", D),
    ("exit_shift", D),
)
VI = {name: k for k, (name, _) in enumerate(VNAMES)}
PREFIXES = (D, E2, E3, E4, E5)
UP = 768


def mm(a, b):
    return jnp.dot(a, b, preferred_element_type=F32)


def mm_nt(a, b):
    return lax.dot_general(a, b, (((1,), (1,)), ((), ())), preferred_element_type=F32)


def mm_tn(a, b):
    return lax.dot_general(a, b, (((0,), (0,)), ((), ())), preferred_element_type=F32)


def vrow(V, name):
    k = VI[name]
    return V[k : k + 1, : VNAMES[k][1]]


def mean_last(a):
    return jnp.mean(a, axis=-1, keepdims=True)


def sum_rows(a):
    return jnp.sum(a, axis=0, keepdims=True)


def forward_qkv(r):
    bias = jnp.concatenate([vrow(r.V, "q_bias"), jnp.zeros((1, D), F32), vrow(r.V, "v_bias")], axis=1)
    r.qb[...] = bias

    def body(j, _):
        o = pl.ds(pl.multiple_of(j * D, D), D)
        r.qkv[:, o] = (mm(r.tok[...], r.wqkv[:, o]) + r.qb[:, o]).astype(BF)
        return 0

    lax.fori_loop(0, 3, body, 0)


def half_lanes(h):
    lane = lax.broadcasted_iota(jnp.int32, (LEN, LN), 1)
    return lane < HD if h == 0 else lane >= HD


def pair(r, part, hp):
    return r.qkv[:, pl.ds(pl.multiple_of(part * D + hp * LN, LN), LN)]


def forward_heads(r, hp):
    q, k, v = pair(r, 0, hp), pair(r, 1, hp), pair(r, 2, hp)
    valid = lax.broadcasted_iota(jnp.int32, (1, LEN), 1) < r.length
    out = None
    lse_all = r.lse[...]
    lane = lax.broadcasted_iota(jnp.int32, (LEN, LN), 1)
    for h in range(2):
        qh = jnp.where(half_lanes(h), q, jnp.zeros_like(q))
        s = jnp.where(valid, mm_nt(qh, k) * 0.125, -1e9)
        m = jnp.max(s, axis=1, keepdims=True)
        e = jnp.exp(s - m)
        l = jnp.sum(e, axis=1, keepdims=True)
        low = (e * (1.0 / l)).astype(BF)
        o = mm(low, v)
        out = o if out is None else jnp.where(half_lanes(0), out, o)
        lse_all = jnp.where(lane == 2 * hp + h, m + jnp.log(l), lse_all)
    r.lse[...] = lse_all
    r.mixed[:, pl.ds(pl.multiple_of(hp * LN, LN), LN)] = out.astype(BF)


def rows_of(b, n):
    return pl.ds(pl.multiple_of(b * n, n), n)


def forward_first(r):
    def body(b, _):
        o = rows_of(b, LEN)
        v = r.tok[o, :].astype(F32) + mm(r.mixed[o, :], r.wo[...]) + vrow(r.V, "out_bias")
        cen = v - mean_last(v)
        rstd = lax.rsqrt(mean_last(cen * cen) + EPS)
        xh = cen * rstd
        r.xh1[o, :] = xh
        r.rstd1[o, :] = rstd
        r.first_low[o, :] = (xh * vrow(r.V, "first_gain") + vrow(r.V, "first_shift")).astype(BF)
        return 0

    lax.fori_loop(0, 1, body, 0)


def forward_up(r, j):
    o = pl.ds(pl.multiple_of(j * UP, UP), UP)
    v = mm(r.first_low[...], r.w1[:, o]) + r.V[VI["up_bias"] : VI["up_bias"] + 1, o]
    cdf = 0.5 * (1.0 + lax.erf(v * SQ))
    r.act[:, o] = (v * cdf).astype(BF)
    r.gd[:, o] = (cdf + v * (PHI * jnp.exp(-0.5 * v * v))).astype(BF)


def forward_second(r):
    def body(b, tot):
        o = rows_of(b, LEN)
        first = r.xh1[o, :] * vrow(r.V, "first_gain") + vrow(r.V, "first_shift")
        v = first + mm(r.act[o, :], r.w2[...]) + vrow(r.V, "down_bias")
        cen = v - mean_last(v)
        rstd = lax.rsqrt(mean_last(cen * cen) + EPS)
        xh = cen * rstd
        r.xh2[o, :] = xh
        r.rstd2[o, :] = rstd
        t = lax.broadcasted_iota(jnp.int32, (LEN, 1), 0)
        hid = (xh * vrow(r.V, "second_gain") + vrow(r.V, "second_shift")) * (t < r.length).astype(F32)
        r.hidden[o, :] = hid.astype(BF)
        return tot + sum_rows(hid)

    return lax.fori_loop(0, 1, body, jnp.zeros((1, D), F32))


def head(r, tot):
    inv_len = 1.0 / jnp.full((1, 1), r.length, jnp.int32).astype(F32)
    pooled = tot * inv_len
    cen = pooled - mean_last(pooled)
    rstd = lax.rsqrt(mean_last(cen * cen) + EPS)
    xh = cen * rstd
    gain = vrow(r.V, "exit_gain")
    emb = xh * gain + vrow(r.V, "exit_shift")
    d_emb = jnp.zeros((1, D), F32)
    at = 0
    for m in PREFIXES:
        e = emb[:, :m]
        inv = lax.rsqrt(jnp.sum(e * e, axis=1, keepdims=True) * (1.0 / m) + EPS)
        out = e * inv
        r.nested[:, at : at + m] = out
        c = r.ncot[:, at : at + m]
        g = inv * (c - out * (jnp.sum(c * out, axis=1, keepdims=True) * (1.0 / m)))
        d_emb = d_emb + (g if m == D else jnp.concatenate([g, jnp.zeros((1, D - m), F32)], axis=1))
        at += m
    put_grad(r, "exit_gain", d_emb * xh)
    put_grad(r, "exit_shift", d_emb)
    dx = d_emb * gain
    return rstd * (dx - mean_last(dx) - xh * mean_last(dx * xh)) * inv_len


def put_grad(r, name, value):
    k = VI[name]
    r.VG[k : k + 1, : VNAMES[k][1]] = value


def norm_back(dy, gain, xh, rstd):
    dx = dy * gain
    return rstd * (dx - mean_last(dx) - xh * mean_last(dx * xh))


def backward_second(r, d_pool):
    def body(b, c):
        o = rows_of(b, LEN)
        t = lax.broadcasted_iota(jnp.int32, (LEN, 1), 0)
        dy = (r.hcot[o, :].astype(F32) + d_pool) * (t < r.length).astype(F32)
        xh = r.xh2[o, :]
        res = norm_back(dy, vrow(r.V, "second_gain"), xh, r.rstd2[o, :])
        r.res[o, :] = res
        low = res.astype(BF)
        r.d_outer[o, :] = low
        return (c[0] + sum_rows(dy * xh), c[1] + sum_rows(dy), c[2] + sum_rows(low.astype(F32)))

    z = jnp.zeros((1, D), F32)
    a, b, c = lax.fori_loop(0, 1, body, (z, z, z))
    put_grad(r, "second_gain", a)
    put_grad(r, "second_shift", b)
    put_grad(r, "down_bias", c)


def backward_act(r, j):
    o = pl.ds(pl.multiple_of(j * UP, UP), UP)
    d = (mm_nt(r.d_outer[...], r.w2[o, :]) * r.gd[:, o].astype(F32)).astype(BF)
    r.gd[:, o] = d
    r.VG[VI["up_bias"] : VI["up_bias"] + 1, o] = sum_rows(d.astype(F32))


def backward_first(r):
    def body(b, c):
        o = rows_of(b, LEN)
        dy = mm_nt(r.gd[o, :], r.w1[...]) + r.res[o, :]
        xh = r.xh1[o, :]
        res = norm_back(dy, vrow(r.V, "first_gain"), xh, r.rstd1[o, :])
        r.res[o, :] = res
        low = res.astype(BF)
        r.d_branch[o, :] = low
        return (c[0] + sum_rows(dy * xh), c[1] + sum_rows(dy), c[2] + sum_rows(low.astype(F32)))

    z = jnp.zeros((1, D), F32)
    a, b, c = lax.fori_loop(0, 1, body, (z, z, z))
    put_grad(r, "first_gain", a)
    put_grad(r, "first_shift", b)
    put_grad(r, "out_bias", c)


def backward_mixed(r):
    r.d_mixed[...] = mm_nt(r.d_branch[...], r.wo[...]).astype(BF)


def backward_heads(r, hp):
    q, k, v = pair(r, 0, hp), pair(r, 1, hp), pair(r, 2, hp)
    cols = pl.ds(pl.multiple_of(hp * LN, LN), LN)
    dm = r.d_mixed[:, cols]
    valid = lax.broadcasted_iota(jnp.int32, (1, LEN), 1) < r.length
    lane = lax.broadcasted_iota(jnp.int32, (LEN, LN), 1)
    zero = jnp.zeros_like(q)
    dq = dk = dv = None
    for h in range(2):
        here = half_lanes(h)
        qh, kh, dmh = jnp.where(here, q, zero), jnp.where(here, k, zero), jnp.where(here, dm, zero)
        lse = jnp.sum(jnp.where(lane == 2 * hp + h, r.lse[...], 0.0), axis=1, keepdims=True)
        s = jnp.where(valid, mm_nt(qh, k) * 0.125, -1e9)
        p = jnp.exp(s - lse)
        dp = mm_nt(dmh, v)
        ds = (p * (dp - jnp.sum(dp * p, axis=1, keepdims=True))).astype(BF)
        a, b, c = mm(ds, kh), mm_tn(ds, qh), mm_tn(p.astype(BF), dmh)
        dq, dk, dv = (a, b, c) if dq is None else (dq + a, dk + b, dv + c)
    dq, dk, dv = (dq * 0.125).astype(BF), (dk * 0.125).astype(BF), dv.astype(BF)
    for part, g in ((0, dq), (1, dk), (2, dv)):
        r.dqkv[:, pl.ds(pl.multiple_of(part * D + hp * LN, LN), LN)] = g
    k = VI["q_bias"]
    r.VG[k : k + 1, cols] = sum_rows(dq.astype(F32))
    k = VI["v_bias"]
    r.VG[k : k + 1, cols] = sum_rows(dv.astype(F32))


def backward_tokens(r, b):
    o = rows_of(b, 128)
    v = r.res[o, :]
    for part in range(3):
        v = v + mm_nt(r.dqkv[o, part * D : (part + 1) * D], r.wqkv[:, part * D : (part + 1) * D])
    r.res[o, :] = v


EDGES = ((13824, 16), (18432, 32), (36880, 48), (55344, 64))


def edge_at(row):
    at = 0
    for base, rows in EDGES:
        if base <= row < base + rows:
            return at + row - base
        at += rows
    return None


def weight_grad(r, lhs, rhs, base, rows, w, RB=256, CB=6, hook=None):
    lead = base % 16
    step_rows = RB * w
    F = r.F
    if lead:
        F[0:16] = jnp.zeros((16, LN), F32)

    def body(s, _):
        o = pl.ds(pl.multiple_of(s * RB, RB), RB)
        for ch in range(w // CB):
            g = mm_tn(lhs[:, o], rhs[:, ch * CB * LN : (ch + 1) * CB * LN])
            for j in range(CB):
                F[pl.ds(lead + ch * CB + j, RB, stride=w), :] = g[:, j * LN : (j + 1) * LN]
        if lead:
            @pl.when(s == 0)
            def _():
                e = edge_at(base)
                r.E[e : e + 16 - lead] = F[lead:16]

        U = 256
        to = base - lead + s * step_rows

        def emit(t, _):
            r.FG[pl.ds(pl.multiple_of(to + t * U, 16), U)] = F[pl.ds(pl.multiple_of(t * U, 16), U)].astype(BF)
            return 0

        lax.fori_loop(0, step_rows // U, emit, 0)
        if lead:
            F[0:16] = F[step_rows : step_rows + 16]
        if hook is not None:
            hook(s)
        return 0

    lax.fori_loop(0, rows // RB, body, 0)
    if lead:
        e = edge_at(base + rows * w - lead)
        r.E[e : e + lead] = F[0:lead]


def edge_grads(r, which):
    base, rows = EDGES[which]
    at = 0
    for vbase, cnt in VECS:
        for k in range(cnt):
            row = vbase + k
            if base <= row < base + rows:
                name, j = vec_at(at + k)
                e = edge_at(row)
                r.E[e : e + 1] = r.VG[name : name + 1, j * LN : (j + 1) * LN]
        at += cnt
    if which == len(EDGES) - 1:
        e = edge_at(TOT)
        r.E[e : e + base + rows - TOT] = jnp.zeros((base + rows - TOT, LN), F32)
    e = edge_at(base)
    r.FG[base : base + rows] = r.E[e : e + rows].astype(BF)


def vec_at(row):
    for k, (_, n) in enumerate(VNAMES):
        if row < n // LN:
            return k, row
        row -= n // LN


class Refs:
    def __init__(self, **refs):
        self.__dict__.update(refs)


def relayout_vectors(p, r):
    at = 0
    for base, cnt in VECS:
        g_lo = base // 16
        g_hi = -(-(base + cnt) // 16)
        load_flat(p, r.slots, r.F, g_lo, g_hi)
        for k in range(cnt):
            name, j = vec_at(at + k)
            f = base - 16 * g_lo + k
            r.V[name : name + 1, j * LN : (j + 1) * LN] = r.F[f : f + 1]
        at += cnt


def relayout_matrix(p, r, name, W, RB):
    base, rows, w = {n: (b, k, c) for n, b, k, c in MATS}[name]
    for s in range(rows // RB):
        lo = base + s * RB * w
        g_lo = lo // 16
        load_flat(p, r.slots, r.F, g_lo, -(-(lo + RB * w) // 16))
        tile_rows(r.F, W, lo - 16 * g_lo, s * RB, RB, w)


def tile_rows(F, W, off, row, rows, w, RB=64):
    def body(t, _):
        q = pl.multiple_of(t * RB, RB)
        for j in range(w):
            W[pl.ds(row + q, RB), j * LN : (j + 1) * LN] = F[pl.ds(off + q * w + j, RB, stride=w), :].astype(BF)
        return 0

    lax.fori_loop(0, rows // RB, body, 0)


def forward_kernel(p, slots, length, tok, hcot, ncot, hidden, nested, wqkv, wo, w1, w2, V, VG, qkv, lse, mixed, xh1, rstd1, first_low, act, gd, res, d_outer, F, qb, xh2, rstd2):
    r = Refs(slots=slots, length=length[0], tok=tok, hcot=hcot, ncot=ncot, hidden=hidden, nested=nested, wqkv=wqkv, wo=wo, w1=w1, w2=w2, V=V, VG=VG, qkv=qkv, lse=lse, mixed=mixed, xh1=xh1, rstd1=rstd1, first_low=first_low, act=act, gd=gd, res=res, d_outer=d_outer, F=F, qb=qb, xh2=xh2, rstd2=rstd2)
    relayout_vectors(p, r)
    relayout_matrix(p, r, "wqkv", wqkv, 256)
    forward_qkv(r)
    lse[...] = jnp.zeros_like(lse)
    lax.fori_loop(0, H // 2, lambda hp, c: (forward_heads(r, hp), c)[1], 0)
    relayout_matrix(p, r, "wo", wo, 768)
    forward_first(r)
    relayout_matrix(p, r, "w1", w1, 256)
    lax.fori_loop(0, FF // UP, lambda j, c: (forward_up(r, j), c)[1], 0)
    relayout_matrix(p, r, "w2", w2, 768)
    tot = forward_second(r)
    d_pool = head(r, tot)
    backward_second(r, d_pool)


def forward_local(p, slots, length, tok, hcot, ncot):
    S = jax.ShapeDtypeStruct
    outs = [S((LEN, D), BF), S((1, 1728), F32), S((D, 3 * D), BF), S((D, D), BF), S((D, FF), BF), S((FF, D), BF), S((16, FF), F32), S((16, FF), F32), S((LEN, 3 * D), BF), S((LEN, LN), F32), S((LEN, D), BF), S((LEN, D), F32), S((LEN, 1), F32), S((LEN, D), BF), S((LEN, FF), BF), S((LEN, FF), BF), S((LEN, D), F32), S((LEN, D), BF)]
    vm = pl.BlockSpec(memory_space=pltpu.VMEM)
    sm = pl.BlockSpec(memory_space=pltpu.SMEM)
    return pl.pallas_call(
        functools.partial(forward_kernel, p),
        out_shape=outs,
        in_specs=[vm, sm, vm, vm, vm],
        scratch_shapes=[pltpu.VMEM((6144 + 32, LN), F32), pltpu.VMEM((1, 3 * D), F32), pltpu.VMEM((LEN, D), F32), pltpu.VMEM((LEN, 1), F32)],
        compiler_params=pltpu.CompilerParams(vmem_limit_bytes=60 << 20),
    )(slots, length, tok, hcot, ncot)


def backward_kernel(p, length, tok, V, VG0, qkv, lse, mixed, xh1, rstd1, first_low, act, gd, res, d_outer, wqkv, wo, w1, w2, igrad, FG, VG, d_branch, d_mixed, dqkv, F, E):
    r = Refs(length=length[0], tok=tok, V=V, VG=VG, qkv=qkv, lse=lse, mixed=mixed, xh1=xh1, rstd1=rstd1, first_low=first_low, act=act, gd=gd, res=igrad, d_outer=d_outer, wqkv=wqkv, wo=wo, w1=w1, w2=w2, FG=FG, d_branch=d_branch, d_mixed=d_mixed, dqkv=dqkv, F=F, E=E)
    VG[...] = VG0[...]
    igrad[...] = res[...]
    mats = {n: (b, k, c) for n, b, k, c in MATS}
    weight_grad(r, act, d_outer, *mats["w2"], RB=1024, CB=2)
    edge_grads(r, 3)
    lax.fori_loop(0, FF // UP, lambda j, c: (backward_act(r, j), c)[1], 0)
    weight_grad(r, first_low, gd, *mats["w1"])
    edge_grads(r, 2)
    backward_first(r)
    weight_grad(r, mixed, d_branch, *mats["wo"])
    edge_grads(r, 1)
    backward_mixed(r)
    lax.fori_loop(0, H // 2, lambda hp, c: (backward_heads(r, hp), c)[1], 0)
    weight_grad(r, tok, dqkv, *mats["wqkv"])
    edge_grads(r, 0)
    lax.fori_loop(0, LEN // 128, lambda b, c: (backward_tokens(r, b), c)[1], 0)


def backward_local(p, length, tok, V, VG, qkv, lse, mixed, xh1, rstd1, first_low, act, gd, res, d_outer, wqkv, wo, w1, w2):
    S = jax.ShapeDtypeStruct
    vm = pl.BlockSpec(memory_space=pltpu.VMEM)
    sm = pl.BlockSpec(memory_space=pltpu.SMEM)
    return pl.pallas_call(
        functools.partial(backward_kernel, p),
        out_shape=[S((LEN, D), F32), S((flat_rows(p), LN), BF)],
        in_specs=[sm] + [vm] * 17,
        scratch_shapes=[pltpu.VMEM((16, FF), F32), pltpu.VMEM((LEN, D), BF), pltpu.VMEM((LEN, D), BF), pltpu.VMEM((LEN, 3 * D), BF), pltpu.VMEM((6144 + 32, LN), F32), pltpu.VMEM((160, LN), F32)],
        compiler_params=pltpu.CompilerParams(vmem_limit_bytes=60 << 20),
    )(length, tok, V, VG, qkv, lse, mixed, xh1, rstd1, first_low, act, gd, res, d_outer, wqkv, wo, w1, w2)


class Gather:
    def __init__(self, p, G, ssem, rsem, gosem):
        self.p, self.G, self.ssem, self.rsem, self.gosem = p, G, ssem, rsem, gosem
        self.x, self.y, self.z, self.c = coords()
        x, y, z, c = self.x, self.y, self.z, self.c
        self.me = lin(x, y, z, c)
        half = p.slot // 32 * 16
        self.H = ((0, half), (half, p.slot - half), (0, p.slot))
        self.px, self.py, self.pc = dev(1 - x, y, z, c), dev(x, 1 - y, z, c), dev(x, y, z, 1 - c)

    def enter(self):
        x, y, z, c = self.x, self.y, self.z, self.c
        bar = pltpu.get_barrier_semaphore()

        def greet(to):
            pl.semaphore_signal(bar, inc=1, device_id=to, device_id_type=MESH)

        for to in (self.px, self.py, self.pc):
            greet(to)
        pl.when(z > 0)(lambda: greet(dev(x, y, z - 1, c)))
        pl.when(z < 3)(lambda: greet(dev(x, y, z + 1, c)))
        middle = (z > 0) & (z < 3)
        pl.when(middle)(lambda: pl.semaphore_wait(bar, 5))
        pl.when(jnp.logical_not(middle))(lambda: pl.semaphore_wait(bar, 4))

    def send(self, sl, h, to, t):
        r0, rn = self.H[h]
        ref = self.G.at[sl, pl.ds(r0, rn)]
        pltpu.make_async_remote_copy(src_ref=ref, dst_ref=ref, send_sem=self.ssem.at[sl, t], recv_sem=self.rsem.at[sl, h], device_id=to, device_id_type=MESH).start()

    def wait(self, sl, h, sem=None):
        r0, rn = self.H[h]
        ref = self.G.at[sl, pl.ds(r0, rn)]
        pltpu.make_async_copy(ref, ref, self.rsem.at[sl, h] if sem is None else sem).wait()

    def up(self, sl, h):
        pl.when(self.z < 3)(lambda: self.send(sl, h, dev(self.x, self.y, self.z + 1, self.c), 3))

    def down(self, sl, h):
        pl.when(self.z > 0)(lambda: self.send(sl, h, dev(self.x, self.y, self.z - 1, self.c), 4))

    def core(self, sl, h):
        self.send(sl, h, self.pc, 2)

    def xy(self, sl):
        self.send(sl, 0, self.px, 0)
        self.send(sl, 1, self.py, 1)
        self.send(sl, 1, self.px, 0)
        self.send(sl, 0, self.py, 1)

    def own(self, xy):
        for h in (0, 1):
            self.up(self.me, h)
            self.down(self.me, h)
        if xy:
            self.xy(self.me)
        for h in (0, 1):
            self.core(self.me, h)

    def own_line(self, k):
        self.at(k, lambda zq: self.xy(lin(self.x, self.y, zq, self.c)))

    def go(self, k):
        pl.semaphore_signal(self.gosem.at[k], inc=1, device_id=self.pc, device_id_type=MESH)

    def wait_go(self, k):
        pl.semaphore_wait(self.gosem.at[k], 1)

    def at(self, k, fn):
        if k == 0:
            fn(self.z)
            return
        pl.when(self.z - k >= 0)(lambda: fn(self.z - k))
        pl.when(self.z + k <= 3)(lambda: fn(self.z + k))

    def along_z(self, k, xy):
        x, y, z, c = self.x, self.y, self.z, self.c

        def from_level(zq, on):
            sl = lin(x, y, zq, c)
            self.wait(sl, 0)
            on(sl, 0)
            if xy:
                self.send(sl, 0, self.px, 0)
            self.core(sl, 0)
            self.wait(sl, 1)
            on(sl, 1)
            if xy:
                self.send(sl, 1, self.py, 1)
                self.send(sl, 1, self.px, 0)
                self.send(sl, 0, self.py, 1)
            self.core(sl, 1)

        pl.when(z - k >= 0)(lambda: from_level(z - k, self.up))
        pl.when(z + k <= 3)(lambda: from_level(z + k, self.down))

    def sides(self, k):
        x, y, c = self.x, self.y, self.c

        def fn(zq):
            sl = lin(1 - x, y, zq, c)
            self.wait(sl, 0)
            self.send(sl, 0, self.py, 1)
            self.core(sl, 0)
            sl = lin(x, 1 - y, zq, c)
            self.wait(sl, 1)
            self.send(sl, 1, self.px, 0)
            self.core(sl, 1)

        self.at(k, fn)

    def sides_rest(self, k):
        x, y, c = self.x, self.y, self.c

        def fn(zq):
            sl = lin(1 - x, y, zq, c)
            self.wait(sl, 1)
            self.core(sl, 1)
            sl = lin(x, 1 - y, zq, c)
            self.wait(sl, 0)
            self.core(sl, 0)

        self.at(k, fn)

    def diagonal(self, k):
        def fn(zq):
            sl = lin(1 - self.x, 1 - self.y, zq, self.c)
            for h in (0, 1):
                self.wait(sl, h)
                self.core(sl, h)

        self.at(k, fn)

    def from_sibling(self, xp):
        def body(fs, carry):
            for h in (0, 1):
                self.wait((2 * xp + 1 - self.c) * 8 + fs, h)
            return carry

        lax.fori_loop(0, 8, body, 0)

    def leave(self):
        x, y, z, c = self.x, self.y, self.z, self.c
        W = self.wait

        def body(zq, carry):
            sl = lin(x, y, zq, c)
            for t in (0, 1, 2):
                W(sl, 2, self.ssem.at[sl, t])
            pl.when((zq <= z) & (z < 3))(lambda: W(sl, 2, self.ssem.at[sl, 3]))
            pl.when((zq >= z) & (z > 0))(lambda: W(sl, 2, self.ssem.at[sl, 4]))
            sx = lin(1 - x, y, zq, c)
            W(sx, 0, self.ssem.at[sx, 1])
            W(sx, 2, self.ssem.at[sx, 2])
            sy = lin(x, 1 - y, zq, c)
            W(sy, 1, self.ssem.at[sy, 0])
            W(sy, 2, self.ssem.at[sy, 2])
            sd = lin(1 - x, 1 - y, zq, c)
            W(sd, 2, self.ssem.at[sd, 2])
            return carry

        lax.fori_loop(0, 4, body, 0)


FORWARD_OUT = ("hidden", "nested", "wqkv", "wo", "w1", "w2", "V", "VG", "qkv", "lse", "mixed", "xh1", "rstd1", "first_low", "act", "gd", "res", "d_outer")
FORWARD_SHAPES = dict(
    hidden=((LEN, D), jnp.bfloat16),
    nested=((1, 1728), jnp.float32),
    wqkv=((D, 3 * D), jnp.bfloat16),
    wo=((D, D), jnp.bfloat16),
    w1=((D, FF), jnp.bfloat16),
    w2=((FF, D), jnp.bfloat16),
    V=((16, FF), jnp.float32),
    VG=((16, FF), jnp.float32),
    qkv=((LEN, 3 * D), jnp.bfloat16),
    lse=((LEN, LN), jnp.float32),
    mixed=((LEN, D), jnp.bfloat16),
    xh1=((LEN, D), jnp.float32),
    rstd1=((LEN, 1), jnp.float32),
    first_low=((LEN, D), jnp.bfloat16),
    act=((LEN, FF), jnp.bfloat16),
    gd=((LEN, FF), jnp.bfloat16),
    res=((LEN, D), jnp.float32),
    d_outer=((LEN, D), jnp.bfloat16),
)


def own_slot(p, me, x_ref, F, G):
    start = me * p.sh
    r_first = start // LN
    s = start - r_first * LN
    r0 = r_first % 16
    lead = 32
    F[0 : lead + p.slot + 32] = jnp.zeros((lead + p.slot + 32, LN), F32)
    F[lead : lead + p.rows_in] = pltpu.roll(x_ref[...].astype(F32), s, 1)
    lane = lax.broadcasted_iota(jnp.int32, (p.slot, LN), 1)
    G[me] = jnp.where(lane >= s, F[pl.ds(lead - r0, p.slot), :], F[pl.ds(lead - 1 - r0, p.slot), :]).astype(BF)


def relayout_vector(p, r, which):
    at = sum(cnt for _, cnt in VECS[:which])
    base, cnt = VECS[which]
    g_lo = base // 16
    load_flat(p, r.slots, r.F, g_lo, -(-(base + cnt) // 16), base + cnt)
    for k in range(cnt):
        name, j = vec_at(at + k)
        f = base - 16 * g_lo + k
        r.V[name : name + 1, j * LN : (j + 1) * LN] = r.F[f : f + 1]


def relayout_rows(p, r, name, W, row, rows):
    base, _, w = {n: (b, k, c) for n, b, k, c in MATS}[name]
    lo = base + row * w
    g_lo = lo // 16
    load_flat(p, r.slots, r.F, g_lo, -(-(lo + rows * w) // 16), lo + rows * w)
    tile_rows(r.F, W, lo - 16 * g_lo, row, rows, w)


def gather_forward_kernel(p, x_ref, length, tok, hcot, ncot, *refs):
    n = len(FORWARD_OUT)
    outs = dict(zip(FORWARD_OUT, refs[:n]))
    loc = dict(zip(FORWARD_OUT, refs[n : 2 * n]))
    G, F, qb, xh2, rstd2, ssem, rsem, gosem, osem = refs[2 * n :]
    r = Refs(slots=G, length=length[0], tok=tok, hcot=hcot, ncot=ncot, F=F, qb=qb, xh2=xh2, rstd2=rstd2, **loc)
    g = Gather(p, G, ssem, rsem, gosem)
    own_slot(p, g.me, x_ref, F, G)
    g.enter()
    c0, c1 = g.c == 0, g.c == 1

    started = []

    def out(*names):
        for m in names:
            k = FORWARD_OUT.index(m)
            cp = pltpu.make_async_copy(loc[m], outs[m], osem.at[k])
            cp.start()
            started.append(cp)

    def part_rq_0():
        g.own(True)
        g.sides(0)
        g.go(0)
        g.along_z(1, True)
        g.sides(1)
        g.go(1)
        g.along_z(2, True)
        g.diagonal(0)
        g.sides_rest(0)
        g.sides(2)
        g.along_z(3, True)
        g.sides(3)
        g.diagonal(3)
        g.diagonal(2)
        g.sides_rest(3)
        g.diagonal(1)
        g.sides_rest(1)
        g.sides_rest(2)

    pl.when(c0)(part_rq_0)
    def part_rq_1():
        g.wait_go(0)
        g.own(False)
        g.wait_go(1)
        g.own_line(0)
        g.along_z(1, False)
        g.along_z(2, False)
        g.sides(0)
        g.along_z(3, False)
        g.own_line(3)
        g.own_line(1)
        g.own_line(2)
        g.sides(3)
        g.sides_rest(3)
        g.from_sibling(0)

    pl.when(c1)(part_rq_1)
    relayout_vector(p, r, 0)
    for k in range(3):
        relayout_rows(p, r, "wqkv", r.wqkv, 256 * k, 256)
    out("wqkv")
    def part_qkv_1():
        g.sides(1)
        g.diagonal(0)
        g.sides(2)
        g.from_sibling(1)
        g.sides_rest(0)

    pl.when(c1)(part_qkv_1)
    forward_qkv(r)
    out("qkv")
    r.lse[...] = jnp.zeros_like(r.lse)

    def heads(hp, carry):
        def part_hd1_1():
            g.sides_rest(1)
            g.sides_rest(2)
            g.diagonal(3)

        pl.when((hp == 1) & c1)(part_hd1_1)
        def part_hd3_1():
            g.diagonal(1)

        pl.when((hp == 3) & c1)(part_hd3_1)
        def part_hd5_1():
            g.diagonal(2)

        pl.when((hp == 5) & c1)(part_hd5_1)
        forward_heads(r, hp)
        return carry

    lax.fori_loop(0, H // 2, heads, 0)
    out("lse", "mixed")
    relayout_rows(p, r, "w1", r.w1, 448, 128)
    relayout_rows(p, r, "w1", r.w1, 576, 192)
    relayout_rows(p, r, "w2", r.w2, 0, 768)
    relayout_vector(p, r, 2)
    def part_rwo_0():
        g.from_sibling(0)

    pl.when(c0)(part_rwo_0)
    relayout_rows(p, r, "wo", r.wo, 0, 768)
    relayout_vector(p, r, 1)
    out("wo")
    forward_first(r)
    out("xh1", "rstd1", "first_low")
    relayout_rows(p, r, "w1", r.w1, 0, 256)
    relayout_rows(p, r, "w1", r.w1, 256, 192)
    out("w1")
    def part_up_0():
        g.from_sibling(1)

    pl.when(c0)(part_up_0)
    lax.fori_loop(0, FF // UP, lambda j, c: (forward_up(r, j), c)[1], 0)
    out("act", "gd")
    for k in range(1, 4):
        relayout_rows(p, r, "w2", r.w2, 768 * k, 768)
    relayout_vector(p, r, 3)
    out("w2", "V")
    tot = forward_second(r)
    out("hidden")
    d_pool = head(r, tot)
    out("nested")
    backward_second(r, d_pool)
    out("VG", "res", "d_outer")
    g.leave()
    for cp in started:
        cp.wait()


def gather_forward(p, shard, length, tok, hcot, ncot):
    x = jnp.pad(shard, (0, p.rows_in * LN - p.sh)).reshape(p.rows_in, LN)
    S = jax.ShapeDtypeStruct
    vm = pl.BlockSpec(memory_space=pltpu.VMEM)
    sm = pl.BlockSpec(memory_space=pltpu.SMEM)
    hbm = pl.BlockSpec(memory_space=pl.ANY)
    VM = pltpu.VMEM
    DM = pltpu.SemaphoreType.DMA
    shapes = [FORWARD_SHAPES[m] for m in FORWARD_OUT]
    res = pl.pallas_call(
        functools.partial(gather_forward_kernel, p),
        out_shape=[S(*s) for s in shapes],
        in_specs=[vm, sm, vm, vm, vm],
        out_specs=[hbm] * len(shapes),
        scratch_shapes=[VM(*s) for s in shapes]
        + [VM((p.n, p.slot, LN), BF), VM((6144 + 32, LN), F32), VM((1, 3 * D), F32), VM((LEN, D), F32), VM((LEN, 1), F32)]
        + [DM((p.n, 5)), DM((p.n, 2)), pltpu.SemaphoreType.REGULAR((2,)), DM((len(shapes),))],
        compiler_params=pltpu.CompilerParams(collective_id=0, has_side_effects=True, vmem_limit_bytes=64 << 20),
    )(x, length, tok, hcot, ncot)
    return dict(zip(FORWARD_OUT, res))


SCHEDULE = (
    (2, 1, 0, "diag", 1, 2, 2),
    (4, 1, 0, "diag", 1, 0, 2),
    (7, 1, 1, "yline", 1, 2, 2),
    (7, 1, 0, "xline", 1, 2, 2),
    (9, 0, 0, "diag", 1, 2, 2),
    (10, 1, 1, "diag", 0, 2, 2),
    (11, 1, 0, "xline", 1, 0, 2),
    (11, 1, 1, "diag", 0, 0, 2),
    (11, 1, 1, "yline", 1, 0, 2),
    (12, 0, 0, "diag", 1, 0, 2),
    (12, 0, 0, "xline", 1, 2, 2),
    (13, 1, 1, "xline", 0, 2, 2),
    (14, 1, 1, "xline", 0, 0, 2),
    (14, 1, 1, "own", 1, 2, 1),
    (17, 1, 0, "yline", 0, 2, 2),
    (18, 0, 1, "yline", 1, 2, 2),
    (20, 0, 0, "yline", 0, 0, 2),
    (20, 0, 1, "diag", 0, 0, 2),
    (20, 0, 1, "xline", 0, 0, 2),
    (20, 0, 1, "diag", 0, 2, 2),
    (20, 0, 0, "xline", 1, 0, 2),
    (20, 0, 0, "own", 0, 0, 2),
    (20, 1, 0, "own", 0, 2, 1),
    (21, 0, 1, "xline", 0, 2, 2),
    (21, 0, 0, "yline", 0, 2, 2),
    (21, 1, 0, "yline", 0, 0, 2),
    (21, 0, 1, "yline", 1, 0, 2),
    (21, 1, 0, "own", 0, 0, 2),
    (21, 0, 0, "own", 0, 2, 1),
    (21, 0, 1, "own", 1, 2, 1),
    (22, 0, 1, "own", 1, 0, 2),
    (22, 1, 1, "own", 1, 0, 2),
)


class Scatter:
    def __init__(self, p, FG, R, D0, D1, X, Y, Z, A, sems):
        self.p, self.FG, self.R, self.D0, self.D1, self.X, self.Y, self.Z, self.A = p, FG, R, D0, D1, X, Y, Z, A
        self.sib_s, self.sib_r, self.d_s, self.d_r, self.x_s, self.x_r, self.y_s, self.y_r, self.z_s, self.z_r = sems
        self.x, self.y, self.z, self.c = coords()
        x, y, z, c = self.x, self.y, self.z, self.c
        self.SL = p.slot
        self.half = p.slot // 32 * 16
        self.px, self.py, self.pc = dev(1 - x, y, z, c), dev(x, 1 - y, z, c), dev(x, y, z, 1 - c)

    def zq(self, b):
        d = lax.rem(b + 1, 4)
        z = self.z
        return lax.rem(z % 2 + d % 2, 2) + 2 * lax.rem(z // 2 + d // 2, 2)

    def enter(self):
        x, y, c = self.x, self.y, self.c
        barrier([self.px, self.py, self.pc] + [dev(x, y, self.zq(b), c) for b in range(3)])

    def row0(self, slot):
        return pl.multiple_of((slot * self.p.sh) // LN // 16 * 16, 16)

    def fg(self, slot):
        return self.row0(slot)

    def copy(self, src, dst, ssem, rsem, to):
        return pltpu.make_async_remote_copy(src_ref=src, dst_ref=dst, send_sem=ssem, recv_sem=rsem, device_id=to, device_id_type=MESH)

    def wait(self, ref, sem):
        pltpu.make_async_copy(ref, ref, sem).wait()

    def to_sibling(self, xp):
        def body(k, _):
            dp = 2 * xp + 1 - self.c
            i = 8 * xp + k
            self.copy(self.FG.at[pl.ds(self.row0(dp * 8 + k), self.SL)], self.R.at[i], self.sib_s.at[i], self.sib_r.at[i], self.pc).start()
            return 0

        lax.fori_loop(0, 8, body, 0)

    def add(self, dst, d0, rows, srcs, U=176):
        def body(t, _):
            r = pl.multiple_of(t * U, 16)
            v = None
            for s, s0 in srcs:
                e = s[pl.ds(s0 + r, U)].astype(F32)
                v = e if v is None else v + e
            dst[pl.ds(d0 + r, U)] = v.astype(dst.dtype)
            return 0

        lax.fori_loop(0, rows // U, body, 0)

    def have(self, xp, yq, zq):
        fs = zq * 2 + yq
        i = 8 * xp + fs
        self.wait(self.R.at[i], self.sib_r.at[i])
        return i, self.row0((2 * xp + self.c) * 8 + fs)

    def diag(self, xp, b):
        i, g = self.have(xp, 1 - self.y, self.zq(b))
        half, rest = self.half, self.SL - self.half
        R = self.R.at[i]
        self.add(R, 0, self.SL, [(self.FG, g), (R, 0)])
        self.copy(R.at[pl.ds(0, half)], self.D0.at[b], self.d_s.at[0, b], self.d_r.at[0, b], self.py).start()
        self.copy(R.at[pl.ds(half, rest)], self.D1.at[b], self.d_s.at[1, b], self.d_r.at[1, b], self.px).start()

    def xline(self, xp, b):
        i, g = self.have(xp, self.y, self.zq(b))
        half, rest = self.half, self.SL - self.half
        R = self.R.at[i]
        self.wait(self.D0.at[b], self.d_r.at[0, b])
        self.add(R, half, rest, [(self.FG, g + half), (R, half)])
        self.add(R, 0, half, [(self.FG, g), (R, 0), (self.D0.at[b], 0)])
        self.copy(R, self.X.at[b], self.x_s.at[b], self.x_r.at[b], self.px).start()

    def yline(self, xp, b):
        i, g = self.have(xp, 1 - self.y, self.zq(b))
        half, rest = self.half, self.SL - self.half
        R = self.R.at[i]
        self.wait(self.D1.at[b], self.d_r.at[1, b])
        self.add(R, 0, half, [(self.FG, g), (R, 0)])
        self.add(R, half, rest, [(self.FG, g + half), (R, half), (self.D1.at[b], 0)])
        self.copy(R, self.Y.at[b], self.y_s.at[b], self.y_r.at[b], self.py).start()

    def own(self, xp, b):
        i, g = self.have(xp, self.y, self.zq(b))
        R = self.R.at[i]
        self.wait(self.X.at[b], self.x_r.at[b])
        self.wait(self.Y.at[b], self.y_r.at[b])
        self.add(R, 0, self.SL, [(self.FG, g), (R, 0), (self.X.at[b], 0), (self.Y.at[b], 0)])
        self.copy(R, self.Z.at[b], self.z_s.at[b], self.z_r.at[b], dev(self.x, self.y, self.zq(b), self.c)).start()

    def last(self, xp, out):
        p, SL, A = self.p, self.SL, self.A
        i, g = self.have(xp, self.y, self.z)
        self.wait(self.X.at[3], self.x_r.at[3])
        self.wait(self.Y.at[3], self.y_r.at[3])
        for b in range(3):
            self.wait(self.Z.at[b], self.z_r.at[b])
        self.add(A, 0, SL, [(self.FG, g), (self.R.at[i], 0), (self.X.at[3], 0), (self.Y.at[3], 0)] + [(self.Z.at[b], 0) for b in range(3)])
        start = lin(self.x, self.y, self.z, self.c) * p.sh
        r_first = start // LN
        s = start - r_first * LN
        r0 = r_first % 16
        A[0:SL] = pltpu.roll(A[0:SL], lax.rem(LN - s, LN), 1)
        lane = lax.broadcasted_iota(jnp.int32, (p.rows_in, LN), 1)
        out[...] = jnp.where(lane < LN - s, A[pl.ds(r0, p.rows_in), :], A[pl.ds(r0 + 1, p.rows_in), :])

    def after(self, part, index=None):
        for c in (0, 1):
            for x in (0, 1):
                todo = [e for e in SCHEDULE if e[:3] == (part, c, x)]
                if todo:
                    here = (self.c == c) & (self.x == x)
                    if index is not None:
                        here = here & (index[0] == index[1])

                    def run(todo=todo):
                        for _, _, _, step, xp, b0, n in todo:
                            lax.fori_loop(b0, b0 + n, lambda b, k: (getattr(self, step)(xp, b), k)[1], 0)

                    pl.when(here)(run)

    def leave(self):
        for k in range(16):
            self.wait(self.R.at[k], self.sib_s.at[k])
        for b in range(4):
            self.wait(self.D0.at[b], self.d_s.at[0, b])
            self.wait(self.D1.at[b], self.d_s.at[1, b])
            self.wait(self.X.at[b], self.x_s.at[b])
            self.wait(self.Y.at[b], self.y_s.at[b])
        for b in range(3):
            self.wait(self.Z.at[b], self.z_s.at[b])


BACK_IN = ("act", "d_outer", "w2", "gd", "first_low", "w1", "res", "xh1", "rstd1", "V", "VG", "mixed", "wo", "qkv", "lse", "tok")


def backward_scatter_kernel(p, length, *refs):
    n = len(BACK_IN)
    src = dict(zip(BACK_IN, refs[:n]))
    wqkv_in = refs[n]
    igrad, out = refs[n + 1 : n + 3]
    loc = dict(zip(BACK_IN, refs[n + 3 : 2 * n + 3]))
    FG, F, E, R, D0, D1, X, Y, Z, lsem, osem, *sems = refs[2 * n + 3 :]
    r = Refs(length=length[0], FG=FG, F=F, E=E, **loc)
    r.dqkv, r.d_branch, r.d_mixed = r.act, r.first_low, r.d_outer
    sc = Scatter(p, FG, R, D0, D1, X, Y, Z, F, sems)
    mats = {m: (b, k, c) for m, b, k, c in MATS}
    loads = {m: pltpu.make_async_copy(src[m], loc[m], lsem.at[k]) for k, m in enumerate(BACK_IN)}
    for m in BACK_IN:
        loads[m].start()

    def need(*names):
        for m in names:
            loads[m].wait()

    sc.enter()
    c0, c1 = sc.c == 0, sc.c == 1
    x0, x1 = sc.x == 0, sc.x == 1

    def both(cond, fn):
        pl.when(cond)(fn)

    need("act", "d_outer", "VG")
    weight_grad(r, r.act, r.d_outer, *mats["w2"], RB=1024, CB=2)
    edge_grads(r, 3)
    both(c0, lambda: sc.to_sibling(1))
    sc.after(1)
    need("w2", "gd")

    def act_part(j, carry):
        backward_act(r, j)
        for k in range(4):
            sc.after(2 + k, (j, k))
        return carry

    lax.fori_loop(0, FF // UP, act_part, 0)
    q_loads = [pltpu.make_async_copy(wqkv_in.at[:, pl.ds(k * D, D)], r.w2.at[pl.ds(k * D, D)], lsem.at[n + k]) for k in range(3)]
    for q in q_loads:
        q.start()
    need("first_low")
    weight_grad(r, r.first_low, r.gd, *mats["w1"], hook=lambda i: [sc.after(6 + k, (i, k)) for k in range(2)])
    edge_grads(r, 2)
    both(c1, lambda: sc.to_sibling(1))
    sc.after(8)
    need("w1", "res", "xh1", "rstd1", "V")
    backward_first(r)
    sc.after(9)
    need("mixed")
    weight_grad(r, r.mixed, r.d_branch, *mats["wo"])
    edge_grads(r, 1)
    both(c0, lambda: sc.to_sibling(0))
    sc.after(10)
    need("wo")
    backward_mixed(r)
    sc.after(11)
    need("qkv", "lse")

    def heads(hp, carry):
        backward_heads(r, hp)
        for k in range(6):
            sc.after(12 + k, (hp, k))
        return carry

    lax.fori_loop(0, H // 2, heads, 0)
    need("tok")
    weight_grad(r, r.tok, r.dqkv, *mats["wqkv"], hook=lambda i: [sc.after(18 + k, (i, k)) for k in range(2)])
    edge_grads(r, 0)
    both(c1, lambda: sc.to_sibling(0))
    sc.after(20)
    for q in q_loads:
        q.wait()

    def tokens(b, carry):
        o = rows_of(b, LEN)
        v = r.res[o, :]
        for part in range(3):
            v = v + mm_nt(r.dqkv[o, part * D : (part + 1) * D], r.w2[part * D : (part + 1) * D, :])
        r.res[o, :] = v
        sc.after(21, (b, 0))
        return carry

    lax.fori_loop(0, 1, tokens, 0)
    grad_out = pltpu.make_async_copy(r.res, igrad, osem)
    grad_out.start()
    sc.after(22)
    both(x0, lambda: sc.last(0, out))
    both(x1, lambda: sc.last(1, out))
    sc.leave()
    grad_out.wait()


def backward_scatter(p, length, wqkv, **arrays):
    S = jax.ShapeDtypeStruct
    sm = pl.BlockSpec(memory_space=pltpu.SMEM)
    hbm = pl.BlockSpec(memory_space=pl.ANY)
    ins = [arrays[m] for m in BACK_IN]
    SL = p.slot
    half = SL // 32 * 16
    VM = pltpu.VMEM
    DM = pltpu.SemaphoreType.DMA
    igrad, o = pl.pallas_call(
        functools.partial(backward_scatter_kernel, p),
        out_shape=[S((LEN, D), F32), S((p.rows_in, LN), F32)],
        in_specs=[sm] + [hbm] * (len(ins) + 1),
        out_specs=[hbm, pl.BlockSpec(memory_space=pltpu.VMEM)],
        scratch_shapes=[VM(a.shape, a.dtype) for a in ins]
        + [VM((flat_rows(p), LN), BF), VM((6144 + 32, LN), F32), VM((160, LN), F32), VM((16, SL, LN), BF), VM((4, half, LN), BF), VM((4, SL - half, LN), BF), VM((4, SL, LN), BF), VM((4, SL, LN), BF), VM((3, SL, LN), BF)]
        + [DM((len(ins) + 3,)), DM, DM((16,)), DM((16,)), DM((2, 4)), DM((2, 4)), DM((4,)), DM((4,)), DM((4,)), DM((4,)), DM((3,)), DM((3,))],
        compiler_params=pltpu.CompilerParams(collective_id=1, has_side_effects=True, vmem_limit_bytes=64 << 20),
    )(length, *ins, wqkv)
    return igrad, o.reshape(-1)[: p.sh]


def on_device(p, fast, tokens, lengths, weight_shards, hidden_cotangent, nested_cotangent):
    tok = tokens.reshape(LEN, D)
    hcot = hidden_cotangent.reshape(LEN, D)
    if fast:
        f = gather_forward(p, weight_shards, lengths, tok, hcot, nested_cotangent)
        igrad, shards = backward_scatter(p, lengths, tok=tok, **{m: f[m] for m in BACK_IN + ("wqkv",) if m != "tok"})
    else:
        slots = lax.all_gather(build_slot(p, weight_shards, me_of), AX, axis=0)
        f = dict(zip(FORWARD_OUT, forward_local(p, slots, lengths, tok, hcot, nested_cotangent)))
        igrad, flat = backward_local(p, lengths, tok, *[f[m] for m in FORWARD_OUT[6:] + FORWARD_OUT[2:6]])
        shards = scatter_plain(p, flat)
    return (f["hidden"].reshape(1, LEN, D), f["nested"], igrad.reshape(1, LEN, D), shards)


def solution(mesh):
    in_specs = (
        P(("dp", "fsdp"), None, None),
        P(("dp", "fsdp")),
        P(("dp", "fsdp")),
        P(("dp", "fsdp"), None, None),
        P(("dp", "fsdp"), None),
    )
    out_specs = (
        P(("dp", "fsdp"), None, None),
        P(("dp", "fsdp"), None),
        P(("dp", "fsdp"), None, None),
        P(("dp", "fsdp")),
    )
    p = plan(mesh.shape["dp"] * mesh.shape["fsdp"])
    fast = (mesh.shape["dp"], mesh.shape["fsdp"]) == (4, 8)
    return jax.shard_map(
        functools.partial(on_device, p, fast), mesh=mesh, in_specs=in_specs, out_specs=out_specs, check_vma=False
    )
```

```python
import functools
import math

import jax
import jax.numpy as jnp
from jax import lax
from jax.experimental import pallas as pl
from jax.experimental.pallas import tpu as pltpu
from jax.sharding import PartitionSpec as P

AX = ("dp", "fsdp")
MESH = pl.DeviceIdType.MESH
D = 768
H = 12
HD = 64
FF = 3072
LEN = 512
E2 = 512
E3 = 256
E4 = 128
E5 = 64


epsilon = 1e-05


PAR=7088640; LN=128
class Plan: pass
def plan(n):
    p=Plan(); p.n=n; p.sh=PAR//n
    st=[i*p.sh for i in range(n)]
    p.g0=[s//LN//16 for s in st]
    p.g1=[(s+p.sh-1)//LN//16 for s in st]
    p.slot=16*max(b-a+1 for a,b in zip(p.g0,p.g1))
    p.rows_in=-(-p.sh//LN)
    return p
MATS=[("wqkv",0,D,18),("wo",13836,D,6),("w1",18462,D,24),("w2",36918,FF,6)]
VECS=[(13824,12),(18444,18),(36894,24),(55350,30)]

def build_slot_kernel(p,me_of,x_ref,o_ref,q_ref):
    i=me_of(); start=i*p.sh; r_first=start//LN; s=start-r_first*LN; r0=r_first%16
    lead=32
    q_ref[...]=jnp.zeros_like(q_ref)
    q=pltpu.roll(x_ref[...].astype(jnp.float32),s,1)
    q_ref[lead:lead+p.rows_in]=q
    lane=lax.broadcasted_iota(jnp.int32,(p.slot,LN),1)
    a=q_ref[pl.ds(lead-r0,p.slot),:]
    b=q_ref[pl.ds(lead-1-r0,p.slot),:]
    o_ref[...]=jnp.where(lane>=s,a,b).astype(jnp.bfloat16)

def build_slot(p,shard,me_of):
    x=jnp.pad(shard,(0,p.rows_in*LN-p.sh)).reshape(p.rows_in,LN)
    return pl.pallas_call(functools.partial(build_slot_kernel,p,me_of),out_shape=jax.ShapeDtypeStruct((p.slot,LN),jnp.bfloat16),
        scratch_shapes=[pltpu.VMEM((32+p.slot+32,LN),jnp.float32)])(x)

def load_flat(p,slots,F,g_lo,g_hi,need=None):
    for i in range(p.n):
        a=max(g_lo,p.g0[i]); b=min(g_hi,p.g1[i]+1)
        if a>=b: continue
        shared_first = i>0 and p.g0[i]==p.g1[i-1] and a==p.g0[i]
        a2=a+1 if shared_first else a
        b2=b
        apart=need is not None and need<=(i+1)*p.sh//LN
        if i+1<p.n and p.g1[i]==p.g0[i+1] and b==p.g1[i]+1 and not apart: b2=b-1
        if i+1<p.n and b2<b and b-1>=g_lo:
            g=b-1
            F[16*(g-g_lo):16*(g-g_lo)+16]=slots[i,16*(g-p.g0[i]):16*(g-p.g0[i])+16].astype(jnp.float32)+slots[i+1,0:16].astype(jnp.float32)
        cnt=b2-a2
        if cnt<=0: continue
        U=16
        nb,rem=cnt//U,cnt%U
        def body(t,_,i=i,a2=a2):
            src=pl.multiple_of(16*(a2-p.g0[i])+t*16*U,16); dst=pl.multiple_of(16*(a2-g_lo)+t*16*U,16)
            F[pl.ds(dst,16*U)]=slots[i,pl.ds(src,16*U)].astype(jnp.float32)
            return 0
        lax.fori_loop(0,nb,body,0)
        if rem:
            src=16*(a2-p.g0[i])+nb*16*U; dst=16*(a2-g_lo)+nb*16*U
            F[dst:dst+16*rem]=slots[i,src:src+16*rem].astype(jnp.float32)

def coords():
    dp=lax.axis_index("dp"); fs=lax.axis_index("fsdp")
    return dp//2,fs%2,fs//2,dp%2
def dev(x,y,z,c): return (x*2+c, z*2+y)
def lin(x,y,z,c): return (x*2+c)*8+z*2+y
def barrier(partners):
    bar=pltpu.get_barrier_semaphore()
    for q in partners: pl.semaphore_signal(bar,inc=1,device_id=q,device_id_type=MESH)
    pl.semaphore_wait(bar,len(partners))

TOT=PAR//LN
def flat_rows(p): return max(16*p.g0[-1]+p.slot, EDGES[-1][0]+EDGES[-1][1])
def owner_row(rho):
    for k,(name,base,rows,w) in enumerate(MATS):
        if base<=rho<base+rows*w: return ("m",k,(rho-base)//w,(rho-base)%w)
    at=0
    for base,cnt in VECS:
        if base<=rho<base+cnt: return ("v",at+rho-base)
        at+=cnt
    return None

def me_of():
    return lax.axis_index(AX)


def finish_kernel(p, a_ref, out, A):
    SL = p.slot
    start = me_of() * p.sh
    r_first = start // LN
    s = start - r_first * LN
    r0 = r_first % 16
    A[0:SL] = pltpu.roll(a_ref[...], lax.rem(LN - s, LN), 1)
    lane = lax.broadcasted_iota(jnp.int32, (p.rows_in, LN), 1)
    out[...] = jnp.where(lane < LN - s, A[pl.ds(r0, p.rows_in), :], A[pl.ds(r0 + 1, p.rows_in), :])


def scatter_plain(p, flat):
    parts = jnp.concatenate([flat[16 * g : 16 * g + p.slot] for g in p.g0]).astype(jnp.float32)
    mine = lax.psum_scatter(parts, AX, scatter_dimension=0, tiled=True)
    o = pl.pallas_call(
        functools.partial(finish_kernel, p),
        out_shape=jax.ShapeDtypeStruct((p.rows_in, LN), jnp.float32),
        scratch_shapes=[pltpu.VMEM((p.slot + 32, LN), jnp.float32)],
    )(mine)
    return o.reshape(-1)[: p.sh]

EPS = 1e-05
F32 = jnp.float32
BF = jnp.bfloat16
SQ = math.sqrt(0.5)
PHI = 1.0 / math.sqrt(2.0 * math.pi)
VNAMES = (
    ("q_bias", D),
    ("v_bias", D),
    ("out_bias", D),
    ("first_gain", D),
    ("first_shift", D),
    ("up_bias", FF),
    ("down_bias", D),
    ("second_gain", D),
    ("second_shift", D),
    ("exit_gain", D),
    ("exit_shift", D),
)
VI = {name: k for k, (name, _) in enumerate(VNAMES)}
PREFIXES = (D, E2, E3, E4, E5)
UP = 768


def mm(a, b):
    return jnp.dot(a, b, preferred_element_type=F32)


def mm_nt(a, b):
    return lax.dot_general(a, b, (((1,), (1,)), ((), ())), preferred_element_type=F32)


def mm_tn(a, b):
    return lax.dot_general(a, b, (((0,), (0,)), ((), ())), preferred_element_type=F32)


def vrow(V, name):
    k = VI[name]
    return V[k : k + 1, : VNAMES[k][1]]


def mean_last(a):
    return jnp.mean(a, axis=-1, keepdims=True)


def sum_rows(a):
    return jnp.sum(a, axis=0, keepdims=True)


def forward_qkv(r):
    bias = jnp.concatenate([vrow(r.V, "q_bias"), jnp.zeros((1, D), F32), vrow(r.V, "v_bias")], axis=1)
    r.qb[...] = bias

    def body(j, _):
        o = pl.ds(pl.multiple_of(j * D, D), D)
        r.qkv[:, o] = (mm(r.tok[...], r.wqkv[:, o]) + r.qb[:, o]).astype(BF)
        return 0

    lax.fori_loop(0, 3, body, 0)


def half_lanes(h):
    lane = lax.broadcasted_iota(jnp.int32, (LEN, LN), 1)
    return lane < HD if h == 0 else lane >= HD


def pair(r, part, hp):
    return r.qkv[:, pl.ds(pl.multiple_of(part * D + hp * LN, LN), LN)]


def forward_heads(r, hp):
    q, k, v = pair(r, 0, hp), pair(r, 1, hp), pair(r, 2, hp)
    valid = lax.broadcasted_iota(jnp.int32, (1, LEN), 1) < r.length
    out = None
    lse_all = r.lse[...]
    lane = lax.broadcasted_iota(jnp.int32, (LEN, LN), 1)
    for h in range(2):
        qh = jnp.where(half_lanes(h), q, jnp.zeros_like(q))
        s = jnp.where(valid, mm_nt(qh, k) * 0.125, -1e9)
        m = jnp.max(s, axis=1, keepdims=True)
        e = jnp.exp(s - m)
        l = jnp.sum(e, axis=1, keepdims=True)
        low = (e * (1.0 / l)).astype(BF)
        o = mm(low, v)
        out = o if out is None else jnp.where(half_lanes(0), out, o)
        lse_all = jnp.where(lane == 2 * hp + h, m + jnp.log(l), lse_all)
    r.lse[...] = lse_all
    r.mixed[:, pl.ds(pl.multiple_of(hp * LN, LN), LN)] = out.astype(BF)


def rows_of(b, n):
    return pl.ds(pl.multiple_of(b * n, n), n)


def forward_first(r):
    def body(b, _):
        o = rows_of(b, LEN)
        v = r.tok[o, :].astype(F32) + mm(r.mixed[o, :], r.wo[...]) + vrow(r.V, "out_bias")
        cen = v - mean_last(v)
        rstd = lax.rsqrt(mean_last(cen * cen) + EPS)
        xh = cen * rstd
        r.xh1[o, :] = xh
        r.rstd1[o, :] = rstd
        r.first_low[o, :] = (xh * vrow(r.V, "first_gain") + vrow(r.V, "first_shift")).astype(BF)
        return 0

    lax.fori_loop(0, 1, body, 0)


def forward_up(r, j):
    o = pl.ds(pl.multiple_of(j * UP, UP), UP)
    v = mm(r.first_low[...], r.w1[:, o]) + r.V[VI["up_bias"] : VI["up_bias"] + 1, o]
    cdf = 0.5 * (1.0 + lax.erf(v * SQ))
    r.act[:, o] = (v * cdf).astype(BF)
    r.gd[:, o] = (cdf + v * (PHI * jnp.exp(-0.5 * v * v))).astype(BF)


def forward_second(r):
    def body(b, tot):
        o = rows_of(b, LEN)
        first = r.xh1[o, :] * vrow(r.V, "first_gain") + vrow(r.V, "first_shift")
        v = first + mm(r.act[o, :], r.w2[...]) + vrow(r.V, "down_bias")
        cen = v - mean_last(v)
        rstd = lax.rsqrt(mean_last(cen * cen) + EPS)
        xh = cen * rstd
        r.xh2[o, :] = xh
        r.rstd2[o, :] = rstd
        t = lax.broadcasted_iota(jnp.int32, (LEN, 1), 0)
        hid = (xh * vrow(r.V, "second_gain") + vrow(r.V, "second_shift")) * (t < r.length).astype(F32)
        r.hidden[o, :] = hid.astype(BF)
        return tot + sum_rows(hid)

    return lax.fori_loop(0, 1, body, jnp.zeros((1, D), F32))


def head(r, tot):
    inv_len = 1.0 / jnp.full((1, 1), r.length, jnp.int32).astype(F32)
    pooled = tot * inv_len
    cen = pooled - mean_last(pooled)
    rstd = lax.rsqrt(mean_last(cen * cen) + EPS)
    xh = cen * rstd
    gain = vrow(r.V, "exit_gain")
    emb = xh * gain + vrow(r.V, "exit_shift")
    d_emb = jnp.zeros((1, D), F32)
    at = 0
    for m in PREFIXES:
        e = emb[:, :m]
        inv = lax.rsqrt(jnp.sum(e * e, axis=1, keepdims=True) * (1.0 / m) + EPS)
        out = e * inv
        r.nested[:, at : at + m] = out
        c = r.ncot[:, at : at + m]
        g = inv * (c - out * (jnp.sum(c * out, axis=1, keepdims=True) * (1.0 / m)))
        d_emb = d_emb + (g if m == D else jnp.concatenate([g, jnp.zeros((1, D - m), F32)], axis=1))
        at += m
    put_grad(r, "exit_gain", d_emb * xh)
    put_grad(r, "exit_shift", d_emb)
    dx = d_emb * gain
    return rstd * (dx - mean_last(dx) - xh * mean_last(dx * xh)) * inv_len


def put_grad(r, name, value):
    k = VI[name]
    r.VG[k : k + 1, : VNAMES[k][1]] = value


def norm_back(dy, gain, xh, rstd):
    dx = dy * gain
    return rstd * (dx - mean_last(dx) - xh * mean_last(dx * xh))


def backward_second(r, d_pool):
    def body(b, c):
        o = rows_of(b, LEN)
        t = lax.broadcasted_iota(jnp.int32, (LEN, 1), 0)
        dy = (r.hcot[o, :].astype(F32) + d_pool) * (t < r.length).astype(F32)
        xh = r.xh2[o, :]
        res = norm_back(dy, vrow(r.V, "second_gain"), xh, r.rstd2[o, :])
        r.res[o, :] = res
        low = res.astype(BF)
        r.d_outer[o, :] = low
        return (c[0] + sum_rows(dy * xh), c[1] + sum_rows(dy), c[2] + sum_rows(low.astype(F32)))

    z = jnp.zeros((1, D), F32)
    a, b, c = lax.fori_loop(0, 1, body, (z, z, z))
    put_grad(r, "second_gain", a)
    put_grad(r, "second_shift", b)
    put_grad(r, "down_bias", c)


def backward_act(r, j):
    o = pl.ds(pl.multiple_of(j * UP, UP), UP)
    d = (mm_nt(r.d_outer[...], r.w2[o, :]) * r.gd[:, o].astype(F32)).astype(BF)
    r.gd[:, o] = d
    r.VG[VI["up_bias"] : VI["up_bias"] + 1, o] = sum_rows(d.astype(F32))


def backward_first(r):
    def body(b, c):
        o = rows_of(b, LEN)
        dy = mm_nt(r.gd[o, :], r.w1[...]) + r.res[o, :]
        xh = r.xh1[o, :]
        res = norm_back(dy, vrow(r.V, "first_gain"), xh, r.rstd1[o, :])
        r.res[o, :] = res
        low = res.astype(BF)
        r.d_branch[o, :] = low
        return (c[0] + sum_rows(dy * xh), c[1] + sum_rows(dy), c[2] + sum_rows(low.astype(F32)))

    z = jnp.zeros((1, D), F32)
    a, b, c = lax.fori_loop(0, 1, body, (z, z, z))
    put_grad(r, "first_gain", a)
    put_grad(r, "first_shift", b)
    put_grad(r, "out_bias", c)


def backward_mixed(r):
    r.d_mixed[...] = mm_nt(r.d_branch[...], r.wo[...]).astype(BF)


def backward_heads(r, hp):
    q, k, v = pair(r, 0, hp), pair(r, 1, hp), pair(r, 2, hp)
    cols = pl.ds(pl.multiple_of(hp * LN, LN), LN)
    dm = r.d_mixed[:, cols]
    valid = lax.broadcasted_iota(jnp.int32, (1, LEN), 1) < r.length
    lane = lax.broadcasted_iota(jnp.int32, (LEN, LN), 1)
    zero = jnp.zeros_like(q)
    dq = dk = dv = None
    for h in range(2):
        here = half_lanes(h)
        qh, kh, dmh = jnp.where(here, q, zero), jnp.where(here, k, zero), jnp.where(here, dm, zero)
        lse = jnp.sum(jnp.where(lane == 2 * hp + h, r.lse[...], 0.0), axis=1, keepdims=True)
        s = jnp.where(valid, mm_nt(qh, k) * 0.125, -1e9)
        p = jnp.exp(s - lse)
        dp = mm_nt(dmh, v)
        ds = (p * (dp - jnp.sum(dp * p, axis=1, keepdims=True))).astype(BF)
        a, b, c = mm(ds, kh), mm_tn(ds, qh), mm_tn(p.astype(BF), dmh)
        dq, dk, dv = (a, b, c) if dq is None else (dq + a, dk + b, dv + c)
    dq, dk, dv = (dq * 0.125).astype(BF), (dk * 0.125).astype(BF), dv.astype(BF)
    for part, g in ((0, dq), (1, dk), (2, dv)):
        r.dqkv[:, pl.ds(pl.multiple_of(part * D + hp * LN, LN), LN)] = g
    k = VI["q_bias"]
    r.VG[k : k + 1, cols] = sum_rows(dq.astype(F32))
    k = VI["v_bias"]
    r.VG[k : k + 1, cols] = sum_rows(dv.astype(F32))


def backward_tokens(r, b):
    o = rows_of(b, 128)
    v = r.res[o, :]
    for part in range(3):
        v = v + mm_nt(r.dqkv[o, part * D : (part + 1) * D], r.wqkv[:, part * D : (part + 1) * D])
    r.res[o, :] = v


EDGES = ((13824, 16), (18432, 32), (36880, 48), (55344, 64))


def edge_at(row):
    at = 0
    for base, rows in EDGES:
        if base <= row < base + rows:
            return at + row - base
        at += rows
    return None


def weight_grad(r, lhs, rhs, base, rows, w, RB=256, CB=6, hook=None):
    lead = base % 16
    step_rows = RB * w
    F = r.F
    if lead:
        F[0:16] = jnp.zeros((16, LN), F32)

    def body(s, _):
        o = pl.ds(pl.multiple_of(s * RB, RB), RB)
        for ch in range(w // CB):
            g = mm_tn(lhs[:, o], rhs[:, ch * CB * LN : (ch + 1) * CB * LN])
            for j in range(CB):
                F[pl.ds(lead + ch * CB + j, RB, stride=w), :] = g[:, j * LN : (j + 1) * LN]
        if lead:
            @pl.when(s == 0)
            def _():
                e = edge_at(base)
                r.E[e : e + 16 - lead] = F[lead:16]

        U = 256
        to = base - lead + s * step_rows

        def emit(t, _):
            r.FG[pl.ds(pl.multiple_of(to + t * U, 16), U)] = F[pl.ds(pl.multiple_of(t * U, 16), U)].astype(BF)
            return 0

        lax.fori_loop(0, step_rows // U, emit, 0)
        if lead:
            F[0:16] = F[step_rows : step_rows + 16]
        if hook is not None:
            hook(s)
        return 0

    lax.fori_loop(0, rows // RB, body, 0)
    if lead:
        e = edge_at(base + rows * w - lead)
        r.E[e : e + lead] = F[0:lead]


def edge_grads(r, which):
    base, rows = EDGES[which]
    at = 0
    for vbase, cnt in VECS:
        for k in range(cnt):
            row = vbase + k
            if base <= row < base + rows:
                name, j = vec_at(at + k)
                e = edge_at(row)
                r.E[e : e + 1] = r.VG[name : name + 1, j * LN : (j + 1) * LN]
        at += cnt
    if which == len(EDGES) - 1:
        e = edge_at(TOT)
        r.E[e : e + base + rows - TOT] = jnp.zeros((base + rows - TOT, LN), F32)
    e = edge_at(base)
    r.FG[base : base + rows] = r.E[e : e + rows].astype(BF)


def vec_at(row):
    for k, (_, n) in enumerate(VNAMES):
        if row < n // LN:
            return k, row
        row -= n // LN


class Refs:
    def __init__(self, **refs):
        self.__dict__.update(refs)


def relayout_vectors(p, r):
    at = 0
    for base, cnt in VECS:
        g_lo = base // 16
        g_hi = -(-(base + cnt) // 16)
        load_flat(p, r.slots, r.F, g_lo, g_hi)
        for k in range(cnt):
            name, j = vec_at(at + k)
            f = base - 16 * g_lo + k
            r.V[name : name + 1, j * LN : (j + 1) * LN] = r.F[f : f + 1]
        at += cnt


def relayout_matrix(p, r, name, W, RB):
    base, rows, w = {n: (b, k, c) for n, b, k, c in MATS}[name]
    for s in range(rows // RB):
        lo = base + s * RB * w
        g_lo = lo // 16
        load_flat(p, r.slots, r.F, g_lo, -(-(lo + RB * w) // 16))
        tile_rows(r.F, W, lo - 16 * g_lo, s * RB, RB, w)


def tile_rows(F, W, off, row, rows, w, RB=64):
    def body(t, _):
        q = pl.multiple_of(t * RB, RB)
        for j in range(w):
            W[pl.ds(row + q, RB), j * LN : (j + 1) * LN] = F[pl.ds(off + q * w + j, RB, stride=w), :].astype(BF)
        return 0

    lax.fori_loop(0, rows // RB, body, 0)


def forward_kernel(p, slots, length, tok, hcot, ncot, hidden, nested, wqkv, wo, w1, w2, V, VG, qkv, lse, mixed, xh1, rstd1, first_low, act, gd, res, d_outer, F, qb, xh2, rstd2):
    r = Refs(slots=slots, length=length[0], tok=tok, hcot=hcot, ncot=ncot, hidden=hidden, nested=nested, wqkv=wqkv, wo=wo, w1=w1, w2=w2, V=V, VG=VG, qkv=qkv, lse=lse, mixed=mixed, xh1=xh1, rstd1=rstd1, first_low=first_low, act=act, gd=gd, res=res, d_outer=d_outer, F=F, qb=qb, xh2=xh2, rstd2=rstd2)
    relayout_vectors(p, r)
    relayout_matrix(p, r, "wqkv", wqkv, 256)
    forward_qkv(r)
    lse[...] = jnp.zeros_like(lse)
    lax.fori_loop(0, H // 2, lambda hp, c: (forward_heads(r, hp), c)[1], 0)
    relayout_matrix(p, r, "wo", wo, 768)
    forward_first(r)
    relayout_matrix(p, r, "w1", w1, 256)
    lax.fori_loop(0, FF // UP, lambda j, c: (forward_up(r, j), c)[1], 0)
    relayout_matrix(p, r, "w2", w2, 768)
    tot = forward_second(r)
    d_pool = head(r, tot)
    backward_second(r, d_pool)


def forward_local(p, slots, length, tok, hcot, ncot):
    S = jax.ShapeDtypeStruct
    outs = [S((LEN, D), BF), S((1, 1728), F32), S((D, 3 * D), BF), S((D, D), BF), S((D, FF), BF), S((FF, D), BF), S((16, FF), F32), S((16, FF), F32), S((LEN, 3 * D), BF), S((LEN, LN), F32), S((LEN, D), BF), S((LEN, D), F32), S((LEN, 1), F32), S((LEN, D), BF), S((LEN, FF), BF), S((LEN, FF), BF), S((LEN, D), F32), S((LEN, D), BF)]
    vm = pl.BlockSpec(memory_space=pltpu.VMEM)
    sm = pl.BlockSpec(memory_space=pltpu.SMEM)
    return pl.pallas_call(
        functools.partial(forward_kernel, p),
        out_shape=outs,
        in_specs=[vm, sm, vm, vm, vm],
        scratch_shapes=[pltpu.VMEM((6144 + 32, LN), F32), pltpu.VMEM((1, 3 * D), F32), pltpu.VMEM((LEN, D), F32), pltpu.VMEM((LEN, 1), F32)],
        compiler_params=pltpu.CompilerParams(vmem_limit_bytes=60 << 20),
    )(slots, length, tok, hcot, ncot)


def backward_kernel(p, length, tok, V, VG0, qkv, lse, mixed, xh1, rstd1, first_low, act, gd, res, d_outer, wqkv, wo, w1, w2, igrad, FG, VG, d_branch, d_mixed, dqkv, F, E):
    r = Refs(length=length[0], tok=tok, V=V, VG=VG, qkv=qkv, lse=lse, mixed=mixed, xh1=xh1, rstd1=rstd1, first_low=first_low, act=act, gd=gd, res=igrad, d_outer=d_outer, wqkv=wqkv, wo=wo, w1=w1, w2=w2, FG=FG, d_branch=d_branch, d_mixed=d_mixed, dqkv=dqkv, F=F, E=E)
    VG[...] = VG0[...]
    igrad[...] = res[...]
    mats = {n: (b, k, c) for n, b, k, c in MATS}
    weight_grad(r, act, d_outer, *mats["w2"], RB=1024, CB=2)
    edge_grads(r, 3)
    lax.fori_loop(0, FF // UP, lambda j, c: (backward_act(r, j), c)[1], 0)
    weight_grad(r, first_low, gd, *mats["w1"])
    edge_grads(r, 2)
    backward_first(r)
    weight_grad(r, mixed, d_branch, *mats["wo"])
    edge_grads(r, 1)
    backward_mixed(r)
    lax.fori_loop(0, H // 2, lambda hp, c: (backward_heads(r, hp), c)[1], 0)
    weight_grad(r, tok, dqkv, *mats["wqkv"])
    edge_grads(r, 0)
    lax.fori_loop(0, LEN // 128, lambda b, c: (backward_tokens(r, b), c)[1], 0)


def backward_local(p, length, tok, V, VG, qkv, lse, mixed, xh1, rstd1, first_low, act, gd, res, d_outer, wqkv, wo, w1, w2):
    S = jax.ShapeDtypeStruct
    vm = pl.BlockSpec(memory_space=pltpu.VMEM)
    sm = pl.BlockSpec(memory_space=pltpu.SMEM)
    return pl.pallas_call(
        functools.partial(backward_kernel, p),
        out_shape=[S((LEN, D), F32), S((flat_rows(p), LN), BF)],
        in_specs=[sm] + [vm] * 17,
        scratch_shapes=[pltpu.VMEM((16, FF), F32), pltpu.VMEM((LEN, D), BF), pltpu.VMEM((LEN, D), BF), pltpu.VMEM((LEN, 3 * D), BF), pltpu.VMEM((6144 + 32, LN), F32), pltpu.VMEM((160, LN), F32)],
        compiler_params=pltpu.CompilerParams(vmem_limit_bytes=60 << 20),
    )(length, tok, V, VG, qkv, lse, mixed, xh1, rstd1, first_low, act, gd, res, d_outer, wqkv, wo, w1, w2)


class Gather:
    def __init__(self, p, G, ssem, rsem, gosem):
        self.p, self.G, self.ssem, self.rsem, self.gosem = p, G, ssem, rsem, gosem
        self.x, self.y, self.z, self.c = coords()
        x, y, z, c = self.x, self.y, self.z, self.c
        self.me = lin(x, y, z, c)
        half = p.slot // 32 * 16
        self.H = ((0, half), (half, p.slot - half), (0, p.slot))
        self.px, self.py, self.pc = dev(1 - x, y, z, c), dev(x, 1 - y, z, c), dev(x, y, z, 1 - c)

    def enter(self):
        x, y, z, c = self.x, self.y, self.z, self.c
        bar = pltpu.get_barrier_semaphore()

        def greet(to):
            pl.semaphore_signal(bar, inc=1, device_id=to, device_id_type=MESH)

        for to in (self.px, self.py, self.pc):
            greet(to)
        pl.when(z > 0)(lambda: greet(dev(x, y, z - 1, c)))
        pl.when(z < 3)(lambda: greet(dev(x, y, z + 1, c)))
        middle = (z > 0) & (z < 3)
        pl.when(middle)(lambda: pl.semaphore_wait(bar, 5))
        pl.when(jnp.logical_not(middle))(lambda: pl.semaphore_wait(bar, 4))

    def send(self, sl, h, to, t):
        r0, rn = self.H[h]
        ref = self.G.at[sl, pl.ds(r0, rn)]
        pltpu.make_async_remote_copy(src_ref=ref, dst_ref=ref, send_sem=self.ssem.at[sl, t], recv_sem=self.rsem.at[sl, h], device_id=to, device_id_type=MESH).start()

    def wait(self, sl, h, sem=None):
        r0, rn = self.H[h]
        ref = self.G.at[sl, pl.ds(r0, rn)]
        pltpu.make_async_copy(ref, ref, self.rsem.at[sl, h] if sem is None else sem).wait()

    def up(self, sl, h):
        pl.when(self.z < 3)(lambda: self.send(sl, h, dev(self.x, self.y, self.z + 1, self.c), 3))

    def down(self, sl, h):
        pl.when(self.z > 0)(lambda: self.send(sl, h, dev(self.x, self.y, self.z - 1, self.c), 4))

    def core(self, sl, h):
        self.send(sl, h, self.pc, 2)

    def xy(self, sl):
        self.send(sl, 0, self.px, 0)
        self.send(sl, 1, self.py, 1)
        self.send(sl, 1, self.px, 0)
        self.send(sl, 0, self.py, 1)

    def own(self, xy):
        for h in (0, 1):
            self.up(self.me, h)
            self.down(self.me, h)
        if xy:
            self.xy(self.me)
        for h in (0, 1):
            self.core(self.me, h)

    def own_line(self, k):
        self.at(k, lambda zq: self.xy(lin(self.x, self.y, zq, self.c)))

    def go(self, k):
        pl.semaphore_signal(self.gosem.at[k], inc=1, device_id=self.pc, device_id_type=MESH)

    def wait_go(self, k):
        pl.semaphore_wait(self.gosem.at[k], 1)

    def at(self, k, fn):
        if k == 0:
            fn(self.z)
            return
        pl.when(self.z - k >= 0)(lambda: fn(self.z - k))
        pl.when(self.z + k <= 3)(lambda: fn(self.z + k))

    def along_z(self, k, xy):
        x, y, z, c = self.x, self.y, self.z, self.c

        def from_level(zq, on):
            sl = lin(x, y, zq, c)
            self.wait(sl, 0)
            on(sl, 0)
            if xy:
                self.send(sl, 0, self.px, 0)
            self.core(sl, 0)
            self.wait(sl, 1)
            on(sl, 1)
            if xy:
                self.send(sl, 1, self.py, 1)
                self.send(sl, 1, self.px, 0)
                self.send(sl, 0, self.py, 1)
            self.core(sl, 1)

        pl.when(z - k >= 0)(lambda: from_level(z - k, self.up))
        pl.when(z + k <= 3)(lambda: from_level(z + k, self.down))

    def sides(self, k):
        x, y, c = self.x, self.y, self.c

        def fn(zq):
            sl = lin(1 - x, y, zq, c)
            self.wait(sl, 0)
            self.send(sl, 0, self.py, 1)
            self.core(sl, 0)
            sl = lin(x, 1 - y, zq, c)
            self.wait(sl, 1)
            self.send(sl, 1, self.px, 0)
            self.core(sl, 1)

        self.at(k, fn)

    def sides_rest(self, k):
        x, y, c = self.x, self.y, self.c

        def fn(zq):
            sl = lin(1 - x, y, zq, c)
            self.wait(sl, 1)
            self.core(sl, 1)
            sl = lin(x, 1 - y, zq, c)
            self.wait(sl, 0)
            self.core(sl, 0)

        self.at(k, fn)

    def diagonal(self, k):
        def fn(zq):
            sl = lin(1 - self.x, 1 - self.y, zq, self.c)
            for h in (0, 1):
                self.wait(sl, h)
                self.core(sl, h)

        self.at(k, fn)

    def from_sibling(self, xp):
        def body(fs, carry):
            for h in (0, 1):
                self.wait((2 * xp + 1 - self.c) * 8 + fs, h)
            return carry

        lax.fori_loop(0, 8, body, 0)

    def leave(self):
        x, y, z, c = self.x, self.y, self.z, self.c
        W = self.wait

        def body(zq, carry):
            sl = lin(x, y, zq, c)
            for t in (0, 1, 2):
                W(sl, 2, self.ssem.at[sl, t])
            pl.when((zq <= z) & (z < 3))(lambda: W(sl, 2, self.ssem.at[sl, 3]))
            pl.when((zq >= z) & (z > 0))(lambda: W(sl, 2, self.ssem.at[sl, 4]))
            sx = lin(1 - x, y, zq, c)
            W(sx, 0, self.ssem.at[sx, 1])
            W(sx, 2, self.ssem.at[sx, 2])
            sy = lin(x, 1 - y, zq, c)
            W(sy, 1, self.ssem.at[sy, 0])
            W(sy, 2, self.ssem.at[sy, 2])
            sd = lin(1 - x, 1 - y, zq, c)
            W(sd, 2, self.ssem.at[sd, 2])
            return carry

        lax.fori_loop(0, 4, body, 0)


FORWARD_OUT = ("hidden", "nested", "wqkv", "wo", "w1", "w2", "V", "VG", "qkv", "lse", "mixed", "xh1", "rstd1", "first_low", "act", "gd", "res", "d_outer")
FORWARD_SHAPES = dict(
    hidden=((LEN, D), jnp.bfloat16),
    nested=((1, 1728), jnp.float32),
    wqkv=((D, 3 * D), jnp.bfloat16),
    wo=((D, D), jnp.bfloat16),
    w1=((D, FF), jnp.bfloat16),
    w2=((FF, D), jnp.bfloat16),
    V=((16, FF), jnp.float32),
    VG=((16, FF), jnp.float32),
    qkv=((LEN, 3 * D), jnp.bfloat16),
    lse=((LEN, LN), jnp.float32),
    mixed=((LEN, D), jnp.bfloat16),
    xh1=((LEN, D), jnp.float32),
    rstd1=((LEN, 1), jnp.float32),
    first_low=((LEN, D), jnp.bfloat16),
    act=((LEN, FF), jnp.bfloat16),
    gd=((LEN, FF), jnp.bfloat16),
    res=((LEN, D), jnp.float32),
    d_outer=((LEN, D), jnp.bfloat16),
)


def own_slot(p, me, x_ref, F, G):
    start = me * p.sh
    r_first = start // LN
    s = start - r_first * LN
    r0 = r_first % 16
    lead = 32
    F[0 : lead + p.slot + 32] = jnp.zeros((lead + p.slot + 32, LN), F32)
    F[lead : lead + p.rows_in] = pltpu.roll(x_ref[...].astype(F32), s, 1)
    lane = lax.broadcasted_iota(jnp.int32, (p.slot, LN), 1)
    G[me] = jnp.where(lane >= s, F[pl.ds(lead - r0, p.slot), :], F[pl.ds(lead - 1 - r0, p.slot), :]).astype(BF)


def relayout_vector(p, r, which):
    at = sum(cnt for _, cnt in VECS[:which])
    base, cnt = VECS[which]
    g_lo = base // 16
    load_flat(p, r.slots, r.F, g_lo, -(-(base + cnt) // 16), base + cnt)
    for k in range(cnt):
        name, j = vec_at(at + k)
        f = base - 16 * g_lo + k
        r.V[name : name + 1, j * LN : (j + 1) * LN] = r.F[f : f + 1]


def relayout_rows(p, r, name, W, row, rows):
    base, _, w = {n: (b, k, c) for n, b, k, c in MATS}[name]
    lo = base + row * w
    g_lo = lo // 16
    load_flat(p, r.slots, r.F, g_lo, -(-(lo + rows * w) // 16), lo + rows * w)
    tile_rows(r.F, W, lo - 16 * g_lo, row, rows, w)


def gather_forward_kernel(p, x_ref, length, tok, hcot, ncot, *refs):
    n = len(FORWARD_OUT)
    outs = dict(zip(FORWARD_OUT, refs[:n]))
    loc = dict(zip(FORWARD_OUT, refs[n : 2 * n]))
    G, F, qb, xh2, rstd2, ssem, rsem, gosem, osem = refs[2 * n :]
    r = Refs(slots=G, length=length[0], tok=tok, hcot=hcot, ncot=ncot, F=F, qb=qb, xh2=xh2, rstd2=rstd2, **loc)
    g = Gather(p, G, ssem, rsem, gosem)
    own_slot(p, g.me, x_ref, F, G)
    g.enter()
    c0, c1 = g.c == 0, g.c == 1

    started = []

    def out(*names):
        for m in names:
            k = FORWARD_OUT.index(m)
            cp = pltpu.make_async_copy(loc[m], outs[m], osem.at[k])
            cp.start()
            started.append(cp)

    def part_rq_0():
        g.own(True)
        g.sides(0)
        g.go(0)
        g.along_z(1, True)
        g.sides(1)
        g.go(1)
        g.along_z(2, True)
        g.diagonal(0)
        g.sides_rest(0)
        g.sides(2)
        g.along_z(3, True)
        g.sides(3)
        g.diagonal(3)
        g.diagonal(2)
        g.sides_rest(3)
        g.diagonal(1)
        g.sides_rest(1)
        g.sides_rest(2)

    pl.when(c0)(part_rq_0)
    def part_rq_1():
        g.wait_go(0)
        g.own(False)
        g.wait_go(1)
        g.own_line(0)
        g.along_z(1, False)
        g.along_z(2, False)
        g.sides(0)
        g.along_z(3, False)
        g.own_line(3)
        g.own_line(1)
        g.own_line(2)
        g.sides(3)
        g.sides_rest(3)
        g.from_sibling(0)

    pl.when(c1)(part_rq_1)
    relayout_vector(p, r, 0)
    for k in range(3):
        relayout_rows(p, r, "wqkv", r.wqkv, 256 * k, 256)
    out("wqkv")
    def part_qkv_1():
        g.sides(1)
        g.diagonal(0)
        g.sides(2)
        g.from_sibling(1)
        g.sides_rest(0)

    pl.when(c1)(part_qkv_1)
    forward_qkv(r)
    out("qkv")
    r.lse[...] = jnp.zeros_like(r.lse)

    def heads(hp, carry):
        def part_hd1_1():
            g.sides_rest(1)
            g.sides_rest(2)
            g.diagonal(3)

        pl.when((hp == 1) & c1)(part_hd1_1)
        def part_hd3_1():
            g.diagonal(1)

        pl.when((hp == 3) & c1)(part_hd3_1)
        def part_hd5_1():
            g.diagonal(2)

        pl.when((hp == 5) & c1)(part_hd5_1)
        forward_heads(r, hp)
        return carry

    lax.fori_loop(0, H // 2, heads, 0)
    out("lse", "mixed")
    relayout_rows(p, r, "w1", r.w1, 448, 128)
    relayout_rows(p, r, "w1", r.w1, 576, 192)
    relayout_rows(p, r, "w2", r.w2, 0, 768)
    relayout_vector(p, r, 2)
    def part_rwo_0():
        g.from_sibling(0)

    pl.when(c0)(part_rwo_0)
    relayout_rows(p, r, "wo", r.wo, 0, 768)
    relayout_vector(p, r, 1)
    out("wo")
    forward_first(r)
    out("xh1", "rstd1", "first_low")
    relayout_rows(p, r, "w1", r.w1, 0, 256)
    relayout_rows(p, r, "w1", r.w1, 256, 192)
    out("w1")
    def part_up_0():
        g.from_sibling(1)

    pl.when(c0)(part_up_0)
    lax.fori_loop(0, FF // UP, lambda j, c: (forward_up(r, j), c)[1], 0)
    out("act", "gd")
    for k in range(1, 4):
        relayout_rows(p, r, "w2", r.w2, 768 * k, 768)
    relayout_vector(p, r, 3)
    out("w2", "V")
    tot = forward_second(r)
    out("hidden")
    d_pool = head(r, tot)
    out("nested")
    backward_second(r, d_pool)
    out("VG", "res", "d_outer")
    g.leave()
    for cp in started:
        cp.wait()


def gather_forward(p, shard, length, tok, hcot, ncot):
    x = jnp.pad(shard, (0, p.rows_in * LN - p.sh)).reshape(p.rows_in, LN)
    S = jax.ShapeDtypeStruct
    vm = pl.BlockSpec(memory_space=pltpu.VMEM)
    sm = pl.BlockSpec(memory_space=pltpu.SMEM)
    hbm = pl.BlockSpec(memory_space=pl.ANY)
    VM = pltpu.VMEM
    DM = pltpu.SemaphoreType.DMA
    shapes = [FORWARD_SHAPES[m] for m in FORWARD_OUT]
    res = pl.pallas_call(
        functools.partial(gather_forward_kernel, p),
        out_shape=[S(*s) for s in shapes],
        in_specs=[vm, sm, vm, vm, vm],
        out_specs=[hbm] * len(shapes),
        scratch_shapes=[VM(*s) for s in shapes]
        + [VM((p.n, p.slot, LN), BF), VM((6144 + 32, LN), F32), VM((1, 3 * D), F32), VM((LEN, D), F32), VM((LEN, 1), F32)]
        + [DM((p.n, 5)), DM((p.n, 2)), pltpu.SemaphoreType.REGULAR((2,)), DM((len(shapes),))],
        compiler_params=pltpu.CompilerParams(collective_id=0, has_side_effects=True, vmem_limit_bytes=64 << 20),
    )(x, length, tok, hcot, ncot)
    return dict(zip(FORWARD_OUT, res))


SCHEDULE = (
    (4, 1, 0, "diag", 1, 1, 2),
    (7, 1, 0, "diag", 1, 3, 1),
    (8, 1, 0, "xline", 1, 1, 1),
    (9, 0, 0, "diag", 1, 0, 1),
    (10, 0, 0, "diag", 1, 3, 1),
    (10, 1, 0, "diag", 1, 0, 1),
    (11, 0, 0, "diag", 1, 2, 1),
    (11, 0, 1, "yline", 1, 0, 1),
    (11, 1, 1, "yline", 1, 1, 1),
    (11, 0, 0, "diag", 1, 1, 1),
    (13, 1, 1, "diag", 0, 1, 1),
    (14, 1, 1, "diag", 0, 2, 1),
    (14, 1, 0, "yline", 0, 1, 1),
    (14, 0, 0, "xline", 1, 0, 1),
    (14, 1, 1, "diag", 0, 0, 1),
    (15, 0, 1, "yline", 1, 1, 1),
    (15, 1, 1, "own", 1, 1, 1),
    (16, 1, 1, "xline", 0, 1, 1),
    (16, 1, 0, "yline", 0, 2, 1),
    (16, 0, 0, "xline", 1, 1, 1),
    (17, 0, 0, "xline", 1, 3, 1),
    (17, 1, 1, "xline", 0, 2, 1),
    (17, 1, 1, "diag", 0, 3, 1),
    (18, 1, 0, "own", 0, 1, 1),
    (18, 1, 1, "yline", 1, 2, 1),
    (19, 1, 0, "yline", 0, 0, 1),
    (19, 1, 1, "xline", 0, 0, 1),
    (19, 0, 0, "xline", 1, 2, 1),
    (20, 0, 0, "yline", 0, 1, 2),
    (20, 0, 1, "diag", 0, 0, 2),
    (20, 1, 1, "own", 1, 2, 1),
    (20, 1, 0, "own", 0, 2, 1),
    (20, 0, 1, "yline", 1, 2, 1),
    (21, 0, 1, "diag", 0, 2, 1),
    (21, 1, 1, "yline", 1, 0, 1),
    (21, 0, 0, "own", 0, 1, 1),
    (21, 0, 1, "own", 1, 1, 1),
    (21, 0, 0, "yline", 0, 0, 1),
    (21, 0, 0, "own", 0, 2, 1),
    (21, 0, 1, "xline", 0, 1, 1),
    (21, 0, 1, "own", 1, 0, 1),
    (22, 0, 1, "yline", 1, 3, 1),
    (22, 1, 1, "own", 1, 0, 1),
    (22, 1, 0, "yline", 0, 3, 1),
    (22, 1, 0, "xline", 1, 0, 1),
    (22, 0, 1, "xline", 0, 0, 1),
    (22, 0, 1, "own", 1, 2, 1),
    (22, 0, 1, "xline", 0, 2, 1),
    (22, 0, 0, "own", 0, 0, 1),
    (22, 0, 1, "diag", 0, 3, 1),
    (22, 0, 0, "yline", 0, 3, 1),
    (22, 0, 1, "xline", 0, 3, 1),
    (22, 1, 0, "own", 0, 0, 1),
    (22, 1, 0, "xline", 1, 2, 2),
    (22, 1, 1, "xline", 0, 3, 1),
    (22, 1, 1, "yline", 1, 3, 1),
)


class Scatter:
    def __init__(self, p, FG, R, D0, D1, X, Y, Z, A, sems):
        self.p, self.FG, self.R, self.D0, self.D1, self.X, self.Y, self.Z, self.A = p, FG, R, D0, D1, X, Y, Z, A
        self.sib_s, self.sib_r, self.d_s, self.d_r, self.x_s, self.x_r, self.y_s, self.y_r, self.z_s, self.z_r = sems
        self.x, self.y, self.z, self.c = coords()
        x, y, z, c = self.x, self.y, self.z, self.c
        self.SL = p.slot
        self.half = p.slot // 32 * 16
        self.px, self.py, self.pc = dev(1 - x, y, z, c), dev(x, 1 - y, z, c), dev(x, y, z, 1 - c)

    def zq(self, b):
        d = lax.rem(b + 1, 4)
        z = self.z
        return lax.rem(z % 2 + d % 2, 2) + 2 * lax.rem(z // 2 + d // 2, 2)

    def enter(self):
        x, y, c = self.x, self.y, self.c
        barrier([self.px, self.py, self.pc] + [dev(x, y, self.zq(b), c) for b in range(3)])

    def row0(self, slot):
        return pl.multiple_of((slot * self.p.sh) // LN // 16 * 16, 16)

    def fg(self, slot):
        return self.row0(slot)

    def copy(self, src, dst, ssem, rsem, to):
        return pltpu.make_async_remote_copy(src_ref=src, dst_ref=dst, send_sem=ssem, recv_sem=rsem, device_id=to, device_id_type=MESH)

    def wait(self, ref, sem):
        pltpu.make_async_copy(ref, ref, sem).wait()

    def to_sibling(self, xp):
        def body(k, _):
            dp = 2 * xp + 1 - self.c
            i = 8 * xp + k
            self.copy(self.FG.at[pl.ds(self.row0(dp * 8 + k), self.SL)], self.R.at[i], self.sib_s.at[i], self.sib_r.at[i], self.pc).start()
            return 0

        lax.fori_loop(0, 8, body, 0)

    def add(self, dst, d0, rows, srcs, U=176):
        def body(t, _):
            r = pl.multiple_of(t * U, 16)
            v = None
            for s, s0 in srcs:
                e = s[pl.ds(s0 + r, U)].astype(F32)
                v = e if v is None else v + e
            dst[pl.ds(d0 + r, U)] = v.astype(dst.dtype)
            return 0

        lax.fori_loop(0, rows // U, body, 0)

    def have(self, xp, yq, zq):
        fs = zq * 2 + yq
        i = 8 * xp + fs
        self.wait(self.R.at[i], self.sib_r.at[i])
        return i, self.row0((2 * xp + self.c) * 8 + fs)

    def diag(self, xp, b):
        i, g = self.have(xp, 1 - self.y, self.zq(b))
        half, rest = self.half, self.SL - self.half
        R = self.R.at[i]
        self.add(R, 0, self.SL, [(self.FG, g), (R, 0)])
        self.copy(R.at[pl.ds(0, half)], self.D0.at[b], self.d_s.at[0, b], self.d_r.at[0, b], self.py).start()
        self.copy(R.at[pl.ds(half, rest)], self.D1.at[b], self.d_s.at[1, b], self.d_r.at[1, b], self.px).start()

    def xline(self, xp, b):
        i, g = self.have(xp, self.y, self.zq(b))
        half, rest = self.half, self.SL - self.half
        R = self.R.at[i]
        self.wait(self.D0.at[b], self.d_r.at[0, b])
        self.add(R, half, rest, [(self.FG, g + half), (R, half)])
        self.add(R, 0, half, [(self.FG, g), (R, 0), (self.D0.at[b], 0)])
        self.copy(R, self.X.at[b], self.x_s.at[b], self.x_r.at[b], self.px).start()

    def yline(self, xp, b):
        i, g = self.have(xp, 1 - self.y, self.zq(b))
        half, rest = self.half, self.SL - self.half
        R = self.R.at[i]
        self.wait(self.D1.at[b], self.d_r.at[1, b])
        self.add(R, 0, half, [(self.FG, g), (R, 0)])
        self.add(R, half, rest, [(self.FG, g + half), (R, half), (self.D1.at[b], 0)])
        self.copy(R, self.Y.at[b], self.y_s.at[b], self.y_r.at[b], self.py).start()

    def own(self, xp, b):
        i, g = self.have(xp, self.y, self.zq(b))
        R = self.R.at[i]
        self.wait(self.X.at[b], self.x_r.at[b])
        self.wait(self.Y.at[b], self.y_r.at[b])
        self.add(R, 0, self.SL, [(self.FG, g), (R, 0), (self.X.at[b], 0), (self.Y.at[b], 0)])
        self.copy(R, self.Z.at[b], self.z_s.at[b], self.z_r.at[b], dev(self.x, self.y, self.zq(b), self.c)).start()

    def last(self, xp, out):
        p, SL, A = self.p, self.SL, self.A
        i, g = self.have(xp, self.y, self.z)
        self.wait(self.X.at[3], self.x_r.at[3])
        self.wait(self.Y.at[3], self.y_r.at[3])
        for b in range(3):
            self.wait(self.Z.at[b], self.z_r.at[b])
        self.add(A, 0, SL, [(self.FG, g), (self.R.at[i], 0), (self.X.at[3], 0), (self.Y.at[3], 0)] + [(self.Z.at[b], 0) for b in range(3)])
        start = lin(self.x, self.y, self.z, self.c) * p.sh
        r_first = start // LN
        s = start - r_first * LN
        r0 = r_first % 16
        A[0:SL] = pltpu.roll(A[0:SL], lax.rem(LN - s, LN), 1)
        lane = lax.broadcasted_iota(jnp.int32, (p.rows_in, LN), 1)
        out[...] = jnp.where(lane < LN - s, A[pl.ds(r0, p.rows_in), :], A[pl.ds(r0 + 1, p.rows_in), :])

    def after(self, part, index=None):
        for c in (0, 1):
            for x in (0, 1):
                todo = [e for e in SCHEDULE if e[:3] == (part, c, x)]
                if todo:
                    here = (self.c == c) & (self.x == x)
                    if index is not None:
                        here = here & (index[0] == index[1])

                    def run(todo=todo):
                        for _, _, _, step, xp, b0, n in todo:
                            lax.fori_loop(b0, b0 + n, lambda b, k: (getattr(self, step)(xp, b), k)[1], 0)

                    pl.when(here)(run)

    def leave(self):
        for k in range(16):
            self.wait(self.R.at[k], self.sib_s.at[k])
        for b in range(4):
            self.wait(self.D0.at[b], self.d_s.at[0, b])
            self.wait(self.D1.at[b], self.d_s.at[1, b])
            self.wait(self.X.at[b], self.x_s.at[b])
            self.wait(self.Y.at[b], self.y_s.at[b])
        for b in range(3):
            self.wait(self.Z.at[b], self.z_s.at[b])


BACK_IN = ("act", "d_outer", "w2", "gd", "first_low", "w1", "res", "xh1", "rstd1", "V", "VG", "mixed", "wo", "qkv", "lse", "tok")


def backward_scatter_kernel(p, length, *refs):
    n = len(BACK_IN)
    src = dict(zip(BACK_IN, refs[:n]))
    wqkv_in = refs[n]
    igrad, out = refs[n + 1 : n + 3]
    loc = dict(zip(BACK_IN, refs[n + 3 : 2 * n + 3]))
    FG, F, E, R, D0, D1, X, Y, Z, lsem, osem, *sems = refs[2 * n + 3 :]
    r = Refs(length=length[0], FG=FG, F=F, E=E, **loc)
    r.dqkv, r.d_branch, r.d_mixed = r.act, r.first_low, r.d_outer
    sc = Scatter(p, FG, R, D0, D1, X, Y, Z, F, sems)
    mats = {m: (b, k, c) for m, b, k, c in MATS}
    loads = {m: pltpu.make_async_copy(src[m], loc[m], lsem.at[k]) for k, m in enumerate(BACK_IN)}
    for m in BACK_IN:
        loads[m].start()

    def need(*names):
        for m in names:
            loads[m].wait()

    sc.enter()
    c0, c1 = sc.c == 0, sc.c == 1
    x0, x1 = sc.x == 0, sc.x == 1

    def both(cond, fn):
        pl.when(cond)(fn)

    need("act", "d_outer", "VG")
    weight_grad(r, r.act, r.d_outer, *mats["w2"], RB=1024, CB=2)
    edge_grads(r, 3)
    both(c0, lambda: sc.to_sibling(1))
    sc.after(1)
    need("w2", "gd")

    def act_part(j, carry):
        backward_act(r, j)
        for k in range(4):
            sc.after(2 + k, (j, k))
        return carry

    lax.fori_loop(0, FF // UP, act_part, 0)
    q_loads = [pltpu.make_async_copy(wqkv_in.at[:, pl.ds(k * D, D)], r.w2.at[pl.ds(k * D, D)], lsem.at[n + k]) for k in range(3)]
    for q in q_loads:
        q.start()
    need("first_low")
    weight_grad(r, r.first_low, r.gd, *mats["w1"], hook=lambda i: [sc.after(6 + k, (i, k)) for k in range(2)])
    edge_grads(r, 2)
    both(c1, lambda: sc.to_sibling(1))
    sc.after(8)
    need("w1", "res", "xh1", "rstd1", "V")
    backward_first(r)
    sc.after(9)
    need("mixed")
    weight_grad(r, r.mixed, r.d_branch, *mats["wo"])
    edge_grads(r, 1)
    both(c0, lambda: sc.to_sibling(0))
    sc.after(10)
    need("wo")
    backward_mixed(r)
    sc.after(11)
    need("qkv", "lse")

    def heads(hp, carry):
        backward_heads(r, hp)
        for k in range(6):
            sc.after(12 + k, (hp, k))
        return carry

    lax.fori_loop(0, H // 2, heads, 0)
    need("tok")
    weight_grad(r, r.tok, r.dqkv, *mats["wqkv"], hook=lambda i: [sc.after(18 + k, (i, k)) for k in range(2)])
    edge_grads(r, 0)
    both(c1, lambda: sc.to_sibling(0))
    sc.after(20)
    for q in q_loads:
        q.wait()

    def tokens(b, carry):
        o = rows_of(b, LEN)
        v = r.res[o, :]
        for part in range(3):
            v = v + mm_nt(r.dqkv[o, part * D : (part + 1) * D], r.w2[part * D : (part + 1) * D, :])
        r.res[o, :] = v
        sc.after(21, (b, 0))
        return carry

    lax.fori_loop(0, 1, tokens, 0)
    grad_out = pltpu.make_async_copy(r.res, igrad, osem)
    grad_out.start()
    sc.after(22)
    both(x0, lambda: sc.last(0, out))
    both(x1, lambda: sc.last(1, out))
    sc.leave()
    grad_out.wait()


def backward_scatter(p, length, wqkv, **arrays):
    S = jax.ShapeDtypeStruct
    sm = pl.BlockSpec(memory_space=pltpu.SMEM)
    hbm = pl.BlockSpec(memory_space=pl.ANY)
    ins = [arrays[m] for m in BACK_IN]
    SL = p.slot
    half = SL // 32 * 16
    VM = pltpu.VMEM
    DM = pltpu.SemaphoreType.DMA
    igrad, o = pl.pallas_call(
        functools.partial(backward_scatter_kernel, p),
        out_shape=[S((LEN, D), F32), S((p.rows_in, LN), F32)],
        in_specs=[sm] + [hbm] * (len(ins) + 1),
        out_specs=[hbm, pl.BlockSpec(memory_space=pltpu.VMEM)],
        scratch_shapes=[VM(a.shape, a.dtype) for a in ins]
        + [VM((flat_rows(p), LN), BF), VM((6144 + 32, LN), F32), VM((160, LN), F32), VM((16, SL, LN), BF), VM((4, half, LN), BF), VM((4, SL - half, LN), BF), VM((4, SL, LN), BF), VM((4, SL, LN), BF), VM((3, SL, LN), BF)]
        + [DM((len(ins) + 3,)), DM, DM((16,)), DM((16,)), DM((2, 4)), DM((2, 4)), DM((4,)), DM((4,)), DM((4,)), DM((4,)), DM((3,)), DM((3,))],
        compiler_params=pltpu.CompilerParams(collective_id=1, has_side_effects=True, vmem_limit_bytes=64 << 20),
    )(length, *ins, wqkv)
    return igrad, o


def finish_copies(p, shards, hidden, igrad, nested):
    S = jax.ShapeDtypeStruct
    vm = pl.BlockSpec(memory_space=pltpu.VMEM)

    def kernel(a, b, c, d, a_out, b_out, c_out, d_out):
        a_out[...] = a[...].reshape(p.rows_in * LN)[: p.sh]
        b_out[...] = b[...]
        c_out[...] = c[...]
        d_out[...] = d[...]

    arrays = (shards, hidden, igrad, nested)
    return pl.pallas_call(
        kernel,
        out_shape=[S((p.sh,), F32)] + [S(a.shape, a.dtype) for a in arrays[1:]],
        in_specs=[vm] * 4,
        out_specs=[vm] * 4,
    )(*arrays)


def on_device(p, fast, tokens, lengths, weight_shards, hidden_cotangent, nested_cotangent):
    tok = tokens.reshape(LEN, D)
    hcot = hidden_cotangent.reshape(LEN, D)
    if fast:
        f = gather_forward(p, weight_shards, lengths, tok, hcot, nested_cotangent)
        igrad, shards = backward_scatter(p, lengths, tok=tok, **{m: f[m] for m in BACK_IN + ("wqkv",) if m != "tok"})
        shards, f["hidden"], igrad, f["nested"] = finish_copies(p, shards, f["hidden"], igrad, f["nested"])
    else:
        slots = lax.all_gather(build_slot(p, weight_shards, me_of), AX, axis=0)
        f = dict(zip(FORWARD_OUT, forward_local(p, slots, lengths, tok, hcot, nested_cotangent)))
        igrad, flat = backward_local(p, lengths, tok, *[f[m] for m in FORWARD_OUT[6:] + FORWARD_OUT[2:6]])
        shards = scatter_plain(p, flat)
    return (f["hidden"].reshape(1, LEN, D), f["nested"], igrad.reshape(1, LEN, D), shards)


def solution(mesh):
    in_specs = (
        P(("dp", "fsdp"), None, None),
        P(("dp", "fsdp")),
        P(("dp", "fsdp")),
        P(("dp", "fsdp"), None, None),
        P(("dp", "fsdp"), None),
    )
    out_specs = (
        P(("dp", "fsdp"), None, None),
        P(("dp", "fsdp"), None),
        P(("dp", "fsdp"), None, None),
        P(("dp", "fsdp")),
    )
    p = plan(mesh.shape["dp"] * mesh.shape["fsdp"])
    fast = (mesh.shape["dp"], mesh.shape["fsdp"]) == (4, 8)
    return jax.shard_map(
        functools.partial(on_device, p, fast), mesh=mesh, in_specs=in_specs, out_specs=out_specs, check_vma=False
    )
```

```python
import functools
import math

import jax
import jax.numpy as jnp
from jax import lax
from jax.experimental import pallas as pl
from jax.experimental.pallas import tpu as pltpu
from jax.sharding import PartitionSpec as P

AX = ("dp", "fsdp")
MESH = pl.DeviceIdType.MESH
D = 768
H = 12
HD = 64
FF = 3072
LEN = 512
E2 = 512
E3 = 256
E4 = 128
E5 = 64


epsilon = 1e-05


PAR=7088640; LN=128
class Plan: pass
def plan(n):
    p=Plan(); p.n=n; p.sh=PAR//n
    st=[i*p.sh for i in range(n)]
    p.g0=[s//LN//16 for s in st]
    p.g1=[(s+p.sh-1)//LN//16 for s in st]
    p.slot=16*max(b-a+1 for a,b in zip(p.g0,p.g1))
    p.rows_in=-(-p.sh//LN)
    return p
MATS=[("wqkv",0,D,18),("wo",13836,D,6),("w1",18462,D,24),("w2",36918,FF,6)]
VECS=[(13824,12),(18444,18),(36894,24),(55350,30)]

def build_slot_kernel(p,me_of,x_ref,o_ref,q_ref):
    i=me_of(); start=i*p.sh; r_first=start//LN; s=start-r_first*LN; r0=r_first%16
    lead=32
    q_ref[...]=jnp.zeros_like(q_ref)
    q=pltpu.roll(x_ref[...].astype(jnp.float32),s,1)
    q_ref[lead:lead+p.rows_in]=q
    lane=lax.broadcasted_iota(jnp.int32,(p.slot,LN),1)
    a=q_ref[pl.ds(lead-r0,p.slot),:]
    b=q_ref[pl.ds(lead-1-r0,p.slot),:]
    o_ref[...]=jnp.where(lane>=s,a,b).astype(jnp.bfloat16)

def build_slot(p,shard,me_of):
    x=jnp.pad(shard,(0,p.rows_in*LN-p.sh)).reshape(p.rows_in,LN)
    return pl.pallas_call(functools.partial(build_slot_kernel,p,me_of),out_shape=jax.ShapeDtypeStruct((p.slot,LN),jnp.bfloat16),
        scratch_shapes=[pltpu.VMEM((32+p.slot+32,LN),jnp.float32)])(x)

def load_flat(p,slots,F,g_lo,g_hi,need=None):
    for i in range(p.n):
        a=max(g_lo,p.g0[i]); b=min(g_hi,p.g1[i]+1)
        if a>=b: continue
        shared_first = i>0 and p.g0[i]==p.g1[i-1] and a==p.g0[i]
        a2=a+1 if shared_first else a
        b2=b
        apart=need is not None and need<=(i+1)*p.sh//LN
        if i+1<p.n and p.g1[i]==p.g0[i+1] and b==p.g1[i]+1 and not apart: b2=b-1
        if i+1<p.n and b2<b and b-1>=g_lo:
            g=b-1
            F[16*(g-g_lo):16*(g-g_lo)+16]=slots[i,16*(g-p.g0[i]):16*(g-p.g0[i])+16].astype(jnp.float32)+slots[i+1,0:16].astype(jnp.float32)
        cnt=b2-a2
        if cnt<=0: continue
        U=16
        nb,rem=cnt//U,cnt%U
        def body(t,_,i=i,a2=a2):
            src=pl.multiple_of(16*(a2-p.g0[i])+t*16*U,16); dst=pl.multiple_of(16*(a2-g_lo)+t*16*U,16)
            F[pl.ds(dst,16*U)]=slots[i,pl.ds(src,16*U)].astype(jnp.float32)
            return 0
        lax.fori_loop(0,nb,body,0)
        if rem:
            src=16*(a2-p.g0[i])+nb*16*U; dst=16*(a2-g_lo)+nb*16*U
            F[dst:dst+16*rem]=slots[i,src:src+16*rem].astype(jnp.float32)

def coords():
    dp=lax.axis_index("dp"); fs=lax.axis_index("fsdp")
    return dp//2,fs%2,fs//2,dp%2
def dev(x,y,z,c): return (x*2+c, z*2+y)
def lin(x,y,z,c): return (x*2+c)*8+z*2+y
def barrier(partners):
    bar=pltpu.get_barrier_semaphore()
    for q in partners: pl.semaphore_signal(bar,inc=1,device_id=q,device_id_type=MESH)
    pl.semaphore_wait(bar,len(partners))

TOT=PAR//LN
def flat_rows(p): return max(16*p.g0[-1]+p.slot, EDGES[-1][0]+EDGES[-1][1])
def owner_row(rho):
    for k,(name,base,rows,w) in enumerate(MATS):
        if base<=rho<base+rows*w: return ("m",k,(rho-base)//w,(rho-base)%w)
    at=0
    for base,cnt in VECS:
        if base<=rho<base+cnt: return ("v",at+rho-base)
        at+=cnt
    return None

def me_of():
    return lax.axis_index(AX)


def finish_kernel(p, a_ref, out, A):
    SL = p.slot
    start = me_of() * p.sh
    r_first = start // LN
    s = start - r_first * LN
    r0 = r_first % 16
    A[0:SL] = pltpu.roll(a_ref[...], lax.rem(LN - s, LN), 1)
    lane = lax.broadcasted_iota(jnp.int32, (p.rows_in, LN), 1)
    out[...] = jnp.where(lane < LN - s, A[pl.ds(r0, p.rows_in), :], A[pl.ds(r0 + 1, p.rows_in), :])


def scatter_plain(p, flat):
    parts = jnp.concatenate([flat[16 * g : 16 * g + p.slot] for g in p.g0]).astype(jnp.float32)
    mine = lax.psum_scatter(parts, AX, scatter_dimension=0, tiled=True)
    o = pl.pallas_call(
        functools.partial(finish_kernel, p),
        out_shape=jax.ShapeDtypeStruct((p.rows_in, LN), jnp.float32),
        scratch_shapes=[pltpu.VMEM((p.slot + 32, LN), jnp.float32)],
    )(mine)
    return o.reshape(-1)[: p.sh]

EPS = 1e-05
F32 = jnp.float32
BF = jnp.bfloat16
SQ = math.sqrt(0.5)
PHI = 1.0 / math.sqrt(2.0 * math.pi)
VNAMES = (
    ("q_bias", D),
    ("v_bias", D),
    ("out_bias", D),
    ("first_gain", D),
    ("first_shift", D),
    ("up_bias", FF),
    ("down_bias", D),
    ("second_gain", D),
    ("second_shift", D),
    ("exit_gain", D),
    ("exit_shift", D),
)
VI = {name: k for k, (name, _) in enumerate(VNAMES)}
PREFIXES = (D, E2, E3, E4, E5)
SCALE = 1.0 / math.sqrt(HD)
UP = 768


def mm(a, b):
    return jnp.dot(a, b, preferred_element_type=F32)


def mm_nt(a, b):
    return lax.dot_general(a, b, (((1,), (1,)), ((), ())), preferred_element_type=F32)


def mm_tn(a, b):
    return lax.dot_general(a, b, (((0,), (0,)), ((), ())), preferred_element_type=F32)


def vrow(V, name):
    k = VI[name]
    return V[k : k + 1, : VNAMES[k][1]]


def mean_last(a):
    return jnp.mean(a, axis=-1, keepdims=True)


def sum_rows(a):
    return jnp.sum(a, axis=0, keepdims=True)


def forward_qkv(r):
    bias = jnp.concatenate([vrow(r.V, "q_bias"), jnp.zeros((1, D), F32), vrow(r.V, "v_bias")], axis=1)
    r.qb[...] = bias

    def body(j, _):
        o = pl.ds(pl.multiple_of(j * D, D), D)
        r.qkv[:, o] = (mm(r.tok[...], r.wqkv[:, o]) + r.qb[:, o]).astype(BF)
        return 0

    lax.fori_loop(0, 3, body, 0)


def half_lanes(h):
    lane = lax.broadcasted_iota(jnp.int32, (LEN, LN), 1)
    return lane < HD if h == 0 else lane >= HD


def pair(r, part, hp):
    return r.qkv[:, pl.ds(pl.multiple_of(part * D + hp * LN, LN), LN)]


def forward_heads(r, hp):
    q, k, v = pair(r, 0, hp) * SCALE, pair(r, 1, hp), pair(r, 2, hp)
    valid = lax.broadcasted_iota(jnp.int32, (1, LEN), 1) < r.length
    out = None
    lse_all = r.lse[...]
    lane = lax.broadcasted_iota(jnp.int32, (LEN, LN), 1)
    for h in range(2):
        qh = jnp.where(half_lanes(h), q, jnp.zeros_like(q))
        s = jnp.where(valid, mm_nt(qh, k), -1e9)
        m = jnp.max(s, axis=1, keepdims=True)
        e = jnp.exp(s - m)
        l = jnp.sum(e, axis=1, keepdims=True)
        low = (e * (1.0 / l)).astype(BF)
        o = mm(low, v)
        out = o if out is None else jnp.where(half_lanes(0), out, o)
        lse_all = jnp.where(lane == 2 * hp + h, m + jnp.log(l), lse_all)
    r.lse[...] = lse_all
    r.mixed[:, pl.ds(pl.multiple_of(hp * LN, LN), LN)] = out.astype(BF)


def rows_of(b, n):
    return pl.ds(pl.multiple_of(b * n, n), n)


def forward_first(r):
    def body(b, _):
        o = rows_of(b, LEN)
        v = r.tok[o, :].astype(F32) + mm(r.mixed[o, :], r.wo[...]) + vrow(r.V, "out_bias")
        cen = v - mean_last(v)
        rstd = lax.rsqrt(mean_last(cen * cen) + EPS)
        xh = cen * rstd
        r.xh1[o, :] = xh
        r.rstd1[o, :] = rstd
        r.first_low[o, :] = (xh * vrow(r.V, "first_gain") + vrow(r.V, "first_shift")).astype(BF)
        return 0

    lax.fori_loop(0, 1, body, 0)


def forward_up(r, j):
    o = pl.ds(pl.multiple_of(j * UP, UP), UP)
    v = mm(r.first_low[...], r.w1[:, o]) + r.V[VI["up_bias"] : VI["up_bias"] + 1, o]
    cdf = 0.5 * (1.0 + lax.erf(v * SQ))
    r.act[:, o] = (v * cdf).astype(BF)
    r.gd[:, o] = (cdf + v * (PHI * jnp.exp(-0.5 * v * v))).astype(BF)


def forward_second(r):
    def body(b, tot):
        o = rows_of(b, LEN)
        first = r.xh1[o, :] * vrow(r.V, "first_gain") + vrow(r.V, "first_shift")
        v = first + mm(r.act[o, :], r.w2[...]) + vrow(r.V, "down_bias")
        cen = v - mean_last(v)
        rstd = lax.rsqrt(mean_last(cen * cen) + EPS)
        xh = cen * rstd
        r.xh2[o, :] = xh
        r.rstd2[o, :] = rstd
        t = lax.broadcasted_iota(jnp.int32, (LEN, 1), 0)
        hid = (xh * vrow(r.V, "second_gain") + vrow(r.V, "second_shift")) * (t < r.length).astype(F32)
        r.hidden[o, :] = hid.astype(BF)
        return tot + sum_rows(hid)

    return lax.fori_loop(0, 1, body, jnp.zeros((1, D), F32))


def head(r, tot):
    inv_len = 1.0 / jnp.full((1, 1), r.length, jnp.int32).astype(F32)
    pooled = tot * inv_len
    cen = pooled - mean_last(pooled)
    rstd = lax.rsqrt(mean_last(cen * cen) + EPS)
    xh = cen * rstd
    gain = vrow(r.V, "exit_gain")
    emb = xh * gain + vrow(r.V, "exit_shift")
    d_emb = jnp.zeros((1, D), F32)
    at = 0
    for m in PREFIXES:
        e = emb[:, :m]
        inv = lax.rsqrt(jnp.sum(e * e, axis=1, keepdims=True) * (1.0 / m) + EPS)
        out = e * inv
        r.nested[:, at : at + m] = out
        c = r.ncot[:, at : at + m]
        g = inv * (c - out * (jnp.sum(c * out, axis=1, keepdims=True) * (1.0 / m)))
        d_emb = d_emb + (g if m == D else jnp.concatenate([g, jnp.zeros((1, D - m), F32)], axis=1))
        at += m
    put_grad(r, "exit_gain", d_emb * xh)
    put_grad(r, "exit_shift", d_emb)
    dx = d_emb * gain
    return rstd * (dx - mean_last(dx) - xh * mean_last(dx * xh)) * inv_len


def put_grad(r, name, value):
    k = VI[name]
    r.VG[k : k + 1, : VNAMES[k][1]] = value


def norm_back(dy, gain, xh, rstd):
    dx = dy * gain
    return rstd * (dx - mean_last(dx) - xh * mean_last(dx * xh))


def backward_second(r, d_pool):
    def body(b, c):
        o = rows_of(b, LEN)
        t = lax.broadcasted_iota(jnp.int32, (LEN, 1), 0)
        dy = (r.hcot[o, :].astype(F32) + d_pool) * (t < r.length).astype(F32)
        xh = r.xh2[o, :]
        res = norm_back(dy, vrow(r.V, "second_gain"), xh, r.rstd2[o, :])
        r.res[o, :] = res
        low = res.astype(BF)
        r.d_outer[o, :] = low
        return (c[0] + sum_rows(dy * xh), c[1] + sum_rows(dy), c[2] + sum_rows(low.astype(F32)))

    z = jnp.zeros((1, D), F32)
    a, b, c = lax.fori_loop(0, 1, body, (z, z, z))
    put_grad(r, "second_gain", a)
    put_grad(r, "second_shift", b)
    put_grad(r, "down_bias", c)


def backward_act(r, j):
    o = pl.ds(pl.multiple_of(j * UP, UP), UP)
    d = (mm_nt(r.d_outer[...], r.w2[o, :]) * r.gd[:, o].astype(F32)).astype(BF)
    r.gd[:, o] = d
    r.VG[VI["up_bias"] : VI["up_bias"] + 1, o] = sum_rows(d.astype(F32))


def backward_first(r):
    def body(b, c):
        o = rows_of(b, LEN)
        dy = mm_nt(r.gd[o, :], r.w1[...]) + r.res[o, :]
        xh = r.xh1[o, :]
        res = norm_back(dy, vrow(r.V, "first_gain"), xh, r.rstd1[o, :])
        r.res[o, :] = res
        low = res.astype(BF)
        r.d_branch[o, :] = low
        return (c[0] + sum_rows(dy * xh), c[1] + sum_rows(dy), c[2] + sum_rows(low.astype(F32)))

    z = jnp.zeros((1, D), F32)
    a, b, c = lax.fori_loop(0, 1, body, (z, z, z))
    put_grad(r, "first_gain", a)
    put_grad(r, "first_shift", b)
    put_grad(r, "out_bias", c)


def backward_mixed(r):
    r.d_mixed[...] = mm_nt(r.d_branch[...], r.wo[...]).astype(BF)


def backward_heads(r, hp):
    q, k, v = pair(r, 0, hp) * SCALE, pair(r, 1, hp), pair(r, 2, hp)
    k_scaled = k * SCALE
    cols = pl.ds(pl.multiple_of(hp * LN, LN), LN)
    dm = r.d_mixed[:, cols]
    valid = lax.broadcasted_iota(jnp.int32, (1, LEN), 1) < r.length
    lane = lax.broadcasted_iota(jnp.int32, (LEN, LN), 1)
    zero = jnp.zeros_like(q)
    dm_mixed = dm.astype(F32) * r.mixed[:, cols].astype(F32)
    dq = dk = dv = None
    for h in range(2):
        here = half_lanes(h)
        qh, kh, dmh = jnp.where(here, q, zero), jnp.where(here, k_scaled, zero), jnp.where(here, dm, zero)
        lse = jnp.sum(jnp.where(lane == 2 * hp + h, r.lse[...], 0.0), axis=1, keepdims=True)
        s = jnp.where(valid, mm_nt(qh, k), -1e9)
        p = jnp.exp(s - lse)
        dp = mm_nt(dmh, v)
        delta = jnp.sum(jnp.where(here, dm_mixed, 0.0), axis=1, keepdims=True)
        ds = (p * (dp - delta)).astype(BF)
        a, b, c = mm(ds, kh), mm_tn(ds, qh), mm_tn(p.astype(BF), dmh)
        dq, dk, dv = (a, b, c) if dq is None else (dq + a, dk + b, dv + c)
    dq, dk, dv = dq.astype(BF), dk.astype(BF), dv.astype(BF)
    for part, g in ((0, dq), (1, dk), (2, dv)):
        r.dqkv[:, pl.ds(pl.multiple_of(part * D + hp * LN, LN), LN)] = g
    k = VI["q_bias"]
    r.VG[k : k + 1, cols] = sum_rows(dq.astype(F32))
    k = VI["v_bias"]
    r.VG[k : k + 1, cols] = sum_rows(dv.astype(F32))


def backward_tokens(r, b):
    o = rows_of(b, 128)
    v = r.res[o, :]
    for part in range(3):
        v = v + mm_nt(r.dqkv[o, part * D : (part + 1) * D], r.wqkv[:, part * D : (part + 1) * D])
    r.res[o, :] = v


EDGES = ((13824, 16), (18432, 32), (36880, 48), (55344, 64))


def edge_at(row):
    at = 0
    for base, rows in EDGES:
        if base <= row < base + rows:
            return at + row - base
        at += rows
    return None


def weight_grad(r, lhs, rhs, base, rows, w, RB=256, CB=6, hook=None):
    lead = base % 16
    step_rows = RB * w
    F = r.F
    if lead:
        F[0:16] = jnp.zeros((16, LN), F32)

    def body(s, _):
        o = pl.ds(pl.multiple_of(s * RB, RB), RB)
        for ch in range(w // CB):
            g = mm_tn(lhs[:, o], rhs[:, ch * CB * LN : (ch + 1) * CB * LN])
            for j in range(CB):
                F[pl.ds(lead + ch * CB + j, RB, stride=w), :] = g[:, j * LN : (j + 1) * LN]
        if lead:
            @pl.when(s == 0)
            def _():
                e = edge_at(base)
                r.E[e : e + 16 - lead] = F[lead:16]

        U = 256
        to = base - lead + s * step_rows

        def emit(t, _):
            r.FG[pl.ds(pl.multiple_of(to + t * U, 16), U)] = F[pl.ds(pl.multiple_of(t * U, 16), U)].astype(BF)
            return 0

        lax.fori_loop(0, step_rows // U, emit, 0)
        if lead:
            F[0:16] = F[step_rows : step_rows + 16]
        if hook is not None:
            hook(s)
        return 0

    lax.fori_loop(0, rows // RB, body, 0)
    if lead:
        e = edge_at(base + rows * w - lead)
        r.E[e : e + lead] = F[0:lead]


def edge_grads(r, which):
    base, rows = EDGES[which]
    at = 0
    for vbase, cnt in VECS:
        for k in range(cnt):
            row = vbase + k
            if base <= row < base + rows:
                name, j = vec_at(at + k)
                e = edge_at(row)
                r.E[e : e + 1] = r.VG[name : name + 1, j * LN : (j + 1) * LN]
        at += cnt
    if which == len(EDGES) - 1:
        e = edge_at(TOT)
        r.E[e : e + base + rows - TOT] = jnp.zeros((base + rows - TOT, LN), F32)
    e = edge_at(base)
    r.FG[base : base + rows] = r.E[e : e + rows].astype(BF)


def vec_at(row):
    for k, (_, n) in enumerate(VNAMES):
        if row < n // LN:
            return k, row
        row -= n // LN


class Refs:
    def __init__(self, **refs):
        self.__dict__.update(refs)


def relayout_vectors(p, r):
    at = 0
    for base, cnt in VECS:
        g_lo = base // 16
        g_hi = -(-(base + cnt) // 16)
        load_flat(p, r.slots, r.F, g_lo, g_hi)
        for k in range(cnt):
            name, j = vec_at(at + k)
            f = base - 16 * g_lo + k
            r.V[name : name + 1, j * LN : (j + 1) * LN] = r.F[f : f + 1]
        at += cnt


def relayout_matrix(p, r, name, W, RB):
    base, rows, w = {n: (b, k, c) for n, b, k, c in MATS}[name]
    for s in range(rows // RB):
        lo = base + s * RB * w
        g_lo = lo // 16
        load_flat(p, r.slots, r.F, g_lo, -(-(lo + RB * w) // 16))
        tile_rows(r.F, W, lo - 16 * g_lo, s * RB, RB, w)


def tile_rows(F, W, off, row, rows, w, RB=64):
    def body(t, _):
        q = pl.multiple_of(t * RB, RB)
        for j in range(w):
            W[pl.ds(row + q, RB), j * LN : (j + 1) * LN] = F[pl.ds(off + q * w + j, RB, stride=w), :].astype(BF)
        return 0

    lax.fori_loop(0, rows // RB, body, 0)


def forward_kernel(p, slots, length, tok, hcot, ncot, hidden, nested, wqkv, wo, w1, w2, V, VG, qkv, lse, mixed, xh1, rstd1, first_low, act, gd, res, d_outer, F, qb, xh2, rstd2):
    r = Refs(slots=slots, length=length[0], tok=tok, hcot=hcot, ncot=ncot, hidden=hidden, nested=nested, wqkv=wqkv, wo=wo, w1=w1, w2=w2, V=V, VG=VG, qkv=qkv, lse=lse, mixed=mixed, xh1=xh1, rstd1=rstd1, first_low=first_low, act=act, gd=gd, res=res, d_outer=d_outer, F=F, qb=qb, xh2=xh2, rstd2=rstd2)
    relayout_vectors(p, r)
    relayout_matrix(p, r, "wqkv", wqkv, 256)
    forward_qkv(r)
    lse[...] = jnp.zeros_like(lse)
    lax.fori_loop(0, H // 2, lambda hp, c: (forward_heads(r, hp), c)[1], 0)
    relayout_matrix(p, r, "wo", wo, 768)
    forward_first(r)
    relayout_matrix(p, r, "w1", w1, 256)
    lax.fori_loop(0, FF // UP, lambda j, c: (forward_up(r, j), c)[1], 0)
    relayout_matrix(p, r, "w2", w2, 768)
    tot = forward_second(r)
    d_pool = head(r, tot)
    backward_second(r, d_pool)


def forward_local(p, slots, length, tok, hcot, ncot):
    S = jax.ShapeDtypeStruct
    outs = [S((LEN, D), BF), S((1, 1728), F32), S((D, 3 * D), BF), S((D, D), BF), S((D, FF), BF), S((FF, D), BF), S((16, FF), F32), S((16, FF), F32), S((LEN, 3 * D), BF), S((LEN, LN), F32), S((LEN, D), BF), S((LEN, D), F32), S((LEN, 1), F32), S((LEN, D), BF), S((LEN, FF), BF), S((LEN, FF), BF), S((LEN, D), F32), S((LEN, D), BF)]
    vm = pl.BlockSpec(memory_space=pltpu.VMEM)
    sm = pl.BlockSpec(memory_space=pltpu.SMEM)
    return pl.pallas_call(
        functools.partial(forward_kernel, p),
        out_shape=outs,
        in_specs=[vm, sm, vm, vm, vm],
        scratch_shapes=[pltpu.VMEM((6144 + 32, LN), F32), pltpu.VMEM((1, 3 * D), F32), pltpu.VMEM((LEN, D), F32), pltpu.VMEM((LEN, 1), F32)],
        compiler_params=pltpu.CompilerParams(vmem_limit_bytes=60 << 20),
    )(slots, length, tok, hcot, ncot)


def backward_kernel(p, length, tok, V, VG0, qkv, lse, mixed, xh1, rstd1, first_low, act, gd, res, d_outer, wqkv, wo, w1, w2, igrad, FG, VG, d_branch, d_mixed, dqkv, F, E):
    r = Refs(length=length[0], tok=tok, V=V, VG=VG, qkv=qkv, lse=lse, mixed=mixed, xh1=xh1, rstd1=rstd1, first_low=first_low, act=act, gd=gd, res=igrad, d_outer=d_outer, wqkv=wqkv, wo=wo, w1=w1, w2=w2, FG=FG, d_branch=d_branch, d_mixed=d_mixed, dqkv=dqkv, F=F, E=E)
    VG[...] = VG0[...]
    igrad[...] = res[...]
    mats = {n: (b, k, c) for n, b, k, c in MATS}
    weight_grad(r, act, d_outer, *mats["w2"], RB=1024, CB=2)
    edge_grads(r, 3)
    lax.fori_loop(0, FF // UP, lambda j, c: (backward_act(r, j), c)[1], 0)
    weight_grad(r, first_low, gd, *mats["w1"])
    edge_grads(r, 2)
    backward_first(r)
    weight_grad(r, mixed, d_branch, *mats["wo"])
    edge_grads(r, 1)
    backward_mixed(r)
    lax.fori_loop(0, H // 2, lambda hp, c: (backward_heads(r, hp), c)[1], 0)
    weight_grad(r, tok, dqkv, *mats["wqkv"])
    edge_grads(r, 0)
    lax.fori_loop(0, LEN // 128, lambda b, c: (backward_tokens(r, b), c)[1], 0)


def backward_local(p, length, tok, V, VG, qkv, lse, mixed, xh1, rstd1, first_low, act, gd, res, d_outer, wqkv, wo, w1, w2):
    S = jax.ShapeDtypeStruct
    vm = pl.BlockSpec(memory_space=pltpu.VMEM)
    sm = pl.BlockSpec(memory_space=pltpu.SMEM)
    return pl.pallas_call(
        functools.partial(backward_kernel, p),
        out_shape=[S((LEN, D), F32), S((flat_rows(p), LN), BF)],
        in_specs=[sm] + [vm] * 17,
        scratch_shapes=[pltpu.VMEM((16, FF), F32), pltpu.VMEM((LEN, D), BF), pltpu.VMEM((LEN, D), BF), pltpu.VMEM((LEN, 3 * D), BF), pltpu.VMEM((6144 + 32, LN), F32), pltpu.VMEM((160, LN), F32)],
        compiler_params=pltpu.CompilerParams(vmem_limit_bytes=60 << 20),
    )(length, tok, V, VG, qkv, lse, mixed, xh1, rstd1, first_low, act, gd, res, d_outer, wqkv, wo, w1, w2)


class Gather:
    def __init__(self, p, G, ssem, rsem, gosem):
        self.p, self.G, self.ssem, self.rsem, self.gosem = p, G, ssem, rsem, gosem
        self.x, self.y, self.z, self.c = coords()
        x, y, z, c = self.x, self.y, self.z, self.c
        self.me = lin(x, y, z, c)
        half = p.slot // 32 * 16
        self.H = ((0, half), (half, p.slot - half), (0, p.slot))
        self.px, self.py, self.pc = dev(1 - x, y, z, c), dev(x, 1 - y, z, c), dev(x, y, z, 1 - c)

    def enter(self):
        x, y, z, c = self.x, self.y, self.z, self.c
        bar = pltpu.get_barrier_semaphore()

        def greet(to):
            pl.semaphore_signal(bar, inc=1, device_id=to, device_id_type=MESH)

        for to in (self.px, self.py, self.pc):
            greet(to)
        pl.when(z > 0)(lambda: greet(dev(x, y, z - 1, c)))
        pl.when(z < 3)(lambda: greet(dev(x, y, z + 1, c)))
        middle = (z > 0) & (z < 3)
        pl.when(middle)(lambda: pl.semaphore_wait(bar, 5))
        pl.when(jnp.logical_not(middle))(lambda: pl.semaphore_wait(bar, 4))

    def send(self, sl, h, to, t):
        r0, rn = self.H[h]
        ref = self.G.at[sl, pl.ds(r0, rn)]
        pltpu.make_async_remote_copy(src_ref=ref, dst_ref=ref, send_sem=self.ssem.at[sl, t], recv_sem=self.rsem.at[sl, h], device_id=to, device_id_type=MESH).start()

    def wait(self, sl, h, sem=None):
        r0, rn = self.H[h]
        ref = self.G.at[sl, pl.ds(r0, rn)]
        pltpu.make_async_copy(ref, ref, self.rsem.at[sl, h] if sem is None else sem).wait()

    def up(self, sl, h):
        pl.when(self.z < 3)(lambda: self.send(sl, h, dev(self.x, self.y, self.z + 1, self.c), 3))

    def down(self, sl, h):
        pl.when(self.z > 0)(lambda: self.send(sl, h, dev(self.x, self.y, self.z - 1, self.c), 4))

    def core(self, sl, h):
        self.send(sl, h, self.pc, 2)

    def xy(self, sl):
        self.send(sl, 0, self.px, 0)
        self.send(sl, 1, self.py, 1)
        self.send(sl, 1, self.px, 0)
        self.send(sl, 0, self.py, 1)

    def own(self, xy):
        for h in (0, 1):
            self.up(self.me, h)
            self.down(self.me, h)
        if xy:
            self.xy(self.me)
        for h in (0, 1):
            self.core(self.me, h)

    def own_line(self, k):
        self.at(k, lambda zq: self.xy(lin(self.x, self.y, zq, self.c)))

    def go(self, k):
        pl.semaphore_signal(self.gosem.at[k], inc=1, device_id=self.pc, device_id_type=MESH)

    def wait_go(self, k):
        pl.semaphore_wait(self.gosem.at[k], 1)

    def at(self, k, fn):
        if k == 0:
            fn(self.z)
            return
        pl.when(self.z - k >= 0)(lambda: fn(self.z - k))
        pl.when(self.z + k <= 3)(lambda: fn(self.z + k))

    def along_z(self, k, xy):
        x, y, z, c = self.x, self.y, self.z, self.c

        def from_level(zq, on):
            sl = lin(x, y, zq, c)
            self.wait(sl, 0)
            on(sl, 0)
            if xy:
                self.send(sl, 0, self.px, 0)
            self.core(sl, 0)
            self.wait(sl, 1)
            on(sl, 1)
            if xy:
                self.send(sl, 1, self.py, 1)
                self.send(sl, 1, self.px, 0)
                self.send(sl, 0, self.py, 1)
            self.core(sl, 1)

        pl.when(z - k >= 0)(lambda: from_level(z - k, self.up))
        pl.when(z + k <= 3)(lambda: from_level(z + k, self.down))

    def sides(self, k):
        x, y, c = self.x, self.y, self.c

        def fn(zq):
            sl = lin(1 - x, y, zq, c)
            self.wait(sl, 0)
            self.send(sl, 0, self.py, 1)
            self.core(sl, 0)
            sl = lin(x, 1 - y, zq, c)
            self.wait(sl, 1)
            self.send(sl, 1, self.px, 0)
            self.core(sl, 1)

        self.at(k, fn)

    def sides_rest(self, k):
        x, y, c = self.x, self.y, self.c

        def fn(zq):
            sl = lin(1 - x, y, zq, c)
            self.wait(sl, 1)
            self.core(sl, 1)
            sl = lin(x, 1 - y, zq, c)
            self.wait(sl, 0)
            self.core(sl, 0)

        self.at(k, fn)

    def diagonal(self, k):
        def fn(zq):
            sl = lin(1 - self.x, 1 - self.y, zq, self.c)
            for h in (0, 1):
                self.wait(sl, h)
                self.core(sl, h)

        self.at(k, fn)

    def from_sibling(self, xp):
        def body(fs, carry):
            for h in (0, 1):
                self.wait((2 * xp + 1 - self.c) * 8 + fs, h)
            return carry

        lax.fori_loop(0, 8, body, 0)

    def leave(self):
        x, y, z, c = self.x, self.y, self.z, self.c
        W = self.wait

        def body(zq, carry):
            sl = lin(x, y, zq, c)
            for t in (0, 1, 2):
                W(sl, 2, self.ssem.at[sl, t])
            pl.when((zq <= z) & (z < 3))(lambda: W(sl, 2, self.ssem.at[sl, 3]))
            pl.when((zq >= z) & (z > 0))(lambda: W(sl, 2, self.ssem.at[sl, 4]))
            sx = lin(1 - x, y, zq, c)
            W(sx, 0, self.ssem.at[sx, 1])
            W(sx, 2, self.ssem.at[sx, 2])
            sy = lin(x, 1 - y, zq, c)
            W(sy, 1, self.ssem.at[sy, 0])
            W(sy, 2, self.ssem.at[sy, 2])
            sd = lin(1 - x, 1 - y, zq, c)
            W(sd, 2, self.ssem.at[sd, 2])
            return carry

        lax.fori_loop(0, 4, body, 0)


FORWARD_OUT = ("hidden", "nested", "wqkv", "wo", "w1", "w2", "V", "VG", "qkv", "lse", "mixed", "xh1", "rstd1", "first_low", "act", "gd", "res", "d_outer")
FORWARD_SHAPES = dict(
    hidden=((LEN, D), jnp.bfloat16),
    nested=((1, 1728), jnp.float32),
    wqkv=((D, 3 * D), jnp.bfloat16),
    wo=((D, D), jnp.bfloat16),
    w1=((D, FF), jnp.bfloat16),
    w2=((FF, D), jnp.bfloat16),
    V=((16, FF), jnp.float32),
    VG=((16, FF), jnp.float32),
    qkv=((LEN, 3 * D), jnp.bfloat16),
    lse=((LEN, LN), jnp.float32),
    mixed=((LEN, D), jnp.bfloat16),
    xh1=((LEN, D), jnp.float32),
    rstd1=((LEN, 1), jnp.float32),
    first_low=((LEN, D), jnp.bfloat16),
    act=((LEN, FF), jnp.bfloat16),
    gd=((LEN, FF), jnp.bfloat16),
    res=((LEN, D), jnp.float32),
    d_outer=((LEN, D), jnp.bfloat16),
)


def own_slot(p, me, x_ref, F, G):
    start = me * p.sh
    r_first = start // LN
    s = start - r_first * LN
    r0 = r_first % 16
    lead = 32
    F[0 : lead + p.slot + 32] = jnp.zeros((lead + p.slot + 32, LN), F32)
    F[lead : lead + p.rows_in] = pltpu.roll(x_ref[...].astype(F32), s, 1)
    lane = lax.broadcasted_iota(jnp.int32, (p.slot, LN), 1)
    G[me] = jnp.where(lane >= s, F[pl.ds(lead - r0, p.slot), :], F[pl.ds(lead - 1 - r0, p.slot), :]).astype(BF)


def relayout_vector(p, r, which):
    at = sum(cnt for _, cnt in VECS[:which])
    base, cnt = VECS[which]
    g_lo = base // 16
    load_flat(p, r.slots, r.F, g_lo, -(-(base + cnt) // 16), base + cnt)
    for k in range(cnt):
        name, j = vec_at(at + k)
        f = base - 16 * g_lo + k
        r.V[name : name + 1, j * LN : (j + 1) * LN] = r.F[f : f + 1]


def relayout_rows(p, r, name, W, row, rows):
    base, _, w = {n: (b, k, c) for n, b, k, c in MATS}[name]
    lo = base + row * w
    g_lo = lo // 16
    load_flat(p, r.slots, r.F, g_lo, -(-(lo + rows * w) // 16), lo + rows * w)
    tile_rows(r.F, W, lo - 16 * g_lo, row, rows, w)


def gather_forward_kernel(p, x_ref, length, tok, hcot, ncot, *refs):
    n = len(FORWARD_OUT)
    outs = dict(zip(FORWARD_OUT, refs[:n]))
    loc = dict(zip(FORWARD_OUT, refs[n : 2 * n]))
    G, F, qb, xh2, rstd2, ssem, rsem, gosem, osem = refs[2 * n :]
    r = Refs(slots=G, length=length[0], tok=tok, hcot=hcot, ncot=ncot, F=F, qb=qb, xh2=xh2, rstd2=rstd2, **loc)
    g = Gather(p, G, ssem, rsem, gosem)
    own_slot(p, g.me, x_ref, F, G)
    g.enter()
    c0, c1 = g.c == 0, g.c == 1

    started = []

    def out(*names):
        for m in names:
            k = FORWARD_OUT.index(m)
            cp = pltpu.make_async_copy(loc[m], outs[m], osem.at[k])
            cp.start()
            started.append(cp)

    def part_rq_0():
        g.own(True)
        g.sides(0)
        g.go(0)
        g.along_z(1, True)
        g.sides(1)
        g.sides_rest(0)
        g.diagonal(0)
        g.go(1)
        g.along_z(2, True)
        g.sides(2)
        g.along_z(3, True)
        g.diagonal(1)
        g.sides_rest(1)
        g.sides(3)
        g.sides_rest(3)
        g.diagonal(2)
        g.sides_rest(2)
        g.diagonal(3)

    pl.when(c0)(part_rq_0)
    def part_rq_1():
        g.wait_go(0)
        g.own(False)
        g.wait_go(1)
        g.own_line(0)
        g.along_z(1, False)
        g.sides(0)
        g.along_z(2, False)
        g.own_line(1)
        g.along_z(3, False)
        g.own_line(3)
        g.own_line(2)
        g.from_sibling(0)
        g.sides(3)
        g.sides_rest(0)
        g.diagonal(0)

    pl.when(c1)(part_rq_1)
    relayout_vector(p, r, 0)
    for k in range(3):
        relayout_rows(p, r, "wqkv", r.wqkv, 256 * k, 256)
    out("wqkv")
    def part_qkv_1():
        g.from_sibling(1)
        g.sides(1)

    pl.when(c1)(part_qkv_1)
    forward_qkv(r)
    out("qkv")
    r.lse[...] = jnp.zeros_like(r.lse)

    def heads(hp, carry):
        def part_hd0_1():
            g.sides_rest(1)
            g.sides(2)
            g.sides_rest(3)

        pl.when((hp == 0) & c1)(part_hd0_1)
        def part_hd3_1():
            g.sides_rest(2)
            g.diagonal(3)

        pl.when((hp == 3) & c1)(part_hd3_1)
        def part_hd5_1():
            g.diagonal(1)

        pl.when((hp == 5) & c1)(part_hd5_1)
        forward_heads(r, hp)
        return carry

    lax.fori_loop(0, H // 2, heads, 0)
    out("lse", "mixed")
    def part_rw1b_1():
        g.diagonal(2)

    pl.when(c1)(part_rw1b_1)
    relayout_rows(p, r, "w1", r.w1, 448, 128)
    relayout_rows(p, r, "w1", r.w1, 576, 192)
    relayout_rows(p, r, "w2", r.w2, 0, 768)
    relayout_vector(p, r, 2)
    def part_rwo_0():
        g.from_sibling(0)

    pl.when(c0)(part_rwo_0)
    relayout_rows(p, r, "wo", r.wo, 0, 768)
    relayout_vector(p, r, 1)
    out("wo")
    forward_first(r)
    out("xh1", "rstd1", "first_low")
    def part_rw1a_0():
        g.from_sibling(1)

    pl.when(c0)(part_rw1a_0)
    relayout_rows(p, r, "w1", r.w1, 0, 256)
    relayout_rows(p, r, "w1", r.w1, 256, 192)
    out("w1")
    lax.fori_loop(0, FF // UP, lambda j, c: (forward_up(r, j), c)[1], 0)
    out("act", "gd")
    for k in range(1, 4):
        relayout_rows(p, r, "w2", r.w2, 768 * k, 768)
    relayout_vector(p, r, 3)
    out("w2", "V")
    tot = forward_second(r)
    out("hidden")
    d_pool = head(r, tot)
    out("nested")
    backward_second(r, d_pool)
    out("VG", "res", "d_outer")
    g.leave()
    for cp in started:
        cp.wait()


def gather_forward(p, shard, length, tok, hcot, ncot):
    x = jnp.pad(shard, (0, p.rows_in * LN - p.sh)).reshape(p.rows_in, LN)
    S = jax.ShapeDtypeStruct
    vm = pl.BlockSpec(memory_space=pltpu.VMEM)
    sm = pl.BlockSpec(memory_space=pltpu.SMEM)
    hbm = pl.BlockSpec(memory_space=pl.ANY)
    VM = pltpu.VMEM
    DM = pltpu.SemaphoreType.DMA
    shapes = [FORWARD_SHAPES[m] for m in FORWARD_OUT]
    res = pl.pallas_call(
        functools.partial(gather_forward_kernel, p),
        out_shape=[S(*s) for s in shapes],
        in_specs=[vm, sm, vm, vm, vm],
        out_specs=[hbm] * len(shapes),
        scratch_shapes=[VM(*s) for s in shapes]
        + [VM((p.n, p.slot, LN), BF), VM((6144 + 32, LN), F32), VM((1, 3 * D), F32), VM((LEN, D), F32), VM((LEN, 1), F32)]
        + [DM((p.n, 5)), DM((p.n, 2)), pltpu.SemaphoreType.REGULAR((2,)), DM((len(shapes),))],
        compiler_params=pltpu.CompilerParams(collective_id=0, has_side_effects=True, vmem_limit_bytes=64 << 20),
    )(x, length, tok, hcot, ncot)
    return dict(zip(FORWARD_OUT, res))


SCHEDULE = (
    (4, 1, 0, "diag", 1, 2, 1),
    (5, 1, 0, "diag", 1, 1, 1),
    (8, 1, 1, "yline", 1, 2, 1),
    (8, 1, 0, "xline", 1, 1, 1),
    (10, 1, 1, "yline", 1, 1, 1),
    (10, 1, 0, "diag", 1, 3, 1),
    (10, 0, 0, "diag", 1, 0, 1),
    (11, 0, 0, "diag", 1, 2, 2),
    (12, 1, 1, "diag", 0, 0, 1),
    (12, 0, 0, "diag", 1, 1, 1),
    (13, 1, 1, "diag", 0, 2, 1),
    (13, 1, 1, "diag", 0, 1, 1),
    (13, 1, 0, "yline", 0, 2, 1),
    (14, 1, 1, "diag", 0, 3, 1),
    (14, 0, 0, "xline", 1, 2, 1),
    (15, 0, 1, "yline", 1, 3, 1),
    (16, 1, 1, "xline", 0, 2, 1),
    (16, 0, 0, "xline", 1, 1, 1),
    (16, 1, 0, "yline", 0, 1, 1),
    (17, 1, 1, "own", 1, 1, 1),
    (17, 0, 1, "yline", 1, 2, 1),
    (18, 0, 0, "xline", 1, 0, 1),
    (18, 0, 1, "yline", 1, 1, 1),
    (18, 1, 1, "xline", 0, 1, 1),
    (18, 1, 0, "yline", 0, 3, 1),
    (19, 1, 0, "own", 0, 2, 1),
    (19, 1, 1, "xline", 0, 0, 1),
    (20, 0, 0, "yline", 0, 1, 1),
    (20, 0, 1, "diag", 0, 1, 2),
    (20, 0, 0, "yline", 0, 0, 1),
    (20, 0, 1, "own", 1, 2, 1),
    (20, 1, 0, "xline", 1, 2, 1),
    (21, 1, 1, "yline", 1, 0, 1),
    (21, 0, 1, "diag", 0, 0, 1),
    (21, 0, 1, "own", 1, 1, 1),
    (21, 1, 0, "diag", 1, 0, 1),
    (21, 0, 0, "own", 0, 1, 1),
    (21, 1, 0, "xline", 1, 3, 1),
    (22, 1, 0, "yline", 0, 0, 1),
    (22, 1, 0, "own", 0, 1, 1),
    (22, 1, 0, "own", 0, 0, 1),
    (22, 0, 0, "yline", 0, 2, 1),
    (22, 0, 1, "xline", 0, 1, 1),
    (22, 0, 0, "xline", 1, 3, 1),
    (22, 0, 1, "yline", 1, 0, 1),
    (22, 1, 1, "own", 1, 0, 1),
    (22, 0, 1, "xline", 0, 0, 1),
    (22, 0, 1, "xline", 0, 2, 1),
    (22, 0, 0, "own", 0, 0, 1),
    (22, 0, 0, "own", 0, 2, 1),
    (22, 0, 0, "yline", 0, 3, 1),
    (22, 0, 1, "diag", 0, 3, 1),
    (22, 0, 1, "own", 1, 0, 1),
    (22, 0, 1, "xline", 0, 3, 1),
    (22, 1, 0, "xline", 1, 0, 1),
    (22, 1, 1, "own", 1, 2, 1),
    (22, 1, 1, "xline", 0, 3, 1),
    (22, 1, 1, "yline", 1, 3, 1),
)


class Scatter:
    def __init__(self, p, FG, R, D0, D1, X, Y, Z, A, sems):
        self.p, self.FG, self.R, self.D0, self.D1, self.X, self.Y, self.Z, self.A = p, FG, R, D0, D1, X, Y, Z, A
        self.sib_s, self.sib_r, self.d_s, self.d_r, self.x_s, self.x_r, self.y_s, self.y_r, self.z_s, self.z_r = sems
        self.x, self.y, self.z, self.c = coords()
        x, y, z, c = self.x, self.y, self.z, self.c
        self.SL = p.slot
        self.half = p.slot // 32 * 16
        self.px, self.py, self.pc = dev(1 - x, y, z, c), dev(x, 1 - y, z, c), dev(x, y, z, 1 - c)

    def zq(self, b):
        d = lax.rem(b + 1, 4)
        z = self.z
        return lax.rem(z % 2 + d % 2, 2) + 2 * lax.rem(z // 2 + d // 2, 2)

    def enter(self):
        x, y, c = self.x, self.y, self.c
        barrier([self.px, self.py, self.pc] + [dev(x, y, self.zq(b), c) for b in range(3)])

    def row0(self, slot):
        return pl.multiple_of((slot * self.p.sh) // LN // 16 * 16, 16)

    def fg(self, slot):
        return self.row0(slot)

    def copy(self, src, dst, ssem, rsem, to):
        return pltpu.make_async_remote_copy(src_ref=src, dst_ref=dst, send_sem=ssem, recv_sem=rsem, device_id=to, device_id_type=MESH)

    def wait(self, ref, sem):
        pltpu.make_async_copy(ref, ref, sem).wait()

    def to_sibling(self, xp):
        def body(k, _):
            dp = 2 * xp + 1 - self.c
            i = 8 * xp + k
            self.copy(self.FG.at[pl.ds(self.row0(dp * 8 + k), self.SL)], self.R.at[i], self.sib_s.at[i], self.sib_r.at[i], self.pc).start()
            return 0

        lax.fori_loop(0, 8, body, 0)

    def add(self, dst, d0, rows, srcs, U=176):
        def body(t, _):
            r = pl.multiple_of(t * U, 16)
            v = None
            for s, s0 in srcs:
                e = s[pl.ds(s0 + r, U)].astype(F32)
                v = e if v is None else v + e
            dst[pl.ds(d0 + r, U)] = v.astype(dst.dtype)
            return 0

        lax.fori_loop(0, rows // U, body, 0)

    def have(self, xp, yq, zq):
        fs = zq * 2 + yq
        i = 8 * xp + fs
        self.wait(self.R.at[i], self.sib_r.at[i])
        return i, self.row0((2 * xp + self.c) * 8 + fs)

    def diag(self, xp, b):
        i, g = self.have(xp, 1 - self.y, self.zq(b))
        half, rest = self.half, self.SL - self.half
        R = self.R.at[i]
        self.add(R, 0, self.SL, [(self.FG, g), (R, 0)])
        self.copy(R.at[pl.ds(0, half)], self.D0.at[b], self.d_s.at[0, b], self.d_r.at[0, b], self.py).start()
        self.copy(R.at[pl.ds(half, rest)], self.D1.at[b], self.d_s.at[1, b], self.d_r.at[1, b], self.px).start()

    def xline(self, xp, b):
        i, g = self.have(xp, self.y, self.zq(b))
        half, rest = self.half, self.SL - self.half
        R = self.R.at[i]
        self.wait(self.D0.at[b], self.d_r.at[0, b])
        self.add(R, half, rest, [(self.FG, g + half), (R, half)])
        self.add(R, 0, half, [(self.FG, g), (R, 0), (self.D0.at[b], 0)])
        self.copy(R, self.X.at[b], self.x_s.at[b], self.x_r.at[b], self.px).start()

    def yline(self, xp, b):
        i, g = self.have(xp, 1 - self.y, self.zq(b))
        half, rest = self.half, self.SL - self.half
        R = self.R.at[i]
        self.wait(self.D1.at[b], self.d_r.at[1, b])
        self.add(R, 0, half, [(self.FG, g), (R, 0)])
        self.add(R, half, rest, [(self.FG, g + half), (R, half), (self.D1.at[b], 0)])
        self.copy(R, self.Y.at[b], self.y_s.at[b], self.y_r.at[b], self.py).start()

    def own(self, xp, b):
        i, g = self.have(xp, self.y, self.zq(b))
        R = self.R.at[i]
        self.wait(self.X.at[b], self.x_r.at[b])
        self.wait(self.Y.at[b], self.y_r.at[b])
        self.add(R, 0, self.SL, [(self.FG, g), (R, 0), (self.X.at[b], 0), (self.Y.at[b], 0)])
        self.copy(R, self.Z.at[b], self.z_s.at[b], self.z_r.at[b], dev(self.x, self.y, self.zq(b), self.c)).start()

    def last(self, xp, out):
        p, SL, A = self.p, self.SL, self.A
        i, g = self.have(xp, self.y, self.z)
        self.wait(self.X.at[3], self.x_r.at[3])
        self.wait(self.Y.at[3], self.y_r.at[3])
        for b in range(3):
            self.wait(self.Z.at[b], self.z_r.at[b])
        self.add(A, 0, SL, [(self.FG, g), (self.R.at[i], 0), (self.X.at[3], 0), (self.Y.at[3], 0)] + [(self.Z.at[b], 0) for b in range(3)])
        start = lin(self.x, self.y, self.z, self.c) * p.sh
        r_first = start // LN
        s = start - r_first * LN
        r0 = r_first % 16
        A[0:SL] = pltpu.roll(A[0:SL], lax.rem(LN - s, LN), 1)
        lane = lax.broadcasted_iota(jnp.int32, (p.rows_in, LN), 1)
        out[...] = jnp.where(lane < LN - s, A[pl.ds(r0, p.rows_in), :], A[pl.ds(r0 + 1, p.rows_in), :])

    def after(self, part, index=None):
        for c in (0, 1):
            for x in (0, 1):
                todo = [e for e in SCHEDULE if e[:3] == (part, c, x)]
                if todo:
                    here = (self.c == c) & (self.x == x)
                    if index is not None:
                        here = here & (index[0] == index[1])

                    def run(todo=todo):
                        for _, _, _, step, xp, b0, n in todo:
                            lax.fori_loop(b0, b0 + n, lambda b, k: (getattr(self, step)(xp, b), k)[1], 0)

                    pl.when(here)(run)

    def leave(self):
        for k in range(16):
            self.wait(self.R.at[k], self.sib_s.at[k])
        for b in range(4):
            self.wait(self.D0.at[b], self.d_s.at[0, b])
            self.wait(self.D1.at[b], self.d_s.at[1, b])
            self.wait(self.X.at[b], self.x_s.at[b])
            self.wait(self.Y.at[b], self.y_s.at[b])
        for b in range(3):
            self.wait(self.Z.at[b], self.z_s.at[b])


BACK_IN = ("act", "d_outer", "w2", "gd", "first_low", "w1", "res", "xh1", "rstd1", "V", "VG", "mixed", "wo", "qkv", "lse", "tok")


def backward_scatter_kernel(p, length, *refs):
    n = len(BACK_IN)
    src = dict(zip(BACK_IN, refs[:n]))
    wqkv_in = refs[n]
    igrad, out = refs[n + 1 : n + 3]
    loc = dict(zip(BACK_IN, refs[n + 3 : 2 * n + 3]))
    FG, F, E, R, D0, D1, X, Y, Z, lsem, osem, *sems = refs[2 * n + 3 :]
    r = Refs(length=length[0], FG=FG, F=F, E=E, **loc)
    r.dqkv, r.d_branch, r.d_mixed = r.act, r.first_low, r.d_outer
    sc = Scatter(p, FG, R, D0, D1, X, Y, Z, F, sems)
    mats = {m: (b, k, c) for m, b, k, c in MATS}
    loads = {m: pltpu.make_async_copy(src[m], loc[m], lsem.at[k]) for k, m in enumerate(BACK_IN)}
    for m in BACK_IN:
        loads[m].start()

    def need(*names):
        for m in names:
            loads[m].wait()

    sc.enter()
    c0, c1 = sc.c == 0, sc.c == 1
    x0, x1 = sc.x == 0, sc.x == 1

    def both(cond, fn):
        pl.when(cond)(fn)

    need("act", "d_outer", "VG")
    weight_grad(r, r.act, r.d_outer, *mats["w2"], RB=1024, CB=2)
    edge_grads(r, 3)
    both(c0, lambda: sc.to_sibling(1))
    sc.after(1)
    need("w2", "gd")

    def act_part(j, carry):
        backward_act(r, j)
        for k in range(4):
            sc.after(2 + k, (j, k))
        return carry

    lax.fori_loop(0, FF // UP, act_part, 0)
    q_loads = [pltpu.make_async_copy(wqkv_in.at[:, pl.ds(k * D, D)], r.w2.at[pl.ds(k * D, D)], lsem.at[n + k]) for k in range(3)]
    for q in q_loads:
        q.start()
    need("first_low")
    weight_grad(r, r.first_low, r.gd, *mats["w1"], hook=lambda i: [sc.after(6 + k, (i, k)) for k in range(2)])
    edge_grads(r, 2)
    both(c1, lambda: sc.to_sibling(1))
    sc.after(8)
    need("w1", "res", "xh1", "rstd1", "V")
    backward_first(r)
    sc.after(9)
    need("mixed")
    weight_grad(r, r.mixed, r.d_branch, *mats["wo"])
    edge_grads(r, 1)
    both(c0, lambda: sc.to_sibling(0))
    sc.after(10)
    need("wo")
    backward_mixed(r)
    sc.after(11)
    need("qkv", "lse")

    def heads(hp, carry):
        backward_heads(r, hp)
        for k in range(6):
            sc.after(12 + k, (hp, k))
        return carry

    lax.fori_loop(0, H // 2, heads, 0)
    need("tok")
    weight_grad(r, r.tok, r.dqkv, *mats["wqkv"], hook=lambda i: [sc.after(18 + k, (i, k)) for k in range(2)])
    edge_grads(r, 0)
    both(c1, lambda: sc.to_sibling(0))
    sc.after(20)
    for q in q_loads:
        q.wait()

    def tokens(b, carry):
        o = rows_of(b, LEN)
        v = r.res[o, :]
        for part in range(3):
            v = v + mm_nt(r.dqkv[o, part * D : (part + 1) * D], r.w2[part * D : (part + 1) * D, :])
        r.res[o, :] = v
        sc.after(21, (b, 0))
        return carry

    lax.fori_loop(0, 1, tokens, 0)
    grad_out = pltpu.make_async_copy(r.res, igrad, osem)
    grad_out.start()
    sc.after(22)
    both(x0, lambda: sc.last(0, out))
    both(x1, lambda: sc.last(1, out))
    sc.leave()
    grad_out.wait()


def backward_scatter(p, length, wqkv, **arrays):
    S = jax.ShapeDtypeStruct
    sm = pl.BlockSpec(memory_space=pltpu.SMEM)
    hbm = pl.BlockSpec(memory_space=pl.ANY)
    ins = [arrays[m] for m in BACK_IN]
    SL = p.slot
    half = SL // 32 * 16
    VM = pltpu.VMEM
    DM = pltpu.SemaphoreType.DMA
    igrad, o = pl.pallas_call(
        functools.partial(backward_scatter_kernel, p),
        out_shape=[S((LEN, D), F32), S((p.rows_in, LN), F32)],
        in_specs=[sm] + [hbm] * (len(ins) + 1),
        out_specs=[hbm, pl.BlockSpec(memory_space=pltpu.VMEM)],
        scratch_shapes=[VM(a.shape, a.dtype) for a in ins]
        + [VM((flat_rows(p), LN), BF), VM((6144 + 32, LN), F32), VM((160, LN), F32), VM((16, SL, LN), BF), VM((4, half, LN), BF), VM((4, SL - half, LN), BF), VM((4, SL, LN), BF), VM((4, SL, LN), BF), VM((3, SL, LN), BF)]
        + [DM((len(ins) + 3,)), DM, DM((16,)), DM((16,)), DM((2, 4)), DM((2, 4)), DM((4,)), DM((4,)), DM((4,)), DM((4,)), DM((3,)), DM((3,))],
        compiler_params=pltpu.CompilerParams(collective_id=1, has_side_effects=True, vmem_limit_bytes=64 << 20),
    )(length, *ins, wqkv)
    return igrad, o


def finish_copies(p, shards, hidden, igrad, nested):
    S = jax.ShapeDtypeStruct
    vm = pl.BlockSpec(memory_space=pltpu.VMEM)

    def kernel(a, b, c, d, a_out, b_out, c_out, d_out):
        a_out[...] = a[...].reshape(p.rows_in * LN)[: p.sh]
        b_out[...] = b[...]
        c_out[...] = c[...]
        d_out[...] = d[...]

    arrays = (shards, hidden, igrad, nested)
    return pl.pallas_call(
        kernel,
        out_shape=[S((p.sh,), F32)] + [S(a.shape, a.dtype) for a in arrays[1:]],
        in_specs=[vm] * 4,
        out_specs=[vm] * 4,
    )(*arrays)


def on_device(p, fast, tokens, lengths, weight_shards, hidden_cotangent, nested_cotangent):
    tok = tokens.reshape(LEN, D)
    hcot = hidden_cotangent.reshape(LEN, D)
    if fast:
        f = gather_forward(p, weight_shards, lengths, tok, hcot, nested_cotangent)
        igrad, shards = backward_scatter(p, lengths, tok=tok, **{m: f[m] for m in BACK_IN + ("wqkv",) if m != "tok"})
        shards, f["hidden"], igrad, f["nested"] = finish_copies(p, shards, f["hidden"], igrad, f["nested"])
    else:
        slots = lax.all_gather(build_slot(p, weight_shards, me_of), AX, axis=0)
        f = dict(zip(FORWARD_OUT, forward_local(p, slots, lengths, tok, hcot, nested_cotangent)))
        igrad, flat = backward_local(p, lengths, tok, *[f[m] for m in FORWARD_OUT[6:] + FORWARD_OUT[2:6]])
        shards = scatter_plain(p, flat)
    return (f["hidden"].reshape(1, LEN, D), f["nested"], igrad.reshape(1, LEN, D), shards)


def solution(mesh):
    in_specs = (
        P(("dp", "fsdp"), None, None),
        P(("dp", "fsdp")),
        P(("dp", "fsdp")),
        P(("dp", "fsdp"), None, None),
        P(("dp", "fsdp"), None),
    )
    out_specs = (
        P(("dp", "fsdp"), None, None),
        P(("dp", "fsdp"), None),
        P(("dp", "fsdp"), None, None),
        P(("dp", "fsdp")),
    )
    p = plan(mesh.shape["dp"] * mesh.shape["fsdp"])
    fast = (mesh.shape["dp"], mesh.shape["fsdp"]) == (4, 8)
    return jax.shard_map(
        functools.partial(on_device, p, fast), mesh=mesh, in_specs=in_specs, out_specs=out_specs, check_vma=False
    )
```

```python
import functools
import math

import jax
import jax.numpy as jnp
from jax import lax
from jax.experimental import pallas as pl
from jax.experimental.pallas import tpu as pltpu
from jax.sharding import PartitionSpec as P

AX = ("dp", "fsdp")
MESH = pl.DeviceIdType.MESH
D = 768
H = 12
HD = 64
FF = 3072
LEN = 512
E2 = 512
E3 = 256
E4 = 128
E5 = 64


epsilon = 1e-05


PAR=7088640; LN=128
class Plan: pass
def plan(n):
    p=Plan(); p.n=n; p.sh=PAR//n
    st=[i*p.sh for i in range(n)]
    p.g0=[s//LN//16 for s in st]
    p.g1=[(s+p.sh-1)//LN//16 for s in st]
    p.slot=16*max(b-a+1 for a,b in zip(p.g0,p.g1))
    p.rows_in=-(-p.sh//LN)
    return p
MATS=[("wqkv",0,D,18),("wo",13836,D,6),("w1",18462,D,24),("w2",36918,FF,6)]
VECS=[(13824,12),(18444,18),(36894,24),(55350,30)]

def build_slot_kernel(p,me_of,x_ref,o_ref,q_ref):
    i=me_of(); start=i*p.sh; r_first=start//LN; s=start-r_first*LN; r0=r_first%16
    lead=32
    q_ref[...]=jnp.zeros_like(q_ref)
    q=pltpu.roll(x_ref[...].astype(jnp.float32),s,1)
    q_ref[lead:lead+p.rows_in]=q
    lane=lax.broadcasted_iota(jnp.int32,(p.slot,LN),1)
    a=q_ref[pl.ds(lead-r0,p.slot),:]
    b=q_ref[pl.ds(lead-1-r0,p.slot),:]
    o_ref[...]=jnp.where(lane>=s,a,b).astype(jnp.bfloat16)

def build_slot(p,shard,me_of):
    x=jnp.pad(shard,(0,p.rows_in*LN-p.sh)).reshape(p.rows_in,LN)
    return pl.pallas_call(functools.partial(build_slot_kernel,p,me_of),out_shape=jax.ShapeDtypeStruct((p.slot,LN),jnp.bfloat16),
        scratch_shapes=[pltpu.VMEM((32+p.slot+32,LN),jnp.float32)])(x)

def load_flat(p,slots,F,g_lo,g_hi,need=None):
    for i in range(p.n):
        a=max(g_lo,p.g0[i]); b=min(g_hi,p.g1[i]+1)
        if a>=b: continue
        shared_first = i>0 and p.g0[i]==p.g1[i-1] and a==p.g0[i]
        a2=a+1 if shared_first else a
        b2=b
        apart=need is not None and need<=(i+1)*p.sh//LN
        if i+1<p.n and p.g1[i]==p.g0[i+1] and b==p.g1[i]+1 and not apart: b2=b-1
        if i+1<p.n and b2<b and b-1>=g_lo:
            g=b-1
            F[16*(g-g_lo):16*(g-g_lo)+16]=slots[i,16*(g-p.g0[i]):16*(g-p.g0[i])+16].astype(jnp.float32)+slots[i+1,0:16].astype(jnp.float32)
        cnt=b2-a2
        if cnt<=0: continue
        U=16
        nb,rem=cnt//U,cnt%U
        def body(t,_,i=i,a2=a2):
            src=pl.multiple_of(16*(a2-p.g0[i])+t*16*U,16); dst=pl.multiple_of(16*(a2-g_lo)+t*16*U,16)
            F[pl.ds(dst,16*U)]=slots[i,pl.ds(src,16*U)].astype(jnp.float32)
            return 0
        lax.fori_loop(0,nb,body,0)
        if rem:
            src=16*(a2-p.g0[i])+nb*16*U; dst=16*(a2-g_lo)+nb*16*U
            F[dst:dst+16*rem]=slots[i,src:src+16*rem].astype(jnp.float32)

def coords():
    dp=lax.axis_index("dp"); fs=lax.axis_index("fsdp")
    return dp//2,fs%2,fs//2,dp%2
def dev(x,y,z,c): return (x*2+c, z*2+y)
def lin(x,y,z,c): return (x*2+c)*8+z*2+y
def barrier(partners):
    bar=pltpu.get_barrier_semaphore()
    for q in partners: pl.semaphore_signal(bar,inc=1,device_id=q,device_id_type=MESH)
    pl.semaphore_wait(bar,len(partners))

TOT=PAR//LN
def flat_rows(p): return max(16*p.g0[-1]+p.slot, EDGES[-1][0]+EDGES[-1][1])
def owner_row(rho):
    for k,(name,base,rows,w) in enumerate(MATS):
        if base<=rho<base+rows*w: return ("m",k,(rho-base)//w,(rho-base)%w)
    at=0
    for base,cnt in VECS:
        if base<=rho<base+cnt: return ("v",at+rho-base)
        at+=cnt
    return None

def me_of():
    return lax.axis_index(AX)


def finish_kernel(p, a_ref, out, A):
    SL = p.slot
    start = me_of() * p.sh
    r_first = start // LN
    s = start - r_first * LN
    r0 = r_first % 16
    A[0:SL] = pltpu.roll(a_ref[...], lax.rem(LN - s, LN), 1)
    lane = lax.broadcasted_iota(jnp.int32, (p.rows_in, LN), 1)
    out[...] = jnp.where(lane < LN - s, A[pl.ds(r0, p.rows_in), :], A[pl.ds(r0 + 1, p.rows_in), :])


def scatter_plain(p, flat):
    parts = jnp.concatenate([flat[16 * g : 16 * g + p.slot] for g in p.g0]).astype(jnp.float32)
    mine = lax.psum_scatter(parts, AX, scatter_dimension=0, tiled=True)
    o = pl.pallas_call(
        functools.partial(finish_kernel, p),
        out_shape=jax.ShapeDtypeStruct((p.rows_in, LN), jnp.float32),
        scratch_shapes=[pltpu.VMEM((p.slot + 32, LN), jnp.float32)],
    )(mine)
    return o.reshape(-1)[: p.sh]

EPS = 1e-05
F32 = jnp.float32
BF = jnp.bfloat16
SQ = math.sqrt(0.5)
PHI = 1.0 / math.sqrt(2.0 * math.pi)
VNAMES = (
    ("q_bias", D),
    ("v_bias", D),
    ("out_bias", D),
    ("first_gain", D),
    ("first_shift", D),
    ("up_bias", FF),
    ("down_bias", D),
    ("second_gain", D),
    ("second_shift", D),
    ("exit_gain", D),
    ("exit_shift", D),
)
VI = {name: k for k, (name, _) in enumerate(VNAMES)}
PREFIXES = (D, E2, E3, E4, E5)
SCALE = 1.0 / math.sqrt(HD)
UP = 768


def mm(a, b):
    return jnp.dot(a, b, preferred_element_type=F32)


def mm_nt(a, b):
    return lax.dot_general(a, b, (((1,), (1,)), ((), ())), preferred_element_type=F32)


def mm_tn(a, b):
    return lax.dot_general(a, b, (((0,), (0,)), ((), ())), preferred_element_type=F32)


def vrow(V, name):
    k = VI[name]
    return V[k : k + 1, : VNAMES[k][1]]


def mean_last(a):
    return jnp.mean(a, axis=-1, keepdims=True)


def sum_rows(a):
    return jnp.sum(a, axis=0, keepdims=True)


def forward_qkv(r):
    bias = jnp.concatenate([vrow(r.V, "q_bias"), jnp.zeros((1, D), F32), vrow(r.V, "v_bias")], axis=1)
    r.qb[...] = bias

    def body(j, _):
        o = pl.ds(pl.multiple_of(j * D, D), D)
        r.qkv[:, o] = (mm(r.tok[...], r.wqkv[:, o]) + r.qb[:, o]).astype(BF)
        return 0

    lax.fori_loop(0, 3, body, 0)


def half_lanes(h):
    lane = lax.broadcasted_iota(jnp.int32, (LEN, LN), 1)
    return lane < HD if h == 0 else lane >= HD


def pair(r, part, hp):
    return r.qkv[:, pl.ds(pl.multiple_of(part * D + hp * LN, LN), LN)]


def forward_heads(r, hp):
    q, k, v = pair(r, 0, hp) * SCALE, pair(r, 1, hp), pair(r, 2, hp)
    valid = lax.broadcasted_iota(jnp.int32, (1, LEN), 1) < r.length
    out = None
    lse_all = r.lse[...]
    lane = lax.broadcasted_iota(jnp.int32, (LEN, LN), 1)
    for h in range(2):
        qh = jnp.where(half_lanes(h), q, jnp.zeros_like(q))
        s = jnp.where(valid, mm_nt(qh, k), -1e9)
        m = jnp.max(s, axis=1, keepdims=True)
        e = jnp.exp(s - m)
        l = jnp.sum(e, axis=1, keepdims=True)
        low = (e * (1.0 / l)).astype(BF)
        o = mm(low, v)
        out = o if out is None else jnp.where(half_lanes(0), out, o)
        lse_all = jnp.where(lane == 2 * hp + h, m + jnp.log(l), lse_all)
    r.lse[...] = lse_all
    r.mixed[:, pl.ds(pl.multiple_of(hp * LN, LN), LN)] = out.astype(BF)


def rows_of(b, n):
    return pl.ds(pl.multiple_of(b * n, n), n)


def forward_first(r):
    def body(b, _):
        o = rows_of(b, LEN)
        v = r.tok[o, :].astype(F32) + mm(r.mixed[o, :], r.wo[...]) + vrow(r.V, "out_bias")
        cen = v - mean_last(v)
        rstd = lax.rsqrt(mean_last(cen * cen) + EPS)
        xh = cen * rstd
        r.xh1[o, :] = xh
        r.rstd1[o, :] = rstd
        r.first_low[o, :] = (xh * vrow(r.V, "first_gain") + vrow(r.V, "first_shift")).astype(BF)
        return 0

    lax.fori_loop(0, 1, body, 0)


def forward_up(r, j):
    o = pl.ds(pl.multiple_of(j * UP, UP), UP)
    v = mm(r.first_low[...], r.w1[:, o]) + r.V[VI["up_bias"] : VI["up_bias"] + 1, o]
    cdf = 0.5 * (1.0 + lax.erf(v * SQ))
    r.act[:, o] = (v * cdf).astype(BF)
    r.gd[:, o] = (cdf + v * (PHI * jnp.exp(-0.5 * v * v))).astype(BF)


def forward_second(r):
    def body(b, tot):
        o = rows_of(b, LEN)
        first = r.xh1[o, :] * vrow(r.V, "first_gain") + vrow(r.V, "first_shift")
        v = first + mm(r.act[o, :], r.w2[...]) + vrow(r.V, "down_bias")
        cen = v - mean_last(v)
        rstd = lax.rsqrt(mean_last(cen * cen) + EPS)
        xh = cen * rstd
        r.xh2[o, :] = xh
        r.rstd2[o, :] = rstd
        t = lax.broadcasted_iota(jnp.int32, (LEN, 1), 0)
        hid = (xh * vrow(r.V, "second_gain") + vrow(r.V, "second_shift")) * (t < r.length).astype(F32)
        r.hidden[o, :] = hid.astype(BF)
        return tot + sum_rows(hid)

    return lax.fori_loop(0, 1, body, jnp.zeros((1, D), F32))


def head(r, tot):
    inv_len = 1.0 / jnp.full((1, 1), r.length, jnp.int32).astype(F32)
    pooled = tot * inv_len
    cen = pooled - mean_last(pooled)
    rstd = lax.rsqrt(mean_last(cen * cen) + EPS)
    xh = cen * rstd
    gain = vrow(r.V, "exit_gain")
    emb = xh * gain + vrow(r.V, "exit_shift")
    d_emb = jnp.zeros((1, D), F32)
    at = 0
    for m in PREFIXES:
        e = emb[:, :m]
        inv = lax.rsqrt(jnp.sum(e * e, axis=1, keepdims=True) * (1.0 / m) + EPS)
        out = e * inv
        r.nested[:, at : at + m] = out
        c = r.ncot[:, at : at + m]
        g = inv * (c - out * (jnp.sum(c * out, axis=1, keepdims=True) * (1.0 / m)))
        d_emb = d_emb + (g if m == D else jnp.concatenate([g, jnp.zeros((1, D - m), F32)], axis=1))
        at += m
    put_grad(r, "exit_gain", d_emb * xh)
    put_grad(r, "exit_shift", d_emb)
    dx = d_emb * gain
    return rstd * (dx - mean_last(dx) - xh * mean_last(dx * xh)) * inv_len


def put_grad(r, name, value):
    k = VI[name]
    r.VG[k : k + 1, : VNAMES[k][1]] = value


def norm_back(dy, gain, xh, rstd):
    dx = dy * gain
    return rstd * (dx - mean_last(dx) - xh * mean_last(dx * xh))


def backward_second(r, d_pool):
    def body(b, c):
        o = rows_of(b, LEN)
        t = lax.broadcasted_iota(jnp.int32, (LEN, 1), 0)
        dy = (r.hcot[o, :].astype(F32) + d_pool) * (t < r.length).astype(F32)
        xh = r.xh2[o, :]
        res = norm_back(dy, vrow(r.V, "second_gain"), xh, r.rstd2[o, :])
        r.res[o, :] = res
        low = res.astype(BF)
        r.d_outer[o, :] = low
        return (c[0] + sum_rows(dy * xh), c[1] + sum_rows(dy), c[2] + sum_rows(low.astype(F32)))

    z = jnp.zeros((1, D), F32)
    a, b, c = lax.fori_loop(0, 1, body, (z, z, z))
    put_grad(r, "second_gain", a)
    put_grad(r, "second_shift", b)
    put_grad(r, "down_bias", c)


def backward_act(r, j):
    o = pl.ds(pl.multiple_of(j * UP, UP), UP)
    d = (mm_nt(r.d_outer[...], r.w2[o, :]) * r.gd[:, o].astype(F32)).astype(BF)
    r.gd[:, o] = d
    r.VG[VI["up_bias"] : VI["up_bias"] + 1, o] = sum_rows(d.astype(F32))


def backward_first(r):
    def body(b, c):
        o = rows_of(b, LEN)
        dy = mm_nt(r.gd[o, :], r.w1[...]) + r.res[o, :]
        xh = r.xh1[o, :]
        res = norm_back(dy, vrow(r.V, "first_gain"), xh, r.rstd1[o, :])
        r.res[o, :] = res
        low = res.astype(BF)
        r.d_branch[o, :] = low
        return (c[0] + sum_rows(dy * xh), c[1] + sum_rows(dy), c[2] + sum_rows(low.astype(F32)))

    z = jnp.zeros((1, D), F32)
    a, b, c = lax.fori_loop(0, 1, body, (z, z, z))
    put_grad(r, "first_gain", a)
    put_grad(r, "first_shift", b)
    put_grad(r, "out_bias", c)


def backward_mixed(r):
    r.d_mixed[...] = mm_nt(r.d_branch[...], r.wo[...]).astype(BF)


def backward_heads(r, hp):
    q, k, v = pair(r, 0, hp) * SCALE, pair(r, 1, hp), pair(r, 2, hp)
    k_scaled = k * SCALE
    cols = pl.ds(pl.multiple_of(hp * LN, LN), LN)
    dm = r.d_mixed[:, cols]
    valid = lax.broadcasted_iota(jnp.int32, (1, LEN), 1) < r.length
    lane = lax.broadcasted_iota(jnp.int32, (LEN, LN), 1)
    zero = jnp.zeros_like(q)
    dm_mixed = dm.astype(F32) * r.mixed[:, cols].astype(F32)
    dq = dk = dv = None
    for h in range(2):
        here = half_lanes(h)
        qh, kh, dmh = jnp.where(here, q, zero), jnp.where(here, k_scaled, zero), jnp.where(here, dm, zero)
        lse = jnp.sum(jnp.where(lane == 2 * hp + h, r.lse[...], 0.0), axis=1, keepdims=True)
        s = jnp.where(valid, mm_nt(qh, k), -1e9)
        p = jnp.exp(s - lse)
        dp = mm_nt(dmh, v)
        delta = jnp.sum(jnp.where(here, dm_mixed, 0.0), axis=1, keepdims=True)
        ds = (p * (dp - delta)).astype(BF)
        a, b, c = mm(ds, kh), mm_tn(ds, qh), mm_tn(p.astype(BF), dmh)
        dq, dk, dv = (a, b, c) if dq is None else (dq + a, dk + b, dv + c)
    dq, dk, dv = dq.astype(BF), dk.astype(BF), dv.astype(BF)
    for part, g in ((0, dq), (1, dk), (2, dv)):
        r.dqkv[:, pl.ds(pl.multiple_of(part * D + hp * LN, LN), LN)] = g
    k = VI["q_bias"]
    r.VG[k : k + 1, cols] = sum_rows(dq.astype(F32))
    k = VI["v_bias"]
    r.VG[k : k + 1, cols] = sum_rows(dv.astype(F32))


def backward_tokens(r, b):
    o = rows_of(b, 128)
    v = r.res[o, :]
    for part in range(3):
        v = v + mm_nt(r.dqkv[o, part * D : (part + 1) * D], r.wqkv[:, part * D : (part + 1) * D])
    r.res[o, :] = v


EDGES = ((13824, 16), (18432, 32), (36880, 48), (55344, 64))


def edge_at(row):
    at = 0
    for base, rows in EDGES:
        if base <= row < base + rows:
            return at + row - base
        at += rows
    return None


def weight_grad(r, lhs, rhs, base, rows, w, RB=256, CB=6, hook=None):
    lead = base % 16
    step_rows = RB * w
    F = r.F
    if lead:
        F[0:16] = jnp.zeros((16, LN), F32)

    def body(s, _):
        o = pl.ds(pl.multiple_of(s * RB, RB), RB)
        for ch in range(w // CB):
            g = mm_tn(lhs[:, o], rhs[:, ch * CB * LN : (ch + 1) * CB * LN])
            for j in range(CB):
                F[pl.ds(lead + ch * CB + j, RB, stride=w), :] = g[:, j * LN : (j + 1) * LN]
        if lead:
            @pl.when(s == 0)
            def _():
                e = edge_at(base)
                r.E[e : e + 16 - lead] = F[lead:16]

        U = 256
        to = base - lead + s * step_rows

        def emit(t, _):
            r.FG[pl.ds(pl.multiple_of(to + t * U, 16), U)] = F[pl.ds(pl.multiple_of(t * U, 16), U)].astype(BF)
            return 0

        lax.fori_loop(0, step_rows // U, emit, 0)
        if lead:
            F[0:16] = F[step_rows : step_rows + 16]
        if hook is not None:
            hook(s)
        return 0

    lax.fori_loop(0, rows // RB, body, 0)
    if lead:
        e = edge_at(base + rows * w - lead)
        r.E[e : e + lead] = F[0:lead]


def edge_grads(r, which):
    base, rows = EDGES[which]
    at = 0
    for vbase, cnt in VECS:
        for k in range(cnt):
            row = vbase + k
            if base <= row < base + rows:
                name, j = vec_at(at + k)
                e = edge_at(row)
                r.E[e : e + 1] = r.VG[name : name + 1, j * LN : (j + 1) * LN]
        at += cnt
    if which == len(EDGES) - 1:
        e = edge_at(TOT)
        r.E[e : e + base + rows - TOT] = jnp.zeros((base + rows - TOT, LN), F32)
    e = edge_at(base)
    r.FG[base : base + rows] = r.E[e : e + rows].astype(BF)


def vec_at(row):
    for k, (_, n) in enumerate(VNAMES):
        if row < n // LN:
            return k, row
        row -= n // LN


class Refs:
    def __init__(self, **refs):
        self.__dict__.update(refs)


def relayout_vectors(p, r):
    at = 0
    for base, cnt in VECS:
        g_lo = base // 16
        g_hi = -(-(base + cnt) // 16)
        load_flat(p, r.slots, r.F, g_lo, g_hi)
        for k in range(cnt):
            name, j = vec_at(at + k)
            f = base - 16 * g_lo + k
            r.V[name : name + 1, j * LN : (j + 1) * LN] = r.F[f : f + 1]
        at += cnt


def relayout_matrix(p, r, name, W, RB):
    base, rows, w = {n: (b, k, c) for n, b, k, c in MATS}[name]
    for s in range(rows // RB):
        lo = base + s * RB * w
        g_lo = lo // 16
        load_flat(p, r.slots, r.F, g_lo, -(-(lo + RB * w) // 16))
        tile_rows(r.F, W, lo - 16 * g_lo, s * RB, RB, w)


def tile_rows(F, W, off, row, rows, w, RB=64):
    def body(t, _):
        q = pl.multiple_of(t * RB, RB)
        for j in range(w):
            W[pl.ds(row + q, RB), j * LN : (j + 1) * LN] = F[pl.ds(off + q * w + j, RB, stride=w), :].astype(BF)
        return 0

    lax.fori_loop(0, rows // RB, body, 0)


def forward_kernel(p, slots, length, tok, hcot, ncot, hidden, nested, wqkv, wo, w1, w2, V, VG, qkv, lse, mixed, xh1, rstd1, first_low, act, gd, res, d_outer, F, qb, xh2, rstd2):
    r = Refs(slots=slots, length=length[0], tok=tok, hcot=hcot, ncot=ncot, hidden=hidden, nested=nested, wqkv=wqkv, wo=wo, w1=w1, w2=w2, V=V, VG=VG, qkv=qkv, lse=lse, mixed=mixed, xh1=xh1, rstd1=rstd1, first_low=first_low, act=act, gd=gd, res=res, d_outer=d_outer, F=F, qb=qb, xh2=xh2, rstd2=rstd2)
    relayout_vectors(p, r)
    relayout_matrix(p, r, "wqkv", wqkv, 256)
    forward_qkv(r)
    lse[...] = jnp.zeros_like(lse)
    lax.fori_loop(0, H // 2, lambda hp, c: (forward_heads(r, hp), c)[1], 0)
    relayout_matrix(p, r, "wo", wo, 768)
    forward_first(r)
    relayout_matrix(p, r, "w1", w1, 256)
    lax.fori_loop(0, FF // UP, lambda j, c: (forward_up(r, j), c)[1], 0)
    relayout_matrix(p, r, "w2", w2, 768)
    tot = forward_second(r)
    d_pool = head(r, tot)
    backward_second(r, d_pool)


def forward_local(p, slots, length, tok, hcot, ncot):
    S = jax.ShapeDtypeStruct
    outs = [S((LEN, D), BF), S((1, 1728), F32), S((D, 3 * D), BF), S((D, D), BF), S((D, FF), BF), S((FF, D), BF), S((16, FF), F32), S((16, FF), F32), S((LEN, 3 * D), BF), S((LEN, LN), F32), S((LEN, D), BF), S((LEN, D), F32), S((LEN, 1), F32), S((LEN, D), BF), S((LEN, FF), BF), S((LEN, FF), BF), S((LEN, D), F32), S((LEN, D), BF)]
    vm = pl.BlockSpec(memory_space=pltpu.VMEM)
    sm = pl.BlockSpec(memory_space=pltpu.SMEM)
    return pl.pallas_call(
        functools.partial(forward_kernel, p),
        out_shape=outs,
        in_specs=[vm, sm, vm, vm, vm],
        scratch_shapes=[pltpu.VMEM((6144 + 32, LN), F32), pltpu.VMEM((1, 3 * D), F32), pltpu.VMEM((LEN, D), F32), pltpu.VMEM((LEN, 1), F32)],
        compiler_params=pltpu.CompilerParams(vmem_limit_bytes=60 << 20),
    )(slots, length, tok, hcot, ncot)


def backward_kernel(p, length, tok, V, VG0, qkv, lse, mixed, xh1, rstd1, first_low, act, gd, res, d_outer, wqkv, wo, w1, w2, igrad, FG, VG, d_branch, d_mixed, dqkv, F, E):
    r = Refs(length=length[0], tok=tok, V=V, VG=VG, qkv=qkv, lse=lse, mixed=mixed, xh1=xh1, rstd1=rstd1, first_low=first_low, act=act, gd=gd, res=igrad, d_outer=d_outer, wqkv=wqkv, wo=wo, w1=w1, w2=w2, FG=FG, d_branch=d_branch, d_mixed=d_mixed, dqkv=dqkv, F=F, E=E)
    VG[...] = VG0[...]
    igrad[...] = res[...]
    mats = {n: (b, k, c) for n, b, k, c in MATS}
    weight_grad(r, act, d_outer, *mats["w2"], RB=1024, CB=2)
    edge_grads(r, 3)
    lax.fori_loop(0, FF // UP, lambda j, c: (backward_act(r, j), c)[1], 0)
    weight_grad(r, first_low, gd, *mats["w1"])
    edge_grads(r, 2)
    backward_first(r)
    weight_grad(r, mixed, d_branch, *mats["wo"])
    edge_grads(r, 1)
    backward_mixed(r)
    lax.fori_loop(0, H // 2, lambda hp, c: (backward_heads(r, hp), c)[1], 0)
    weight_grad(r, tok, dqkv, *mats["wqkv"])
    edge_grads(r, 0)
    lax.fori_loop(0, LEN // 128, lambda b, c: (backward_tokens(r, b), c)[1], 0)


def backward_local(p, length, tok, V, VG, qkv, lse, mixed, xh1, rstd1, first_low, act, gd, res, d_outer, wqkv, wo, w1, w2):
    S = jax.ShapeDtypeStruct
    vm = pl.BlockSpec(memory_space=pltpu.VMEM)
    sm = pl.BlockSpec(memory_space=pltpu.SMEM)
    return pl.pallas_call(
        functools.partial(backward_kernel, p),
        out_shape=[S((LEN, D), F32), S((flat_rows(p), LN), BF)],
        in_specs=[sm] + [vm] * 17,
        scratch_shapes=[pltpu.VMEM((16, FF), F32), pltpu.VMEM((LEN, D), BF), pltpu.VMEM((LEN, D), BF), pltpu.VMEM((LEN, 3 * D), BF), pltpu.VMEM((6144 + 32, LN), F32), pltpu.VMEM((160, LN), F32)],
        compiler_params=pltpu.CompilerParams(vmem_limit_bytes=60 << 20),
    )(length, tok, V, VG, qkv, lse, mixed, xh1, rstd1, first_low, act, gd, res, d_outer, wqkv, wo, w1, w2)


class Gather:
    def __init__(self, p, G, ssem, rsem, gosem):
        self.p, self.G, self.ssem, self.rsem, self.gosem = p, G, ssem, rsem, gosem
        self.x, self.y, self.z, self.c = coords()
        x, y, z, c = self.x, self.y, self.z, self.c
        self.me = lin(x, y, z, c)
        half = p.slot // 32 * 16
        self.H = ((0, half), (half, p.slot - half), (0, p.slot))
        self.px, self.py, self.pc = dev(1 - x, y, z, c), dev(x, 1 - y, z, c), dev(x, y, z, 1 - c)

    def enter(self):
        x, y, z, c = self.x, self.y, self.z, self.c
        bar = pltpu.get_barrier_semaphore()

        def greet(to):
            pl.semaphore_signal(bar, inc=1, device_id=to, device_id_type=MESH)

        for to in (self.px, self.py, self.pc):
            greet(to)
        pl.when(z > 0)(lambda: greet(dev(x, y, z - 1, c)))
        pl.when(z < 3)(lambda: greet(dev(x, y, z + 1, c)))
        middle = (z > 0) & (z < 3)
        pl.when(middle)(lambda: pl.semaphore_wait(bar, 5))
        pl.when(jnp.logical_not(middle))(lambda: pl.semaphore_wait(bar, 4))

    def send(self, sl, h, to, t):
        r0, rn = self.H[h]
        ref = self.G.at[sl, pl.ds(r0, rn)]
        pltpu.make_async_remote_copy(src_ref=ref, dst_ref=ref, send_sem=self.ssem.at[sl, t], recv_sem=self.rsem.at[sl, h], device_id=to, device_id_type=MESH).start()

    def wait(self, sl, h, sem=None):
        r0, rn = self.H[h]
        ref = self.G.at[sl, pl.ds(r0, rn)]
        pltpu.make_async_copy(ref, ref, self.rsem.at[sl, h] if sem is None else sem).wait()

    def up(self, sl, h):
        pl.when(self.z < 3)(lambda: self.send(sl, h, dev(self.x, self.y, self.z + 1, self.c), 3))

    def down(self, sl, h):
        pl.when(self.z > 0)(lambda: self.send(sl, h, dev(self.x, self.y, self.z - 1, self.c), 4))

    def core(self, sl, h):
        self.send(sl, h, self.pc, 2)

    def xy(self, sl):
        self.send(sl, 0, self.px, 0)
        self.send(sl, 1, self.py, 1)
        self.send(sl, 1, self.px, 0)
        self.send(sl, 0, self.py, 1)

    def own(self, xy):
        for h in (0, 1):
            self.up(self.me, h)
            self.down(self.me, h)
        if xy:
            self.xy(self.me)
        for h in (0, 1):
            self.core(self.me, h)

    def own_line(self, k):
        self.at(k, lambda zq: self.xy(lin(self.x, self.y, zq, self.c)))

    def go(self, k):
        pl.semaphore_signal(self.gosem.at[k], inc=1, device_id=self.pc, device_id_type=MESH)

    def wait_go(self, k):
        pl.semaphore_wait(self.gosem.at[k], 1)

    def at(self, k, fn):
        if k == 0:
            fn(self.z)
            return
        pl.when(self.z - k >= 0)(lambda: fn(self.z - k))
        pl.when(self.z + k <= 3)(lambda: fn(self.z + k))

    def along_z(self, k, xy):
        x, y, z, c = self.x, self.y, self.z, self.c

        def from_level(zq, on):
            sl = lin(x, y, zq, c)
            self.wait(sl, 0)
            on(sl, 0)
            if xy:
                self.send(sl, 0, self.px, 0)
            self.core(sl, 0)
            self.wait(sl, 1)
            on(sl, 1)
            if xy:
                self.send(sl, 1, self.py, 1)
                self.send(sl, 1, self.px, 0)
                self.send(sl, 0, self.py, 1)
            self.core(sl, 1)

        pl.when(z - k >= 0)(lambda: from_level(z - k, self.up))
        pl.when(z + k <= 3)(lambda: from_level(z + k, self.down))

    def sides(self, k):
        x, y, c = self.x, self.y, self.c

        def fn(zq):
            sl = lin(1 - x, y, zq, c)
            self.wait(sl, 0)
            self.send(sl, 0, self.py, 1)
            self.core(sl, 0)
            sl = lin(x, 1 - y, zq, c)
            self.wait(sl, 1)
            self.send(sl, 1, self.px, 0)
            self.core(sl, 1)

        self.at(k, fn)

    def sides_rest(self, k):
        x, y, c = self.x, self.y, self.c

        def fn(zq):
            sl = lin(1 - x, y, zq, c)
            self.wait(sl, 1)
            self.core(sl, 1)
            sl = lin(x, 1 - y, zq, c)
            self.wait(sl, 0)
            self.core(sl, 0)

        self.at(k, fn)

    def diagonal(self, k):
        def fn(zq):
            sl = lin(1 - self.x, 1 - self.y, zq, self.c)
            for h in (0, 1):
                self.wait(sl, h)
                self.core(sl, h)

        self.at(k, fn)

    def from_sibling(self, xp):
        def body(fs, carry):
            for h in (0, 1):
                self.wait((2 * xp + 1 - self.c) * 8 + fs, h)
            return carry

        lax.fori_loop(0, 8, body, 0)

    def leave(self):
        x, y, z, c = self.x, self.y, self.z, self.c
        W = self.wait

        def body(zq, carry):
            sl = lin(x, y, zq, c)
            for t in (0, 1, 2):
                W(sl, 2, self.ssem.at[sl, t])
            pl.when((zq <= z) & (z < 3))(lambda: W(sl, 2, self.ssem.at[sl, 3]))
            pl.when((zq >= z) & (z > 0))(lambda: W(sl, 2, self.ssem.at[sl, 4]))
            sx = lin(1 - x, y, zq, c)
            W(sx, 0, self.ssem.at[sx, 1])
            W(sx, 2, self.ssem.at[sx, 2])
            sy = lin(x, 1 - y, zq, c)
            W(sy, 1, self.ssem.at[sy, 0])
            W(sy, 2, self.ssem.at[sy, 2])
            sd = lin(1 - x, 1 - y, zq, c)
            W(sd, 2, self.ssem.at[sd, 2])
            return carry

        lax.fori_loop(0, 4, body, 0)


FORWARD_OUT = ("hidden", "nested", "wqkv", "wo", "w1", "w2", "V", "VG", "qkv", "lse", "mixed", "xh1", "rstd1", "first_low", "act", "gd", "res", "d_outer")
FORWARD_SHAPES = dict(
    hidden=((LEN, D), jnp.bfloat16),
    nested=((1, 1728), jnp.float32),
    wqkv=((D, 3 * D), jnp.bfloat16),
    wo=((D, D), jnp.bfloat16),
    w1=((D, FF), jnp.bfloat16),
    w2=((FF, D), jnp.bfloat16),
    V=((16, FF), jnp.float32),
    VG=((16, FF), jnp.float32),
    qkv=((LEN, 3 * D), jnp.bfloat16),
    lse=((LEN, LN), jnp.float32),
    mixed=((LEN, D), jnp.bfloat16),
    xh1=((LEN, D), jnp.float32),
    rstd1=((LEN, 1), jnp.float32),
    first_low=((LEN, D), jnp.bfloat16),
    act=((LEN, FF), jnp.bfloat16),
    gd=((LEN, FF), jnp.bfloat16),
    res=((LEN, D), jnp.float32),
    d_outer=((LEN, D), jnp.bfloat16),
)


def own_slot(p, me, x_ref, F, G):
    start = me * p.sh
    r_first = start // LN
    s = start - r_first * LN
    r0 = r_first % 16
    lead = 32
    F[0 : lead + p.slot + 32] = jnp.zeros((lead + p.slot + 32, LN), F32)
    full = p.sh // LN
    rest = p.sh - full * LN
    F[lead : lead + full] = x_ref[: full * LN].astype(F32).reshape(full, LN)
    if rest:
        F[lead + full : lead + full + 1, :rest] = x_ref[full * LN :].astype(F32).reshape(1, rest)
    F[lead : lead + p.rows_in] = pltpu.roll(F[lead : lead + p.rows_in], s, 1)
    lane = lax.broadcasted_iota(jnp.int32, (p.slot, LN), 1)
    G[me] = jnp.where(lane >= s, F[pl.ds(lead - r0, p.slot), :], F[pl.ds(lead - 1 - r0, p.slot), :]).astype(BF)


def relayout_vector(p, r, which):
    at = sum(cnt for _, cnt in VECS[:which])
    base, cnt = VECS[which]
    g_lo = base // 16
    load_flat(p, r.slots, r.F, g_lo, -(-(base + cnt) // 16), base + cnt)
    for k in range(cnt):
        name, j = vec_at(at + k)
        f = base - 16 * g_lo + k
        r.V[name : name + 1, j * LN : (j + 1) * LN] = r.F[f : f + 1]


def relayout_rows(p, r, name, W, row, rows):
    base, _, w = {n: (b, k, c) for n, b, k, c in MATS}[name]
    lo = base + row * w
    g_lo = lo // 16
    load_flat(p, r.slots, r.F, g_lo, -(-(lo + rows * w) // 16), lo + rows * w)
    tile_rows(r.F, W, lo - 16 * g_lo, row, rows, w)


def gather_forward_kernel(p, x_ref, length, tok, hcot, ncot, *refs):
    n = len(FORWARD_OUT)
    outs = dict(zip(FORWARD_OUT, refs[:n]))
    loc = dict(zip(FORWARD_OUT, refs[n : 2 * n]))
    G, F, qb, xh2, rstd2, ssem, rsem, gosem, osem = refs[2 * n :]
    r = Refs(slots=G, length=length[0], tok=tok, hcot=hcot, ncot=ncot, F=F, qb=qb, xh2=xh2, rstd2=rstd2, **loc)
    g = Gather(p, G, ssem, rsem, gosem)
    own_slot(p, g.me, x_ref, F, G)
    g.enter()
    c0, c1 = g.c == 0, g.c == 1

    started = []

    def out(*names):
        for m in names:
            k = FORWARD_OUT.index(m)
            cp = pltpu.make_async_copy(loc[m], outs[m], osem.at[k])
            cp.start()
            started.append(cp)

    def part_rq_0():
        g.own(True)
        g.sides(0)
        g.go(0)
        g.along_z(1, True)
        g.sides(1)
        g.sides_rest(0)
        g.diagonal(0)
        g.go(1)
        g.along_z(2, True)
        g.sides(2)
        g.along_z(3, True)
        g.diagonal(1)
        g.sides_rest(1)
        g.sides(3)
        g.sides_rest(3)
        g.diagonal(2)
        g.sides_rest(2)
        g.diagonal(3)

    pl.when(c0)(part_rq_0)
    def part_rq_1():
        g.wait_go(0)
        g.own(False)
        g.wait_go(1)
        g.own_line(0)
        g.along_z(1, False)
        g.sides(0)
        g.along_z(2, False)
        g.own_line(1)
        g.along_z(3, False)
        g.own_line(3)
        g.own_line(2)
        g.from_sibling(0)
        g.sides(3)
        g.sides_rest(0)
        g.diagonal(0)

    pl.when(c1)(part_rq_1)
    relayout_vector(p, r, 0)
    for k in range(3):
        relayout_rows(p, r, "wqkv", r.wqkv, 256 * k, 256)
    out("wqkv")
    def part_qkv_1():
        g.from_sibling(1)
        g.sides(1)

    pl.when(c1)(part_qkv_1)
    forward_qkv(r)
    out("qkv")
    r.lse[...] = jnp.zeros_like(r.lse)

    def heads(hp, carry):
        def part_hd0_1():
            g.sides_rest(1)
            g.sides(2)
            g.sides_rest(3)

        pl.when((hp == 0) & c1)(part_hd0_1)
        def part_hd3_1():
            g.sides_rest(2)
            g.diagonal(3)

        pl.when((hp == 3) & c1)(part_hd3_1)
        def part_hd5_1():
            g.diagonal(1)

        pl.when((hp == 5) & c1)(part_hd5_1)
        forward_heads(r, hp)
        return carry

    lax.fori_loop(0, H // 2, heads, 0)
    out("lse", "mixed")
    def part_rw1b_1():
        g.diagonal(2)

    pl.when(c1)(part_rw1b_1)
    relayout_rows(p, r, "w1", r.w1, 448, 128)
    relayout_rows(p, r, "w1", r.w1, 576, 192)
    relayout_rows(p, r, "w2", r.w2, 0, 768)
    relayout_vector(p, r, 2)
    def part_rwo_0():
        g.from_sibling(0)

    pl.when(c0)(part_rwo_0)
    relayout_rows(p, r, "wo", r.wo, 0, 768)
    relayout_vector(p, r, 1)
    out("wo")
    forward_first(r)
    out("xh1", "rstd1", "first_low")
    def part_rw1a_0():
        g.from_sibling(1)

    pl.when(c0)(part_rw1a_0)
    relayout_rows(p, r, "w1", r.w1, 0, 256)
    relayout_rows(p, r, "w1", r.w1, 256, 192)
    out("w1")
    lax.fori_loop(0, FF // UP, lambda j, c: (forward_up(r, j), c)[1], 0)
    out("act", "gd")
    for k in range(1, 4):
        relayout_rows(p, r, "w2", r.w2, 768 * k, 768)
    relayout_vector(p, r, 3)
    out("w2", "V")
    tot = forward_second(r)
    out("hidden")
    d_pool = head(r, tot)
    out("nested")
    backward_second(r, d_pool)
    out("VG", "res", "d_outer")
    g.leave()
    for cp in started:
        cp.wait()


def gather_forward(p, shard, length, tok, hcot, ncot):
    S = jax.ShapeDtypeStruct
    vm = pl.BlockSpec(memory_space=pltpu.VMEM)
    sm = pl.BlockSpec(memory_space=pltpu.SMEM)
    hbm = pl.BlockSpec(memory_space=pl.ANY)
    VM = pltpu.VMEM
    DM = pltpu.SemaphoreType.DMA
    shapes = [FORWARD_SHAPES[m] for m in FORWARD_OUT]
    res = pl.pallas_call(
        functools.partial(gather_forward_kernel, p),
        out_shape=[S(*s) for s in shapes],
        in_specs=[vm, sm, vm, vm, vm],
        out_specs=[hbm] * len(shapes),
        scratch_shapes=[VM(*s) for s in shapes]
        + [VM((p.n, p.slot, LN), BF), VM((6144 + 32, LN), F32), VM((1, 3 * D), F32), VM((LEN, D), F32), VM((LEN, 1), F32)]
        + [DM((p.n, 5)), DM((p.n, 2)), pltpu.SemaphoreType.REGULAR((2,)), DM((len(shapes),))],
        compiler_params=pltpu.CompilerParams(collective_id=0, has_side_effects=True, vmem_limit_bytes=64 << 20),
    )(shard, length, tok, hcot, ncot)
    return dict(zip(FORWARD_OUT, res))


SCHEDULE = (
    (4, 1, 0, "diag", 1, 2, 1),
    (5, 1, 0, "diag", 1, 1, 1),
    (8, 1, 1, "yline", 1, 2, 1),
    (8, 1, 0, "xline", 1, 1, 1),
    (10, 1, 1, "yline", 1, 1, 1),
    (10, 1, 0, "diag", 1, 3, 1),
    (10, 0, 0, "diag", 1, 0, 1),
    (11, 0, 0, "diag", 1, 2, 2),
    (12, 1, 1, "diag", 0, 0, 1),
    (12, 0, 0, "diag", 1, 1, 1),
    (13, 1, 1, "diag", 0, 2, 1),
    (13, 1, 1, "diag", 0, 1, 1),
    (13, 1, 0, "yline", 0, 2, 1),
    (14, 1, 1, "diag", 0, 3, 1),
    (14, 0, 0, "xline", 1, 2, 1),
    (15, 0, 1, "yline", 1, 3, 1),
    (16, 1, 1, "xline", 0, 2, 1),
    (16, 0, 0, "xline", 1, 1, 1),
    (16, 1, 0, "yline", 0, 1, 1),
    (17, 1, 1, "own", 1, 1, 1),
    (17, 0, 1, "yline", 1, 2, 1),
    (18, 0, 0, "xline", 1, 0, 1),
    (18, 0, 1, "yline", 1, 1, 1),
    (18, 1, 1, "xline", 0, 1, 1),
    (18, 1, 0, "yline", 0, 3, 1),
    (19, 1, 0, "own", 0, 2, 1),
    (19, 1, 1, "xline", 0, 0, 1),
    (20, 0, 0, "yline", 0, 1, 1),
    (20, 0, 1, "diag", 0, 1, 2),
    (20, 0, 0, "yline", 0, 0, 1),
    (20, 0, 1, "own", 1, 2, 1),
    (20, 1, 0, "xline", 1, 2, 1),
    (21, 1, 1, "yline", 1, 0, 1),
    (21, 0, 1, "diag", 0, 0, 1),
    (21, 0, 1, "own", 1, 1, 1),
    (21, 1, 0, "diag", 1, 0, 1),
    (21, 0, 0, "own", 0, 1, 1),
    (21, 1, 0, "xline", 1, 3, 1),
    (22, 1, 0, "yline", 0, 0, 1),
    (22, 1, 0, "own", 0, 1, 1),
    (22, 1, 0, "own", 0, 0, 1),
    (22, 0, 0, "yline", 0, 2, 1),
    (22, 0, 1, "xline", 0, 1, 1),
    (22, 0, 0, "xline", 1, 3, 1),
    (22, 0, 1, "yline", 1, 0, 1),
    (22, 1, 1, "own", 1, 0, 1),
    (22, 0, 1, "xline", 0, 0, 1),
    (22, 0, 1, "xline", 0, 2, 1),
    (22, 0, 0, "own", 0, 0, 1),
    (22, 0, 0, "own", 0, 2, 1),
    (22, 0, 0, "yline", 0, 3, 1),
    (22, 0, 1, "diag", 0, 3, 1),
    (22, 0, 1, "own", 1, 0, 1),
    (22, 0, 1, "xline", 0, 3, 1),
    (22, 1, 0, "xline", 1, 0, 1),
    (22, 1, 1, "own", 1, 2, 1),
    (22, 1, 1, "xline", 0, 3, 1),
    (22, 1, 1, "yline", 1, 3, 1),
)


class Scatter:
    def __init__(self, p, FG, R, D0, D1, X, Y, Z, A, sems):
        self.p, self.FG, self.R, self.D0, self.D1, self.X, self.Y, self.Z, self.A = p, FG, R, D0, D1, X, Y, Z, A
        self.sib_s, self.sib_r, self.d_s, self.d_r, self.x_s, self.x_r, self.y_s, self.y_r, self.z_s, self.z_r = sems
        self.x, self.y, self.z, self.c = coords()
        x, y, z, c = self.x, self.y, self.z, self.c
        self.SL = p.slot
        self.half = p.slot // 32 * 16
        self.px, self.py, self.pc = dev(1 - x, y, z, c), dev(x, 1 - y, z, c), dev(x, y, z, 1 - c)

    def zq(self, b):
        d = lax.rem(b + 1, 4)
        z = self.z
        return lax.rem(z % 2 + d % 2, 2) + 2 * lax.rem(z // 2 + d // 2, 2)

    def enter(self):
        x, y, c = self.x, self.y, self.c
        barrier([self.px, self.py, self.pc] + [dev(x, y, self.zq(b), c) for b in range(3)])

    def row0(self, slot):
        return pl.multiple_of((slot * self.p.sh) // LN // 16 * 16, 16)

    def fg(self, slot):
        return self.row0(slot)

    def copy(self, src, dst, ssem, rsem, to):
        return pltpu.make_async_remote_copy(src_ref=src, dst_ref=dst, send_sem=ssem, recv_sem=rsem, device_id=to, device_id_type=MESH)

    def wait(self, ref, sem):
        pltpu.make_async_copy(ref, ref, sem).wait()

    def to_sibling(self, xp):
        def body(k, _):
            dp = 2 * xp + 1 - self.c
            i = 8 * xp + k
            self.copy(self.FG.at[pl.ds(self.row0(dp * 8 + k), self.SL)], self.R.at[i], self.sib_s.at[i], self.sib_r.at[i], self.pc).start()
            return 0

        lax.fori_loop(0, 8, body, 0)

    def add(self, dst, d0, rows, srcs, U=176):
        def body(t, _):
            r = pl.multiple_of(t * U, 16)
            v = None
            for s, s0 in srcs:
                e = s[pl.ds(s0 + r, U)].astype(F32)
                v = e if v is None else v + e
            dst[pl.ds(d0 + r, U)] = v.astype(dst.dtype)
            return 0

        lax.fori_loop(0, rows // U, body, 0)

    def have(self, xp, yq, zq):
        fs = zq * 2 + yq
        i = 8 * xp + fs
        self.wait(self.R.at[i], self.sib_r.at[i])
        return i, self.row0((2 * xp + self.c) * 8 + fs)

    def diag(self, xp, b):
        i, g = self.have(xp, 1 - self.y, self.zq(b))
        half, rest = self.half, self.SL - self.half
        R = self.R.at[i]
        self.add(R, 0, self.SL, [(self.FG, g), (R, 0)])
        self.copy(R.at[pl.ds(0, half)], self.D0.at[b], self.d_s.at[0, b], self.d_r.at[0, b], self.py).start()
        self.copy(R.at[pl.ds(half, rest)], self.D1.at[b], self.d_s.at[1, b], self.d_r.at[1, b], self.px).start()

    def xline(self, xp, b):
        i, g = self.have(xp, self.y, self.zq(b))
        half, rest = self.half, self.SL - self.half
        R = self.R.at[i]
        self.wait(self.D0.at[b], self.d_r.at[0, b])
        self.add(R, half, rest, [(self.FG, g + half), (R, half)])
        self.add(R, 0, half, [(self.FG, g), (R, 0), (self.D0.at[b], 0)])
        self.copy(R, self.X.at[b], self.x_s.at[b], self.x_r.at[b], self.px).start()

    def yline(self, xp, b):
        i, g = self.have(xp, 1 - self.y, self.zq(b))
        half, rest = self.half, self.SL - self.half
        R = self.R.at[i]
        self.wait(self.D1.at[b], self.d_r.at[1, b])
        self.add(R, 0, half, [(self.FG, g), (R, 0)])
        self.add(R, half, rest, [(self.FG, g + half), (R, half), (self.D1.at[b], 0)])
        self.copy(R, self.Y.at[b], self.y_s.at[b], self.y_r.at[b], self.py).start()

    def own(self, xp, b):
        i, g = self.have(xp, self.y, self.zq(b))
        R = self.R.at[i]
        self.wait(self.X.at[b], self.x_r.at[b])
        self.wait(self.Y.at[b], self.y_r.at[b])
        self.add(R, 0, self.SL, [(self.FG, g), (R, 0), (self.X.at[b], 0), (self.Y.at[b], 0)])
        self.copy(R, self.Z.at[b], self.z_s.at[b], self.z_r.at[b], dev(self.x, self.y, self.zq(b), self.c)).start()

    def last(self, xp, out):
        p, SL, A = self.p, self.SL, self.A
        i, g = self.have(xp, self.y, self.z)
        self.wait(self.X.at[3], self.x_r.at[3])
        self.wait(self.Y.at[3], self.y_r.at[3])
        for b in range(3):
            self.wait(self.Z.at[b], self.z_r.at[b])
        self.add(A, 0, SL, [(self.FG, g), (self.R.at[i], 0), (self.X.at[3], 0), (self.Y.at[3], 0)] + [(self.Z.at[b], 0) for b in range(3)])
        start = lin(self.x, self.y, self.z, self.c) * p.sh
        r_first = start // LN
        s = start - r_first * LN
        r0 = r_first % 16
        A[0:SL] = pltpu.roll(A[0:SL], lax.rem(LN - s, LN), 1)
        lane = lax.broadcasted_iota(jnp.int32, (p.rows_in, LN), 1)
        out[...] = jnp.where(lane < LN - s, A[pl.ds(r0, p.rows_in), :], A[pl.ds(r0 + 1, p.rows_in), :])

    def after(self, part, index=None):
        for c in (0, 1):
            for x in (0, 1):
                todo = [e for e in SCHEDULE if e[:3] == (part, c, x)]
                if todo:
                    here = (self.c == c) & (self.x == x)
                    if index is not None:
                        here = here & (index[0] == index[1])

                    def run(todo=todo):
                        for _, _, _, step, xp, b0, n in todo:
                            lax.fori_loop(b0, b0 + n, lambda b, k: (getattr(self, step)(xp, b), k)[1], 0)

                    pl.when(here)(run)

    def leave(self):
        for k in range(16):
            self.wait(self.R.at[k], self.sib_s.at[k])
        for b in range(4):
            self.wait(self.D0.at[b], self.d_s.at[0, b])
            self.wait(self.D1.at[b], self.d_s.at[1, b])
            self.wait(self.X.at[b], self.x_s.at[b])
            self.wait(self.Y.at[b], self.y_s.at[b])
        for b in range(3):
            self.wait(self.Z.at[b], self.z_s.at[b])


BACK_IN = ("act", "d_outer", "w2", "gd", "first_low", "w1", "res", "xh1", "rstd1", "V", "VG", "mixed", "wo", "qkv", "lse", "tok")


def backward_scatter_kernel(p, length, *refs):
    n = len(BACK_IN)
    src = dict(zip(BACK_IN, refs[:n]))
    wqkv_in = refs[n]
    igrad, out = refs[n + 1 : n + 3]
    loc = dict(zip(BACK_IN, refs[n + 3 : 2 * n + 3]))
    FG, F, E, R, D0, D1, X, Y, Z, lsem, osem, *sems = refs[2 * n + 3 :]
    r = Refs(length=length[0], FG=FG, F=F, E=E, **loc)
    r.dqkv, r.d_branch, r.d_mixed = r.act, r.first_low, r.d_outer
    sc = Scatter(p, FG, R, D0, D1, X, Y, Z, F, sems)
    mats = {m: (b, k, c) for m, b, k, c in MATS}
    loads = {m: pltpu.make_async_copy(src[m], loc[m], lsem.at[k]) for k, m in enumerate(BACK_IN)}
    for m in BACK_IN:
        loads[m].start()

    def need(*names):
        for m in names:
            loads[m].wait()

    sc.enter()
    c0, c1 = sc.c == 0, sc.c == 1
    x0, x1 = sc.x == 0, sc.x == 1

    def both(cond, fn):
        pl.when(cond)(fn)

    need("act", "d_outer", "VG")
    weight_grad(r, r.act, r.d_outer, *mats["w2"], RB=1024, CB=2)
    edge_grads(r, 3)
    both(c0, lambda: sc.to_sibling(1))
    sc.after(1)
    need("w2", "gd")

    def act_part(j, carry):
        backward_act(r, j)
        for k in range(4):
            sc.after(2 + k, (j, k))
        return carry

    lax.fori_loop(0, FF // UP, act_part, 0)
    q_loads = [pltpu.make_async_copy(wqkv_in.at[:, pl.ds(k * D, D)], r.w2.at[pl.ds(k * D, D)], lsem.at[n + k]) for k in range(3)]
    for q in q_loads:
        q.start()
    need("first_low")
    weight_grad(r, r.first_low, r.gd, *mats["w1"], hook=lambda i: [sc.after(6 + k, (i, k)) for k in range(2)])
    edge_grads(r, 2)
    both(c1, lambda: sc.to_sibling(1))
    sc.after(8)
    need("w1", "res", "xh1", "rstd1", "V")
    backward_first(r)
    sc.after(9)
    need("mixed")
    weight_grad(r, r.mixed, r.d_branch, *mats["wo"])
    edge_grads(r, 1)
    both(c0, lambda: sc.to_sibling(0))
    sc.after(10)
    need("wo")
    backward_mixed(r)
    sc.after(11)
    need("qkv", "lse")

    def heads(hp, carry):
        backward_heads(r, hp)
        for k in range(6):
            sc.after(12 + k, (hp, k))
        return carry

    lax.fori_loop(0, H // 2, heads, 0)
    need("tok")
    weight_grad(r, r.tok, r.dqkv, *mats["wqkv"], hook=lambda i: [sc.after(18 + k, (i, k)) for k in range(2)])
    edge_grads(r, 0)
    both(c1, lambda: sc.to_sibling(0))
    sc.after(20)
    for q in q_loads:
        q.wait()

    def tokens(b, carry):
        o = rows_of(b, LEN)
        v = r.res[o, :]
        for part in range(3):
            v = v + mm_nt(r.dqkv[o, part * D : (part + 1) * D], r.w2[part * D : (part + 1) * D, :])
        r.res[o, :] = v
        sc.after(21, (b, 0))
        return carry

    lax.fori_loop(0, 1, tokens, 0)
    grad_out = pltpu.make_async_copy(r.res, igrad, osem)
    grad_out.start()
    sc.after(22)
    both(x0, lambda: sc.last(0, out))
    both(x1, lambda: sc.last(1, out))
    sc.leave()
    grad_out.wait()


def backward_scatter(p, length, wqkv, **arrays):
    S = jax.ShapeDtypeStruct
    sm = pl.BlockSpec(memory_space=pltpu.SMEM)
    hbm = pl.BlockSpec(memory_space=pl.ANY)
    ins = [arrays[m] for m in BACK_IN]
    SL = p.slot
    half = SL // 32 * 16
    VM = pltpu.VMEM
    DM = pltpu.SemaphoreType.DMA
    igrad, o = pl.pallas_call(
        functools.partial(backward_scatter_kernel, p),
        out_shape=[S((LEN, D), F32), S((p.rows_in, LN), F32)],
        in_specs=[sm] + [hbm] * (len(ins) + 1),
        out_specs=[hbm, pl.BlockSpec(memory_space=pltpu.VMEM)],
        scratch_shapes=[VM(a.shape, a.dtype) for a in ins]
        + [VM((flat_rows(p), LN), BF), VM((6144 + 32, LN), F32), VM((160, LN), F32), VM((16, SL, LN), BF), VM((4, half, LN), BF), VM((4, SL - half, LN), BF), VM((4, SL, LN), BF), VM((4, SL, LN), BF), VM((3, SL, LN), BF)]
        + [DM((len(ins) + 3,)), DM, DM((16,)), DM((16,)), DM((2, 4)), DM((2, 4)), DM((4,)), DM((4,)), DM((4,)), DM((4,)), DM((3,)), DM((3,))],
        compiler_params=pltpu.CompilerParams(collective_id=1, has_side_effects=True, vmem_limit_bytes=64 << 20),
    )(length, *ins, wqkv)
    return igrad, o


def finish_copies(p, shards, hidden, igrad, nested):
    S = jax.ShapeDtypeStruct
    vm = pl.BlockSpec(memory_space=pltpu.VMEM)

    def kernel(a, b, c, d, a_out, b_out, c_out, d_out):
        a_out[...] = a[...].reshape(p.rows_in * LN)[: p.sh]
        b_out[...] = b[...]
        c_out[...] = c[...]
        d_out[...] = d[...]

    arrays = (shards, hidden, igrad, nested)
    return pl.pallas_call(
        kernel,
        out_shape=[S((p.sh,), F32)] + [S(a.shape, a.dtype) for a in arrays[1:]],
        in_specs=[vm] * 4,
        out_specs=[vm] * 4,
    )(*arrays)


def on_device(p, fast, tokens, lengths, weight_shards, hidden_cotangent, nested_cotangent):
    tok = tokens.reshape(LEN, D)
    hcot = hidden_cotangent.reshape(LEN, D)
    if fast:
        f = gather_forward(p, weight_shards, lengths, tok, hcot, nested_cotangent)
        igrad, shards = backward_scatter(p, lengths, tok=tok, **{m: f[m] for m in BACK_IN + ("wqkv",) if m != "tok"})
        shards, f["hidden"], igrad, f["nested"] = finish_copies(p, shards, f["hidden"], igrad, f["nested"])
    else:
        slots = lax.all_gather(build_slot(p, weight_shards, me_of), AX, axis=0)
        f = dict(zip(FORWARD_OUT, forward_local(p, slots, lengths, tok, hcot, nested_cotangent)))
        igrad, flat = backward_local(p, lengths, tok, *[f[m] for m in FORWARD_OUT[6:] + FORWARD_OUT[2:6]])
        shards = scatter_plain(p, flat)
    return (f["hidden"].reshape(1, LEN, D), f["nested"], igrad.reshape(1, LEN, D), shards)


def solution(mesh):
    in_specs = (
        P(("dp", "fsdp"), None, None),
        P(("dp", "fsdp")),
        P(("dp", "fsdp")),
        P(("dp", "fsdp"), None, None),
        P(("dp", "fsdp"), None),
    )
    out_specs = (
        P(("dp", "fsdp"), None, None),
        P(("dp", "fsdp"), None),
        P(("dp", "fsdp"), None, None),
        P(("dp", "fsdp")),
    )
    p = plan(mesh.shape["dp"] * mesh.shape["fsdp"])
    fast = (mesh.shape["dp"], mesh.shape["fsdp"]) == (4, 8)
    return jax.shard_map(
        functools.partial(on_device, p, fast), mesh=mesh, in_specs=in_specs, out_specs=out_specs, check_vma=False
    )
```

```python
import functools
import math

import jax
import jax.numpy as jnp
from jax import lax
from jax.experimental import pallas as pl
from jax.experimental.pallas import tpu as pltpu
from jax.sharding import PartitionSpec as P

AX = ("dp", "fsdp")
MESH = pl.DeviceIdType.MESH
D = 768
H = 12
HD = 64
FF = 3072
LEN = 512
E2 = 512
E3 = 256
E4 = 128
E5 = 64


epsilon = 1e-05


PAR=7088640; LN=128
class Plan: pass
def plan(n):
    p=Plan(); p.n=n; p.sh=PAR//n
    st=[i*p.sh for i in range(n)]
    p.g0=[s//LN//16 for s in st]
    p.g1=[(s+p.sh-1)//LN//16 for s in st]
    p.slot=16*max(b-a+1 for a,b in zip(p.g0,p.g1))
    p.rows_in=-(-p.sh//LN)
    return p
MATS=[("wqkv",0,D,18),("wo",13836,D,6),("w1",18462,D,24),("w2",36918,FF,6)]
VECS=[(13824,12),(18444,18),(36894,24),(55350,30)]

def build_slot_kernel(p,me_of,x_ref,o_ref,q_ref):
    i=me_of(); start=i*p.sh; r_first=start//LN; s=start-r_first*LN; r0=r_first%16
    lead=32
    q_ref[...]=jnp.zeros_like(q_ref)
    q=pltpu.roll(x_ref[...].astype(jnp.float32),s,1)
    q_ref[lead:lead+p.rows_in]=q
    lane=lax.broadcasted_iota(jnp.int32,(p.slot,LN),1)
    a=q_ref[pl.ds(lead-r0,p.slot),:]
    b=q_ref[pl.ds(lead-1-r0,p.slot),:]
    o_ref[...]=jnp.where(lane>=s,a,b).astype(jnp.bfloat16)

def build_slot(p,shard,me_of):
    x=jnp.pad(shard,(0,p.rows_in*LN-p.sh)).reshape(p.rows_in,LN)
    return pl.pallas_call(functools.partial(build_slot_kernel,p,me_of),out_shape=jax.ShapeDtypeStruct((p.slot,LN),jnp.bfloat16),
        scratch_shapes=[pltpu.VMEM((32+p.slot+32,LN),jnp.float32)])(x)

def load_flat(p,slots,F,g_lo,g_hi,need=None):
    for i in range(p.n):
        a=max(g_lo,p.g0[i]); b=min(g_hi,p.g1[i]+1)
        if a>=b: continue
        shared_first = i>0 and p.g0[i]==p.g1[i-1] and a==p.g0[i]
        a2=a+1 if shared_first else a
        b2=b
        apart=need is not None and need<=(i+1)*p.sh//LN
        if i+1<p.n and p.g1[i]==p.g0[i+1] and b==p.g1[i]+1 and not apart: b2=b-1
        if i+1<p.n and b2<b and b-1>=g_lo:
            g=b-1
            F[16*(g-g_lo):16*(g-g_lo)+16]=slots[i,16*(g-p.g0[i]):16*(g-p.g0[i])+16].astype(jnp.float32)+slots[i+1,0:16].astype(jnp.float32)
        cnt=b2-a2
        if cnt<=0: continue
        U=16
        nb,rem=cnt//U,cnt%U
        def body(t,_,i=i,a2=a2):
            src=pl.multiple_of(16*(a2-p.g0[i])+t*16*U,16); dst=pl.multiple_of(16*(a2-g_lo)+t*16*U,16)
            F[pl.ds(dst,16*U)]=slots[i,pl.ds(src,16*U)].astype(jnp.float32)
            return 0
        lax.fori_loop(0,nb,body,0)
        if rem:
            src=16*(a2-p.g0[i])+nb*16*U; dst=16*(a2-g_lo)+nb*16*U
            F[dst:dst+16*rem]=slots[i,src:src+16*rem].astype(jnp.float32)

def coords():
    dp=lax.axis_index("dp"); fs=lax.axis_index("fsdp")
    return dp//2,fs%2,fs//2,dp%2
def dev(x,y,z,c): return (x*2+c, z*2+y)
def lin(x,y,z,c): return (x*2+c)*8+z*2+y
def barrier(partners):
    bar=pltpu.get_barrier_semaphore()
    for q in partners: pl.semaphore_signal(bar,inc=1,device_id=q,device_id_type=MESH)
    pl.semaphore_wait(bar,len(partners))

TOT=PAR//LN
def flat_rows(p): return max(16*p.g0[-1]+p.slot, EDGES[-1][0]+EDGES[-1][1])
def owner_row(rho):
    for k,(name,base,rows,w) in enumerate(MATS):
        if base<=rho<base+rows*w: return ("m",k,(rho-base)//w,(rho-base)%w)
    at=0
    for base,cnt in VECS:
        if base<=rho<base+cnt: return ("v",at+rho-base)
        at+=cnt
    return None

def me_of():
    return lax.axis_index(AX)


def finish_kernel(p, a_ref, out, A):
    SL = p.slot
    start = me_of() * p.sh
    r_first = start // LN
    s = start - r_first * LN
    r0 = r_first % 16
    A[0:SL] = pltpu.roll(a_ref[...], lax.rem(LN - s, LN), 1)
    lane = lax.broadcasted_iota(jnp.int32, (p.rows_in, LN), 1)
    out[...] = jnp.where(lane < LN - s, A[pl.ds(r0, p.rows_in), :], A[pl.ds(r0 + 1, p.rows_in), :])


def scatter_plain(p, flat):
    parts = jnp.concatenate([flat[16 * g : 16 * g + p.slot] for g in p.g0]).astype(jnp.float32)
    mine = lax.psum_scatter(parts, AX, scatter_dimension=0, tiled=True)
    o = pl.pallas_call(
        functools.partial(finish_kernel, p),
        out_shape=jax.ShapeDtypeStruct((p.rows_in, LN), jnp.float32),
        scratch_shapes=[pltpu.VMEM((p.slot + 32, LN), jnp.float32)],
    )(mine)
    return o.reshape(-1)[: p.sh]

EPS = 1e-05
F32 = jnp.float32
BF = jnp.bfloat16
SQ = math.sqrt(0.5)
PHI = 1.0 / math.sqrt(2.0 * math.pi)
VNAMES = (
    ("q_bias", D),
    ("v_bias", D),
    ("out_bias", D),
    ("first_gain", D),
    ("first_shift", D),
    ("up_bias", FF),
    ("down_bias", D),
    ("second_gain", D),
    ("second_shift", D),
    ("exit_gain", D),
    ("exit_shift", D),
)
VI = {name: k for k, (name, _) in enumerate(VNAMES)}
PREFIXES = (D, E2, E3, E4, E5)
SCALE = 1.0 / math.sqrt(HD)
UP = 768


def mm(a, b):
    return jnp.dot(a, b, preferred_element_type=F32)


def mm_nt(a, b):
    return lax.dot_general(a, b, (((1,), (1,)), ((), ())), preferred_element_type=F32)


def mm_tn(a, b):
    return lax.dot_general(a, b, (((0,), (0,)), ((), ())), preferred_element_type=F32)


def vrow(V, name):
    k = VI[name]
    return V[k : k + 1, : VNAMES[k][1]]


def mean_last(a):
    return jnp.mean(a, axis=-1, keepdims=True)


def sum_rows(a):
    return jnp.sum(a, axis=0, keepdims=True)


def forward_qkv(r):
    bias = jnp.concatenate([vrow(r.V, "q_bias"), jnp.zeros((1, D), F32), vrow(r.V, "v_bias")], axis=1)
    r.qb[...] = bias

    def body(j, _):
        o = pl.ds(pl.multiple_of(j * D, D), D)
        r.qkv[:, o] = (mm(r.tok[...], r.wqkv[:, o]) + r.qb[:, o]).astype(BF)
        return 0

    lax.fori_loop(0, 3, body, 0)


def half_lanes(h):
    lane = lax.broadcasted_iota(jnp.int32, (LEN, LN), 1)
    return lane < HD if h == 0 else lane >= HD


def pair(r, part, hp):
    return r.qkv[:, pl.ds(pl.multiple_of(part * D + hp * LN, LN), LN)]


def forward_heads(r, hp):
    q, k, v = pair(r, 0, hp) * SCALE, pair(r, 1, hp), pair(r, 2, hp)
    valid = lax.broadcasted_iota(jnp.int32, (1, LEN), 1) < r.length
    out = None
    lse_all = r.lse[...]
    lane = lax.broadcasted_iota(jnp.int32, (LEN, LN), 1)
    for h in range(2):
        qh = jnp.where(half_lanes(h), q, jnp.zeros_like(q))
        s = jnp.where(valid, mm_nt(qh, k), -1e9)
        m = jnp.max(s, axis=1, keepdims=True)
        e = jnp.exp(s - m)
        l = jnp.sum(e, axis=1, keepdims=True)
        low = (e * (1.0 / l)).astype(BF)
        o = mm(low, v)
        out = o if out is None else jnp.where(half_lanes(0), out, o)
        lse_all = jnp.where(lane == 2 * hp + h, m + jnp.log(l), lse_all)
    r.lse[...] = lse_all
    r.mixed[:, pl.ds(pl.multiple_of(hp * LN, LN), LN)] = out.astype(BF)


def rows_of(b, n):
    return pl.ds(pl.multiple_of(b * n, n), n)


def forward_first(r):
    def body(b, _):
        o = rows_of(b, LEN)
        v = r.tok[o, :].astype(F32) + mm(r.mixed[o, :], r.wo[...]) + vrow(r.V, "out_bias")
        cen = v - mean_last(v)
        rstd = lax.rsqrt(mean_last(cen * cen) + EPS)
        xh = cen * rstd
        r.xh1[o, :] = xh
        r.rstd1[o, :] = rstd
        r.first_low[o, :] = (xh * vrow(r.V, "first_gain") + vrow(r.V, "first_shift")).astype(BF)
        return 0

    lax.fori_loop(0, 1, body, 0)


def forward_up(r, j):
    o = pl.ds(pl.multiple_of(j * UP, UP), UP)
    v = mm(r.first_low[...], r.w1[:, o]) + r.V[VI["up_bias"] : VI["up_bias"] + 1, o]
    cdf = 0.5 * (1.0 + lax.erf(v * SQ))
    r.act[:, o] = (v * cdf).astype(BF)
    r.gd[:, o] = (cdf + v * (PHI * jnp.exp(-0.5 * v * v))).astype(BF)


def forward_second(r):
    def body(b, tot):
        o = rows_of(b, LEN)
        first = r.xh1[o, :] * vrow(r.V, "first_gain") + vrow(r.V, "first_shift")
        v = first + mm(r.act[o, :], r.w2[...]) + vrow(r.V, "down_bias")
        cen = v - mean_last(v)
        rstd = lax.rsqrt(mean_last(cen * cen) + EPS)
        xh = cen * rstd
        r.xh2[o, :] = xh
        r.rstd2[o, :] = rstd
        t = lax.broadcasted_iota(jnp.int32, (LEN, 1), 0)
        hid = (xh * vrow(r.V, "second_gain") + vrow(r.V, "second_shift")) * (t < r.length).astype(F32)
        r.hidden[o, :] = hid.astype(BF)
        return tot + sum_rows(hid)

    return lax.fori_loop(0, 1, body, jnp.zeros((1, D), F32))


def head(r, tot):
    inv_len = 1.0 / jnp.full((1, 1), r.length, jnp.int32).astype(F32)
    pooled = tot * inv_len
    cen = pooled - mean_last(pooled)
    rstd = lax.rsqrt(mean_last(cen * cen) + EPS)
    xh = cen * rstd
    gain = vrow(r.V, "exit_gain")
    emb = xh * gain + vrow(r.V, "exit_shift")
    d_emb = jnp.zeros((1, D), F32)
    at = 0
    for m in PREFIXES:
        e = emb[:, :m]
        inv = lax.rsqrt(jnp.sum(e * e, axis=1, keepdims=True) * (1.0 / m) + EPS)
        out = e * inv
        r.nested[:, at : at + m] = out
        c = r.ncot[:, at : at + m]
        g = inv * (c - out * (jnp.sum(c * out, axis=1, keepdims=True) * (1.0 / m)))
        d_emb = d_emb + (g if m == D else jnp.concatenate([g, jnp.zeros((1, D - m), F32)], axis=1))
        at += m
    put_grad(r, "exit_gain", d_emb * xh)
    put_grad(r, "exit_shift", d_emb)
    dx = d_emb * gain
    return rstd * (dx - mean_last(dx) - xh * mean_last(dx * xh)) * inv_len


def put_grad(r, name, value):
    k = VI[name]
    r.VG[k : k + 1, : VNAMES[k][1]] = value


def norm_back(dy, gain, xh, rstd):
    dx = dy * gain
    return rstd * (dx - mean_last(dx) - xh * mean_last(dx * xh))


def backward_second(r, d_pool):
    def body(b, c):
        o = rows_of(b, LEN)
        t = lax.broadcasted_iota(jnp.int32, (LEN, 1), 0)
        dy = (r.hcot[o, :].astype(F32) + d_pool) * (t < r.length).astype(F32)
        xh = r.xh2[o, :]
        res = norm_back(dy, vrow(r.V, "second_gain"), xh, r.rstd2[o, :])
        r.res[o, :] = res
        low = res.astype(BF)
        r.d_outer[o, :] = low
        return (c[0] + sum_rows(dy * xh), c[1] + sum_rows(dy), c[2] + sum_rows(low.astype(F32)))

    z = jnp.zeros((1, D), F32)
    a, b, c = lax.fori_loop(0, 1, body, (z, z, z))
    put_grad(r, "second_gain", a)
    put_grad(r, "second_shift", b)
    put_grad(r, "down_bias", c)


def backward_act(r, j):
    o = pl.ds(pl.multiple_of(j * UP, UP), UP)
    d = (mm_nt(r.d_outer[...], r.w2[o, :]) * r.gd[:, o].astype(F32)).astype(BF)
    r.gd[:, o] = d
    r.VG[VI["up_bias"] : VI["up_bias"] + 1, o] = sum_rows(d.astype(F32))


def backward_first(r):
    def body(b, c):
        o = rows_of(b, LEN)
        dy = mm_nt(r.gd[o, :], r.w1[...]) + r.res[o, :]
        xh = r.xh1[o, :]
        res = norm_back(dy, vrow(r.V, "first_gain"), xh, r.rstd1[o, :])
        r.res[o, :] = res
        low = res.astype(BF)
        r.d_branch[o, :] = low
        return (c[0] + sum_rows(dy * xh), c[1] + sum_rows(dy), c[2] + sum_rows(low.astype(F32)))

    z = jnp.zeros((1, D), F32)
    a, b, c = lax.fori_loop(0, 1, body, (z, z, z))
    put_grad(r, "first_gain", a)
    put_grad(r, "first_shift", b)
    put_grad(r, "out_bias", c)


def backward_mixed(r):
    r.d_mixed[...] = mm_nt(r.d_branch[...], r.wo[...]).astype(BF)


def backward_heads(r, hp):
    q, k, v = pair(r, 0, hp) * SCALE, pair(r, 1, hp), pair(r, 2, hp)
    k_scaled = k * SCALE
    cols = pl.ds(pl.multiple_of(hp * LN, LN), LN)
    dm = r.d_mixed[:, cols]
    valid = lax.broadcasted_iota(jnp.int32, (1, LEN), 1) < r.length
    lane = lax.broadcasted_iota(jnp.int32, (LEN, LN), 1)
    zero = jnp.zeros_like(q)
    dm_mixed = dm.astype(F32) * r.mixed[:, cols].astype(F32)
    dq = dk = dv = None
    for h in range(2):
        here = half_lanes(h)
        qh, kh, dmh = jnp.where(here, q, zero), jnp.where(here, k_scaled, zero), jnp.where(here, dm, zero)
        lse = jnp.sum(jnp.where(lane == 2 * hp + h, r.lse[...], 0.0), axis=1, keepdims=True)
        s = jnp.where(valid, mm_nt(qh, k), -1e9)
        p = jnp.exp(s - lse)
        dp = mm_nt(dmh, v)
        delta = jnp.sum(jnp.where(here, dm_mixed, 0.0), axis=1, keepdims=True)
        ds = (p * (dp - delta)).astype(BF)
        a, b, c = mm(ds, kh), mm_tn(ds, qh), mm_tn(p.astype(BF), dmh)
        dq, dk, dv = (a, b, c) if dq is None else (dq + a, dk + b, dv + c)
    dq, dk, dv = dq.astype(BF), dk.astype(BF), dv.astype(BF)
    for part, g in ((0, dq), (1, dk), (2, dv)):
        r.dqkv[:, pl.ds(pl.multiple_of(part * D + hp * LN, LN), LN)] = g
    k = VI["q_bias"]
    r.VG[k : k + 1, cols] = sum_rows(dq.astype(F32))
    k = VI["v_bias"]
    r.VG[k : k + 1, cols] = sum_rows(dv.astype(F32))


def backward_tokens(r, b):
    o = rows_of(b, 128)
    v = r.res[o, :]
    for part in range(3):
        v = v + mm_nt(r.dqkv[o, part * D : (part + 1) * D], r.wqkv[:, part * D : (part + 1) * D])
    r.res[o, :] = v


EDGES = ((13824, 16), (18432, 32), (36880, 48), (55344, 64))


def edge_at(row):
    at = 0
    for base, rows in EDGES:
        if base <= row < base + rows:
            return at + row - base
        at += rows
    return None


def weight_grad(r, lhs, rhs, base, rows, w, RB=256, CB=6, hook=None):
    lead = base % 16
    step_rows = RB * w
    F = r.F
    if lead:
        F[0:16] = jnp.zeros((16, LN), F32)

    def body(s, _):
        o = pl.ds(pl.multiple_of(s * RB, RB), RB)
        for ch in range(w // CB):
            g = mm_tn(lhs[:, o], rhs[:, ch * CB * LN : (ch + 1) * CB * LN])
            for j in range(CB):
                F[pl.ds(lead + ch * CB + j, RB, stride=w), :] = g[:, j * LN : (j + 1) * LN]
        if lead:
            @pl.when(s == 0)
            def _():
                e = edge_at(base)
                r.E[e : e + 16 - lead] = F[lead:16]

        U = 256
        to = base - lead + s * step_rows

        def emit(t, _):
            r.FG[pl.ds(pl.multiple_of(to + t * U, 16), U)] = F[pl.ds(pl.multiple_of(t * U, 16), U)].astype(BF)
            return 0

        lax.fori_loop(0, step_rows // U, emit, 0)
        if lead:
            F[0:16] = F[step_rows : step_rows + 16]
        if hook is not None:
            hook(s)
        return 0

    lax.fori_loop(0, rows // RB, body, 0)
    if lead:
        e = edge_at(base + rows * w - lead)
        r.E[e : e + lead] = F[0:lead]


def edge_grads(r, which):
    base, rows = EDGES[which]
    at = 0
    for vbase, cnt in VECS:
        for k in range(cnt):
            row = vbase + k
            if base <= row < base + rows:
                name, j = vec_at(at + k)
                e = edge_at(row)
                r.E[e : e + 1] = r.VG[name : name + 1, j * LN : (j + 1) * LN]
        at += cnt
    if which == len(EDGES) - 1:
        e = edge_at(TOT)
        r.E[e : e + base + rows - TOT] = jnp.zeros((base + rows - TOT, LN), F32)
    e = edge_at(base)
    r.FG[base : base + rows] = r.E[e : e + rows].astype(BF)


def vec_at(row):
    for k, (_, n) in enumerate(VNAMES):
        if row < n // LN:
            return k, row
        row -= n // LN


class Refs:
    def __init__(self, **refs):
        self.__dict__.update(refs)


def relayout_vectors(p, r):
    at = 0
    for base, cnt in VECS:
        g_lo = base // 16
        g_hi = -(-(base + cnt) // 16)
        load_flat(p, r.slots, r.F, g_lo, g_hi)
        for k in range(cnt):
            name, j = vec_at(at + k)
            f = base - 16 * g_lo + k
            r.V[name : name + 1, j * LN : (j + 1) * LN] = r.F[f : f + 1]
        at += cnt


def relayout_matrix(p, r, name, W, RB):
    base, rows, w = {n: (b, k, c) for n, b, k, c in MATS}[name]
    for s in range(rows // RB):
        lo = base + s * RB * w
        g_lo = lo // 16
        load_flat(p, r.slots, r.F, g_lo, -(-(lo + RB * w) // 16))
        tile_rows(r.F, W, lo - 16 * g_lo, s * RB, RB, w)


def tile_rows(F, W, off, row, rows, w, RB=64):
    def body(t, _):
        q = pl.multiple_of(t * RB, RB)
        for j in range(w):
            W[pl.ds(row + q, RB), j * LN : (j + 1) * LN] = F[pl.ds(off + q * w + j, RB, stride=w), :].astype(BF)
        return 0

    lax.fori_loop(0, rows // RB, body, 0)


def forward_kernel(p, slots, length, tok, hcot, ncot, hidden, nested, wqkv, wo, w1, w2, V, VG, qkv, lse, mixed, xh1, rstd1, first_low, act, gd, res, d_outer, F, qb, xh2, rstd2):
    r = Refs(slots=slots, length=length[0], tok=tok, hcot=hcot, ncot=ncot, hidden=hidden, nested=nested, wqkv=wqkv, wo=wo, w1=w1, w2=w2, V=V, VG=VG, qkv=qkv, lse=lse, mixed=mixed, xh1=xh1, rstd1=rstd1, first_low=first_low, act=act, gd=gd, res=res, d_outer=d_outer, F=F, qb=qb, xh2=xh2, rstd2=rstd2)
    relayout_vectors(p, r)
    relayout_matrix(p, r, "wqkv", wqkv, 256)
    forward_qkv(r)
    lse[...] = jnp.zeros_like(lse)
    lax.fori_loop(0, H // 2, lambda hp, c: (forward_heads(r, hp), c)[1], 0)
    relayout_matrix(p, r, "wo", wo, 768)
    forward_first(r)
    relayout_matrix(p, r, "w1", w1, 256)
    lax.fori_loop(0, FF // UP, lambda j, c: (forward_up(r, j), c)[1], 0)
    relayout_matrix(p, r, "w2", w2, 768)
    tot = forward_second(r)
    d_pool = head(r, tot)
    backward_second(r, d_pool)


def forward_local(p, slots, length, tok, hcot, ncot):
    S = jax.ShapeDtypeStruct
    outs = [S((LEN, D), BF), S((1, 1728), F32), S((D, 3 * D), BF), S((D, D), BF), S((D, FF), BF), S((FF, D), BF), S((16, FF), F32), S((16, FF), F32), S((LEN, 3 * D), BF), S((LEN, LN), F32), S((LEN, D), BF), S((LEN, D), F32), S((LEN, 1), F32), S((LEN, D), BF), S((LEN, FF), BF), S((LEN, FF), BF), S((LEN, D), F32), S((LEN, D), BF)]
    vm = pl.BlockSpec(memory_space=pltpu.VMEM)
    sm = pl.BlockSpec(memory_space=pltpu.SMEM)
    return pl.pallas_call(
        functools.partial(forward_kernel, p),
        out_shape=outs,
        in_specs=[vm, sm, vm, vm, vm],
        scratch_shapes=[pltpu.VMEM((6144 + 64, LN), F32), pltpu.VMEM((1, 3 * D), F32), pltpu.VMEM((LEN, D), F32), pltpu.VMEM((LEN, 1), F32)],
        compiler_params=pltpu.CompilerParams(vmem_limit_bytes=60 << 20),
    )(slots, length, tok, hcot, ncot)


def backward_kernel(p, length, tok, V, VG0, qkv, lse, mixed, xh1, rstd1, first_low, act, gd, res, d_outer, wqkv, wo, w1, w2, igrad, FG, VG, d_branch, d_mixed, dqkv, F, E):
    r = Refs(length=length[0], tok=tok, V=V, VG=VG, qkv=qkv, lse=lse, mixed=mixed, xh1=xh1, rstd1=rstd1, first_low=first_low, act=act, gd=gd, res=igrad, d_outer=d_outer, wqkv=wqkv, wo=wo, w1=w1, w2=w2, FG=FG, d_branch=d_branch, d_mixed=d_mixed, dqkv=dqkv, F=F, E=E)
    VG[...] = VG0[...]
    igrad[...] = res[...]
    mats = {n: (b, k, c) for n, b, k, c in MATS}
    weight_grad(r, act, d_outer, *mats["w2"], RB=1024, CB=2)
    edge_grads(r, 3)
    lax.fori_loop(0, FF // UP, lambda j, c: (backward_act(r, j), c)[1], 0)
    weight_grad(r, first_low, gd, *mats["w1"])
    edge_grads(r, 2)
    backward_first(r)
    weight_grad(r, mixed, d_branch, *mats["wo"])
    edge_grads(r, 1)
    backward_mixed(r)
    lax.fori_loop(0, H // 2, lambda hp, c: (backward_heads(r, hp), c)[1], 0)
    weight_grad(r, tok, dqkv, *mats["wqkv"])
    edge_grads(r, 0)
    lax.fori_loop(0, LEN // 128, lambda b, c: (backward_tokens(r, b), c)[1], 0)


def backward_local(p, length, tok, V, VG, qkv, lse, mixed, xh1, rstd1, first_low, act, gd, res, d_outer, wqkv, wo, w1, w2):
    S = jax.ShapeDtypeStruct
    vm = pl.BlockSpec(memory_space=pltpu.VMEM)
    sm = pl.BlockSpec(memory_space=pltpu.SMEM)
    return pl.pallas_call(
        functools.partial(backward_kernel, p),
        out_shape=[S((LEN, D), F32), S((flat_rows(p), LN), BF)],
        in_specs=[sm] + [vm] * 17,
        scratch_shapes=[pltpu.VMEM((16, FF), F32), pltpu.VMEM((LEN, D), BF), pltpu.VMEM((LEN, D), BF), pltpu.VMEM((LEN, 3 * D), BF), pltpu.VMEM((6144 + 64, LN), F32), pltpu.VMEM((160, LN), F32)],
        compiler_params=pltpu.CompilerParams(vmem_limit_bytes=60 << 20),
    )(length, tok, V, VG, qkv, lse, mixed, xh1, rstd1, first_low, act, gd, res, d_outer, wqkv, wo, w1, w2)


class Gather:
    def __init__(self, p, G, ssem, rsem, gosem):
        self.p, self.G, self.ssem, self.rsem, self.gosem = p, G, ssem, rsem, gosem
        self.x, self.y, self.z, self.c = coords()
        x, y, z, c = self.x, self.y, self.z, self.c
        self.me = lin(x, y, z, c)
        half = p.slot // 32 * 16
        self.H = ((0, half), (half, p.slot - half), (0, p.slot))
        self.px, self.py, self.pc = dev(1 - x, y, z, c), dev(x, 1 - y, z, c), dev(x, y, z, 1 - c)

    def enter(self):
        x, y, z, c = self.x, self.y, self.z, self.c
        bar = pltpu.get_barrier_semaphore()

        def greet(to):
            pl.semaphore_signal(bar, inc=1, device_id=to, device_id_type=MESH)

        for to in (self.px, self.py, self.pc):
            greet(to)
        pl.when(z > 0)(lambda: greet(dev(x, y, z - 1, c)))
        pl.when(z < 3)(lambda: greet(dev(x, y, z + 1, c)))
        middle = (z > 0) & (z < 3)
        pl.when(middle)(lambda: pl.semaphore_wait(bar, 5))
        pl.when(jnp.logical_not(middle))(lambda: pl.semaphore_wait(bar, 4))

    def send(self, sl, h, to, t):
        r0, rn = self.H[h]
        ref = self.G.at[sl, pl.ds(r0, rn)]
        pltpu.make_async_remote_copy(src_ref=ref, dst_ref=ref, send_sem=self.ssem.at[sl, t], recv_sem=self.rsem.at[sl, h], device_id=to, device_id_type=MESH).start()

    def wait(self, sl, h, sem=None):
        r0, rn = self.H[h]
        ref = self.G.at[sl, pl.ds(r0, rn)]
        pltpu.make_async_copy(ref, ref, self.rsem.at[sl, h] if sem is None else sem).wait()

    def up(self, sl, h):
        pl.when(self.z < 3)(lambda: self.send(sl, h, dev(self.x, self.y, self.z + 1, self.c), 3))

    def down(self, sl, h):
        pl.when(self.z > 0)(lambda: self.send(sl, h, dev(self.x, self.y, self.z - 1, self.c), 4))

    def core(self, sl, h):
        self.send(sl, h, self.pc, 2)

    def xy(self, sl):
        self.send(sl, 0, self.px, 0)
        self.send(sl, 1, self.py, 1)
        self.send(sl, 1, self.px, 0)
        self.send(sl, 0, self.py, 1)

    def own(self, xy):
        for h in (0, 1):
            self.up(self.me, h)
            self.down(self.me, h)
        if xy:
            self.xy(self.me)
        for h in (0, 1):
            self.core(self.me, h)

    def own_line(self, k):
        self.at(k, lambda zq: self.xy(lin(self.x, self.y, zq, self.c)))

    def go(self, k):
        pl.semaphore_signal(self.gosem.at[k], inc=1, device_id=self.pc, device_id_type=MESH)

    def wait_go(self, k):
        pl.semaphore_wait(self.gosem.at[k], 1)

    def at(self, k, fn):
        if k == 0:
            fn(self.z)
            return
        pl.when(self.z - k >= 0)(lambda: fn(self.z - k))
        pl.when(self.z + k <= 3)(lambda: fn(self.z + k))

    def along_z(self, k, xy):
        x, y, z, c = self.x, self.y, self.z, self.c

        def from_level(zq, on):
            sl = lin(x, y, zq, c)
            self.wait(sl, 0)
            on(sl, 0)
            if xy:
                self.send(sl, 0, self.px, 0)
            self.core(sl, 0)
            self.wait(sl, 1)
            on(sl, 1)
            if xy:
                self.send(sl, 1, self.py, 1)
                self.send(sl, 1, self.px, 0)
                self.send(sl, 0, self.py, 1)
            self.core(sl, 1)

        pl.when(z - k >= 0)(lambda: from_level(z - k, self.up))
        pl.when(z + k <= 3)(lambda: from_level(z + k, self.down))

    def sides(self, k):
        x, y, c = self.x, self.y, self.c

        def fn(zq):
            sl = lin(1 - x, y, zq, c)
            self.wait(sl, 0)
            self.send(sl, 0, self.py, 1)
            self.core(sl, 0)
            sl = lin(x, 1 - y, zq, c)
            self.wait(sl, 1)
            self.send(sl, 1, self.px, 0)
            self.core(sl, 1)

        self.at(k, fn)

    def sides_rest(self, k):
        x, y, c = self.x, self.y, self.c

        def fn(zq):
            sl = lin(1 - x, y, zq, c)
            self.wait(sl, 1)
            self.core(sl, 1)
            sl = lin(x, 1 - y, zq, c)
            self.wait(sl, 0)
            self.core(sl, 0)

        self.at(k, fn)

    def diagonal(self, k):
        def fn(zq):
            sl = lin(1 - self.x, 1 - self.y, zq, self.c)
            for h in (0, 1):
                self.wait(sl, h)
                self.core(sl, h)

        self.at(k, fn)

    def from_sibling(self, xp):
        def body(fs, carry):
            for h in (0, 1):
                self.wait((2 * xp + 1 - self.c) * 8 + fs, h)
            return carry

        lax.fori_loop(0, 8, body, 0)

    def leave(self):
        x, y, z, c = self.x, self.y, self.z, self.c
        W = self.wait

        def body(zq, carry):
            sl = lin(x, y, zq, c)
            for t in (0, 1, 2):
                W(sl, 2, self.ssem.at[sl, t])
            pl.when((zq <= z) & (z < 3))(lambda: W(sl, 2, self.ssem.at[sl, 3]))
            pl.when((zq >= z) & (z > 0))(lambda: W(sl, 2, self.ssem.at[sl, 4]))
            sx = lin(1 - x, y, zq, c)
            W(sx, 0, self.ssem.at[sx, 1])
            W(sx, 2, self.ssem.at[sx, 2])
            sy = lin(x, 1 - y, zq, c)
            W(sy, 1, self.ssem.at[sy, 0])
            W(sy, 2, self.ssem.at[sy, 2])
            sd = lin(1 - x, 1 - y, zq, c)
            W(sd, 2, self.ssem.at[sd, 2])
            return carry

        lax.fori_loop(0, 4, body, 0)


FORWARD_OUT = ("hidden", "nested", "wqkv", "wo", "w1", "w2", "V", "VG", "qkv", "lse", "mixed", "xh1", "rstd1", "first_low", "act", "gd", "res", "d_outer")
FORWARD_SHAPES = dict(
    hidden=((LEN, D), jnp.bfloat16),
    nested=((1, 1728), jnp.float32),
    wqkv=((D, 3 * D), jnp.bfloat16),
    wo=((D, D), jnp.bfloat16),
    w1=((D, FF), jnp.bfloat16),
    w2=((FF, D), jnp.bfloat16),
    V=((16, FF), jnp.float32),
    VG=((16, FF), jnp.float32),
    qkv=((LEN, 3 * D), jnp.bfloat16),
    lse=((LEN, LN), jnp.float32),
    mixed=((LEN, D), jnp.bfloat16),
    xh1=((LEN, D), jnp.float32),
    rstd1=((LEN, 1), jnp.float32),
    first_low=((LEN, D), jnp.bfloat16),
    act=((LEN, FF), jnp.bfloat16),
    gd=((LEN, FF), jnp.bfloat16),
    res=((LEN, D), jnp.float32),
    d_outer=((LEN, D), jnp.bfloat16),
)


def own_slot(p, me, x_ref, F, G):
    start = me * p.sh
    r_first = start // LN
    s = start - r_first * LN
    r0 = r_first % 16
    lead = 32
    F[0 : lead + p.slot + 32] = jnp.zeros((lead + p.slot + 32, LN), F32)
    full = p.sh // LN
    rest = p.sh - full * LN
    F[lead : lead + full] = x_ref[: full * LN].astype(F32).reshape(full, LN)
    if rest:
        F[lead + full : lead + full + 1, :rest] = x_ref[full * LN :].astype(F32).reshape(1, rest)
    F[lead : lead + p.rows_in] = pltpu.roll(F[lead : lead + p.rows_in], s, 1)
    lane = lax.broadcasted_iota(jnp.int32, (p.slot, LN), 1)
    G[me] = jnp.where(lane >= s, F[pl.ds(lead - r0, p.slot), :], F[pl.ds(lead - 1 - r0, p.slot), :]).astype(BF)


def relayout_vector(p, r, which):
    at = sum(cnt for _, cnt in VECS[:which])
    base, cnt = VECS[which]
    g_lo = base // 16
    load_flat(p, r.slots, r.F, g_lo, -(-(base + cnt) // 16), base + cnt)
    for k in range(cnt):
        name, j = vec_at(at + k)
        f = base - 16 * g_lo + k
        r.V[name : name + 1, j * LN : (j + 1) * LN] = r.F[f : f + 1]


def relayout_rows(p, r, name, W, row, rows):
    base, _, w = {n: (b, k, c) for n, b, k, c in MATS}[name]
    lo = base + row * w
    g_lo = lo // 16
    load_flat(p, r.slots, r.F, g_lo, -(-(lo + rows * w) // 16), lo + rows * w)
    tile_rows(r.F, W, lo - 16 * g_lo, row, rows, w)


def gather_forward_kernel(p, x_ref, length, tok, hcot, ncot, *refs):
    n = len(FORWARD_OUT)
    outs = dict(zip(FORWARD_OUT, refs[:n]))
    loc = dict(zip(FORWARD_OUT, refs[n : 2 * n]))
    G, F, qb, xh2, rstd2, ssem, rsem, gosem, osem = refs[2 * n :]
    r = Refs(slots=G, length=length[0], tok=tok, hcot=hcot, ncot=ncot, F=F, qb=qb, xh2=xh2, rstd2=rstd2, **loc)
    g = Gather(p, G, ssem, rsem, gosem)
    own_slot(p, g.me, x_ref, F, G)
    g.enter()
    c0, c1 = g.c == 0, g.c == 1

    started = []

    def out(*names):
        for m in names:
            k = FORWARD_OUT.index(m)
            cp = pltpu.make_async_copy(loc[m], outs[m], osem.at[k])
            cp.start()
            started.append(cp)

    def part_rq_0():
        g.own(True)
        g.sides(0)
        g.go(0)
        g.along_z(1, True)
        g.sides(1)
        g.sides_rest(0)
        g.diagonal(0)
        g.go(1)
        g.along_z(2, True)
        g.sides(2)
        g.along_z(3, True)
        g.diagonal(1)
        g.sides_rest(1)
        g.sides(3)
        g.sides_rest(3)
        g.diagonal(2)
        g.sides_rest(2)
        g.diagonal(3)

    pl.when(c0)(part_rq_0)
    def part_rq_1():
        g.wait_go(0)
        g.own(False)
        g.wait_go(1)
        g.own_line(0)
        g.along_z(1, False)
        g.sides(0)
        g.along_z(2, False)
        g.own_line(1)
        g.along_z(3, False)
        g.own_line(3)
        g.own_line(2)
        g.from_sibling(0)
        g.sides(3)
        g.sides_rest(0)
        g.diagonal(0)

    pl.when(c1)(part_rq_1)
    relayout_vector(p, r, 0)
    for k in range(3):
        relayout_rows(p, r, "wqkv", r.wqkv, 256 * k, 256)
    out("wqkv")
    def part_qkv_1():
        g.from_sibling(1)
        g.sides(1)

    pl.when(c1)(part_qkv_1)
    forward_qkv(r)
    out("qkv")
    r.lse[...] = jnp.zeros_like(r.lse)

    def heads(hp, carry):
        def part_hd0_1():
            g.sides_rest(1)
            g.sides(2)
            g.sides_rest(3)

        pl.when((hp == 0) & c1)(part_hd0_1)
        def part_hd3_1():
            g.sides_rest(2)
            g.diagonal(3)

        pl.when((hp == 3) & c1)(part_hd3_1)
        def part_hd5_1():
            g.diagonal(1)

        pl.when((hp == 5) & c1)(part_hd5_1)
        forward_heads(r, hp)
        return carry

    lax.fori_loop(0, H // 2, heads, 0)
    out("lse", "mixed")
    def part_rw1b_1():
        g.diagonal(2)

    pl.when(c1)(part_rw1b_1)
    relayout_rows(p, r, "w1", r.w1, 448, 128)
    relayout_rows(p, r, "w1", r.w1, 576, 192)
    relayout_rows(p, r, "w2", r.w2, 0, 768)
    relayout_vector(p, r, 2)
    def part_rwo_0():
        g.from_sibling(0)

    pl.when(c0)(part_rwo_0)
    relayout_rows(p, r, "wo", r.wo, 0, 768)
    relayout_vector(p, r, 1)
    out("wo")
    forward_first(r)
    out("xh1", "rstd1", "first_low")
    def part_rw1a_0():
        g.from_sibling(1)

    pl.when(c0)(part_rw1a_0)
    relayout_rows(p, r, "w1", r.w1, 0, 256)
    relayout_rows(p, r, "w1", r.w1, 256, 192)
    out("w1")
    lax.fori_loop(0, FF // UP, lambda j, c: (forward_up(r, j), c)[1], 0)
    out("act", "gd")
    for k in range(1, 4):
        relayout_rows(p, r, "w2", r.w2, 768 * k, 768)
    relayout_vector(p, r, 3)
    out("w2", "V")
    tot = forward_second(r)
    out("hidden")
    d_pool = head(r, tot)
    out("nested")
    backward_second(r, d_pool)
    out("VG", "res", "d_outer")
    g.leave()
    for cp in started:
        cp.wait()


def gather_forward(p, shard, length, tok, hcot, ncot):
    S = jax.ShapeDtypeStruct
    vm = pl.BlockSpec(memory_space=pltpu.VMEM)
    sm = pl.BlockSpec(memory_space=pltpu.SMEM)
    hbm = pl.BlockSpec(memory_space=pl.ANY)
    VM = pltpu.VMEM
    DM = pltpu.SemaphoreType.DMA
    shapes = [FORWARD_SHAPES[m] for m in FORWARD_OUT]
    res = pl.pallas_call(
        functools.partial(gather_forward_kernel, p),
        out_shape=[S(*s) for s in shapes],
        in_specs=[vm, sm, vm, vm, vm],
        out_specs=[hbm] * len(shapes),
        scratch_shapes=[VM(*s) for s in shapes]
        + [VM((p.n, p.slot, LN), BF), VM((6144 + 64, LN), F32), VM((1, 3 * D), F32), VM((LEN, D), F32), VM((LEN, 1), F32)]
        + [DM((p.n, 5)), DM((p.n, 2)), pltpu.SemaphoreType.REGULAR((2,)), DM((len(shapes),))],
        compiler_params=pltpu.CompilerParams(collective_id=0, has_side_effects=True, vmem_limit_bytes=64 << 20),
    )(shard, length, tok, hcot, ncot)
    return dict(zip(FORWARD_OUT, res))


SCHEDULE = (
    (4, 1, 0, "diag", 1, 2, 1),
    (5, 1, 0, "diag", 1, 1, 1),
    (8, 1, 1, "yline", 1, 2, 1),
    (8, 1, 0, "xline", 1, 1, 1),
    (10, 1, 1, "yline", 1, 1, 1),
    (10, 1, 0, "diag", 1, 3, 1),
    (10, 0, 0, "diag", 1, 0, 1),
    (11, 0, 0, "diag", 1, 2, 2),
    (12, 1, 1, "diag", 0, 0, 1),
    (12, 0, 0, "diag", 1, 1, 1),
    (13, 1, 1, "diag", 0, 2, 1),
    (13, 1, 1, "diag", 0, 1, 1),
    (13, 1, 0, "yline", 0, 2, 1),
    (14, 1, 1, "diag", 0, 3, 1),
    (14, 0, 0, "xline", 1, 2, 1),
    (15, 0, 1, "yline", 1, 3, 1),
    (16, 1, 1, "xline", 0, 2, 1),
    (16, 0, 0, "xline", 1, 1, 1),
    (16, 1, 0, "yline", 0, 1, 1),
    (17, 1, 1, "own", 1, 1, 1),
    (17, 0, 1, "yline", 1, 2, 1),
    (18, 0, 0, "xline", 1, 0, 1),
    (18, 0, 1, "yline", 1, 1, 1),
    (18, 1, 1, "xline", 0, 1, 1),
    (18, 1, 0, "yline", 0, 3, 1),
    (19, 1, 0, "own", 0, 2, 1),
    (19, 1, 1, "xline", 0, 0, 1),
    (20, 0, 0, "yline", 0, 1, 1),
    (20, 0, 1, "diag", 0, 1, 2),
    (20, 0, 0, "yline", 0, 0, 1),
    (20, 0, 1, "own", 1, 2, 1),
    (20, 1, 0, "xline", 1, 2, 1),
    (21, 1, 1, "yline", 1, 0, 1),
    (21, 0, 1, "diag", 0, 0, 1),
    (21, 0, 1, "own", 1, 1, 1),
    (21, 1, 0, "diag", 1, 0, 1),
    (21, 0, 0, "own", 0, 1, 1),
    (21, 1, 0, "xline", 1, 3, 1),
    (22, 1, 0, "yline", 0, 0, 1),
    (22, 1, 0, "own", 0, 1, 1),
    (22, 1, 0, "own", 0, 0, 1),
    (22, 0, 0, "yline", 0, 2, 1),
    (22, 0, 1, "xline", 0, 1, 1),
    (22, 0, 0, "xline", 1, 3, 1),
    (22, 0, 1, "yline", 1, 0, 1),
    (22, 1, 1, "own", 1, 0, 1),
    (22, 0, 1, "xline", 0, 0, 1),
    (22, 0, 1, "xline", 0, 2, 1),
    (22, 0, 0, "own", 0, 0, 1),
    (22, 0, 0, "own", 0, 2, 1),
    (22, 0, 0, "yline", 0, 3, 1),
    (22, 0, 1, "diag", 0, 3, 1),
    (22, 0, 1, "own", 1, 0, 1),
    (22, 0, 1, "xline", 0, 3, 1),
    (22, 1, 0, "xline", 1, 0, 1),
    (22, 1, 1, "own", 1, 2, 1),
    (22, 1, 1, "xline", 0, 3, 1),
    (22, 1, 1, "yline", 1, 3, 1),
)


class Scatter:
    def __init__(self, p, FG, R, D0, D1, X, Y, Z, A, sems):
        self.p, self.FG, self.R, self.D0, self.D1, self.X, self.Y, self.Z, self.A = p, FG, R, D0, D1, X, Y, Z, A
        self.sib_s, self.sib_r, self.d_s, self.d_r, self.x_s, self.x_r, self.y_s, self.y_r, self.z_s, self.z_r = sems
        self.x, self.y, self.z, self.c = coords()
        x, y, z, c = self.x, self.y, self.z, self.c
        self.SL = p.slot
        self.half = p.slot // 32 * 16
        self.px, self.py, self.pc = dev(1 - x, y, z, c), dev(x, 1 - y, z, c), dev(x, y, z, 1 - c)

    def zq(self, b):
        d = lax.rem(b + 1, 4)
        z = self.z
        return lax.rem(z % 2 + d % 2, 2) + 2 * lax.rem(z // 2 + d // 2, 2)

    def enter(self):
        x, y, c = self.x, self.y, self.c
        barrier([self.px, self.py, self.pc] + [dev(x, y, self.zq(b), c) for b in range(3)])

    def row0(self, slot):
        return pl.multiple_of((slot * self.p.sh) // LN // 16 * 16, 16)

    def fg(self, slot):
        return self.row0(slot)

    def copy(self, src, dst, ssem, rsem, to):
        return pltpu.make_async_remote_copy(src_ref=src, dst_ref=dst, send_sem=ssem, recv_sem=rsem, device_id=to, device_id_type=MESH)

    def wait(self, ref, sem):
        pltpu.make_async_copy(ref, ref, sem).wait()

    def to_sibling(self, xp):
        def body(k, _):
            dp = 2 * xp + 1 - self.c
            i = 8 * xp + k
            self.copy(self.FG.at[pl.ds(self.row0(dp * 8 + k), self.SL)], self.R.at[i], self.sib_s.at[i], self.sib_r.at[i], self.pc).start()
            return 0

        lax.fori_loop(0, 8, body, 0)

    def add(self, dst, d0, rows, srcs, U=176):
        def body(t, _):
            r = pl.multiple_of(t * U, 16)
            v = None
            for s, s0 in srcs:
                e = s[pl.ds(s0 + r, U)].astype(F32)
                v = e if v is None else v + e
            dst[pl.ds(d0 + r, U)] = v.astype(dst.dtype)
            return 0

        lax.fori_loop(0, rows // U, body, 0)

    def have(self, xp, yq, zq):
        fs = zq * 2 + yq
        i = 8 * xp + fs
        self.wait(self.R.at[i], self.sib_r.at[i])
        return i, self.row0((2 * xp + self.c) * 8 + fs)

    def diag(self, xp, b):
        i, g = self.have(xp, 1 - self.y, self.zq(b))
        half, rest = self.half, self.SL - self.half
        R = self.R.at[i]
        self.add(R, 0, self.SL, [(self.FG, g), (R, 0)])
        self.copy(R.at[pl.ds(0, half)], self.D0.at[b], self.d_s.at[0, b], self.d_r.at[0, b], self.py).start()
        self.copy(R.at[pl.ds(half, rest)], self.D1.at[b], self.d_s.at[1, b], self.d_r.at[1, b], self.px).start()

    def xline(self, xp, b):
        i, g = self.have(xp, self.y, self.zq(b))
        half, rest = self.half, self.SL - self.half
        R = self.R.at[i]
        self.wait(self.D0.at[b], self.d_r.at[0, b])
        self.add(R, half, rest, [(self.FG, g + half), (R, half)])
        self.add(R, 0, half, [(self.FG, g), (R, 0), (self.D0.at[b], 0)])
        self.copy(R, self.X.at[b], self.x_s.at[b], self.x_r.at[b], self.px).start()

    def yline(self, xp, b):
        i, g = self.have(xp, 1 - self.y, self.zq(b))
        half, rest = self.half, self.SL - self.half
        R = self.R.at[i]
        self.wait(self.D1.at[b], self.d_r.at[1, b])
        self.add(R, 0, half, [(self.FG, g), (R, 0)])
        self.add(R, half, rest, [(self.FG, g + half), (R, half), (self.D1.at[b], 0)])
        self.copy(R, self.Y.at[b], self.y_s.at[b], self.y_r.at[b], self.py).start()

    def own(self, xp, b):
        i, g = self.have(xp, self.y, self.zq(b))
        R = self.R.at[i]
        self.wait(self.X.at[b], self.x_r.at[b])
        self.wait(self.Y.at[b], self.y_r.at[b])
        self.add(R, 0, self.SL, [(self.FG, g), (R, 0), (self.X.at[b], 0), (self.Y.at[b], 0)])
        self.copy(R, self.Z.at[b], self.z_s.at[b], self.z_r.at[b], dev(self.x, self.y, self.zq(b), self.c)).start()

    def last(self, xp, out):
        p, SL, A = self.p, self.SL, self.A
        i, g = self.have(xp, self.y, self.z)
        self.wait(self.X.at[3], self.x_r.at[3])
        self.wait(self.Y.at[3], self.y_r.at[3])
        for b in range(3):
            self.wait(self.Z.at[b], self.z_r.at[b])
        self.add(A, 0, SL, [(self.FG, g), (self.R.at[i], 0), (self.X.at[3], 0), (self.Y.at[3], 0)] + [(self.Z.at[b], 0) for b in range(3)])
        start = lin(self.x, self.y, self.z, self.c) * p.sh
        r_first = start // LN
        s = start - r_first * LN
        r0 = r_first % 16
        A[0:SL] = pltpu.roll(A[0:SL], lax.rem(LN - s, LN), 1)
        lane = lax.broadcasted_iota(jnp.int32, (p.rows_in, LN), 1)
        out[...] = jnp.where(lane < LN - s, A[pl.ds(r0, p.rows_in), :], A[pl.ds(r0 + 1, p.rows_in), :])

    def after(self, part, index=None):
        for c in (0, 1):
            for x in (0, 1):
                todo = [e for e in SCHEDULE if e[:3] == (part, c, x)]
                if todo:
                    here = (self.c == c) & (self.x == x)
                    if index is not None:
                        here = here & (index[0] == index[1])

                    def run(todo=todo):
                        for _, _, _, step, xp, b0, n in todo:
                            lax.fori_loop(b0, b0 + n, lambda b, k: (getattr(self, step)(xp, b), k)[1], 0)

                    pl.when(here)(run)

    def leave(self):
        for k in range(16):
            self.wait(self.R.at[k], self.sib_s.at[k])
        for b in range(4):
            self.wait(self.D0.at[b], self.d_s.at[0, b])
            self.wait(self.D1.at[b], self.d_s.at[1, b])
            self.wait(self.X.at[b], self.x_s.at[b])
            self.wait(self.Y.at[b], self.y_s.at[b])
        for b in range(3):
            self.wait(self.Z.at[b], self.z_s.at[b])


BACK_IN = ("act", "d_outer", "w2", "gd", "first_low", "w1", "res", "xh1", "rstd1", "V", "VG", "mixed", "wo", "qkv", "lse", "tok")


def backward_scatter_kernel(p, length, *refs):
    n = len(BACK_IN)
    src = dict(zip(BACK_IN, refs[:n]))
    wqkv_in = refs[n]
    igrad, out = refs[n + 1 : n + 3]
    loc = dict(zip(BACK_IN, refs[n + 3 : 2 * n + 3]))
    FG, F, E, R, D0, D1, X, Y, Z, lsem, osem, *sems = refs[2 * n + 3 :]
    r = Refs(length=length[0], FG=FG, F=F, E=E, **loc)
    r.dqkv, r.d_branch, r.d_mixed = r.act, r.first_low, r.d_outer
    sc = Scatter(p, FG, R, D0, D1, X, Y, Z, F, sems)
    mats = {m: (b, k, c) for m, b, k, c in MATS}
    loads = {m: pltpu.make_async_copy(src[m], loc[m], lsem.at[k]) for k, m in enumerate(BACK_IN)}
    for m in BACK_IN:
        loads[m].start()

    def need(*names):
        for m in names:
            loads[m].wait()

    sc.enter()
    c0, c1 = sc.c == 0, sc.c == 1
    x0, x1 = sc.x == 0, sc.x == 1

    def both(cond, fn):
        pl.when(cond)(fn)

    need("act", "d_outer", "VG")
    weight_grad(r, r.act, r.d_outer, *mats["w2"], RB=1024, CB=2)
    edge_grads(r, 3)
    both(c0, lambda: sc.to_sibling(1))
    sc.after(1)
    need("w2", "gd")

    def act_part(j, carry):
        backward_act(r, j)
        for k in range(4):
            sc.after(2 + k, (j, k))
        return carry

    lax.fori_loop(0, FF // UP, act_part, 0)
    q_loads = [pltpu.make_async_copy(wqkv_in.at[:, pl.ds(k * D, D)], r.w2.at[pl.ds(k * D, D)], lsem.at[n + k]) for k in range(3)]
    for q in q_loads:
        q.start()
    need("first_low")
    weight_grad(r, r.first_low, r.gd, *mats["w1"], hook=lambda i: [sc.after(6 + k, (i, k)) for k in range(2)])
    edge_grads(r, 2)
    both(c1, lambda: sc.to_sibling(1))
    sc.after(8)
    need("w1", "res", "xh1", "rstd1", "V")
    backward_first(r)
    sc.after(9)
    need("mixed")
    weight_grad(r, r.mixed, r.d_branch, *mats["wo"])
    edge_grads(r, 1)
    both(c0, lambda: sc.to_sibling(0))
    sc.after(10)
    need("wo")
    backward_mixed(r)
    sc.after(11)
    need("qkv", "lse")

    def heads(hp, carry):
        backward_heads(r, hp)
        for k in range(6):
            sc.after(12 + k, (hp, k))
        return carry

    lax.fori_loop(0, H // 2, heads, 0)
    need("tok")
    weight_grad(r, r.tok, r.dqkv, *mats["wqkv"], hook=lambda i: [sc.after(18 + k, (i, k)) for k in range(2)])
    edge_grads(r, 0)
    both(c1, lambda: sc.to_sibling(0))
    sc.after(20)
    for q in q_loads:
        q.wait()

    def tokens(b, carry):
        o = rows_of(b, LEN)
        v = r.res[o, :]
        for part in range(3):
            v = v + mm_nt(r.dqkv[o, part * D : (part + 1) * D], r.w2[part * D : (part + 1) * D, :])
        r.res[o, :] = v
        sc.after(21, (b, 0))
        return carry

    lax.fori_loop(0, 1, tokens, 0)
    grad_out = pltpu.make_async_copy(r.res, igrad, osem)
    grad_out.start()
    sc.after(22)
    both(x0, lambda: sc.last(0, out))
    both(x1, lambda: sc.last(1, out))
    sc.leave()
    grad_out.wait()


def backward_scatter(p, length, wqkv, **arrays):
    S = jax.ShapeDtypeStruct
    sm = pl.BlockSpec(memory_space=pltpu.SMEM)
    hbm = pl.BlockSpec(memory_space=pl.ANY)
    ins = [arrays[m] for m in BACK_IN]
    SL = p.slot
    half = SL // 32 * 16
    VM = pltpu.VMEM
    DM = pltpu.SemaphoreType.DMA
    igrad, o = pl.pallas_call(
        functools.partial(backward_scatter_kernel, p),
        out_shape=[S((LEN, D), F32), S((p.rows_in, LN), F32)],
        in_specs=[sm] + [hbm] * (len(ins) + 1),
        out_specs=[hbm, pl.BlockSpec(memory_space=pltpu.VMEM)],
        scratch_shapes=[VM(a.shape, a.dtype) for a in ins]
        + [VM((flat_rows(p), LN), BF), VM((6144 + 64, LN), F32), VM((160, LN), F32), VM((16, SL, LN), BF), VM((4, half, LN), BF), VM((4, SL - half, LN), BF), VM((4, SL, LN), BF), VM((4, SL, LN), BF), VM((3, SL, LN), BF)]
        + [DM((len(ins) + 3,)), DM, DM((16,)), DM((16,)), DM((2, 4)), DM((2, 4)), DM((4,)), DM((4,)), DM((4,)), DM((4,)), DM((3,)), DM((3,))],
        compiler_params=pltpu.CompilerParams(collective_id=1, has_side_effects=True, vmem_limit_bytes=64 << 20),
    )(length, *ins, wqkv)
    return igrad, o


def finish_copies(p, shards, hidden, igrad, nested):
    S = jax.ShapeDtypeStruct
    vm = pl.BlockSpec(memory_space=pltpu.VMEM)

    def kernel(a, b, c, d, a_out, b_out, c_out, d_out):
        a_out[...] = a[...].reshape(p.rows_in * LN)[: p.sh]
        b_out[...] = b[...]
        c_out[...] = c[...]
        d_out[...] = d[...]

    arrays = (shards, hidden, igrad, nested)
    return pl.pallas_call(
        kernel,
        out_shape=[S((p.sh,), F32)] + [S(a.shape, a.dtype) for a in arrays[1:]],
        in_specs=[vm] * 4,
        out_specs=[vm] * 4,
    )(*arrays)


def on_device(p, fast, tokens, lengths, weight_shards, hidden_cotangent, nested_cotangent):
    tok = tokens.reshape(LEN, D)
    hcot = hidden_cotangent.reshape(LEN, D)
    if fast:
        f = gather_forward(p, weight_shards, lengths, tok, hcot, nested_cotangent)
        igrad, shards = backward_scatter(p, lengths, tok=tok, **{m: f[m] for m in BACK_IN + ("wqkv",) if m != "tok"})
        shards, f["hidden"], igrad, f["nested"] = finish_copies(p, shards, f["hidden"], igrad, f["nested"])
    else:
        slots = lax.all_gather(build_slot(p, weight_shards, me_of), AX, axis=0)
        f = dict(zip(FORWARD_OUT, forward_local(p, slots, lengths, tok, hcot, nested_cotangent)))
        igrad, flat = backward_local(p, lengths, tok, *[f[m] for m in FORWARD_OUT[6:] + FORWARD_OUT[2:6]])
        shards = scatter_plain(p, flat)
    return (f["hidden"].reshape(1, LEN, D), f["nested"], igrad.reshape(1, LEN, D), shards)


def solution(mesh):
    in_specs = (
        P(("dp", "fsdp"), None, None),
        P(("dp", "fsdp")),
        P(("dp", "fsdp")),
        P(("dp", "fsdp"), None, None),
        P(("dp", "fsdp"), None),
    )
    out_specs = (
        P(("dp", "fsdp"), None, None),
        P(("dp", "fsdp"), None),
        P(("dp", "fsdp"), None, None),
        P(("dp", "fsdp")),
    )
    p = plan(mesh.shape["dp"] * mesh.shape["fsdp"])
    fast = (mesh.shape["dp"], mesh.shape["fsdp"]) == (4, 8)
    return jax.shard_map(
        functools.partial(on_device, p, fast), mesh=mesh, in_specs=in_specs, out_specs=out_specs, check_vma=False
    )
```

```python
import functools
import math

import jax
import jax.numpy as jnp
from jax import lax
from jax.experimental import pallas as pl
from jax.experimental.pallas import tpu as pltpu
from jax.sharding import PartitionSpec as P

AX = ("dp", "fsdp")
MESH = pl.DeviceIdType.MESH
D = 768
H = 12
HD = 64
FF = 3072
LEN = 512
E2 = 512
E3 = 256
E4 = 128
E5 = 64


epsilon = 1e-05


PAR=7088640; LN=128
class Plan: pass
def plan(n):
    p=Plan(); p.n=n; p.sh=PAR//n
    st=[i*p.sh for i in range(n)]
    p.g0=[s//LN//16 for s in st]
    p.g1=[(s+p.sh-1)//LN//16 for s in st]
    p.slot=16*max(b-a+1 for a,b in zip(p.g0,p.g1))
    p.rows_in=-(-p.sh//LN)
    return p
MATS=[("wqkv",0,D,18),("wo",13836,D,6),("w1",18462,D,24),("w2",36918,FF,6)]
VECS=[(13824,12),(18444,18),(36894,24),(55350,30)]

def build_slot_kernel(p,me_of,x_ref,o_ref,q_ref):
    i=me_of(); start=i*p.sh; r_first=start//LN; s=start-r_first*LN; r0=r_first%16
    lead=32
    q_ref[...]=jnp.zeros_like(q_ref)
    q=pltpu.roll(x_ref[...].astype(jnp.float32),s,1)
    q_ref[lead:lead+p.rows_in]=q
    lane=lax.broadcasted_iota(jnp.int32,(p.slot,LN),1)
    a=q_ref[pl.ds(lead-r0,p.slot),:]
    b=q_ref[pl.ds(lead-1-r0,p.slot),:]
    o_ref[...]=jnp.where(lane>=s,a,b).astype(jnp.bfloat16)

def build_slot(p,shard,me_of):
    x=jnp.pad(shard,(0,p.rows_in*LN-p.sh)).reshape(p.rows_in,LN)
    return pl.pallas_call(functools.partial(build_slot_kernel,p,me_of),out_shape=jax.ShapeDtypeStruct((p.slot,LN),jnp.bfloat16),
        scratch_shapes=[pltpu.VMEM((32+p.slot+32,LN),jnp.float32)])(x)

def load_flat(p,slots,F,g_lo,g_hi,need=None):
    for i in range(p.n):
        a=max(g_lo,p.g0[i]); b=min(g_hi,p.g1[i]+1)
        if a>=b: continue
        shared_first = i>0 and p.g0[i]==p.g1[i-1] and a==p.g0[i]
        a2=a+1 if shared_first else a
        b2=b
        apart=need is not None and need<=(i+1)*p.sh//LN
        if i+1<p.n and p.g1[i]==p.g0[i+1] and b==p.g1[i]+1 and not apart: b2=b-1
        if i+1<p.n and b2<b and b-1>=g_lo:
            g=b-1
            F[16*(g-g_lo):16*(g-g_lo)+16]=slots[i,16*(g-p.g0[i]):16*(g-p.g0[i])+16].astype(jnp.float32)+slots[i+1,0:16].astype(jnp.float32)
        cnt=b2-a2
        if cnt<=0: continue
        U=16
        nb,rem=cnt//U,cnt%U
        def body(t,_,i=i,a2=a2):
            src=pl.multiple_of(16*(a2-p.g0[i])+t*16*U,16); dst=pl.multiple_of(16*(a2-g_lo)+t*16*U,16)
            F[pl.ds(dst,16*U)]=slots[i,pl.ds(src,16*U)].astype(jnp.float32)
            return 0
        lax.fori_loop(0,nb,body,0)
        if rem:
            src=16*(a2-p.g0[i])+nb*16*U; dst=16*(a2-g_lo)+nb*16*U
            F[dst:dst+16*rem]=slots[i,src:src+16*rem].astype(jnp.float32)

def coords():
    dp=lax.axis_index("dp"); fs=lax.axis_index("fsdp")
    return dp//2,fs%2,fs//2,dp%2
def dev(x,y,z,c): return (x*2+c, z*2+y)
def lin(x,y,z,c): return (x*2+c)*8+z*2+y
def barrier(partners):
    bar=pltpu.get_barrier_semaphore()
    for q in partners: pl.semaphore_signal(bar,inc=1,device_id=q,device_id_type=MESH)
    pl.semaphore_wait(bar,len(partners))

TOT=PAR//LN
def flat_rows(p): return max(16*p.g0[-1]+p.slot, EDGES[-1][0]+EDGES[-1][1])
def owner_row(rho):
    for k,(name,base,rows,w) in enumerate(MATS):
        if base<=rho<base+rows*w: return ("m",k,(rho-base)//w,(rho-base)%w)
    at=0
    for base,cnt in VECS:
        if base<=rho<base+cnt: return ("v",at+rho-base)
        at+=cnt
    return None

def me_of():
    return lax.axis_index(AX)


def finish_kernel(p, a_ref, out, A):
    SL = p.slot
    start = me_of() * p.sh
    r_first = start // LN
    s = start - r_first * LN
    r0 = r_first % 16
    A[0:SL] = pltpu.roll(a_ref[...], lax.rem(LN - s, LN), 1)
    lane = lax.broadcasted_iota(jnp.int32, (p.rows_in, LN), 1)
    out[...] = jnp.where(lane < LN - s, A[pl.ds(r0, p.rows_in), :], A[pl.ds(r0 + 1, p.rows_in), :])


def scatter_plain(p, flat):
    parts = jnp.concatenate([flat[16 * g : 16 * g + p.slot] for g in p.g0]).astype(jnp.float32)
    mine = lax.psum_scatter(parts, AX, scatter_dimension=0, tiled=True)
    o = pl.pallas_call(
        functools.partial(finish_kernel, p),
        out_shape=jax.ShapeDtypeStruct((p.rows_in, LN), jnp.float32),
        scratch_shapes=[pltpu.VMEM((p.slot + 32, LN), jnp.float32)],
    )(mine)
    return o.reshape(-1)[: p.sh]

EPS = 1e-05
F32 = jnp.float32
BF = jnp.bfloat16
SQ = math.sqrt(0.5)
PHI = 1.0 / math.sqrt(2.0 * math.pi)
VNAMES = (
    ("q_bias", D),
    ("v_bias", D),
    ("out_bias", D),
    ("first_gain", D),
    ("first_shift", D),
    ("up_bias", FF),
    ("down_bias", D),
    ("second_gain", D),
    ("second_shift", D),
    ("exit_gain", D),
    ("exit_shift", D),
)
VI = {name: k for k, (name, _) in enumerate(VNAMES)}
PREFIXES = (D, E2, E3, E4, E5)
SCALE = 1.0 / math.sqrt(HD)
UP = 768


def mm(a, b):
    return jnp.dot(a, b, preferred_element_type=F32)


def mm_nt(a, b):
    return lax.dot_general(a, b, (((1,), (1,)), ((), ())), preferred_element_type=F32)


def mm_tn(a, b):
    return lax.dot_general(a, b, (((0,), (0,)), ((), ())), preferred_element_type=F32)


def vrow(V, name):
    k = VI[name]
    return V[k : k + 1, : VNAMES[k][1]]


def mean_last(a):
    return jnp.mean(a, axis=-1, keepdims=True)


def sum_rows(a):
    return jnp.sum(a, axis=0, keepdims=True)


def forward_qkv(r):
    bias = jnp.concatenate([vrow(r.V, "q_bias"), jnp.zeros((1, D), F32), vrow(r.V, "v_bias")], axis=1)
    r.qb[...] = bias

    def body(j, _):
        o = pl.ds(pl.multiple_of(j * D, D), D)
        r.qkv[:, o] = (mm(r.tok[...], r.wqkv[:, o]) + r.qb[:, o]).astype(BF)
        return 0

    lax.fori_loop(0, 3, body, 0)


def half_lanes(h):
    lane = lax.broadcasted_iota(jnp.int32, (LEN, LN), 1)
    return lane < HD if h == 0 else lane >= HD


def pair(r, part, hp):
    return r.qkv[:, pl.ds(pl.multiple_of(part * D + hp * LN, LN), LN)]


def forward_heads(r, hp):
    q, k, v = pair(r, 0, hp) * SCALE, pair(r, 1, hp), pair(r, 2, hp)
    valid = lax.broadcasted_iota(jnp.int32, (1, LEN), 1) < r.length
    out = None
    lse_all = r.lse[...]
    lane = lax.broadcasted_iota(jnp.int32, (LEN, LN), 1)
    for h in range(2):
        qh = jnp.where(half_lanes(h), q, jnp.zeros_like(q))
        s = jnp.where(valid, mm_nt(qh, k), -1e9)
        m = jnp.max(s, axis=1, keepdims=True)
        e = jnp.exp(s - m)
        l = jnp.sum(e, axis=1, keepdims=True)
        low = (e * (1.0 / l)).astype(BF)
        o = mm(low, v)
        out = o if out is None else jnp.where(half_lanes(0), out, o)
        lse_all = jnp.where(lane == 2 * hp + h, m + jnp.log(l), lse_all)
    r.lse[...] = lse_all
    r.mixed[:, pl.ds(pl.multiple_of(hp * LN, LN), LN)] = out.astype(BF)


def rows_of(b, n):
    return pl.ds(pl.multiple_of(b * n, n), n)


def forward_first(r):
    def body(b, _):
        o = rows_of(b, LEN)
        v = r.tok[o, :].astype(F32) + mm(r.mixed[o, :], r.wo[...]) + vrow(r.V, "out_bias")
        cen = v - mean_last(v)
        rstd = lax.rsqrt(mean_last(cen * cen) + EPS)
        xh = cen * rstd
        r.xh1[o, :] = xh
        r.rstd1[o, :] = rstd
        r.first_low[o, :] = (xh * vrow(r.V, "first_gain") + vrow(r.V, "first_shift")).astype(BF)
        return 0

    lax.fori_loop(0, 1, body, 0)


def forward_up(r, j):
    o = pl.ds(pl.multiple_of(j * UP, UP), UP)
    v = mm(r.first_low[...], r.w1[:, o]) + r.V[VI["up_bias"] : VI["up_bias"] + 1, o]
    cdf = 0.5 * (1.0 + lax.erf(v * SQ))
    r.act[:, o] = (v * cdf).astype(BF)
    r.gd[:, o] = (cdf + v * (PHI * jnp.exp(-0.5 * v * v))).astype(BF)


def forward_second(r):
    def body(b, tot):
        o = rows_of(b, LEN)
        first = r.xh1[o, :] * vrow(r.V, "first_gain") + vrow(r.V, "first_shift")
        v = first + mm(r.act[o, :], r.w2[...]) + vrow(r.V, "down_bias")
        cen = v - mean_last(v)
        rstd = lax.rsqrt(mean_last(cen * cen) + EPS)
        xh = cen * rstd
        r.xh2[o, :] = xh
        r.rstd2[o, :] = rstd
        t = lax.broadcasted_iota(jnp.int32, (LEN, 1), 0)
        hid = (xh * vrow(r.V, "second_gain") + vrow(r.V, "second_shift")) * (t < r.length).astype(F32)
        r.hidden[o, :] = hid.astype(BF)
        return tot + sum_rows(hid)

    return lax.fori_loop(0, 1, body, jnp.zeros((1, D), F32))


def head(r, tot):
    inv_len = 1.0 / jnp.full((1, 1), r.length, jnp.int32).astype(F32)
    pooled = tot * inv_len
    cen = pooled - mean_last(pooled)
    rstd = lax.rsqrt(mean_last(cen * cen) + EPS)
    xh = cen * rstd
    gain = vrow(r.V, "exit_gain")
    emb = xh * gain + vrow(r.V, "exit_shift")
    d_emb = jnp.zeros((1, D), F32)
    at = 0
    for m in PREFIXES:
        e = emb[:, :m]
        inv = lax.rsqrt(jnp.sum(e * e, axis=1, keepdims=True) * (1.0 / m) + EPS)
        out = e * inv
        r.nested[:, at : at + m] = out
        c = r.ncot[:, at : at + m]
        g = inv * (c - out * (jnp.sum(c * out, axis=1, keepdims=True) * (1.0 / m)))
        d_emb = d_emb + (g if m == D else jnp.concatenate([g, jnp.zeros((1, D - m), F32)], axis=1))
        at += m
    put_grad(r, "exit_gain", d_emb * xh)
    put_grad(r, "exit_shift", d_emb)
    dx = d_emb * gain
    return rstd * (dx - mean_last(dx) - xh * mean_last(dx * xh)) * inv_len


def put_grad(r, name, value):
    k = VI[name]
    r.VG[k : k + 1, : VNAMES[k][1]] = value


def norm_back(dy, gain, xh, rstd):
    dx = dy * gain
    return rstd * (dx - mean_last(dx) - xh * mean_last(dx * xh))


def backward_second(r, d_pool):
    def body(b, c):
        o = rows_of(b, LEN)
        t = lax.broadcasted_iota(jnp.int32, (LEN, 1), 0)
        dy = (r.hcot[o, :].astype(F32) + d_pool) * (t < r.length).astype(F32)
        xh = r.xh2[o, :]
        res = norm_back(dy, vrow(r.V, "second_gain"), xh, r.rstd2[o, :])
        r.res[o, :] = res
        low = res.astype(BF)
        r.d_outer[o, :] = low
        return (c[0] + sum_rows(dy * xh), c[1] + sum_rows(dy), c[2] + sum_rows(low.astype(F32)))

    z = jnp.zeros((1, D), F32)
    a, b, c = lax.fori_loop(0, 1, body, (z, z, z))
    put_grad(r, "second_gain", a)
    put_grad(r, "second_shift", b)
    put_grad(r, "down_bias", c)


def backward_act(r, j):
    o = pl.ds(pl.multiple_of(j * UP, UP), UP)
    d = (mm_nt(r.d_outer[...], r.w2[o, :]) * r.gd[:, o].astype(F32)).astype(BF)
    r.gd[:, o] = d
    r.VG[VI["up_bias"] : VI["up_bias"] + 1, o] = sum_rows(d.astype(F32))


def backward_first(r):
    def body(b, c):
        o = rows_of(b, LEN)
        dy = mm_nt(r.gd[o, :], r.w1[...]) + r.res[o, :]
        xh = r.xh1[o, :]
        res = norm_back(dy, vrow(r.V, "first_gain"), xh, r.rstd1[o, :])
        r.res[o, :] = res
        low = res.astype(BF)
        r.d_branch[o, :] = low
        return (c[0] + sum_rows(dy * xh), c[1] + sum_rows(dy), c[2] + sum_rows(low.astype(F32)))

    z = jnp.zeros((1, D), F32)
    a, b, c = lax.fori_loop(0, 1, body, (z, z, z))
    put_grad(r, "first_gain", a)
    put_grad(r, "first_shift", b)
    put_grad(r, "out_bias", c)


def backward_mixed(r):
    r.d_mixed[...] = mm_nt(r.d_branch[...], r.wo[...]).astype(BF)


def backward_heads(r, hp):
    q, k, v = pair(r, 0, hp) * SCALE, pair(r, 1, hp), pair(r, 2, hp)
    k_scaled = k * SCALE
    cols = pl.ds(pl.multiple_of(hp * LN, LN), LN)
    dm = r.d_mixed[:, cols]
    valid = lax.broadcasted_iota(jnp.int32, (1, LEN), 1) < r.length
    lane = lax.broadcasted_iota(jnp.int32, (LEN, LN), 1)
    zero = jnp.zeros_like(q)
    dm_mixed = dm.astype(F32) * r.mixed[:, cols].astype(F32)
    dq = dk = dv = None
    for h in range(2):
        here = half_lanes(h)
        qh, kh, dmh = jnp.where(here, q, zero), jnp.where(here, k_scaled, zero), jnp.where(here, dm, zero)
        lse = jnp.sum(jnp.where(lane == 2 * hp + h, r.lse[...], 0.0), axis=1, keepdims=True)
        s = jnp.where(valid, mm_nt(qh, k), -1e9)
        p = jnp.exp(s - lse)
        dp = mm_nt(dmh, v)
        delta = jnp.sum(jnp.where(here, dm_mixed, 0.0), axis=1, keepdims=True)
        ds = (p * (dp - delta)).astype(BF)
        a, b, c = mm(ds, kh), mm_tn(ds, qh), mm_tn(p.astype(BF), dmh)
        dq, dk, dv = (a, b, c) if dq is None else (dq + a, dk + b, dv + c)
    dq, dk, dv = dq.astype(BF), dk.astype(BF), dv.astype(BF)
    for part, g in ((0, dq), (1, dk), (2, dv)):
        r.dqkv[:, pl.ds(pl.multiple_of(part * D + hp * LN, LN), LN)] = g
    k = VI["q_bias"]
    r.VG[k : k + 1, cols] = sum_rows(dq.astype(F32))
    k = VI["v_bias"]
    r.VG[k : k + 1, cols] = sum_rows(dv.astype(F32))


def backward_tokens(r, b):
    o = rows_of(b, 128)
    v = r.res[o, :]
    for part in range(3):
        v = v + mm_nt(r.dqkv[o, part * D : (part + 1) * D], r.wqkv[:, part * D : (part + 1) * D])
    r.res[o, :] = v


EDGES = ((13824, 16), (18432, 32), (36880, 48), (55344, 64))


def edge_at(row):
    at = 0
    for base, rows in EDGES:
        if base <= row < base + rows:
            return at + row - base
        at += rows
    return None


def weight_grad(r, lhs, rhs, base, rows, w, RB=256, CB=6, hook=None):
    lead = base % 16
    step_rows = RB * w
    F = r.F
    if lead:
        F[0:16] = jnp.zeros((16, LN), F32)

    def body(s, _):
        o = pl.ds(pl.multiple_of(s * RB, RB), RB)
        for ch in range(w // CB):
            g = mm_tn(lhs[:, o], rhs[:, ch * CB * LN : (ch + 1) * CB * LN])
            for j in range(CB):
                F[pl.ds(lead + ch * CB + j, RB, stride=w), :] = g[:, j * LN : (j + 1) * LN]
        if lead:
            @pl.when(s == 0)
            def _():
                e = edge_at(base)
                r.E[e : e + 16 - lead] = F[lead:16]

        U = 768
        to = base - lead + s * step_rows

        def emit(t, _):
            r.FG[pl.ds(pl.multiple_of(to + t * U, 16), U)] = F[pl.ds(pl.multiple_of(t * U, 16), U)].astype(BF)
            return 0

        lax.fori_loop(0, step_rows // U, emit, 0)
        if lead:
            F[0:16] = F[step_rows : step_rows + 16]
        if hook is not None:
            hook(s)
        return 0

    lax.fori_loop(0, rows // RB, body, 0)
    if lead:
        e = edge_at(base + rows * w - lead)
        r.E[e : e + lead] = F[0:lead]


def edge_grads(r, which):
    base, rows = EDGES[which]
    at = 0
    for vbase, cnt in VECS:
        for k in range(cnt):
            row = vbase + k
            if base <= row < base + rows:
                name, j = vec_at(at + k)
                e = edge_at(row)
                r.E[e : e + 1] = r.VG[name : name + 1, j * LN : (j + 1) * LN]
        at += cnt
    if which == len(EDGES) - 1:
        e = edge_at(TOT)
        r.E[e : e + base + rows - TOT] = jnp.zeros((base + rows - TOT, LN), F32)
    e = edge_at(base)
    r.FG[base : base + rows] = r.E[e : e + rows].astype(BF)


def vec_at(row):
    for k, (_, n) in enumerate(VNAMES):
        if row < n // LN:
            return k, row
        row -= n // LN


class Refs:
    def __init__(self, **refs):
        self.__dict__.update(refs)


def relayout_vectors(p, r):
    at = 0
    for base, cnt in VECS:
        g_lo = base // 16
        g_hi = -(-(base + cnt) // 16)
        load_flat(p, r.slots, r.F, g_lo, g_hi)
        for k in range(cnt):
            name, j = vec_at(at + k)
            f = base - 16 * g_lo + k
            r.V[name : name + 1, j * LN : (j + 1) * LN] = r.F[f : f + 1]
        at += cnt


def relayout_matrix(p, r, name, W, RB):
    base, rows, w = {n: (b, k, c) for n, b, k, c in MATS}[name]
    for s in range(rows // RB):
        lo = base + s * RB * w
        g_lo = lo // 16
        load_flat(p, r.slots, r.F, g_lo, -(-(lo + RB * w) // 16))
        tile_rows(r.F, W, lo - 16 * g_lo, s * RB, RB, w)


def tile_rows(F, W, off, row, rows, w, RB=64):
    def body(t, _):
        q = pl.multiple_of(t * RB, RB)
        for j in range(w):
            W[pl.ds(row + q, RB), j * LN : (j + 1) * LN] = F[pl.ds(off + q * w + j, RB, stride=w), :].astype(BF)
        return 0

    lax.fori_loop(0, rows // RB, body, 0)


def forward_kernel(p, slots, length, tok, hcot, ncot, hidden, nested, wqkv, wo, w1, w2, V, VG, qkv, lse, mixed, xh1, rstd1, first_low, act, gd, res, d_outer, F, qb, xh2, rstd2):
    r = Refs(slots=slots, length=length[0], tok=tok, hcot=hcot, ncot=ncot, hidden=hidden, nested=nested, wqkv=wqkv, wo=wo, w1=w1, w2=w2, V=V, VG=VG, qkv=qkv, lse=lse, mixed=mixed, xh1=xh1, rstd1=rstd1, first_low=first_low, act=act, gd=gd, res=res, d_outer=d_outer, F=F, qb=qb, xh2=xh2, rstd2=rstd2)
    relayout_vectors(p, r)
    relayout_matrix(p, r, "wqkv", wqkv, 256)
    forward_qkv(r)
    lse[...] = jnp.zeros_like(lse)
    lax.fori_loop(0, H // 2, lambda hp, c: (forward_heads(r, hp), c)[1], 0)
    relayout_matrix(p, r, "wo", wo, 768)
    forward_first(r)
    relayout_matrix(p, r, "w1", w1, 256)
    lax.fori_loop(0, FF // UP, lambda j, c: (forward_up(r, j), c)[1], 0)
    relayout_matrix(p, r, "w2", w2, 768)
    tot = forward_second(r)
    d_pool = head(r, tot)
    backward_second(r, d_pool)


def forward_local(p, slots, length, tok, hcot, ncot):
    S = jax.ShapeDtypeStruct
    outs = [S((LEN, D), BF), S((1, 1728), F32), S((D, 3 * D), BF), S((D, D), BF), S((D, FF), BF), S((FF, D), BF), S((16, FF), F32), S((16, FF), F32), S((LEN, 3 * D), BF), S((LEN, LN), F32), S((LEN, D), BF), S((LEN, D), F32), S((LEN, 1), F32), S((LEN, D), BF), S((LEN, FF), BF), S((LEN, FF), BF), S((LEN, D), F32), S((LEN, D), BF)]
    vm = pl.BlockSpec(memory_space=pltpu.VMEM)
    sm = pl.BlockSpec(memory_space=pltpu.SMEM)
    return pl.pallas_call(
        functools.partial(forward_kernel, p),
        out_shape=outs,
        in_specs=[vm, sm, vm, vm, vm],
        scratch_shapes=[pltpu.VMEM((6144 + 64, LN), F32), pltpu.VMEM((1, 3 * D), F32), pltpu.VMEM((LEN, D), F32), pltpu.VMEM((LEN, 1), F32)],
        compiler_params=pltpu.CompilerParams(vmem_limit_bytes=60 << 20),
    )(slots, length, tok, hcot, ncot)


def backward_kernel(p, length, tok, V, VG0, qkv, lse, mixed, xh1, rstd1, first_low, act, gd, res, d_outer, wqkv, wo, w1, w2, igrad, FG, VG, d_branch, d_mixed, dqkv, F, E):
    r = Refs(length=length[0], tok=tok, V=V, VG=VG, qkv=qkv, lse=lse, mixed=mixed, xh1=xh1, rstd1=rstd1, first_low=first_low, act=act, gd=gd, res=igrad, d_outer=d_outer, wqkv=wqkv, wo=wo, w1=w1, w2=w2, FG=FG, d_branch=d_branch, d_mixed=d_mixed, dqkv=dqkv, F=F, E=E)
    VG[...] = VG0[...]
    igrad[...] = res[...]
    mats = {n: (b, k, c) for n, b, k, c in MATS}
    weight_grad(r, act, d_outer, *mats["w2"], RB=1024, CB=2)
    edge_grads(r, 3)
    lax.fori_loop(0, FF // UP, lambda j, c: (backward_act(r, j), c)[1], 0)
    weight_grad(r, first_low, gd, *mats["w1"])
    edge_grads(r, 2)
    backward_first(r)
    weight_grad(r, mixed, d_branch, *mats["wo"])
    edge_grads(r, 1)
    backward_mixed(r)
    lax.fori_loop(0, H // 2, lambda hp, c: (backward_heads(r, hp), c)[1], 0)
    weight_grad(r, tok, dqkv, *mats["wqkv"])
    edge_grads(r, 0)
    lax.fori_loop(0, LEN // 128, lambda b, c: (backward_tokens(r, b), c)[1], 0)


def backward_local(p, length, tok, V, VG, qkv, lse, mixed, xh1, rstd1, first_low, act, gd, res, d_outer, wqkv, wo, w1, w2):
    S = jax.ShapeDtypeStruct
    vm = pl.BlockSpec(memory_space=pltpu.VMEM)
    sm = pl.BlockSpec(memory_space=pltpu.SMEM)
    return pl.pallas_call(
        functools.partial(backward_kernel, p),
        out_shape=[S((LEN, D), F32), S((flat_rows(p), LN), BF)],
        in_specs=[sm] + [vm] * 17,
        scratch_shapes=[pltpu.VMEM((16, FF), F32), pltpu.VMEM((LEN, D), BF), pltpu.VMEM((LEN, D), BF), pltpu.VMEM((LEN, 3 * D), BF), pltpu.VMEM((6144 + 64, LN), F32), pltpu.VMEM((160, LN), F32)],
        compiler_params=pltpu.CompilerParams(vmem_limit_bytes=60 << 20),
    )(length, tok, V, VG, qkv, lse, mixed, xh1, rstd1, first_low, act, gd, res, d_outer, wqkv, wo, w1, w2)


class Gather:
    def __init__(self, p, G, ssem, rsem, gosem):
        self.p, self.G, self.ssem, self.rsem, self.gosem = p, G, ssem, rsem, gosem
        self.x, self.y, self.z, self.c = coords()
        x, y, z, c = self.x, self.y, self.z, self.c
        self.me = lin(x, y, z, c)
        half = p.slot // 32 * 16
        self.H = ((0, half), (half, p.slot - half), (0, p.slot))
        self.px, self.py, self.pc = dev(1 - x, y, z, c), dev(x, 1 - y, z, c), dev(x, y, z, 1 - c)

    def enter(self):
        x, y, z, c = self.x, self.y, self.z, self.c
        bar = pltpu.get_barrier_semaphore()

        def greet(to):
            pl.semaphore_signal(bar, inc=1, device_id=to, device_id_type=MESH)

        for to in (self.px, self.py, self.pc):
            greet(to)
        pl.when(z > 0)(lambda: greet(dev(x, y, z - 1, c)))
        pl.when(z < 3)(lambda: greet(dev(x, y, z + 1, c)))
        middle = (z > 0) & (z < 3)
        pl.when(middle)(lambda: pl.semaphore_wait(bar, 5))
        pl.when(jnp.logical_not(middle))(lambda: pl.semaphore_wait(bar, 4))

    def send(self, sl, h, to, t):
        r0, rn = self.H[h]
        ref = self.G.at[sl, pl.ds(r0, rn)]
        pltpu.make_async_remote_copy(src_ref=ref, dst_ref=ref, send_sem=self.ssem.at[sl, t], recv_sem=self.rsem.at[sl, h], device_id=to, device_id_type=MESH).start()

    def wait(self, sl, h, sem=None):
        r0, rn = self.H[h]
        ref = self.G.at[sl, pl.ds(r0, rn)]
        pltpu.make_async_copy(ref, ref, self.rsem.at[sl, h] if sem is None else sem).wait()

    def up(self, sl, h):
        pl.when(self.z < 3)(lambda: self.send(sl, h, dev(self.x, self.y, self.z + 1, self.c), 3))

    def down(self, sl, h):
        pl.when(self.z > 0)(lambda: self.send(sl, h, dev(self.x, self.y, self.z - 1, self.c), 4))

    def core(self, sl, h):
        self.send(sl, h, self.pc, 2)

    def xy(self, sl):
        self.send(sl, 0, self.px, 0)
        self.send(sl, 1, self.py, 1)
        self.send(sl, 1, self.px, 0)
        self.send(sl, 0, self.py, 1)

    def own(self, xy):
        for h in (0, 1):
            self.up(self.me, h)
            self.down(self.me, h)
        if xy:
            self.xy(self.me)
        for h in (0, 1):
            self.core(self.me, h)

    def own_line(self, k):
        self.at(k, lambda zq: self.xy(lin(self.x, self.y, zq, self.c)))

    def go(self, k):
        pl.semaphore_signal(self.gosem.at[k], inc=1, device_id=self.pc, device_id_type=MESH)

    def wait_go(self, k):
        pl.semaphore_wait(self.gosem.at[k], 1)

    def at(self, k, fn):
        if k == 0:
            fn(self.z)
            return
        pl.when(self.z - k >= 0)(lambda: fn(self.z - k))
        pl.when(self.z + k <= 3)(lambda: fn(self.z + k))

    def along_z(self, k, xy):
        x, y, z, c = self.x, self.y, self.z, self.c

        def from_level(zq, on):
            sl = lin(x, y, zq, c)
            self.wait(sl, 0)
            on(sl, 0)
            if xy:
                self.send(sl, 0, self.px, 0)
            self.core(sl, 0)
            self.wait(sl, 1)
            on(sl, 1)
            if xy:
                self.send(sl, 1, self.py, 1)
                self.send(sl, 1, self.px, 0)
                self.send(sl, 0, self.py, 1)
            self.core(sl, 1)

        pl.when(z - k >= 0)(lambda: from_level(z - k, self.up))
        pl.when(z + k <= 3)(lambda: from_level(z + k, self.down))

    def sides(self, k):
        x, y, c = self.x, self.y, self.c

        def fn(zq):
            sl = lin(1 - x, y, zq, c)
            self.wait(sl, 0)
            self.send(sl, 0, self.py, 1)
            self.core(sl, 0)
            sl = lin(x, 1 - y, zq, c)
            self.wait(sl, 1)
            self.send(sl, 1, self.px, 0)
            self.core(sl, 1)

        self.at(k, fn)

    def sides_rest(self, k):
        x, y, c = self.x, self.y, self.c

        def fn(zq):
            sl = lin(1 - x, y, zq, c)
            self.wait(sl, 1)
            self.core(sl, 1)
            sl = lin(x, 1 - y, zq, c)
            self.wait(sl, 0)
            self.core(sl, 0)

        self.at(k, fn)

    def diagonal(self, k):
        def fn(zq):
            sl = lin(1 - self.x, 1 - self.y, zq, self.c)
            for h in (0, 1):
                self.wait(sl, h)
                self.core(sl, h)

        self.at(k, fn)

    def from_sibling(self, xp):
        def body(fs, carry):
            for h in (0, 1):
                self.wait((2 * xp + 1 - self.c) * 8 + fs, h)
            return carry

        lax.fori_loop(0, 8, body, 0)

    def leave(self):
        x, y, z, c = self.x, self.y, self.z, self.c
        W = self.wait

        def body(zq, carry):
            sl = lin(x, y, zq, c)
            for t in (0, 1, 2):
                W(sl, 2, self.ssem.at[sl, t])
            pl.when((zq <= z) & (z < 3))(lambda: W(sl, 2, self.ssem.at[sl, 3]))
            pl.when((zq >= z) & (z > 0))(lambda: W(sl, 2, self.ssem.at[sl, 4]))
            sx = lin(1 - x, y, zq, c)
            W(sx, 0, self.ssem.at[sx, 1])
            W(sx, 2, self.ssem.at[sx, 2])
            sy = lin(x, 1 - y, zq, c)
            W(sy, 1, self.ssem.at[sy, 0])
            W(sy, 2, self.ssem.at[sy, 2])
            sd = lin(1 - x, 1 - y, zq, c)
            W(sd, 2, self.ssem.at[sd, 2])
            return carry

        lax.fori_loop(0, 4, body, 0)


FORWARD_OUT = ("hidden", "nested", "wqkv", "wo", "w1", "w2", "V", "VG", "qkv", "lse", "mixed", "xh1", "rstd1", "first_low", "act", "gd", "res", "d_outer")
FORWARD_SHAPES = dict(
    hidden=((LEN, D), jnp.bfloat16),
    nested=((1, 1728), jnp.float32),
    wqkv=((D, 3 * D), jnp.bfloat16),
    wo=((D, D), jnp.bfloat16),
    w1=((D, FF), jnp.bfloat16),
    w2=((FF, D), jnp.bfloat16),
    V=((16, FF), jnp.float32),
    VG=((16, FF), jnp.float32),
    qkv=((LEN, 3 * D), jnp.bfloat16),
    lse=((LEN, LN), jnp.float32),
    mixed=((LEN, D), jnp.bfloat16),
    xh1=((LEN, D), jnp.float32),
    rstd1=((LEN, 1), jnp.float32),
    first_low=((LEN, D), jnp.bfloat16),
    act=((LEN, FF), jnp.bfloat16),
    gd=((LEN, FF), jnp.bfloat16),
    res=((LEN, D), jnp.float32),
    d_outer=((LEN, D), jnp.bfloat16),
)


def own_slot(p, me, x_ref, F, G):
    start = me * p.sh
    r_first = start // LN
    s = start - r_first * LN
    r0 = r_first % 16
    lead = 32
    F[0 : lead + p.slot + 32] = jnp.zeros((lead + p.slot + 32, LN), F32)
    full = p.sh // LN
    rest = p.sh - full * LN
    F[lead : lead + full] = x_ref[: full * LN].astype(F32).reshape(full, LN)
    if rest:
        F[lead + full : lead + full + 1, :rest] = x_ref[full * LN :].astype(F32).reshape(1, rest)
    F[lead : lead + p.rows_in] = pltpu.roll(F[lead : lead + p.rows_in], s, 1)
    lane = lax.broadcasted_iota(jnp.int32, (p.slot, LN), 1)
    G[me] = jnp.where(lane >= s, F[pl.ds(lead - r0, p.slot), :], F[pl.ds(lead - 1 - r0, p.slot), :]).astype(BF)


def relayout_vector(p, r, which):
    at = sum(cnt for _, cnt in VECS[:which])
    base, cnt = VECS[which]
    g_lo = base // 16
    load_flat(p, r.slots, r.F, g_lo, -(-(base + cnt) // 16), base + cnt)
    for k in range(cnt):
        name, j = vec_at(at + k)
        f = base - 16 * g_lo + k
        r.V[name : name + 1, j * LN : (j + 1) * LN] = r.F[f : f + 1]


def relayout_rows(p, r, name, W, row, rows):
    base, _, w = {n: (b, k, c) for n, b, k, c in MATS}[name]
    lo = base + row * w
    g_lo = lo // 16
    load_flat(p, r.slots, r.F, g_lo, -(-(lo + rows * w) // 16), lo + rows * w)
    tile_rows(r.F, W, lo - 16 * g_lo, row, rows, w)


def gather_forward_kernel(p, x_ref, length, tok, hcot, ncot, *refs):
    n = len(FORWARD_OUT)
    outs = dict(zip(FORWARD_OUT, refs[:n]))
    loc = dict(zip(FORWARD_OUT, refs[n : 2 * n]))
    G, F, qb, xh2, rstd2, ssem, rsem, gosem, osem = refs[2 * n :]
    r = Refs(slots=G, length=length[0], tok=tok, hcot=hcot, ncot=ncot, F=F, qb=qb, xh2=xh2, rstd2=rstd2, **loc)
    g = Gather(p, G, ssem, rsem, gosem)
    own_slot(p, g.me, x_ref, F, G)
    g.enter()
    c0, c1 = g.c == 0, g.c == 1

    started = []

    def out(*names):
        for m in names:
            k = FORWARD_OUT.index(m)
            cp = pltpu.make_async_copy(loc[m], outs[m], osem.at[k])
            cp.start()
            started.append(cp)

    def part_rq_0():
        g.own(True)
        g.sides(0)
        g.go(0)
        g.along_z(1, True)
        g.sides(1)
        g.sides_rest(0)
        g.diagonal(0)
        g.go(1)
        g.along_z(2, True)
        g.sides(2)
        g.along_z(3, True)
        g.diagonal(1)
        g.sides_rest(1)
        g.sides(3)
        g.sides_rest(3)
        g.diagonal(2)
        g.sides_rest(2)
        g.diagonal(3)

    pl.when(c0)(part_rq_0)
    def part_rq_1():
        g.wait_go(0)
        g.own(False)
        g.wait_go(1)
        g.own_line(0)
        g.along_z(1, False)
        g.sides(0)
        g.along_z(2, False)
        g.own_line(1)
        g.along_z(3, False)
        g.own_line(3)
        g.own_line(2)
        g.from_sibling(0)
        g.sides(3)
        g.sides_rest(0)
        g.diagonal(0)

    pl.when(c1)(part_rq_1)
    relayout_vector(p, r, 0)
    for k in range(3):
        relayout_rows(p, r, "wqkv", r.wqkv, 256 * k, 256)
    out("wqkv")
    def part_qkv_1():
        g.from_sibling(1)
        g.sides(1)

    pl.when(c1)(part_qkv_1)
    forward_qkv(r)
    out("qkv")
    r.lse[...] = jnp.zeros_like(r.lse)

    def heads(hp, carry):
        def part_hd0_1():
            g.sides_rest(1)
            g.sides(2)
            g.sides_rest(3)

        pl.when((hp == 0) & c1)(part_hd0_1)
        def part_hd3_1():
            g.sides_rest(2)
            g.diagonal(3)

        pl.when((hp == 3) & c1)(part_hd3_1)
        def part_hd5_1():
            g.diagonal(1)

        pl.when((hp == 5) & c1)(part_hd5_1)
        forward_heads(r, hp)
        return carry

    lax.fori_loop(0, H // 2, heads, 0)
    out("lse", "mixed")
    def part_rw1b_1():
        g.diagonal(2)

    pl.when(c1)(part_rw1b_1)
    relayout_rows(p, r, "w1", r.w1, 448, 128)
    relayout_rows(p, r, "w1", r.w1, 576, 192)
    relayout_rows(p, r, "w2", r.w2, 0, 768)
    relayout_vector(p, r, 2)
    def part_rwo_0():
        g.from_sibling(0)

    pl.when(c0)(part_rwo_0)
    relayout_rows(p, r, "wo", r.wo, 0, 768)
    relayout_vector(p, r, 1)
    out("wo")
    forward_first(r)
    out("xh1", "rstd1", "first_low")
    def part_rw1a_0():
        g.from_sibling(1)

    pl.when(c0)(part_rw1a_0)
    relayout_rows(p, r, "w1", r.w1, 0, 256)
    relayout_rows(p, r, "w1", r.w1, 256, 192)
    out("w1")
    lax.fori_loop(0, FF // UP, lambda j, c: (forward_up(r, j), c)[1], 0)
    out("act", "gd")
    for k in range(1, 4):
        relayout_rows(p, r, "w2", r.w2, 768 * k, 768)
    relayout_vector(p, r, 3)
    out("w2", "V")
    tot = forward_second(r)
    out("hidden")
    d_pool = head(r, tot)
    out("nested")
    backward_second(r, d_pool)
    out("VG", "res", "d_outer")
    g.leave()
    for cp in started:
        cp.wait()


def gather_forward(p, shard, length, tok, hcot, ncot):
    S = jax.ShapeDtypeStruct
    vm = pl.BlockSpec(memory_space=pltpu.VMEM)
    sm = pl.BlockSpec(memory_space=pltpu.SMEM)
    hbm = pl.BlockSpec(memory_space=pl.ANY)
    VM = pltpu.VMEM
    DM = pltpu.SemaphoreType.DMA
    shapes = [FORWARD_SHAPES[m] for m in FORWARD_OUT]
    res = pl.pallas_call(
        functools.partial(gather_forward_kernel, p),
        out_shape=[S(*s) for s in shapes],
        in_specs=[vm, sm, vm, vm, vm],
        out_specs=[hbm] * len(shapes),
        scratch_shapes=[VM(*s) for s in shapes]
        + [VM((p.n, p.slot, LN), BF), VM((6144 + 64, LN), F32), VM((1, 3 * D), F32), VM((LEN, D), F32), VM((LEN, 1), F32)]
        + [DM((p.n, 5)), DM((p.n, 2)), pltpu.SemaphoreType.REGULAR((2,)), DM((len(shapes),))],
        compiler_params=pltpu.CompilerParams(collective_id=0, has_side_effects=True, vmem_limit_bytes=64 << 20),
    )(shard, length, tok, hcot, ncot)
    return dict(zip(FORWARD_OUT, res))


SCHEDULE = (
    (4, 1, 0, "diag", 1, 2, 1),
    (5, 1, 0, "diag", 1, 1, 1),
    (8, 1, 1, "yline", 1, 2, 1),
    (8, 1, 0, "xline", 1, 1, 1),
    (10, 1, 1, "yline", 1, 1, 1),
    (10, 1, 0, "diag", 1, 3, 1),
    (10, 0, 0, "diag", 1, 0, 1),
    (11, 0, 0, "diag", 1, 2, 2),
    (12, 1, 1, "diag", 0, 0, 1),
    (12, 0, 0, "diag", 1, 1, 1),
    (13, 1, 1, "diag", 0, 2, 1),
    (13, 1, 1, "diag", 0, 1, 1),
    (13, 1, 0, "yline", 0, 2, 1),
    (14, 1, 1, "diag", 0, 3, 1),
    (14, 0, 0, "xline", 1, 2, 1),
    (15, 0, 1, "yline", 1, 3, 1),
    (16, 1, 1, "xline", 0, 2, 1),
    (16, 0, 0, "xline", 1, 1, 1),
    (16, 1, 0, "yline", 0, 1, 1),
    (17, 1, 1, "own", 1, 1, 1),
    (17, 0, 1, "yline", 1, 2, 1),
    (18, 0, 0, "xline", 1, 0, 1),
    (18, 0, 1, "yline", 1, 1, 1),
    (18, 1, 1, "xline", 0, 1, 1),
    (18, 1, 0, "yline", 0, 3, 1),
    (19, 1, 0, "own", 0, 2, 1),
    (19, 1, 1, "xline", 0, 0, 1),
    (20, 0, 0, "yline", 0, 1, 1),
    (20, 0, 1, "diag", 0, 1, 2),
    (20, 0, 0, "yline", 0, 0, 1),
    (20, 0, 1, "own", 1, 2, 1),
    (20, 1, 0, "xline", 1, 2, 1),
    (21, 1, 1, "yline", 1, 0, 1),
    (21, 0, 1, "diag", 0, 0, 1),
    (21, 0, 1, "own", 1, 1, 1),
    (21, 1, 0, "diag", 1, 0, 1),
    (21, 0, 0, "own", 0, 1, 1),
    (21, 1, 0, "xline", 1, 3, 1),
    (22, 1, 0, "yline", 0, 0, 1),
    (22, 1, 0, "own", 0, 1, 1),
    (22, 1, 0, "own", 0, 0, 1),
    (22, 0, 0, "yline", 0, 2, 1),
    (22, 0, 1, "xline", 0, 1, 1),
    (22, 0, 0, "xline", 1, 3, 1),
    (22, 0, 1, "yline", 1, 0, 1),
    (22, 1, 1, "own", 1, 0, 1),
    (22, 0, 1, "xline", 0, 0, 1),
    (22, 0, 1, "xline", 0, 2, 1),
    (22, 0, 0, "own", 0, 0, 1),
    (22, 0, 0, "own", 0, 2, 1),
    (22, 0, 0, "yline", 0, 3, 1),
    (22, 0, 1, "diag", 0, 3, 1),
    (22, 0, 1, "own", 1, 0, 1),
    (22, 0, 1, "xline", 0, 3, 1),
    (22, 1, 0, "xline", 1, 0, 1),
    (22, 1, 1, "own", 1, 2, 1),
    (22, 1, 1, "xline", 0, 3, 1),
    (22, 1, 1, "yline", 1, 3, 1),
)


class Scatter:
    def __init__(self, p, FG, R, D0, D1, X, Y, Z, A, sems):
        self.p, self.FG, self.R, self.D0, self.D1, self.X, self.Y, self.Z, self.A = p, FG, R, D0, D1, X, Y, Z, A
        self.sib_s, self.sib_r, self.d_s, self.d_r, self.x_s, self.x_r, self.y_s, self.y_r, self.z_s, self.z_r = sems
        self.x, self.y, self.z, self.c = coords()
        x, y, z, c = self.x, self.y, self.z, self.c
        self.SL = p.slot
        self.half = p.slot // 32 * 16
        self.px, self.py, self.pc = dev(1 - x, y, z, c), dev(x, 1 - y, z, c), dev(x, y, z, 1 - c)

    def zq(self, b):
        d = lax.rem(b + 1, 4)
        z = self.z
        return lax.rem(z % 2 + d % 2, 2) + 2 * lax.rem(z // 2 + d // 2, 2)

    def enter(self):
        x, y, c = self.x, self.y, self.c
        barrier([self.px, self.py, self.pc] + [dev(x, y, self.zq(b), c) for b in range(3)])

    def row0(self, slot):
        return pl.multiple_of((slot * self.p.sh) // LN // 16 * 16, 16)

    def fg(self, slot):
        return self.row0(slot)

    def copy(self, src, dst, ssem, rsem, to):
        return pltpu.make_async_remote_copy(src_ref=src, dst_ref=dst, send_sem=ssem, recv_sem=rsem, device_id=to, device_id_type=MESH)

    def wait(self, ref, sem):
        pltpu.make_async_copy(ref, ref, sem).wait()

    def to_sibling(self, xp):
        def body(k, _):
            dp = 2 * xp + 1 - self.c
            i = 8 * xp + k
            self.copy(self.FG.at[pl.ds(self.row0(dp * 8 + k), self.SL)], self.R.at[i], self.sib_s.at[i], self.sib_r.at[i], self.pc).start()
            return 0

        lax.fori_loop(0, 8, body, 0)

    def add(self, dst, d0, rows, srcs, U=176):
        def body(t, _):
            r = pl.multiple_of(t * U, 16)
            v = None
            for s, s0 in srcs:
                e = s[pl.ds(s0 + r, U)].astype(F32)
                v = e if v is None else v + e
            dst[pl.ds(d0 + r, U)] = v.astype(dst.dtype)
            return 0

        lax.fori_loop(0, rows // U, body, 0)

    def have(self, xp, yq, zq):
        fs = zq * 2 + yq
        i = 8 * xp + fs
        self.wait(self.R.at[i], self.sib_r.at[i])
        return i, self.row0((2 * xp + self.c) * 8 + fs)

    def diag(self, xp, b):
        i, g = self.have(xp, 1 - self.y, self.zq(b))
        half, rest = self.half, self.SL - self.half
        R = self.R.at[i]
        self.add(R, 0, self.SL, [(self.FG, g), (R, 0)])
        self.copy(R.at[pl.ds(0, half)], self.D0.at[b], self.d_s.at[0, b], self.d_r.at[0, b], self.py).start()
        self.copy(R.at[pl.ds(half, rest)], self.D1.at[b], self.d_s.at[1, b], self.d_r.at[1, b], self.px).start()

    def xline(self, xp, b):
        i, g = self.have(xp, self.y, self.zq(b))
        half, rest = self.half, self.SL - self.half
        R = self.R.at[i]
        self.wait(self.D0.at[b], self.d_r.at[0, b])
        self.add(R, half, rest, [(self.FG, g + half), (R, half)])
        self.add(R, 0, half, [(self.FG, g), (R, 0), (self.D0.at[b], 0)])
        self.copy(R, self.X.at[b], self.x_s.at[b], self.x_r.at[b], self.px).start()

    def yline(self, xp, b):
        i, g = self.have(xp, 1 - self.y, self.zq(b))
        half, rest = self.half, self.SL - self.half
        R = self.R.at[i]
        self.wait(self.D1.at[b], self.d_r.at[1, b])
        self.add(R, 0, half, [(self.FG, g), (R, 0)])
        self.add(R, half, rest, [(self.FG, g + half), (R, half), (self.D1.at[b], 0)])
        self.copy(R, self.Y.at[b], self.y_s.at[b], self.y_r.at[b], self.py).start()

    def own(self, xp, b):
        i, g = self.have(xp, self.y, self.zq(b))
        R = self.R.at[i]
        self.wait(self.X.at[b], self.x_r.at[b])
        self.wait(self.Y.at[b], self.y_r.at[b])
        self.add(R, 0, self.SL, [(self.FG, g), (R, 0), (self.X.at[b], 0), (self.Y.at[b], 0)])
        self.copy(R, self.Z.at[b], self.z_s.at[b], self.z_r.at[b], dev(self.x, self.y, self.zq(b), self.c)).start()

    def last(self, xp, out):
        p, SL, A = self.p, self.SL, self.A
        i, g = self.have(xp, self.y, self.z)
        self.wait(self.X.at[3], self.x_r.at[3])
        self.wait(self.Y.at[3], self.y_r.at[3])
        for b in range(3):
            self.wait(self.Z.at[b], self.z_r.at[b])
        self.add(A, 0, SL, [(self.FG, g), (self.R.at[i], 0), (self.X.at[3], 0), (self.Y.at[3], 0)] + [(self.Z.at[b], 0) for b in range(3)])
        start = lin(self.x, self.y, self.z, self.c) * p.sh
        r_first = start // LN
        s = start - r_first * LN
        r0 = r_first % 16
        A[0:SL] = pltpu.roll(A[0:SL], lax.rem(LN - s, LN), 1)
        lane = lax.broadcasted_iota(jnp.int32, (p.rows_in, LN), 1)
        out[...] = jnp.where(lane < LN - s, A[pl.ds(r0, p.rows_in), :], A[pl.ds(r0 + 1, p.rows_in), :])

    def after(self, part, index=None):
        for c in (0, 1):
            for x in (0, 1):
                todo = [e for e in SCHEDULE if e[:3] == (part, c, x)]
                if todo:
                    here = (self.c == c) & (self.x == x)
                    if index is not None:
                        here = here & (index[0] == index[1])

                    def run(todo=todo):
                        for _, _, _, step, xp, b0, n in todo:
                            lax.fori_loop(b0, b0 + n, lambda b, k: (getattr(self, step)(xp, b), k)[1], 0)

                    pl.when(here)(run)

    def leave(self):
        for k in range(16):
            self.wait(self.R.at[k], self.sib_s.at[k])
        for b in range(4):
            self.wait(self.D0.at[b], self.d_s.at[0, b])
            self.wait(self.D1.at[b], self.d_s.at[1, b])
            self.wait(self.X.at[b], self.x_s.at[b])
            self.wait(self.Y.at[b], self.y_s.at[b])
        for b in range(3):
            self.wait(self.Z.at[b], self.z_s.at[b])


BACK_IN = ("act", "d_outer", "w2", "gd", "first_low", "w1", "res", "xh1", "rstd1", "V", "VG", "mixed", "wo", "qkv", "lse", "tok")


def backward_scatter_kernel(p, length, *refs):
    n = len(BACK_IN)
    src = dict(zip(BACK_IN, refs[:n]))
    wqkv_in = refs[n]
    igrad, out = refs[n + 1 : n + 3]
    loc = dict(zip(BACK_IN, refs[n + 3 : 2 * n + 3]))
    FG, F, E, R, D0, D1, X, Y, Z, lsem, osem, *sems = refs[2 * n + 3 :]
    r = Refs(length=length[0], FG=FG, F=F, E=E, **loc)
    r.dqkv, r.d_branch, r.d_mixed = r.act, r.first_low, r.d_outer
    sc = Scatter(p, FG, R, D0, D1, X, Y, Z, F, sems)
    mats = {m: (b, k, c) for m, b, k, c in MATS}
    loads = {m: pltpu.make_async_copy(src[m], loc[m], lsem.at[k]) for k, m in enumerate(BACK_IN)}
    for m in BACK_IN:
        loads[m].start()

    def need(*names):
        for m in names:
            loads[m].wait()

    sc.enter()
    c0, c1 = sc.c == 0, sc.c == 1
    x0, x1 = sc.x == 0, sc.x == 1

    def both(cond, fn):
        pl.when(cond)(fn)

    need("act", "d_outer", "VG")
    weight_grad(r, r.act, r.d_outer, *mats["w2"], RB=1024, CB=2)
    edge_grads(r, 3)
    both(c0, lambda: sc.to_sibling(1))
    sc.after(1)
    need("w2", "gd")

    def act_part(j, carry):
        backward_act(r, j)
        for k in range(4):
            sc.after(2 + k, (j, k))
        return carry

    lax.fori_loop(0, FF // UP, act_part, 0)
    q_loads = [pltpu.make_async_copy(wqkv_in.at[:, pl.ds(k * D, D)], r.w2.at[pl.ds(k * D, D)], lsem.at[n + k]) for k in range(3)]
    for q in q_loads:
        q.start()
    need("first_low")
    weight_grad(r, r.first_low, r.gd, *mats["w1"], hook=lambda i: [sc.after(6 + k, (i, k)) for k in range(2)])
    edge_grads(r, 2)
    both(c1, lambda: sc.to_sibling(1))
    sc.after(8)
    need("w1", "res", "xh1", "rstd1", "V")
    backward_first(r)
    sc.after(9)
    need("mixed")
    weight_grad(r, r.mixed, r.d_branch, *mats["wo"])
    edge_grads(r, 1)
    both(c0, lambda: sc.to_sibling(0))
    sc.after(10)
    need("wo")
    backward_mixed(r)
    sc.after(11)
    need("qkv", "lse")

    def heads(hp, carry):
        backward_heads(r, hp)
        for k in range(6):
            sc.after(12 + k, (hp, k))
        return carry

    lax.fori_loop(0, H // 2, heads, 0)
    need("tok")
    weight_grad(r, r.tok, r.dqkv, *mats["wqkv"], hook=lambda i: [sc.after(18 + k, (i, k)) for k in range(2)])
    edge_grads(r, 0)
    both(c1, lambda: sc.to_sibling(0))
    sc.after(20)
    for q in q_loads:
        q.wait()

    def tokens(b, carry):
        o = rows_of(b, LEN)
        v = r.res[o, :]
        for part in range(3):
            v = v + mm_nt(r.dqkv[o, part * D : (part + 1) * D], r.w2[part * D : (part + 1) * D, :])
        r.res[o, :] = v
        sc.after(21, (b, 0))
        return carry

    lax.fori_loop(0, 1, tokens, 0)
    grad_out = pltpu.make_async_copy(r.res, igrad, osem)
    grad_out.start()
    sc.after(22)
    both(x0, lambda: sc.last(0, out))
    both(x1, lambda: sc.last(1, out))
    sc.leave()
    grad_out.wait()


def backward_scatter(p, length, wqkv, **arrays):
    S = jax.ShapeDtypeStruct
    sm = pl.BlockSpec(memory_space=pltpu.SMEM)
    hbm = pl.BlockSpec(memory_space=pl.ANY)
    ins = [arrays[m] for m in BACK_IN]
    SL = p.slot
    half = SL // 32 * 16
    VM = pltpu.VMEM
    DM = pltpu.SemaphoreType.DMA
    igrad, o = pl.pallas_call(
        functools.partial(backward_scatter_kernel, p),
        out_shape=[S((LEN, D), F32), S((p.rows_in, LN), F32)],
        in_specs=[sm] + [hbm] * (len(ins) + 1),
        out_specs=[hbm, pl.BlockSpec(memory_space=pltpu.VMEM)],
        scratch_shapes=[VM(a.shape, a.dtype) for a in ins]
        + [VM((flat_rows(p), LN), BF), VM((6144 + 64, LN), F32), VM((160, LN), F32), VM((16, SL, LN), BF), VM((4, half, LN), BF), VM((4, SL - half, LN), BF), VM((4, SL, LN), BF), VM((4, SL, LN), BF), VM((3, SL, LN), BF)]
        + [DM((len(ins) + 3,)), DM, DM((16,)), DM((16,)), DM((2, 4)), DM((2, 4)), DM((4,)), DM((4,)), DM((4,)), DM((4,)), DM((3,)), DM((3,))],
        compiler_params=pltpu.CompilerParams(collective_id=1, has_side_effects=True, vmem_limit_bytes=64 << 20),
    )(length, *ins, wqkv)
    return igrad, o


def finish_copies(p, shards, hidden, igrad, nested):
    S = jax.ShapeDtypeStruct
    vm = pl.BlockSpec(memory_space=pltpu.VMEM)

    def kernel(a, b, c, d, a_out, b_out, c_out, d_out):
        a_out[...] = a[...].reshape(p.rows_in * LN)[: p.sh]
        b_out[...] = b[...]
        c_out[...] = c[...]
        d_out[...] = d[...]

    arrays = (shards, hidden, igrad, nested)
    return pl.pallas_call(
        kernel,
        out_shape=[S((p.sh,), F32)] + [S(a.shape, a.dtype) for a in arrays[1:]],
        in_specs=[vm] * 4,
        out_specs=[vm] * 4,
    )(*arrays)


def on_device(p, fast, tokens, lengths, weight_shards, hidden_cotangent, nested_cotangent):
    tok = tokens.reshape(LEN, D)
    hcot = hidden_cotangent.reshape(LEN, D)
    if fast:
        f = gather_forward(p, weight_shards, lengths, tok, hcot, nested_cotangent)
        igrad, shards = backward_scatter(p, lengths, tok=tok, **{m: f[m] for m in BACK_IN + ("wqkv",) if m != "tok"})
        shards, f["hidden"], igrad, f["nested"] = finish_copies(p, shards, f["hidden"], igrad, f["nested"])
    else:
        slots = lax.all_gather(build_slot(p, weight_shards, me_of), AX, axis=0)
        f = dict(zip(FORWARD_OUT, forward_local(p, slots, lengths, tok, hcot, nested_cotangent)))
        igrad, flat = backward_local(p, lengths, tok, *[f[m] for m in FORWARD_OUT[6:] + FORWARD_OUT[2:6]])
        shards = scatter_plain(p, flat)
    return (f["hidden"].reshape(1, LEN, D), f["nested"], igrad.reshape(1, LEN, D), shards)


def solution(mesh):
    in_specs = (
        P(("dp", "fsdp"), None, None),
        P(("dp", "fsdp")),
        P(("dp", "fsdp")),
        P(("dp", "fsdp"), None, None),
        P(("dp", "fsdp"), None),
    )
    out_specs = (
        P(("dp", "fsdp"), None, None),
        P(("dp", "fsdp"), None),
        P(("dp", "fsdp"), None, None),
        P(("dp", "fsdp")),
    )
    p = plan(mesh.shape["dp"] * mesh.shape["fsdp"])
    fast = (mesh.shape["dp"], mesh.shape["fsdp"]) == (4, 8)
    return jax.shard_map(
        functools.partial(on_device, p, fast), mesh=mesh, in_specs=in_specs, out_specs=out_specs, check_vma=False
    )
```
